32 devices in a mesh: dp: 16 (over z, y, x), phase: 2 (over core).
Axes of the slice: x: 2, y: 2, z: 4, core: 2. Of those that a mesh axis runs over, the one named last changes fastest.
Arguments:
- inputs: bfloat16 [2, 32, 256, 512], P('phase', 'dp'), may hold values from -6 to 6
- segments: int32 [32, 2, 256], P('dp'), may hold values from 0 to 3, never falling along the last dimension, each value on 1 to 128 neighbouring positions
- delete_target: int32 [32, 256], P('dp'), may hold values from 0 to 1
- place_target: int32 [32, 256], P('dp'), may hold values from 0 to 255
- token_target: int32 [32, 256], P('dp'), may hold values from 0 to 32767
- token_mask: int32 [32, 256], P('dp'), may hold values 0 or 1
- attention_in: bfloat16 [2, 512, 1536], P('phase'), may hold values from -0.25 to 0.25
- attention_out: bfloat16 [2, 512, 512], P('phase'), may hold values from -1.5 to 1.5
- feedforward_in: bfloat16 [2, 512, 2048], P('phase'), may hold values from -0.25 to 0.25
- feedforward_out: bfloat16 [2, 2048, 512], P('phase'), may hold values from -0.125 to 0.125
- norm_gain: float32 [2, 2, 512], P('phase'), may hold values from 0.5 to 1.5
- norm_bias: float32 [2, 2, 512], P('phase'), may hold values from -1.2 to 1.2
- cross_query: bfloat16 [512, 512], replicated, may hold values from -0.25 to 0.25
- cross_keyvalue: bfloat16 [512, 1024], replicated, may hold values from -0.25 to 0.25
- cross_out: bfloat16 [512, 512], replicated, may hold values from -1.5 to 1.5
- cross_gain: float32 [512], replicated, may hold values from 0.5 to 1.5
- cross_bias: float32 [512], replicated, may hold values from -1.2 to 1.2
- head_delete: bfloat16 [512, 2], replicated, may hold values from -0.25 to 0.25
- head_place: bfloat16 [1024, 256], replicated, may hold values from -0.1875 to 0.1875
- head_token: bfloat16 [512, 32768], replicated, may hold values from -0.25 to 0.25
Outputs:
- grad_inputs: float32 [2, 32, 256, 512], P('phase', 'dp')
- grad_attention_in: float32 [2, 512, 1536], P('phase', 'dp')
- grad_attention_out: float32 [2, 512, 512], P('phase', 'dp')
- grad_feedforward_in: float32 [2, 512, 2048], P('phase', 'dp')
- grad_feedforward_out: float32 [2, 2048, 512], P('phase', 'dp')
- grad_norm_gain: float32 [2, 2, 512], P('phase', None, 'dp')
- grad_norm_bias: float32 [2, 2, 512], P('phase', None, 'dp')
- grad_cross_query: float32 [512, 512], P('dp')
- grad_cross_keyvalue: float32 [512, 1024], P('dp')
- grad_cross_out: float32 [512, 512], P('dp')
- grad_cross_gain: float32 [512], P('dp')
- grad_cross_bias: float32 [512], P('dp')
- grad_head_delete: float32 [512, 2], P('dp')
- grad_head_place: float32 [1024, 256], P('dp')
- grad_head_token: float32 [512, 32768], P(None, 'dp')
The draws below stay inside these ranges and needn't reach their ends.
All inputs are finite; a program needn't handle non-finite values. No bound on the sum of `token_mask` on one device may be relied on, other than what follows from the above.
Results may differ from the reference program's by a relative error of at most 0.017.
Values may be sent and summed in bfloat16 or wider, within the bound.
A program may use at most 832 MiB of HBM per device.

```python
import math
import jax
import jax.numpy as jnp
import numpy as np
from jax import lax

D = 512
HEADS = 8
HEAD = 64
FF = 2048
VOCAB = 32768
MAXP = 256
ROW = 256
DOCS = 4
ROWS = 32
TOKENS = 8192


def place_ends(result, key, least, largest):
    shape = result.shape
    place = [jax.random.randint(jax.random.fold_in(key, axis), (), 0, shape[axis]) for axis in range(len(shape))]
    result = result.at[tuple(place)].set(least)
    longest = shape.index(max(shape))
    place[longest] = (place[longest] + 1) % shape[longest]
    return result.at[tuple(place)].set(largest)


def block_scale(own_key, dims, pieces, least, high):
    loudness = 1.0
    for axis_at, shards_of in pieces:
        heights = jax.random.uniform(jax.random.fold_in(jax.random.fold_in(own_key, 6), axis_at), (shards_of,), jnp.float32, least / len(pieces), high / len(pieces))
        loudness = loudness * jnp.repeat(jnp.exp(heights), dims[axis_at] // shards_of).reshape((-1,) + (1,) * (len(dims) - 1 - axis_at))
    return loudness


def rank_table(amount, slope):
    loads = [(1 << 20) // math.isqrt(rank ** slope) + 1 for rank in range(1, amount + 1)]
    width = 1 + sum(loads) // (1 << 30)
    return np.cumsum(np.array([max(1, weight // width) for weight in loads]))


def ranked_ids(key, dims, number_of, lean):
    table = rank_table(number_of, lean)
    ticket = jax.random.randint(jax.random.fold_in(key, 1), dims, 0, int(table[number_of - 1]))
    grade = jnp.searchsorted(jnp.asarray(table, jnp.int32), ticket, side="right")
    return jax.random.permutation(jax.random.fold_in(key, 2), number_of)[grade].astype(jnp.int32)


def split_up(count, total, most, slope):
    loads = [(1 << 20) // math.isqrt(grade ** slope) + 1 for grade in range(2, count + 1)]
    spare, counts = total - most - (count - 1), [1] * (count - 1)
    while spare > 0:
        movable = [i for i in range(count - 1) if counts[i] < most]
        whole, left = sum([loads[i] for i in movable]), spare
        for i in movable:
            extra = min(most - counts[i], max(1, left * loads[i] // whole), spare)
            counts[i] = counts[i] + extra
            spare = spare - extra
    return np.array([most] + counts)


def uneven(stream_key, amount, total, bound, slope):
    if amount == 2:
        one = jax.random.randint(stream_key, (), max(1, total - bound), min(bound, total - 1) + 1)
        return jnp.stack([one, total - one])
    sizes = jnp.asarray(split_up(amount, total, bound, slope), jnp.int32)
    couples = (amount - 1) // 2
    donor, taker = sizes[1:1 + 2 * couples:2], sizes[2:2 + 2 * couples:2]
    room = jnp.minimum(donor - 1, bound - taker)
    passed = jax.random.randint(jax.random.fold_in(stream_key, 1), (couples,), 0, 1 << 20) % (room + 1)
    sizes = sizes.at[1:1 + 2 * couples:2].set(donor - passed).at[2:2 + 2 * couples:2].set(taker + passed)
    return sizes[jax.random.permutation(jax.random.fold_in(stream_key, 2), amount)]


def centred(own_key, extent, spread, limit, pieces=(), kind=jnp.bfloat16):
    loudness = block_scale(own_key, extent, pieces, -0.22, 0.18) if pieces else 1.0
    array = jax.random.normal(own_key, extent, jnp.float32) * spread * loudness
    return jnp.minimum(jnp.maximum(array, -limit), limit).astype(kind)


def setup_inputs(seed: int = 0) -> dict:
    key_list = jax.random.split(jax.random.key(seed), 21)
    return {
        "inputs": centred(key_list[0], (2, ROWS, ROW, D), 1.0, 6.0, ((0, 2), (1, 16))),
        "segments": jax.vmap(lambda own: jnp.searchsorted(jnp.cumsum(uneven(own, DOCS, ROW, ROW // 2, 2)), jnp.arange(ROW), side="right"))(jax.random.split(key_list[1], ROWS * 2)).reshape((ROWS, 2, ROW)).astype(jnp.int32),
        "delete_target": place_ends(jax.random.randint(key_list[2], (ROWS, ROW), 0, 2), jax.random.fold_in(key_list[2], 1), 0, 1).astype(jnp.int32),
        "place_target": place_ends(ranked_ids(key_list[3], (ROWS, ROW), MAXP, 2), jax.random.fold_in(key_list[3], 3), 0, MAXP - 1).astype(jnp.int32),
        "token_target": place_ends(ranked_ids(key_list[4], (ROWS, ROW), VOCAB, 2), jax.random.fold_in(key_list[4], 3), 0, VOCAB - 1).astype(jnp.int32),
        "token_mask": place_ends((jax.random.randint(key_list[5], (ROWS, ROW), 0, 3) < 1).astype(jnp.int32), jax.random.fold_in(key_list[5], 1), 0, 1),
        "attention_in": centred(key_list[6], (2, D, 3 * D), D ** -0.5, 0.25, ((0, 2),)),
        "attention_out": centred(key_list[7], (2, D, D), (D // 32) ** -0.5, 1.5, ((0, 2),)),
        "feedforward_in": centred(key_list[8], (2, D, FF), D ** -0.5, 0.25, ((0, 2),)),
        "feedforward_out": centred(key_list[9], (2, FF, D), FF ** -0.5, 0.125, ((0, 2),)),
        "norm_gain": jnp.clip(1.0 + 0.1 * jax.random.normal(key_list[10], (2, 2, D), jnp.float32), 0.5, 1.5),
        "norm_bias": centred(key_list[11], (2, 2, D), 0.2, 1.2, ((0, 2),), jnp.float32),
        "cross_query": centred(key_list[12], (D, D), D ** -0.5, 0.25),
        "cross_keyvalue": centred(key_list[13], (D, 2 * D), D ** -0.5, 0.25),
        "cross_out": centred(key_list[14], (D, D), (D // 32) ** -0.5, 1.5),
        "cross_gain": jnp.clip(1.0 + 0.1 * jax.random.normal(key_list[15], (D,), jnp.float32), 0.5, 1.5),
        "cross_bias": centred(key_list[16], (D,), 0.2, 1.2, (), jnp.float32),
        "head_delete": centred(key_list[17], (D, 2), D ** -0.5, 0.25),
        "head_place": centred(key_list[18], (2 * D, MAXP), (2 * D) ** -0.5, 0.1875),
        "head_token": centred(key_list[19], (D, VOCAB), D ** -0.5, 0.25),
    }


HIGHEST = lax.Precision.HIGHEST
MASKED_SCORE = -1e+30
NORM_EPSILON = 1e-05

@jax.custom_vjp
def low(v):
    return lax.optimization_barrier(v.astype(jnp.bfloat16)).astype(jnp.float32)

@jax.custom_vjp
def low_back(v):
    return v

def low_keep(v):
    return (low(v), None)

def low_pass(kept, grad):
    return (grad,)

def back_keep(v):
    return (v, None)

def back_low(kept, grad):
    return (low(grad),)
low.defvjp(low_keep, low_pass)
low_back.defvjp(back_keep, back_low)

def matmul(left, right):
    return jnp.dot(left, right, precision=HIGHEST, preferred_element_type=jnp.float32)

def round_both(value):
    return low_back(low(value))

def layer_norm(residual, gain_vec, bias_vec):
    average = lax.optimization_barrier(jnp.mean(residual, axis=-1, keepdims=True))
    centered = residual - average
    variance = lax.optimization_barrier(jnp.mean(centered * centered, axis=-1, keepdims=True))
    return centered * lax.rsqrt(variance + NORM_EPSILON) * gain_vec + bias_vec

def attend(queries, key_part, value_part, allowed):
    length = queries.shape[0]
    query_heads = queries.reshape(length, HEADS, HEAD)
    key_heads = key_part.reshape(key_part.shape[0], HEADS, HEAD)
    value_heads = value_part.reshape(value_part.shape[0], HEADS, HEAD)
    scores = low_back(jnp.einsum('qhd,khd->hqk', query_heads, key_heads, precision=HIGHEST) * HEAD ** (-0.5))
    scores = jnp.where(allowed[None], scores, MASKED_SCORE)
    row_max = lax.optimization_barrier(jnp.max(scores, axis=-1, keepdims=True))
    exp_scores = jnp.exp(scores - row_max)
    prob_rows = low(exp_scores / lax.optimization_barrier(jnp.sum(exp_scores, axis=-1, keepdims=True)))
    mixed = jnp.einsum('hqk,khd->qhd', prob_rows, value_heads, precision=HIGHEST)
    return round_both(mixed.reshape(length, HEADS * HEAD))

def residual_block(states, segment_ids, own_layer, cross_terms):
    qkv_weight, mix_weight, up_weight, down_weight, gains, biases = own_layer
    feature_width = states.shape[1]
    allowed = segment_ids[:, None] == segment_ids[None, :]
    projected = round_both(matmul(states, qkv_weight))
    mixed = attend(projected[:, :feature_width], projected[:, feature_width:2 * feature_width], projected[:, 2 * feature_width:], allowed)
    after = layer_norm(states + low_back(matmul(mixed, mix_weight)), gains[0], biases[0])
    if cross_terms is not None:
        source, source_ids, query_weight, keyvalue_weight, cross_mix, cross_scale, cross_shift = cross_terms
        cross_allowed = segment_ids[:, None] == source_ids[None, :]
        cross_queries = round_both(matmul(low(after), query_weight))
        cross_keys = round_both(matmul(source, keyvalue_weight))
        cross_mixed = attend(cross_queries, cross_keys[:, :feature_width], cross_keys[:, feature_width:], cross_allowed)
        after = layer_norm(after + low_back(matmul(cross_mixed, cross_mix)), cross_scale, cross_shift)
    pre_act = low_back(matmul(low(after), up_weight))
    hidden = low(jax.nn.gelu(pre_act, approximate=True))
    return layer_norm(after + low_back(matmul(hidden, down_weight)), gains[1], biases[1])

def cross_entropy(logits, labels):
    row_max = lax.optimization_barrier(jnp.max(logits, axis=-1, keepdims=True))
    log_total = row_max[:, 0] + jnp.log(lax.optimization_barrier(jnp.sum(jnp.exp(logits - row_max), axis=-1)))
    classes = jnp.arange(logits.shape[-1], dtype=jnp.int32)
    picked = lax.optimization_barrier(jnp.sum(jnp.where(classes[None, :] == labels[:, None], logits, 0.0), axis=-1))
    return log_total - picked

def row_loss(params, packed_row):
    source_states, target_states, segment_ids, delete_rows, place_rows, token_rows, token_flags = packed_row
    qkv_all, mix_all, up_all, down_all, gain_all, bias_all, query_weight, keyvalue_weight, cross_mix, cross_scale, cross_shift, delete_weight, place_weight, token_weight = params
    encoded = residual_block(source_states, segment_ids[0], (qkv_all[0], mix_all[0], up_all[0], down_all[0], gain_all[0], bias_all[0]), None)
    source = round_both(encoded)
    final_out = residual_block(target_states, segment_ids[1], (qkv_all[1], mix_all[1], up_all[1], down_all[1], gain_all[1], bias_all[1]), (source, segment_ids[0], query_weight, keyvalue_weight, cross_mix, cross_scale, cross_shift))
    final_low = low(final_out)
    delete_loss = cross_entropy(low_back(matmul(final_low, delete_weight)), delete_rows)
    pair_rows = jnp.concatenate([final_low[:-1], final_low[1:]], axis=1)
    pair_valid = (segment_ids[1][:-1] == segment_ids[1][1:]).astype(jnp.float32)
    place_loss = cross_entropy(low_back(matmul(pair_rows, place_weight)), place_rows[:-1])
    token_loss = cross_entropy(low_back(matmul(final_low, token_weight)), token_rows)
    return jnp.sum(delete_loss) + jnp.sum(place_loss * pair_valid) + jnp.sum(token_loss * token_flags.astype(jnp.float32))

def reference(inputs, segments, delete_target, place_target, token_target, token_mask, attention_in, attention_out, feedforward_in, feedforward_out, norm_gain, norm_bias, cross_query, cross_keyvalue, cross_out, cross_gain, cross_bias, head_delete, head_place, head_token):
    params = tuple((weight_arr.astype(jnp.float32) for weight_arr in (attention_in, attention_out, feedforward_in, feedforward_out, norm_gain, norm_bias, cross_query, cross_keyvalue, cross_out, cross_gain, cross_bias, head_delete, head_place, head_token)))
    states = inputs.astype(jnp.float32)

    def total(states, params):
        checked = jax.checkpoint(row_loss)

        def step_row(running, packed_row):
            return (running + checked(params, packed_row), None)
        zero_start = jnp.zeros((), states.dtype)
        running, _ = lax.scan(step_row, zero_start, (states[0], states[1], segments, delete_target, place_target, token_target, token_mask))
        return running * float(TOKENS) ** (-0.5)
    total_loss, pull = jax.vjp(total, states, params)
    grad_states, grad_params = pull(jnp.ones_like(total_loss))
    return (grad_states, grad_params[0], grad_params[1], grad_params[2], grad_params[3], grad_params[4], grad_params[5], grad_params[6], grad_params[7], grad_params[8], grad_params[9], grad_params[10], grad_params[11], grad_params[12], grad_params[13])
```

```python
from functools import partial

import jax
import jax.numpy as jnp
from jax import lax
from jax.experimental import pallas as pl
from jax.experimental.pallas import tpu as pltpu
from jax.sharding import PartitionSpec as P

HEADS = 8
HEAD = 64
PAIR = 2 * HEAD
MASKED_SCORE = -1e30
NORM_EPSILON = 1e-05
GROUPS = 16
F32 = jnp.float32
BF16 = jnp.bfloat16
MESH = pl.DeviceIdType.MESH
VMEM = pltpu.VMEM
GELU_C = 0.7978845608028654
GELU_A = 0.044715


def mm(left, right):
    return jnp.dot(left, right, preferred_element_type=F32)


def mm_nt(left, right):
    return lax.dot_general(left, right, (((1,), (1,)), ((), ())), preferred_element_type=F32)


def mm_tn(left, right):
    return lax.dot_general(left, right, (((0,), (0,)), ((), ())), preferred_element_type=F32)


def norm_forward(residual, gain, bias):
    centered = residual - jnp.mean(residual, axis=-1, keepdims=True)
    variance = jnp.mean(centered * centered, axis=-1, keepdims=True)
    return centered * lax.rsqrt(variance + NORM_EPSILON) * gain + bias


def norm_back(residual, gain, grad_out):
    centered = residual - jnp.mean(residual, axis=-1, keepdims=True)
    variance = jnp.mean(centered * centered, axis=-1, keepdims=True)
    scale = lax.rsqrt(variance + NORM_EPSILON)
    unit = centered * scale
    grad_unit = grad_out * gain
    grad_gain = jnp.sum(grad_out * unit, axis=0, keepdims=True)
    grad_bias = jnp.sum(grad_out, axis=0, keepdims=True)
    grad_res = scale * (
        grad_unit
        - jnp.mean(grad_unit, axis=-1, keepdims=True)
        - unit * jnp.mean(grad_unit * unit, axis=-1, keepdims=True)
    )
    return grad_res, grad_gain, grad_bias


def gelu_both(pre):
    square = pre * pre
    bent = jnp.tanh(GELU_C * pre * (1.0 + GELU_A * square))
    half = 0.5 * (1.0 + bent)
    slope = half + (0.5 * GELU_C) * pre * (1.0 - bent * bent) * (1.0 + 3.0 * GELU_A * square)
    return pre * half, slope


def attend_forward(queries, keys, values, allowed, out_ref, totals_ref, rows):
    lane = lax.broadcasted_iota(jnp.int32, (1, PAIR), 1)
    for pair in range(HEADS // 2):
        q, k, v = queries(pair), keys(pair), values(pair)
        mixed = None
        for side in range(2):
            own = (lane < HEAD) if side == 0 else (lane >= HEAD)
            scores = mm_nt(k, jnp.where(own, q * HEAD ** (-0.5), 0))
            scores = jnp.where(allowed, scores, MASKED_SCORE)
            top = jnp.max(scores, axis=0, keepdims=True)
            weights = jnp.exp(scores - top)
            summed = jnp.sum(weights, axis=0, keepdims=True)
            probs = (weights * (1.0 / summed)).astype(BF16)
            totals_ref[2 * pair + side : 2 * pair + side + 1, :] = top + jnp.log(summed)
            part = mm_tn(probs, jnp.where(own, v, 0))
            mixed = part if mixed is None else mixed + part
        out_ref[rows, pair * PAIR : (pair + 1) * PAIR] = mixed.astype(BF16)


def attend_backward(
    queries, keys, values, grads, allowed, totals_ref, put_q, put_k, put_v, between=None
):
    lane = lax.broadcasted_iota(jnp.int32, (1, PAIR), 1)
    for pair in range(HEADS // 2):
        q, k, v, da = queries(pair), keys(pair), values(pair), grads(pair)
        grad_q = grad_k = grad_v = None
        for side in range(2):
            own = (lane < HEAD) if side == 0 else (lane >= HEAD)
            q_own = jnp.where(own, q * HEAD ** (-0.5), 0)
            da_own = jnp.where(own, da, 0)
            scores = jnp.where(allowed, mm_nt(k, q_own), MASKED_SCORE)
            probs = jnp.exp(scores - totals_ref[2 * pair + side : 2 * pair + side + 1, :])
            grad_probs = mm_nt(v, da_own)
            part_v = mm(probs.astype(BF16), da_own)
            shared = jnp.sum(probs * grad_probs, axis=0, keepdims=True)
            grad_scores = (probs * (grad_probs - shared)).astype(BF16)
            part_k = mm(grad_scores, q_own)
            part_q = mm_tn(grad_scores, jnp.where(own, k, 0))
            grad_q = part_q if grad_q is None else grad_q + part_q
            grad_k = part_k if grad_k is None else grad_k + part_k
            grad_v = part_v if grad_v is None else grad_v + part_v
        put_q(pair, (grad_q * HEAD ** (-0.5)).astype(BF16))
        put_k(pair, grad_k.astype(BF16))
        put_v(pair, grad_v.astype(BF16))
        if between is not None:
            between(pair)


def column(pair, offset=0):
    return slice(offset + pair * PAIR, offset + (pair + 1) * PAIR)


def put_shards(ref, first, grad):
    height = grad.shape[0] // GROUPS
    width = ref.shape[2]
    for block in range(grad.shape[1] // width):
        piece = grad[:, block * width : (block + 1) * width].astype(BF16)
        ref[:, first + block * height : first + (block + 1) * height, :] = piece.reshape(
            GROUPS, height, width
        )


def self_forward(
    x_ref, ids_ref, ids_row_ref, qkv_w_ref, mix_w_ref, gain_ref, bias_ref,
    qkv_ref, mixed_ref, res_ref, totals_ref, keep_ref, send_ref,
):
    phase = lax.axis_index("phase")
    count, length = ids_ref.shape[0], ids_ref.shape[1]
    width = x_ref.shape[1]
    for part in range(3):
        cols = slice(part * width, (part + 1) * width)
        qkv_ref[:, cols] = mm(x_ref[...], qkv_w_ref[:, cols]).astype(BF16)
    for row in range(count):
        rows = slice(row * length, (row + 1) * length)
        attend_forward(
            lambda pair: qkv_ref[rows, column(pair)],
            lambda pair: qkv_ref[rows, column(pair, width)],
            lambda pair: qkv_ref[rows, column(pair, 2 * width)],
            ids_ref[row] == ids_row_ref[row],
            mixed_ref, totals_ref.at[row], rows,
        )
    for row in range(count):
        rows = slice(row * length, (row + 1) * length)
        residual = x_ref[rows, :].astype(F32) + mm(mixed_ref[rows, :], mix_w_ref[...])
        res_ref[rows, :] = residual
        after = norm_forward(residual, gain_ref[0:1, :], bias_ref[0:1, :])

        @pl.when(phase == row)
        def _():
            keep_ref[...] = after

        @pl.when(phase != row)
        def _():
            send_ref[...] = after


def load_sided(phase, own_refs, other_refs, enc_refs, dec_refs, sems):
    for i, (own, other, enc, dec) in enumerate(zip(own_refs, other_refs, enc_refs, dec_refs)):
        @pl.when(phase == 0)
        def _():
            pltpu.make_async_copy(own, enc, sems.at[0, i]).start()
            pltpu.make_async_copy(other, dec, sems.at[1, i]).start()

        @pl.when(phase != 0)
        def _():
            pltpu.make_async_copy(other, enc, sems.at[0, i]).start()
            pltpu.make_async_copy(own, dec, sems.at[1, i]).start()

    def wait_enc(i):
        pltpu.make_async_copy(own_refs[i], enc_refs[i], sems.at[0, i]).wait()

    def wait_dec(i):
        pltpu.make_async_copy(own_refs[i], dec_refs[i], sems.at[1, i]).wait()

    return wait_enc, wait_dec


def feed_forward(middle, up_ref, down_ref, hidden_ref, slope_ref):
    width = middle.shape[1]
    low = middle.astype(BF16)
    total = middle
    for part in range(up_ref.shape[1] // width):
        cols = slice(part * width, (part + 1) * width)
        hidden, slope = gelu_both(mm(low, up_ref[:, cols]))
        hidden = hidden.astype(BF16)
        hidden_ref[:, cols] = hidden
        slope_ref[:, cols] = slope.astype(BF16)
        total = total + mm(hidden, down_ref[cols, :])
    return total


def feed_back(grad_res, middle_low, up_ref, down_ref, hidden_ref, slope_ref, put_up, put_down):
    width = grad_res.shape[1]
    branch = grad_res.astype(BF16)
    total = grad_res
    for part in range(up_ref.shape[1] // width):
        cols = slice(part * width, (part + 1) * width)
        put_down(part, mm_tn(hidden_ref[:, cols], branch))
        grad_hidden = mm_nt(branch, down_ref[cols, :])
        grad_pre = (grad_hidden * slope_ref[:, cols].astype(F32)).astype(BF16)
        put_up(part, mm_tn(middle_low, grad_pre))
        total = total + mm_nt(grad_pre, up_ref[:, cols])
    return total


def feed_puts(ref, parts):
    width = ref.shape[2]
    rows = width // GROUPS
    per, tall = GROUPS // parts, parts * rows

    def put_up(part, value):
        put_shards(ref, part * rows, value)

    def put_down(part, value):
        ref[part * per : (part + 1) * per, tall : 2 * tall, :] = value.astype(BF16).reshape(
            per, tall, width
        )

    return put_up, put_down


def class_grads(logits, labels, row_weight, valid):
    lane = lax.broadcasted_iota(jnp.int32, logits.shape, 1)
    logits = jnp.where(lane < valid, logits, -jnp.inf) if valid < logits.shape[1] else logits
    top = jnp.max(logits, axis=-1, keepdims=True)
    weights = jnp.exp(logits - top)
    probs = weights * (1.0 / jnp.sum(weights, axis=-1, keepdims=True))
    return (probs - (lane == labels).astype(F32)) * row_weight


def rows_forward(
    scale, keep_ref, recv_ref, ids_e_ref, ids_d_row_ref, targets_ref,
    up_own, up_other, down_own, down_other, norms_ref,
    cq_w_ref, ckv_w_ref, co_w_ref, cgain_ref, cbias_ref, delete_w_ref, place_w_ref,
    after_e_ref, res_e_ref, after_d_ref, ckv_ref, cq_ref, cmixed_ref, cres_ref, ctotals_ref,
    hid_e_ref, slope_e_ref, hid_d_ref, slope_d_ref, res_d_ref, src_ref,
    low_ref, grad_ref, grad_delete_ref, grad_place_ref,
    up_e, down_e, up_d, down_d, sems,
):
    phase = lax.axis_index("phase")
    width = keep_ref.shape[1]
    wait_enc, wait_dec = load_sided(
        phase, (up_own, down_own), (up_other, down_other), (up_e, down_e), (up_d, down_d), sems
    )

    @pl.when(phase == 0)
    def _():
        after_e_ref[...] = keep_ref[...]
        after_d_ref[...] = recv_ref[...]

    @pl.when(phase != 0)
    def _():
        after_e_ref[...] = recv_ref[...]
        after_d_ref[...] = keep_ref[...]

    wait_enc(0)
    wait_enc(1)
    residual = feed_forward(after_e_ref[...], up_e, down_e, hid_e_ref, slope_e_ref)
    res_e_ref[...] = residual
    src = norm_forward(residual, norms_ref[0:1, :], norms_ref[1:2, :]).astype(BF16)
    src_ref[...] = src
    for part in range(2):
        cols = slice(part * width, (part + 1) * width)
        ckv_ref[:, cols] = mm(src, ckv_w_ref[:, cols]).astype(BF16)
    cq_ref[...] = mm(after_d_ref[...].astype(BF16), cq_w_ref[...]).astype(BF16)
    attend_forward(
        lambda pair: cq_ref[:, column(pair)],
        lambda pair: ckv_ref[:, column(pair)],
        lambda pair: ckv_ref[:, column(pair, width)],
        ids_e_ref[...] == ids_d_row_ref[...],
        cmixed_ref, ctotals_ref, slice(None),
    )
    residual = after_d_ref[...] + mm(cmixed_ref[...], co_w_ref[...])
    cres_ref[...] = residual
    middle = norm_forward(residual, cgain_ref[...], cbias_ref[...])
    wait_dec(0)
    wait_dec(1)
    residual = feed_forward(middle, up_d, down_d, hid_d_ref, slope_d_ref)
    res_d_ref[...] = residual
    low = norm_forward(residual, norms_ref[2:3, :], norms_ref[3:4, :]).astype(BF16)
    low_ref[...] = low
    length = low.shape[0]
    targets = targets_ref[...]
    logits = mm(low, delete_w_ref[...])
    grads = class_grads(logits, targets[:, 0:1], scale, 2).astype(BF16)
    grad_delete_ref[...] = mm_tn(grads, low)[:8]
    grad_low = mm_nt(grads, delete_w_ref[...])
    logits = mm(low, place_w_ref[:width, :]) + pltpu.roll(
        mm(low, place_w_ref[width:, :]), length - 1, 0
    )
    weight = targets[:, 2:3].astype(F32) * scale
    grads = class_grads(logits, targets[:, 1:2], weight, logits.shape[1])
    later = pltpu.roll(grads, 1, 0).astype(BF16)
    grads = grads.astype(BF16)
    classes = grads.shape[1]
    for top, part in enumerate((grads, later)):
        part = mm_tn(low, part).astype(BF16).reshape(GROUPS // 2, 2, width // GROUPS, classes)
        at = slice(top * GROUPS // 2, (top + 1) * GROUPS // 2)
        for half in range(2):
            grad_place_ref[at, :, half * classes : (half + 1) * classes] = part[:, half]
    grad_low = grad_low + mm_nt(grads, place_w_ref[:width, :]) + mm_nt(later, place_w_ref[width:, :])
    grad_ref[...] = grad_low


def rows_backward(
    grad_low_ref, grad_token_ref, ids_e_ref, ids_d_row_ref,
    up_own, up_other, down_own, down_other, norms_ref,
    cq_w_ref, ckv_w_ref, co_w_ref, cgain_ref, cbias_ref,
    after_e_ref, res_e_ref, after_d_ref, ckv_ref, cq_ref, cmixed_ref, cres_ref, ctotals_ref,
    hid_e_ref, slope_e_ref, hid_d_ref, slope_d_ref, res_d_ref, src_ref, grad_place_ref,
    keep_ref, send_ref, own_ref, other_ref, cross_ref, vectors_ref,
    up_e, down_e, up_d, down_d, grad_e, grad_d, after_e_grad, after_d_grad, gq_ref, gckv_ref, sems, out_sems,
):
    phase = lax.axis_index("phase")
    width = grad_low_ref.shape[1]
    wait_enc, wait_dec = load_sided(
        phase, (up_own, down_own), (up_other, down_other), (up_e, down_e), (up_d, down_d), sems
    )
    grad_out = grad_low_ref[...] + grad_token_ref[...]
    grad_res, gain_grad, bias_grad = norm_back(res_d_ref[...], norms_ref[2:3, :], grad_out)
    vectors_ref[2:3, :] = gain_grad
    vectors_ref[3:4, :] = bias_grad
    cres = cres_ref[...]
    middle_low = norm_forward(cres, cgain_ref[...], cbias_ref[...]).astype(BF16)
    wait_dec(0)
    wait_dec(1)
    grad_middle = feed_back(grad_res, middle_low, up_d, down_d, hid_d_ref, slope_d_ref, *feed_puts(grad_d, 4))
    move_d = [
        pltpu.make_async_copy(grad_d, own_ref, out_sems.at[0]),
        pltpu.make_async_copy(grad_d, other_ref, out_sems.at[0]),
    ]

    @pl.when(phase == 0)
    def _():
        move_d[1].start()

    @pl.when(phase != 0)
    def _():
        move_d[0].start()

    grad_res, gain_grad, bias_grad = norm_back(cres, cgain_ref[...], grad_middle)
    vectors_ref[4:5, :] = gain_grad
    vectors_ref[5:6, :] = bias_grad
    branch = grad_res.astype(BF16)
    after_low = after_d_ref[...].astype(BF16)
    rows = width // GROUPS
    put_shards(cross_ref, 3 * rows, mm_tn(cmixed_ref[...], branch))
    grad_mixed = mm_nt(branch, co_w_ref[...]).astype(BF16)

    def put_q(pair, value):
        gq_ref[:, column(pair)] = value

    def put_k(pair, value):
        gckv_ref[:, column(pair)] = value

    def put_v(pair, value):
        gckv_ref[:, column(pair, width)] = value

    attend_backward(
        lambda pair: cq_ref[:, column(pair)],
        lambda pair: ckv_ref[:, column(pair)],
        lambda pair: ckv_ref[:, column(pair, width)],
        lambda pair: grad_mixed[:, column(pair)],
        ids_e_ref[...] == ids_d_row_ref[...],
        ctotals_ref, put_q, put_k, put_v,
    )
    grad_q = gq_ref[...]
    grad_kv = gckv_ref[...]
    put_shards(cross_ref, 0, mm_tn(after_low, grad_q))
    put_shards(cross_ref, rows, mm_tn(src_ref[...], grad_kv))
    cross_ref[:, 4 * rows : 5 * rows, :] = grad_place_ref[...]
    after_d_grad[...] = grad_res + mm_nt(grad_q, cq_w_ref[...])
    grad_src = mm_nt(grad_kv, ckv_w_ref[...]).astype(BF16).astype(F32)
    grad_res, gain_grad, bias_grad = norm_back(res_e_ref[...], norms_ref[0:1, :], grad_src)
    vectors_ref[0:1, :] = gain_grad
    vectors_ref[1:2, :] = bias_grad
    vectors_ref[6:8, :] = jnp.zeros((2, width), F32)
    wait_enc(0)
    wait_enc(1)
    after_e_grad[...] = feed_back(
        grad_res, after_e_ref[...].astype(BF16), up_e, down_e, hid_e_ref, slope_e_ref,
        *feed_puts(grad_e, 4),
    )
    move_e = [
        pltpu.make_async_copy(grad_e, own_ref, out_sems.at[1]),
        pltpu.make_async_copy(grad_e, other_ref, out_sems.at[1]),
    ]

    @pl.when(phase == 0)
    def _():
        move_e[0].start()
        keep_ref[...] = after_e_grad[...]
        send_ref[...] = after_d_grad[...]

    @pl.when(phase != 0)
    def _():
        move_e[1].start()
        keep_ref[...] = after_d_grad[...]
        send_ref[...] = after_e_grad[...]

    move_d[0].wait()
    move_e[0].wait()


def self_backward(
    keep_ref, recv_ref, x_ref, ids_ref, ids_row_ref, qkv_w_ref, mix_w_ref, gain_ref,
    qkv_ref, mixed_ref, res_ref, totals_ref,
    grad_x_ref, shards_ref, vectors_ref,
    after_grad, grad_qkv,
):
    phase = lax.axis_index("phase")
    count, length = ids_ref.shape[0], ids_ref.shape[1]
    width = x_ref.shape[1]
    for row in range(count):
        rows = slice(row * length, (row + 1) * length)

        @pl.when(phase == row)
        def _():
            after_grad[rows, :] = keep_ref[...]

        @pl.when(phase != row)
        def _():
            after_grad[rows, :] = recv_ref[...]

    grad_res, gain_grad, bias_grad = norm_back(res_ref[...], gain_ref[0:1, :], after_grad[...])
    vectors_ref[0:1, :] = gain_grad
    vectors_ref[1:2, :] = bias_grad
    vectors_ref[2:8, :] = jnp.zeros((6, width), F32)
    grad_x_ref[...] = grad_res
    branch = grad_res.astype(BF16)
    rows_each = width // GROUPS
    put_shards(shards_ref, 3 * rows_each, mm_tn(mixed_ref[...], branch))
    grad_mixed = mm_nt(branch, mix_w_ref[...]).astype(BF16)
    for row in range(count):
        rows = slice(row * length, (row + 1) * length)

        def put(offset):
            def store(pair, value):
                grad_qkv[rows, column(pair, offset)] = value

            return store

        attend_backward(
            lambda pair: qkv_ref[rows, column(pair)],
            lambda pair: qkv_ref[rows, column(pair, width)],
            lambda pair: qkv_ref[rows, column(pair, 2 * width)],
            lambda pair: grad_mixed[rows, column(pair)],
            ids_ref[row] == ids_row_ref[row],
            totals_ref.at[row], put(0), put(width), put(2 * width),
        )
    for part in range(3):
        cols = slice(part * width, (part + 1) * width)
        put_shards(shards_ref, part * rows_each, mm_tn(x_ref[...], grad_qkv[:, cols]))
    grad_x_ref[...] += mm_nt(grad_qkv[...], qkv_w_ref[...])


def token_forward(low_ref, weight_ref, probs_ref, totals_ref):
    logits = mm_nt(weight_ref[...], low_ref[...])
    top = jnp.max(logits, axis=0, keepdims=True)
    weights = jnp.exp(logits - top)
    summed = jnp.sum(weights, axis=0, keepdims=True)
    probs_ref[0] = (weights * (1.0 / summed)).astype(BF16)
    totals_ref[0] = top + jnp.log(summed)


def token_backward(
    scale, probs_ref, share_ref, label_ref, low_ref, weight_ref, grad_low_ref, grad_weight_ref, total
):
    step = pl.program_id(0)
    labels = label_ref[0]
    shape = probs_ref.shape[1:]
    offset = (lax.axis_index("dp") * 2 + lax.axis_index("phase")) * shape[0]
    chosen = lax.broadcasted_iota(jnp.int32, shape, 0) == labels - offset
    grads = probs_ref[0].astype(F32) * share_ref[0] - chosen.astype(F32)
    grads = (grads * jnp.where(labels >= 0, scale, 0.0)).astype(BF16)
    grad_low = mm_tn(grads, weight_ref[...]).astype(BF16)
    cap = grad_low_ref.shape[1]
    for block in range(grad_low_ref.shape[0]):
        grad_low_ref[block] = grad_low[block * cap : (block + 1) * cap]
    part = mm(grads, low_ref[...])

    @pl.when(step == 0)
    def _():
        total[...] = part

    @pl.when(step != 0)
    def _():
        total[...] += part

    @pl.when(step == pl.num_programs(0) - 1)
    def _():
        grad_weight_ref[...] = total[...].T


def place_of(dp):
    return lax.rem(dp, 2), lax.rem(dp // 2, 2), dp // 4


def index_of(x, y, z):
    return (z * 2 + y) * 2 + x


def greet(devices):
    barrier = pltpu.get_barrier_semaphore()
    for dp, phase in devices:
        pl.semaphore_signal(barrier, inc=1, device_id=(dp, phase), device_id_type=MESH)
    pl.semaphore_wait(barrier, len(devices))


def remote(src, dst, send, recv, device):
    return pltpu.make_async_remote_copy(
        src_ref=src, dst_ref=dst, send_sem=send, recv_sem=recv, device_id=device, device_id_type=MESH
    )


def gather_kernel(block_ref, out_ref, send, recv, local):
    dp, phase = lax.axis_index("dp"), lax.axis_index("phase")
    x, y, z = place_of(dp)
    x_first = phase == 0
    zs = [lax.rem(z + k, 4) for k in (1, 2, 3)]
    second = index_of(jnp.where(x_first, 1 - x, x), jnp.where(x_first, y, 1 - y), z)
    third = index_of(jnp.where(x_first, x, 1 - x), jnp.where(x_first, 1 - y, y), z)
    greet([(index_of(x, y, k), phase) for k in zs] + [(second, phase), (third, phase), (dp, 1 - phase)])
    own = pltpu.make_async_copy(block_ref, out_ref.at[phase, z, y, x], local.at[0])
    own.start()
    started = []
    first = []
    for k in range(3):
        copy = remote(
            block_ref, out_ref.at[phase, z, y, x], send.at[k], recv.at[k], (index_of(x, y, zs[k]), phase)
        )
        copy.start()
        first.append(copy)
    cross = []

    def to_core(slot, src):
        copy = remote(src, src, send.at[slot], recv.at[slot], (dp, 1 - phase))
        copy.start()
        cross.append(copy)

    mine = remote(block_ref, out_ref.at[phase, z, y, x], send.at[3], recv.at[3], (dp, 1 - phase))
    mine.start()
    cross.append(mine)
    own.wait()
    seconds = []
    x2 = jnp.where(x_first, 1 - x, x)
    y2 = jnp.where(x_first, y, 1 - y)
    x3 = jnp.where(x_first, x, 1 - x)
    y3 = jnp.where(x_first, 1 - y, y)

    def relay(slot, zz, yy, xx, device, into):
        src = out_ref.at[phase, zz, yy, xx]
        copy = remote(src, src, send.at[slot], recv.at[slot], (device, phase))
        copy.start()
        into.append(copy)

    thirds = []
    relay(4, z, y, x, second, seconds)
    relay(8, z, y, x, third, thirds)
    sources = [lax.rem(z + 4 - k, 4) for k in (1, 2, 3)]
    for k in range(3):
        first[k].wait_recv()
        relay(5 + k, sources[k], y, x, second, seconds)
        relay(9 + k, sources[k], y, x, third, thirds)
        to_core(16 + k, out_ref.at[phase, sources[k], y, x])
    order = [z] + sources
    for k in range(4):
        seconds[k].wait_recv()
        relay(12 + k, order[k], y2, x2, third, thirds)
        to_core(19 + k, out_ref.at[phase, order[k], y2, x2])
    for k in range(8):
        thirds_k = thirds[k]
        thirds_k.wait_recv()
        where_y, where_x = (y3, x3) if k < 4 else (1 - y, 1 - x)
        to_core(23 + k, out_ref.at[phase, order[k % 4], where_y, where_x])
    for copy in cross:
        copy.wait_recv()
    for copy in first + seconds + thirds + cross:
        copy.wait_send()


def gather_blocks(block, number):
    dp = lax.axis_size("dp")
    if dp != GROUPS:
        return lax.all_gather(lax.all_gather(block, "dp"), "phase")
    rows, width = block.shape
    out = pl.pallas_call(
        gather_kernel,
        out_shape=jax.ShapeDtypeStruct((2, 4, 2, 2, rows, width), block.dtype),
        in_specs=[pl.BlockSpec(memory_space=pl.ANY)],
        out_specs=pl.BlockSpec(memory_space=pl.ANY),
        scratch_shapes=[
            pltpu.SemaphoreType.DMA((31,)), pltpu.SemaphoreType.DMA((31,)), pltpu.SemaphoreType.DMA((1,)),
        ],
        compiler_params=pltpu.CompilerParams(collective_id=number, has_side_effects=True),
        name="gather_blocks",
    )(block)
    return out.reshape(2, dp, rows, width)


def scatter_kernel(part_ref, out_ref, core_in, third_out, third_in, second_out, second_in, z_out, z_in, send, recv):
    dp, phase = lax.axis_index("dp"), lax.axis_index("phase")
    x, y, z = place_of(dp)
    x_first = phase == 0
    x2 = jnp.where(x_first, 1 - x, x)
    y2 = jnp.where(x_first, y, 1 - y)
    x3 = jnp.where(x_first, x, 1 - x)
    y3 = jnp.where(x_first, 1 - y, y)
    second, third = index_of(x2, y2, z), index_of(x3, y3, z)
    zs = [lax.rem(z + k, 4) for k in (1, 2, 3)]
    greet([(index_of(x, y, k), phase) for k in zs] + [(second, phase), (third, phase), (dp, 1 - phase)])
    order = [lax.rem(z + k, 4) for k in (1, 2, 3, 0)]
    spots = (
        [(zz, 1 - y, 1 - x) for zz in order]
        + [(zz, y3, x3) for zz in order]
        + [(zz, y2, x2) for zz in order]
        + [(zz, y, x) for zz in order]
    )
    theirs = (
        [(zz, 1 - y, 1 - x) for zz in order]
        + [(zz, y2, x2) for zz in order]
        + [(zz, y3, x3) for zz in order]
        + [(zz, y, x) for zz in order]
    )
    cores = []
    for j in range(16):
        zz, yy, xx = theirs[j]
        copy = remote(part_ref.at[1 - phase, zz, yy, xx], core_in.at[j], send.at[j], recv.at[j], (dp, 1 - phase))
        copy.start()
        cores.append(copy)

    def both(j):
        zz, yy, xx = spots[j]
        cores[j].wait_recv()
        return part_ref[phase, zz, yy, xx].astype(F32) + core_in[j].astype(F32)

    thirds = []
    for j in range(8):
        third_out[j] = both(j).astype(BF16)
        copy = remote(third_out.at[j], third_in.at[j], send.at[16 + j], recv.at[16 + j], (third, phase))
        copy.start()
        thirds.append(copy)
    seconds = []
    for j in range(4):
        total = both(8 + j)
        thirds[j].wait_recv()
        second_out[j] = (total + third_in[j].astype(F32)).astype(BF16)
        copy = remote(second_out.at[j], second_in.at[j], send.at[24 + j], recv.at[24 + j], (second, phase))
        copy.start()
        seconds.append(copy)
    along = []
    for j in range(4):
        total = both(12 + j)
        thirds[4 + j].wait_recv()
        total = total + third_in[4 + j].astype(F32)
        seconds[j].wait_recv()
        total = total + second_in[j].astype(F32)
        if j < 3:
            z_out[j] = total.astype(BF16)
            copy = remote(z_out.at[j], z_in.at[j], send.at[28 + j], recv.at[28 + j], (index_of(x, y, zs[j]), phase))
            copy.start()
            along.append(copy)
        else:
            for copy in along:
                copy.wait_recv()
            out_ref[...] = total + z_in[0].astype(F32) + z_in[1].astype(F32) + z_in[2].astype(F32)
    for copy in cores + thirds + seconds + along:
        copy.wait_send()


def scatter_blocks(part, number):
    dp = lax.axis_size("dp")
    if dp != GROUPS:
        part = lax.psum_scatter(part.astype(F32), "phase", scatter_dimension=0, tiled=False)
        return lax.psum_scatter(part, "dp", scatter_dimension=0, tiled=False)
    rows, width = part.shape[2:]
    return pl.pallas_call(
        scatter_kernel,
        out_shape=jax.ShapeDtypeStruct((rows, width), F32),
        in_specs=[pl.BlockSpec(memory_space=VMEM)],
        out_specs=pl.BlockSpec(memory_space=VMEM),
        scratch_shapes=[VMEM((n, rows, width), BF16) for n in (16, 8, 8, 4, 4, 3, 3)]
        + [pltpu.SemaphoreType.DMA((31,)), pltpu.SemaphoreType.DMA((31,))],
        compiler_params=pltpu.CompilerParams(
            collective_id=number, has_side_effects=True, vmem_limit_bytes=48 * 1024 * 1024
        ),
        name="scatter_blocks",
    )(part.reshape(2, 4, 2, 2, rows, width))


def share_kernel(totals_ref, share_ref, near_in, joined, far_in, send, recv):
    dp, phase = lax.axis_index("dp"), lax.axis_index("phase")
    x, y, z = place_of(dp)
    near = [
        (index_of(lax.rem(x + a, 2), lax.rem(y + b, 2), z), lax.rem(phase + c, 2))
        for a in range(2) for b in range(2) for c in range(2) if a + b + c
    ]
    far = [(index_of(x, y, lax.rem(z + k, 4)), phase) for k in (1, 2, 3)]
    greet(near + far)

    def join(parts):
        top = parts[0]
        for part in parts[1:]:
            top = jnp.maximum(top, part)
        summed = jnp.exp(parts[0] - top)
        for part in parts[1:]:
            summed = summed + jnp.exp(part - top)
        return top + jnp.log(summed)

    copies = []
    for j, device in enumerate(near):
        copies.append(remote(totals_ref, near_in.at[j], send.at[j], recv.at[j], device))
        copies[-1].start()
    for copy in copies:
        copy.wait_recv()
    total = join([totals_ref[...]] + [near_in[j] for j in range(7)])
    joined[...] = total
    for j, device in enumerate(far):
        copies.append(remote(joined, far_in.at[j], send.at[7 + j], recv.at[7 + j], device))
        copies[-1].start()
    for copy in copies[7:]:
        copy.wait_recv()
    share_ref[...] = jnp.exp(totals_ref[...] - join([total] + [far_in[j] for j in range(3)]))
    for copy in copies:
        copy.wait_send()


def token_shares(totals, number):
    if lax.axis_size("dp") != GROUPS:
        top = lax.pmax(totals, ("dp", "phase"))
        return jnp.exp(totals - top) / lax.psum(jnp.exp(totals - top), ("dp", "phase"))
    flat = totals.reshape(-1, 128)
    rows = flat.shape[0]
    share = pl.pallas_call(
        share_kernel,
        out_shape=jax.ShapeDtypeStruct((rows, 128), F32),
        in_specs=[pl.BlockSpec(memory_space=VMEM)],
        out_specs=pl.BlockSpec(memory_space=VMEM),
        scratch_shapes=[
            VMEM((7, rows, 128), F32), VMEM((rows, 128), F32), VMEM((3, rows, 128), F32),
            pltpu.SemaphoreType.DMA((10,)), pltpu.SemaphoreType.DMA((10,)),
        ],
        compiler_params=pltpu.CompilerParams(collective_id=number, has_side_effects=True),
        name="token_shares",
    )(flat)
    return share.reshape(totals.shape)


class Exchange:
    def __init__(self, send, recv):
        self.dp, self.phase = lax.axis_index("dp"), lax.axis_index("phase")
        self.x, self.y, self.z = place_of(self.dp)
        x, y, z = self.x, self.y, self.z
        self.along_x, self.along_y = index_of(1 - x, y, z), index_of(x, 1 - y, z)
        self.zs = [lax.rem(z + k, 4) for k in (1, 2, 3)]
        self.send, self.recv, self.used, self.copies = send, recv, 0, []

    def greet(self):
        devices = [(index_of(self.x, self.y, k), self.phase) for k in self.zs]
        greet(devices + [(self.along_x, self.phase), (self.along_y, self.phase), (self.dp, 1 - self.phase)])

    def copy(self, src, dst, device):
        copy = remote(src, dst, self.send.at[self.used], self.recv.at[self.used], device)
        self.used += 1
        copy.start()
        self.copies.append(copy)
        return copy

    def to_core(self, src, dst):
        return self.copy(src, dst, (self.dp, 1 - self.phase))

    def first(self, batch, part):
        start, size, x_first = part
        rows = pl.ds(start, size)
        if x_first:
            src, device = batch.shards.at[:, :, 1 - self.x, rows], self.along_x
        else:
            src, device = batch.shards.at[:, 1 - self.y, :, rows], self.along_y
        return self.copy(src, batch.in1.at[:, :, rows], (device, self.phase))

    def second(self, batch, part):
        start, size, x_first = part
        rows = pl.ds(start, size)
        x, y, in1 = self.x, self.y, batch.in1
        other, device = (1 - y, self.along_y) if x_first else (1 - x, self.along_x)

        def add(i, _):
            zz, which = i // 2, lax.rem(i, 2)
            mine = batch.shards[zz, which, x, rows] if x_first else batch.shards[zz, y, which, rows]
            in1[zz, which, rows] = (in1[zz, which, rows].astype(F32) + mine.astype(F32)).astype(BF16)
            return 0

        lax.fori_loop(0, 8, add, 0)
        return self.copy(in1.at[:, other, rows], batch.in2.at[:, rows], (device, self.phase))

    def third(self, batch, part):
        start, size, x_first = part
        rows = pl.ds(start, size)
        own = self.y if x_first else self.x
        in1, in2 = batch.in1, batch.in2

        def add(zz, _):
            in2[zz, rows] = (in2[zz, rows].astype(F32) + in1[zz, own, rows].astype(F32)).astype(BF16)
            return 0

        lax.fori_loop(0, 4, add, 0)
        return [
            self.copy(in2.at[zz, rows], batch.in3.at[j, rows], (index_of(self.x, self.y, zz), self.phase))
            for j, zz in enumerate(self.zs)
        ]

    def last(self, batch, part, put):
        start, size, _ = part
        rows = pl.ds(start, size)
        in3 = batch.in3
        total = batch.in2[self.z, rows].astype(F32) + in3[0, rows].astype(F32)
        put(rows, total + in3[1, rows].astype(F32) + in3[2, rows].astype(F32))

    def finish(self):
        for copy in self.copies:
            copy.wait_send()


class Batch:
    def __init__(self, exchange, shards, in1, in2, in3, put, parts):
        self.exchange, self.shards, self.in1, self.in2, self.in3 = exchange, shards, in1, in2, in3
        self.put, self.parts = put, parts
        self.waits = [None] * len(parts)

    def from_core(self, copy, own):
        copy.wait_recv()
        shards = self.shards
        for i, part in enumerate(self.parts):
            rows = pl.ds(part[0], part[1])

            def add(j, _):
                at = (j // 4, lax.rem(j // 2, 2), lax.rem(j, 2), rows)
                shards[at] = (shards[at].astype(F32) + own[at].astype(F32)).astype(BF16)
                return 0

            lax.fori_loop(0, GROUPS, add, 0)
            self.waits[i] = self.exchange.first(self, part)

    def start(self):
        for i, part in enumerate(self.parts):
            self.waits[i] = self.exchange.first(self, part)

    def second(self):
        for i, part in enumerate(self.parts):
            self.waits[i].wait_recv()
            self.waits[i] = self.exchange.second(self, part)

    def third(self):
        for i, part in enumerate(self.parts):
            self.waits[i].wait_recv()
            self.waits[i] = self.exchange.third(self, part)

    def last(self):
        for i, part in enumerate(self.parts):
            for copy in self.waits[i]:
                copy.wait_recv()
            self.exchange.last(self, part, self.put)


FF_PARTS = ((0, 64, True), (64, 64, False))
CROSS_PARTS = ((0, 48, False), (48, 32, True))


def backward_kernel(
    grad_low_ref, grad_token_ref, ids_e_ref, ids_d_row_ref,
    up_own, up_other, down_own, down_other, norms_ref,
    cq_w_ref, ckv_w_ref, co_w_ref, cgain_ref, cbias_ref,
    after_e_ref, res_e_ref, after_d_ref, ckv_ref, cq_ref, cmixed_ref, cres_ref, ctotals_ref,
    hid_e_any, slope_e_any, hid_d_any, slope_d_any, res_d_ref, src_ref, grad_place_ref, grad_delete_ref,
    x_ref, ids_ref, ids_row_ref, qkv_w_ref, mix_w_ref, gain_ref,
    qkv_ref, mixed_ref, res_ref, totals_ref,
    grad_x_ref, red_ff_ref, red_attention_ref, red_cross_ref, vectors_ref,
    up, down, hid, slope, grad_d, grad_e, grad_c, grad_a, core_d, core_e, core_c,
    in1_d, in1_e, in1_c, in1_a, in2_d, in2_e, in2_c, in2_a, in3_d, in3_e, in3_c, in3_a,
    after_grads, after_in, gq_ref, gckv_ref, grad_qkv, sums, vec_own, vec_core, vec_1, vec_2, vec_3, vec_in,
    sems, send, recv,
):
    phase = lax.axis_index("phase")
    ex = Exchange(send, recv)
    ex.greet()
    width = grad_low_ref.shape[1]
    each = width // GROUPS
    length = grad_low_ref.shape[0]

    def load(own_side, i):
        hidden, slopes = (hid_e_any, slope_e_any) if own_side == 0 else (hid_d_any, slope_d_any)

        @pl.when(phase == own_side)
        def _():
            pltpu.make_async_copy(up_own, up, sems.at[i]).start()
            pltpu.make_async_copy(down_own, down, sems.at[i + 1]).start()

        @pl.when(phase != own_side)
        def _():
            pltpu.make_async_copy(up_other, up, sems.at[i]).start()
            pltpu.make_async_copy(down_other, down, sems.at[i + 1]).start()

        pltpu.make_async_copy(hidden, hid, sems.at[i + 2]).start()
        pltpu.make_async_copy(slopes, slope, sems.at[i + 3]).start()

    def loaded(i):
        for k, (src, dst) in enumerate(
            ((up_own, up), (down_own, down), (hid_e_any, hid), (slope_e_any, slope))
        ):
            pltpu.make_async_copy(src, dst, sems.at[i + k]).wait()

    def puts(ref):
        def put_up(part, value):
            ref[0, :, :, :, part * each : (part + 1) * each, :] = value.astype(BF16).reshape(
                4, 2, 2, each, width
            )

        def put_down(part, value):
            ref[1, part] = value.astype(BF16).reshape(2, 2, width // 4, width)

        return put_up, put_down

    batch_d = Batch(ex, core_d, in1_d, in2_d, in3_d, None, FF_PARTS)
    batch_e = Batch(ex, core_e, in1_e, in2_e, in3_e, None, FF_PARTS)
    batch_c = Batch(ex, core_c, in1_c, in2_c, in3_c, None, CROSS_PARTS)
    batch_a = Batch(ex, grad_a, in1_a, in2_a, in3_a, None, FF_PARTS)

    load(1, 0)
    grad_out = grad_low_ref[...] + grad_token_ref[...]
    grad_res, gain_grad, bias_grad = norm_back(res_d_ref[...], norms_ref[2:3, :], grad_out)
    vec_own[2:3, :] = gain_grad
    vec_own[3:4, :] = bias_grad
    vec_own[6:8, :] = grad_delete_ref[0:2, :]
    cres = cres_ref[...]
    middle_low = norm_forward(cres, cgain_ref[...], cbias_ref[...]).astype(BF16)
    loaded(0)
    grad_middle = feed_back(grad_res, middle_low, up, down, hid, slope, *puts(grad_d))
    from_d = ex.to_core(grad_d.at[1 - phase], core_d)
    load(0, 4)
    grad_res, gain_grad, bias_grad = norm_back(cres, cgain_ref[...], grad_middle)
    vec_own[4:5, :] = gain_grad
    vec_own[5:6, :] = bias_grad
    branch = grad_res.astype(BF16)

    def put_cross(first, value):
        half_rows = grad_c.shape[4]
        value = value.astype(BF16).reshape(4, 2, 2, each, width)
        for at in range(0, each, 16):
            half, row = divmod(first + at, half_rows)
            grad_c[half, :, :, :, row : row + 16, :] = value[:, :, :, at : at + 16, :]

    put_cross(3 * each, mm_tn(cmixed_ref[...], branch))
    put_cross(4 * each, grad_place_ref[...])
    grad_mixed = mm_nt(branch, co_w_ref[...]).astype(BF16)

    def put_q(pair, value):
        gq_ref[:, column(pair)] = value

    def put_k(pair, value):
        gckv_ref[:, column(pair)] = value

    def put_v(pair, value):
        gckv_ref[:, column(pair, width)] = value

    def between(pair):
        if pair == 2:
            batch_d.from_core(from_d, grad_d.at[phase])

    attend_backward(
        lambda pair: cq_ref[:, column(pair)],
        lambda pair: ckv_ref[:, column(pair)],
        lambda pair: ckv_ref[:, column(pair, width)],
        lambda pair: grad_mixed[:, column(pair)],
        ids_e_ref[...] == ids_d_row_ref[...],
        ctotals_ref, put_q, put_k, put_v, between,
    )
    grad_q = gq_ref[...]
    put_cross(0, mm_tn(after_d_ref[...].astype(BF16), grad_q))
    for part in range(2):
        put_cross((1 + part) * each, mm_tn(src_ref[...], gckv_ref[:, part * width : (part + 1) * width]))
    from_c = ex.to_core(grad_c.at[1 - phase], core_c)
    after_grads[1] = grad_res + mm_nt(grad_q, cq_w_ref[...])
    grad_src = mm_nt(gckv_ref[...], ckv_w_ref[...]).astype(BF16).astype(F32)
    grad_res, gain_grad, bias_grad = norm_back(res_e_ref[...], norms_ref[0:1, :], grad_src)
    vec_own[0:1, :] = gain_grad
    vec_own[1:2, :] = bias_grad
    from_v = ex.to_core(vec_own, vec_core)
    loaded(4)
    after_grads[0] = feed_back(
        grad_res, after_e_ref[...].astype(BF16), up, down, hid, slope, *puts(grad_e)
    )
    from_e = ex.to_core(grad_e.at[1 - phase], core_e)
    from_after = ex.to_core(after_grads.at[1 - phase], after_in)
    batch_c.from_core(from_c, grad_c.at[phase])
    first_vectors = []
    for turn in range(2):
        row = phase if turn == 0 else 1 - phase
        rows = pl.ds(pl.multiple_of(row * length, length), length)
        if turn == 0:
            grad_after = after_grads[phase]
        else:
            from_after.wait_recv()
            grad_after = after_in[...]
        grad_res, gain_grad, bias_grad = norm_back(res_ref[rows, :], gain_ref[0:1, :], grad_after)
        first_vectors.append((gain_grad, bias_grad))
        grad_x_ref[rows, :] = grad_res
        branch = grad_res.astype(BF16)
        if turn == 0:
            first_branch, first_rows = branch, rows
        grad_mixed = mm_nt(branch, mix_w_ref[...]).astype(BF16)

        def put(offset):
            def store(pair, value):
                grad_qkv[rows, column(pair, offset)] = value

            return store

        def between(pair):
            if turn == 0 and pair == 1:
                batch_e.from_core(from_e, grad_e.at[phase])
            if turn == 0 and pair == 3:
                batch_d.second()

        attend_backward(
            lambda pair: qkv_ref[rows, column(pair)],
            lambda pair: qkv_ref[rows, column(pair, width)],
            lambda pair: qkv_ref[rows, column(pair, 2 * width)],
            lambda pair: grad_mixed[:, column(pair)],
            ids_ref[row] == ids_row_ref[row],
            totals_ref.at[row], put(0), put(width), put(2 * width), between,
        )
    shape = (4, 2, 2, each, width)
    grad_mix = mm_tn(mixed_ref[first_rows, :], first_branch) + mm_tn(mixed_ref[rows, :], branch)
    grad_a[:, :, :, 3 * each :, :] = grad_mix.astype(BF16).reshape(shape)
    for part in range(3):
        cols = slice(part * width, (part + 1) * width)
        value = mm_tn(x_ref[...], grad_qkv[:, cols])
        grad_a[:, :, :, part * each : (part + 1) * each, :] = value.astype(BF16).reshape(shape)
    batch_a.start()
    batch_c.second()
    grad_x_ref[...] += mm_nt(grad_qkv[...], qkv_w_ref[...])
    from_v.wait_recv()
    vec_1[0:8, :] = vec_own[...] + vec_core[...]
    vec_1[8:9, :] = first_vectors[0][0] + first_vectors[1][0]
    vec_1[9:10, :] = first_vectors[0][1] + first_vectors[1][1]
    vec_1[10:16, :] = jnp.zeros((6, width), F32)
    vec_x = ex.copy(vec_1, vec_in.at[0], (ex.along_x, phase))

    def put_ff(half):
        def put(rows, value):
            sums[half, rows, :] = value

        return put

    def put_attention(rows, value):
        red_attention_ref[rows, :] = value

    cross_sum = red_cross_ref.at[phase]

    def put_cross_sum(rows, value):
        cross_sum[rows, :] = value

    batch_d.put, batch_e.put, batch_c.put, batch_a.put = put_ff(1), put_ff(0), put_cross_sum, put_attention
    batch_e.second()
    batch_d.third()
    vec_x.wait_recv()
    vec_2[...] = vec_1[...] + vec_in[0]
    vec_y = ex.copy(vec_2, vec_in.at[1], (ex.along_y, phase))
    batch_c.third()
    batch_a.second()
    vec_y.wait_recv()
    vec_3[...] = vec_2[...] + vec_in[1]
    vec_z = [
        ex.copy(vec_3, vec_in.at[2 + j], (index_of(ex.x, ex.y, zz), phase)) for j, zz in enumerate(ex.zs)
    ]
    batch_e.third()
    batch_d.last()
    batch_c.last()
    cross_copy = ex.to_core(cross_sum, red_cross_ref.at[phase])
    batch_a.third()
    batch_e.last()
    ff_copy = ex.to_core(sums.at[1 - phase], red_ff_ref.at[phase])
    red_ff_ref[phase] = sums[phase]
    for copy in vec_z:
        copy.wait_recv()
    vectors_ref[...] = vec_3[...] + vec_in[2] + vec_in[3] + vec_in[4]
    batch_a.last()
    cross_copy.wait_recv()
    ff_copy.wait_recv()
    ex.finish()


def unpack_kernel(ff_ref, attention_ref, cross_halves_ref, qkv_ref, mix_ref, up_ref, down_ref, cq_ref, ckv_ref, co_ref, place_ref):
    width = mix_ref.shape[1]
    high = mix_ref.shape[0]
    for block in range(up_ref.shape[1] // width):
        up_ref[:, block * width : (block + 1) * width] = ff_ref[0, block * high : (block + 1) * high, :]
    down_ref[...] = ff_ref[1]
    for block in range(3):
        qkv_ref[:, block * width : (block + 1) * width] = attention_ref[block * high : (block + 1) * high, :]
    mix_ref[...] = attention_ref[3 * high :, :]
    half_rows = cross_halves_ref.shape[1]

    def cross(start):
        half, row = divmod(start, half_rows)
        return cross_halves_ref[half, row : row + 16, :]

    for start in range(0, 5 * high, 16):
        part, inner = start // high, slice(start % high, start % high + 16)
        if part == 0:
            cq_ref[inner, :] = cross(start)
        elif part < 3:
            ckv_ref[inner, (part - 1) * width : part * width] = cross(start)
        elif part == 3:
            co_ref[inner, :] = cross(start)
        else:
            value = cross(start)
            cols = place_ref.shape[1]
            at = start % high
            place_ref[at : at + 16, :] = value[:, :cols]
            place_ref[high + at : high + at + 16, :] = value[:, cols:]


def whole(shape, dtype):
    return jax.ShapeDtypeStruct(shape, dtype)


def in_vmem(count):
    return [pl.BlockSpec(memory_space=VMEM)] * count


def swap(value):
    return lax.ppermute(value, "phase", [(0, 1), (1, 0)])


def unpacked(shards, height, columns):
    groups, rows, width = shards.shape
    blocks = columns // width
    parts = shards.reshape(groups, blocks, rows // blocks, width)
    return parts.transpose(0, 2, 1, 3).reshape(height, columns)


def token_head(numbers, cap, block_rows, low, flags, labels_all, flags_all, weight, weight_t, scale):
    length, width = low.shape
    dp = lax.axis_size("dp")
    shard = weight_t.shape[0]

    def choice(flags):
        place = jnp.cumsum(flags, axis=-1) - 1
        places = lax.broadcasted_iota(jnp.int32, flags.shape[:-1] + (cap, flags.shape[-1]), flags.ndim - 1)
        return (places == place[..., None, :]) & (flags[..., None, :] > 0)

    chosen = choice(flags)
    packed = mm(chosen.astype(BF16), low).astype(BF16)
    every = gather_blocks(packed, numbers[0]).reshape(2 * dp * cap, width)
    labels = jnp.max(jnp.where(choice(flags_all), labels_all[:, None, :], -1), axis=-1)
    labels = labels.reshape(dp, 2, cap).transpose(1, 0, 2).reshape(2 * dp * cap)
    tall = block_rows
    count = 2 * dp * cap // tall
    probs, totals = pl.pallas_call(
        token_forward,
        grid=(count,),
        out_shape=(whole((count, shard, tall), BF16), whole((count, 1, tall), F32)),
        in_specs=[
            pl.BlockSpec((tall, width), lambda i: (i, 0)),
            pl.BlockSpec((shard, width), lambda i: (0, 0)),
        ],
        out_specs=(
            pl.BlockSpec((1, shard, tall), lambda i: (i, 0, 0)),
            pl.BlockSpec((1, 1, tall), lambda i: (i, 0, 0)),
        ),
        compiler_params=pltpu.CompilerParams(vmem_limit_bytes=48 * 1024 * 1024),
        name="token_forward",
    )(every, weight_t)
    shares = token_shares(totals, numbers[1])
    each = tall // cap
    grad_low, grad_weight = pl.pallas_call(
        partial(token_backward, scale),
        grid=(count,),
        out_shape=(whole((2 * dp, cap, width), BF16), whole((width, shard), F32)),
        in_specs=[
            pl.BlockSpec((1, shard, tall), lambda i: (i, 0, 0)),
            pl.BlockSpec((1, 1, tall), lambda i: (i, 0, 0)),
            pl.BlockSpec((1, 1, tall), lambda i: (i, 0, 0)),
            pl.BlockSpec((tall, width), lambda i: (i, 0)),
            pl.BlockSpec((shard, width), lambda i: (0, 0)),
        ],
        out_specs=(
            pl.BlockSpec((each, cap, width), lambda i: (i, 0, 0)),
            pl.BlockSpec((width, shard), lambda i: (0, 0)),
        ),
        scratch_shapes=[VMEM((shard, width), F32)],
        compiler_params=pltpu.CompilerParams(vmem_limit_bytes=48 * 1024 * 1024),
        name="token_backward",
    )(probs, shares, labels.reshape(count, 1, tall), every, weight_t)
    back = scatter_blocks(grad_low.reshape(2, dp, cap, width), numbers[2])
    return mm_tn(chosen.astype(BF16), back.astype(BF16)), grad_weight


def on_device(
    inputs, segments, delete_target, place_target, token_target, token_mask,
    attention_in, attention_out, feedforward_in, feedforward_out, norm_gain, norm_bias,
    cross_query, cross_keyvalue, cross_out, cross_gain, cross_bias,
    head_delete, head_place, head_token,
):
    phase = lax.axis_index("phase")
    dp_index, dp = lax.axis_index("dp"), lax.axis_size("dp")
    count, length, width = inputs.shape[1:]
    assert count == 2
    hidden = feedforward_in.shape[2]
    scale = float(count * length * dp) ** (-0.5)
    any_space = pl.BlockSpec(memory_space=pl.ANY)
    params = pltpu.CompilerParams(vmem_limit_bytes=56 * 1024 * 1024)

    coded = jnp.where(token_mask == 1, token_target, -1)
    labels_all = lax.all_gather(coded, "dp", tiled=True)
    flags_all = (labels_all >= 0).astype(jnp.int32)

    def row_of(value):
        return lax.dynamic_index_in_dim(value, phase, 0, keepdims=False)

    own_norms = jnp.stack([norm_gain[0, 1], norm_bias[0, 1]])
    up_other, down_other = swap(feedforward_in[0]), swap(feedforward_out[0])
    other_norms = swap(own_norms)
    is_enc = phase == 0
    norms = jnp.concatenate(
        [jnp.where(is_enc, own_norms, other_norms), jnp.where(is_enc, other_norms, own_norms)]
    )
    ids = row_of(segments)
    own_ids = lax.dynamic_index_in_dim(segments, phase, 1, keepdims=False)
    states = inputs[0].reshape(count * length, width)

    qkv, mixed, res, totals, keep, send = pl.pallas_call(
        self_forward,
        out_shape=(
            whole((count * length, 3 * width), BF16),
            whole((count * length, width), BF16),
            whole((count * length, width), F32),
            whole((count, HEADS, length), F32),
            whole((length, width), F32),
            whole((length, width), F32),
        ),
        in_specs=in_vmem(7),
        out_specs=tuple(in_vmem(6)),
        compiler_params=params,
        name="self_forward",
    )(states, own_ids[:, :, None], own_ids[:, None, :], attention_in[0], attention_out[0], norm_gain[0], norm_bias[0])
    received = swap(send)

    ids_e, ids_d_row = ids[0][:, None], ids[1][None, :]
    pair_valid = jnp.concatenate([ids[1, :-1] == ids[1, 1:], jnp.zeros((1,), bool)])
    targets = jnp.stack(
        [row_of(delete_target), row_of(place_target), pair_valid.astype(jnp.int32)], axis=1
    )
    delete_weight = jnp.pad(head_delete, ((0, 0), (0, 126)))
    gain_row, bias_row = cross_gain[None, :], cross_bias[None, :]
    ff_scratch = [
        VMEM((width, hidden), BF16), VMEM((hidden, width), BF16),
        VMEM((width, hidden), BF16), VMEM((hidden, width), BF16),
    ]
    saved_shapes = (
        whole((length, width), F32),
        whole((length, width), F32),
        whole((length, width), F32),
        whole((length, 2 * width), BF16),
        whole((length, width), BF16),
        whole((length, width), BF16),
        whole((length, width), F32),
        whole((HEADS, length), F32),
        whole((length, hidden), BF16), whole((length, hidden), BF16),
        whole((length, hidden), BF16), whole((length, hidden), BF16),
        whole((length, width), F32),
        whole((length, width), BF16),
    )
    classes = head_place.shape[1]
    each = width // GROUPS
    outs = pl.pallas_call(
        partial(rows_forward, scale),
        out_shape=saved_shapes + (
            whole((length, width), BF16),
            whole((length, width), F32),
            whole((8, width), F32),
            whole((GROUPS, each, 2 * classes), BF16),
        ),
        in_specs=in_vmem(5) + [any_space] * 4 + in_vmem(8),
        out_specs=tuple(in_vmem(18)),
        scratch_shapes=ff_scratch + [pltpu.SemaphoreType.DMA((2, 2))],
        compiler_params=params,
        name="rows_forward",
    )(
        keep, received, ids_e, ids_d_row, targets,
        feedforward_in[0], up_other, feedforward_out[0], down_other, norms,
        cross_query, cross_keyvalue, cross_out, gain_row, bias_row, delete_weight, head_place,
    )
    saved = outs[:14]
    low, grad_low, grad_delete, grad_place = outs[14:]

    shard = head_token.shape[1] // (2 * dp)
    weight = lax.dynamic_slice_in_dim(head_token, (dp_index * 2 + phase) * shard, shard, 1)
    weight_t = weight.T
    flags = row_of(token_mask)

    def run_head(numbers, cap, block_rows):
        return token_head(numbers, cap, block_rows, low, flags, labels_all, flags_all, weight, weight_t, scale)

    small = length // 2
    fits = jnp.max(jnp.sum(flags_all, axis=1)) <= small
    grad_token, grad_weight = lax.cond(
        fits, lambda: run_head((1, 2, 3), small, 4 * small), lambda: run_head((4, 5, 6), length, 2 * length)
    )
    other_weight = swap(grad_weight)
    grad_head_token = jnp.concatenate(
        [jnp.where(is_enc, grad_weight, other_weight), jnp.where(is_enc, other_weight, grad_weight)], axis=1
    )

    each = width // GROUPS
    ff_rows = 2 * hidden // GROUPS
    if dp == GROUPS:
        half_rows = 5 * each // 2
        ff_half, attention_rows = ff_rows // 2, 4 * each
        rows_of = (ff_half, ff_half, half_rows, attention_rows)

        def shards(rows, *lead):
            return VMEM(lead + (rows, width), BF16)

        grad_states, red_ff, red_attention, red_cross, vectors = pl.pallas_call(
            backward_kernel,
            out_shape=(
                whole((count * length, width), F32), whole((2, ff_half, width), F32),
                whole((attention_rows, width), F32), whole((2, half_rows, width), F32), whole((16, width), F32),
            ),
            in_specs=in_vmem(4) + [any_space] * 4 + in_vmem(6 + 8) + [any_space] * 4 + in_vmem(14),
            out_specs=tuple(in_vmem(5)),
            scratch_shapes=[
                VMEM((width, hidden), BF16), VMEM((hidden, width), BF16),
                VMEM((length, hidden), BF16), VMEM((length, hidden), BF16),
                shards(ff_half, 2, 4, 2, 2), shards(ff_half, 2, 4, 2, 2), shards(half_rows, 2, 4, 2, 2),
                shards(attention_rows, 4, 2, 2),
                shards(ff_half, 4, 2, 2), shards(ff_half, 4, 2, 2), shards(half_rows, 4, 2, 2),
                *[shards(rows, 4, 2) for rows in rows_of],
                *[shards(rows, 4) for rows in rows_of],
                *[shards(rows, 3) for rows in rows_of],
                VMEM((2, length, width), F32), VMEM((length, width), F32),
                VMEM((length, width), BF16), VMEM((length, 2 * width), BF16), VMEM((count * length, 3 * width), BF16),
                VMEM((2, ff_half, width), F32),
                VMEM((8, width), F32), VMEM((8, width), F32),
                VMEM((16, width), F32), VMEM((16, width), F32), VMEM((16, width), F32), VMEM((5, 16, width), F32),
                pltpu.SemaphoreType.DMA((8,)), pltpu.SemaphoreType.DMA((56,)), pltpu.SemaphoreType.DMA((56,)),
            ],
            compiler_params=pltpu.CompilerParams(
                collective_id=0, has_side_effects=True, vmem_limit_bytes=60 * 1024 * 1024
            ),
            name="backward",
        )(
            grad_low, grad_token, ids_e, ids_d_row,
            feedforward_in[0], up_other, feedforward_out[0], down_other, norms,
            cross_query, cross_keyvalue, cross_out, gain_row, bias_row, *saved, grad_place, grad_delete,
            states, own_ids[:, :, None], own_ids[:, None, :], attention_in[0], attention_out[0], norm_gain[0],
            qkv, mixed, res, totals,
        )
        grads = pl.pallas_call(
            unpack_kernel,
            out_shape=(
                whole((each, 3 * width), F32), whole((each, width), F32), whole((each, hidden), F32),
                whole((hidden // GROUPS, width), F32), whole((each, width), F32), whole((each, 2 * width), F32),
                whole((each, width), F32), whole((2 * each, classes), F32),
            ),
            in_specs=in_vmem(3),
            out_specs=tuple(in_vmem(8)),
            compiler_params=params,
            name="unpack",
        )(red_ff, red_attention, red_cross)
        g_qkv, g_mix, g_up, g_down, g_cq, g_ckv, g_co, g_place = grads
        vectors = lax.dynamic_slice_in_dim(vectors, dp_index * each, each, 1)
        second = jnp.where(is_enc, vectors[0:2], vectors[2:4])
        vector_out = jnp.concatenate([vectors[8:9], second[0:1], vectors[9:10], second[1:2], vectors[4:8]])
    else:
        keep, send, ff_own, ff_other, cross_shards, vectors = pl.pallas_call(
            rows_backward,
            out_shape=(
                whole((length, width), F32), whole((length, width), F32),
                whole((GROUPS, ff_rows, width), BF16), whole((GROUPS, ff_rows, width), BF16),
                whole((GROUPS, 5 * each, width), BF16), whole((8, width), F32),
            ),
            in_specs=in_vmem(4) + [any_space] * 4 + in_vmem(6 + 14 + 1),
            out_specs=(in_vmem(2) + [any_space] * 2 + in_vmem(2)),
            scratch_shapes=ff_scratch + [
                VMEM((GROUPS, ff_rows, width), BF16), VMEM((GROUPS, ff_rows, width), BF16),
                VMEM((length, width), F32), VMEM((length, width), F32),
                VMEM((length, width), BF16), VMEM((length, 2 * width), BF16),
                pltpu.SemaphoreType.DMA((2, 2)), pltpu.SemaphoreType.DMA((2,)),
            ],
            compiler_params=params,
            name="rows_backward",
        )(
            grad_low, grad_token, ids_e, ids_d_row,
            feedforward_in[0], up_other, feedforward_out[0], down_other, norms,
            cross_query, cross_keyvalue, cross_out, gain_row, bias_row, *saved, grad_place,
        )
        received = swap(send)
        ff_received = swap(ff_other)
        half_rows = 5 * each // 2
        cross_keep = lax.dynamic_slice_in_dim(cross_shards, phase * half_rows, half_rows, 1)
        cross_received = swap(lax.dynamic_slice_in_dim(cross_shards, (1 - phase) * half_rows, half_rows, 1))
        shared = jnp.concatenate([vectors[4:6], grad_delete[:2]])
        norm_own = jnp.where(is_enc, vectors[0:2], vectors[2:4])
        norm_other = jnp.where(is_enc, vectors[2:4], vectors[0:2])
        vector_received = swap(jnp.concatenate([norm_other, shared]))
        vector_sums = jnp.concatenate([norm_own, shared]) + vector_received

        grad_states, attention_shards, first_vectors = pl.pallas_call(
            self_backward,
            out_shape=(
                whole((count * length, width), F32), whole((GROUPS, 4 * each, width), BF16), whole((8, width), F32),
            ),
            in_specs=in_vmem(12),
            out_specs=tuple(in_vmem(3)),
            scratch_shapes=[VMEM((count * length, width), F32), VMEM((count * length, 3 * width), BF16)],
            compiler_params=params,
            name="self_backward",
        )(
            keep, received, states, own_ids[:, :, None], own_ids[:, None, :], attention_in[0], attention_out[0],
            norm_gain[0], qkv, mixed, res, totals,
        )

        all_vectors = jnp.stack([
            first_vectors[0], vector_sums[0], first_vectors[1], vector_sums[1],
            vector_sums[2], vector_sums[3], vector_sums[4], vector_sums[5],
        ])
        ff_sum = (ff_own.astype(F32) + ff_received.astype(F32)).astype(BF16)
        cross_sum = (cross_keep.astype(F32) + cross_received.astype(F32)).astype(BF16)
        cross_other = swap(cross_sum)
        cross_all = jnp.concatenate(
            [jnp.where(is_enc, cross_sum, cross_other), jnp.where(is_enc, cross_other, cross_sum)], axis=1
        )
        ff_up = hidden // width * each

        def spread(value):
            return lax.psum_scatter(value.astype(F32), "dp", scatter_dimension=0, tiled=True)

        g_qkv = spread(unpacked(attention_shards[:, : 3 * each], width, 3 * width))
        g_mix = spread(unpacked(attention_shards[:, 3 * each :], width, width))
        g_up = spread(unpacked(ff_sum[:, :ff_up], width, hidden))
        g_down = spread(unpacked(ff_sum[:, ff_up:], hidden, width))
        g_cq = spread(unpacked(cross_all[:, :each], width, width))
        g_ckv = spread(unpacked(cross_all[:, each : 3 * each], width, 2 * width))
        g_co = spread(unpacked(cross_all[:, 3 * each : 4 * each], width, width))
        place = cross_all[:, 4 * each :].reshape(GROUPS, each, 2, classes)
        g_place = spread(place.transpose(0, 2, 1, 3).reshape(2 * width, classes))
        vector_out = lax.psum_scatter(all_vectors, "dp", scatter_dimension=1, tiled=True)
    return (
        grad_states.reshape(1, count, length, width),
        g_qkv[None], g_mix[None], g_up[None], g_down[None],
        vector_out[None, 0:2], vector_out[None, 2:4],
        g_cq, g_ckv, g_co, vector_out[4], vector_out[5], vector_out[6:8].T, g_place, grad_head_token,
    )


def solution(mesh):
    layer, row = P("phase", None, None), P("dp", None)
    return jax.shard_map(
        on_device,
        mesh=mesh,
        in_specs=(P("phase", "dp", None, None), P("dp", None, None), row, row, row, row)
        + (layer,) * 6 + (P(),) * 8,
        out_specs=(P("phase", "dp", None, None),) + (P("phase", "dp", None),) * 4
        + (P("phase", None, "dp"),) * 2 + (row,) * 3 + (P("dp"),) * 2 + (row,) * 2 + (P(None, "dp"),),
        check_vma=False,
    )
```

```python
from functools import partial

import jax
import jax.numpy as jnp
from jax import lax
from jax.experimental import pallas as pl
from jax.experimental.pallas import tpu as pltpu
from jax.sharding import PartitionSpec as P

HEADS = 8
HEAD = 64
PAIR = 2 * HEAD
MASKED_SCORE = -1e30
NORM_EPSILON = 1e-05
GROUPS = 16
F32 = jnp.float32
BF16 = jnp.bfloat16
MESH = pl.DeviceIdType.MESH
VMEM = pltpu.VMEM
GELU_C = 0.7978845608028654
GELU_A = 0.044715


def mm(left, right):
    return jnp.dot(left, right, preferred_element_type=F32)


def mm_nt(left, right):
    return lax.dot_general(left, right, (((1,), (1,)), ((), ())), preferred_element_type=F32)


def mm_tn(left, right):
    return lax.dot_general(left, right, (((0,), (0,)), ((), ())), preferred_element_type=F32)


def norm_forward(residual, gain, bias):
    centered = residual - jnp.mean(residual, axis=-1, keepdims=True)
    variance = jnp.mean(centered * centered, axis=-1, keepdims=True)
    return centered * lax.rsqrt(variance + NORM_EPSILON) * gain + bias


def norm_back(residual, gain, grad_out):
    centered = residual - jnp.mean(residual, axis=-1, keepdims=True)
    variance = jnp.mean(centered * centered, axis=-1, keepdims=True)
    scale = lax.rsqrt(variance + NORM_EPSILON)
    unit = centered * scale
    grad_unit = grad_out * gain
    grad_gain = jnp.sum(grad_out * unit, axis=0, keepdims=True)
    grad_bias = jnp.sum(grad_out, axis=0, keepdims=True)
    grad_res = scale * (
        grad_unit
        - jnp.mean(grad_unit, axis=-1, keepdims=True)
        - unit * jnp.mean(grad_unit * unit, axis=-1, keepdims=True)
    )
    return grad_res, grad_gain, grad_bias


def gelu_both(pre):
    square = pre * pre
    bent = jnp.tanh(GELU_C * pre * (1.0 + GELU_A * square))
    half = 0.5 * (1.0 + bent)
    slope = half + (0.5 * GELU_C) * pre * (1.0 - bent * bent) * (1.0 + 3.0 * GELU_A * square)
    return pre * half, slope


def attend_forward(queries, keys, values, allowed, out_ref, totals_ref, rows):
    lane = lax.broadcasted_iota(jnp.int32, (1, PAIR), 1)
    for pair in range(HEADS // 2):
        q, k, v = queries(pair), keys(pair), values(pair)
        mixed = None
        for side in range(2):
            own = (lane < HEAD) if side == 0 else (lane >= HEAD)
            scores = mm_nt(k, jnp.where(own, q * HEAD ** (-0.5), 0))
            scores = jnp.where(allowed, scores, MASKED_SCORE)
            top = jnp.max(scores, axis=0, keepdims=True)
            weights = jnp.exp(scores - top)
            summed = jnp.sum(weights, axis=0, keepdims=True)
            probs = (weights * (1.0 / summed)).astype(BF16)
            totals_ref[2 * pair + side : 2 * pair + side + 1, :] = top + jnp.log(summed)
            part = mm_tn(probs, jnp.where(own, v, 0))
            mixed = part if mixed is None else mixed + part
        out_ref[rows, pair * PAIR : (pair + 1) * PAIR] = mixed.astype(BF16)


def attend_backward(
    queries, keys, values, grads, allowed, totals_ref, put_q, put_k, put_v, between=None
):
    lane = lax.broadcasted_iota(jnp.int32, (1, PAIR), 1)
    for pair in range(HEADS // 2):
        q, k, v, da = queries(pair), keys(pair), values(pair), grads(pair)
        grad_q = grad_k = grad_v = None
        for side in range(2):
            own = (lane < HEAD) if side == 0 else (lane >= HEAD)
            q_own = jnp.where(own, q * HEAD ** (-0.5), 0)
            da_own = jnp.where(own, da, 0)
            scores = jnp.where(allowed, mm_nt(k, q_own), MASKED_SCORE)
            probs = jnp.exp(scores - totals_ref[2 * pair + side : 2 * pair + side + 1, :])
            grad_probs = mm_nt(v, da_own)
            part_v = mm(probs.astype(BF16), da_own)
            shared = jnp.sum(probs * grad_probs, axis=0, keepdims=True)
            grad_scores = (probs * (grad_probs - shared)).astype(BF16)
            part_k = mm(grad_scores, q_own)
            part_q = mm_tn(grad_scores, jnp.where(own, k, 0))
            grad_q = part_q if grad_q is None else grad_q + part_q
            grad_k = part_k if grad_k is None else grad_k + part_k
            grad_v = part_v if grad_v is None else grad_v + part_v
        put_q(pair, (grad_q * HEAD ** (-0.5)).astype(BF16))
        put_k(pair, grad_k.astype(BF16))
        put_v(pair, grad_v.astype(BF16))
        if between is not None:
            between(pair)


def column(pair, offset=0):
    return slice(offset + pair * PAIR, offset + (pair + 1) * PAIR)


def put_shards(ref, first, grad):
    height = grad.shape[0] // GROUPS
    width = ref.shape[2]
    for block in range(grad.shape[1] // width):
        piece = grad[:, block * width : (block + 1) * width].astype(BF16)
        ref[:, first + block * height : first + (block + 1) * height, :] = piece.reshape(
            GROUPS, height, width
        )


def self_forward(
    x_ref, ids_ref, ids_row_ref, qkv_w_ref, mix_w_ref, gain_ref, bias_ref,
    qkv_ref, mixed_ref, res_ref, totals_ref, keep_ref, send_ref,
):
    phase = lax.axis_index("phase")
    count, length = ids_ref.shape[0], ids_ref.shape[1]
    width = x_ref.shape[1]
    for part in range(3):
        cols = slice(part * width, (part + 1) * width)
        qkv_ref[:, cols] = mm(x_ref[...], qkv_w_ref[:, cols]).astype(BF16)
    for row in range(count):
        rows = slice(row * length, (row + 1) * length)
        attend_forward(
            lambda pair: qkv_ref[rows, column(pair)],
            lambda pair: qkv_ref[rows, column(pair, width)],
            lambda pair: qkv_ref[rows, column(pair, 2 * width)],
            ids_ref[row] == ids_row_ref[row],
            mixed_ref, totals_ref.at[row], rows,
        )
    for row in range(count):
        rows = slice(row * length, (row + 1) * length)
        residual = x_ref[rows, :].astype(F32) + mm(mixed_ref[rows, :], mix_w_ref[...])
        res_ref[rows, :] = residual
        after = norm_forward(residual, gain_ref[0:1, :], bias_ref[0:1, :])

        @pl.when(phase == row)
        def _():
            keep_ref[...] = after

        @pl.when(phase != row)
        def _():
            send_ref[...] = after


def load_sided(phase, own_refs, other_refs, enc_refs, dec_refs, sems):
    for i, (own, other, enc, dec) in enumerate(zip(own_refs, other_refs, enc_refs, dec_refs)):
        @pl.when(phase == 0)
        def _():
            pltpu.make_async_copy(own, enc, sems.at[0, i]).start()
            pltpu.make_async_copy(other, dec, sems.at[1, i]).start()

        @pl.when(phase != 0)
        def _():
            pltpu.make_async_copy(other, enc, sems.at[0, i]).start()
            pltpu.make_async_copy(own, dec, sems.at[1, i]).start()

    def wait_enc(i):
        pltpu.make_async_copy(own_refs[i], enc_refs[i], sems.at[0, i]).wait()

    def wait_dec(i):
        pltpu.make_async_copy(own_refs[i], dec_refs[i], sems.at[1, i]).wait()

    return wait_enc, wait_dec


def feed_forward(middle, up_ref, down_ref, hidden_ref, slope_ref):
    width = middle.shape[1]
    low = middle.astype(BF16)
    total = middle
    for part in range(up_ref.shape[1] // width):
        cols = slice(part * width, (part + 1) * width)
        hidden, slope = gelu_both(mm(low, up_ref[:, cols]))
        hidden = hidden.astype(BF16)
        hidden_ref[:, cols] = hidden
        slope_ref[:, cols] = slope.astype(BF16)
        total = total + mm(hidden, down_ref[cols, :])
    return total


def feed_back(grad_res, middle_low, up_ref, down_ref, hidden_ref, slope_ref, put_up, put_down):
    width = grad_res.shape[1]
    branch = grad_res.astype(BF16)
    total = grad_res
    for part in range(up_ref.shape[1] // width):
        cols = slice(part * width, (part + 1) * width)
        put_down(part, mm_tn(hidden_ref[:, cols], branch))
        grad_hidden = mm_nt(branch, down_ref[cols, :])
        grad_pre = (grad_hidden * slope_ref[:, cols].astype(F32)).astype(BF16)
        put_up(part, mm_tn(middle_low, grad_pre))
        total = total + mm_nt(grad_pre, up_ref[:, cols])
    return total


def feed_puts(ref, parts):
    width = ref.shape[2]
    rows = width // GROUPS
    per, tall = GROUPS // parts, parts * rows

    def put_up(part, value):
        put_shards(ref, part * rows, value)

    def put_down(part, value):
        ref[part * per : (part + 1) * per, tall : 2 * tall, :] = value.astype(BF16).reshape(
            per, tall, width
        )

    return put_up, put_down


def class_grads(logits, labels, row_weight, valid):
    lane = lax.broadcasted_iota(jnp.int32, logits.shape, 1)
    logits = jnp.where(lane < valid, logits, -jnp.inf) if valid < logits.shape[1] else logits
    top = jnp.max(logits, axis=-1, keepdims=True)
    weights = jnp.exp(logits - top)
    probs = weights * (1.0 / jnp.sum(weights, axis=-1, keepdims=True))
    return (probs - (lane == labels).astype(F32)) * row_weight


def rows_forward(
    scale, keep_ref, recv_ref, ids_e_ref, ids_d_row_ref, targets_ref,
    up_own, up_other, down_own, down_other, norms_ref,
    cq_w_ref, ckv_w_ref, co_w_ref, cgain_ref, cbias_ref, delete_w_ref, place_w_ref,
    after_e_ref, res_e_ref, after_d_ref, ckv_ref, cq_ref, cmixed_ref, cres_ref, ctotals_ref,
    hid_e_ref, slope_e_ref, hid_d_ref, slope_d_ref, res_d_ref, src_ref,
    low_ref, grad_ref, grad_delete_ref, grad_place_ref,
    up_e, down_e, up_d, down_d, sems,
):
    phase = lax.axis_index("phase")
    width = keep_ref.shape[1]
    wait_enc, wait_dec = load_sided(
        phase, (up_own, down_own), (up_other, down_other), (up_e, down_e), (up_d, down_d), sems
    )

    @pl.when(phase == 0)
    def _():
        after_e_ref[...] = keep_ref[...]
        after_d_ref[...] = recv_ref[...]

    @pl.when(phase != 0)
    def _():
        after_e_ref[...] = recv_ref[...]
        after_d_ref[...] = keep_ref[...]

    wait_enc(0)
    wait_enc(1)
    encoder_rows(
        after_e_ref, up_e, down_e, norms_ref[0:1, :], norms_ref[1:2, :], ckv_w_ref,
        hid_e_ref, slope_e_ref, res_e_ref, src_ref, ckv_ref,
    )
    middle = cross_rows(
        after_d_ref, ids_e_ref[...] == ids_d_row_ref[...], cq_w_ref, co_w_ref, cgain_ref, cbias_ref,
        cq_ref, ckv_ref, cmixed_ref, cres_ref, ctotals_ref,
    )
    wait_dec(0)
    wait_dec(1)
    targets = targets_ref[...]
    decoder_rows(
        scale, middle, up_d, down_d, norms_ref[2:3, :], norms_ref[3:4, :],
        targets[:, 0:1], targets[:, 1:2], targets[:, 2:3], delete_w_ref, place_w_ref,
        hid_d_ref, slope_d_ref, res_d_ref, low_ref, grad_ref, grad_delete_ref, grad_place_ref,
    )


def encoder_rows(
    after_ref, up, down, gain, bias, ckv_w_ref, hid_ref, slope_ref, res_ref, src_ref, ckv_ref
):
    residual = feed_forward(after_ref[...], up, down, hid_ref, slope_ref)
    res_ref[...] = residual
    src = norm_forward(residual, gain, bias).astype(BF16)
    src_ref[...] = src
    width = src.shape[1]
    for part in range(2):
        cols = slice(part * width, (part + 1) * width)
        ckv_ref[:, cols] = mm(src, ckv_w_ref[:, cols]).astype(BF16)


def cross_rows(
    after_ref, allowed, cq_w_ref, co_w_ref, cgain_ref, cbias_ref, cq_ref, ckv_ref, cmixed_ref, cres_ref, ctotals_ref
):
    width = after_ref.shape[1]
    cq_ref[...] = mm(after_ref[...].astype(BF16), cq_w_ref[...]).astype(BF16)
    attend_forward(
        lambda pair: cq_ref[:, column(pair)],
        lambda pair: ckv_ref[:, column(pair)],
        lambda pair: ckv_ref[:, column(pair, width)],
        allowed, cmixed_ref, ctotals_ref, slice(None),
    )
    residual = after_ref[...] + mm(cmixed_ref[...], co_w_ref[...])
    cres_ref[...] = residual
    return norm_forward(residual, cgain_ref[...], cbias_ref[...])


def decoder_rows(
    scale, middle, up, down, gain, bias, delete_label, place_label, pair_valid, delete_w_ref, place_w_ref,
    hid_ref, slope_ref, res_ref, low_ref, grad_ref, grad_delete_ref, grad_place_ref,
):
    residual = feed_forward(middle, up, down, hid_ref, slope_ref)
    res_ref[...] = residual
    low = norm_forward(residual, gain, bias).astype(BF16)
    low_ref[...] = low
    length, width = low.shape
    logits = mm(low, delete_w_ref[...])
    grads = class_grads(logits, delete_label, scale, 2).astype(BF16)
    grad_delete_ref[...] = mm_tn(grads, low)[:8]
    grad_low = mm_nt(grads, delete_w_ref[...])
    logits = mm(low, place_w_ref[:width, :]) + pltpu.roll(
        mm(low, place_w_ref[width:, :]), length - 1, 0
    )
    weight = pair_valid.astype(F32) * scale
    grads = class_grads(logits, place_label, weight, logits.shape[1])
    later = pltpu.roll(grads, 1, 0).astype(BF16)
    grads = grads.astype(BF16)
    classes = grads.shape[1]
    for top, part in enumerate((grads, later)):
        part = mm_tn(low, part).astype(BF16).reshape(GROUPS // 2, 2, width // GROUPS, classes)
        at = slice(top * GROUPS // 2, (top + 1) * GROUPS // 2)
        for half in range(2):
            grad_place_ref[at, :, half * classes : (half + 1) * classes] = part[:, half]
    grad_low = grad_low + mm_nt(grads, place_w_ref[:width, :]) + mm_nt(later, place_w_ref[width:, :])
    grad_ref[...] = grad_low


def rows_backward(
    grad_low_ref, grad_token_ref, ids_e_ref, ids_d_row_ref,
    up_own, up_other, down_own, down_other, norms_ref,
    cq_w_ref, ckv_w_ref, co_w_ref, cgain_ref, cbias_ref,
    after_e_ref, res_e_ref, after_d_ref, ckv_ref, cq_ref, cmixed_ref, cres_ref, ctotals_ref,
    hid_e_ref, slope_e_ref, hid_d_ref, slope_d_ref, res_d_ref, src_ref, grad_place_ref,
    keep_ref, send_ref, own_ref, other_ref, cross_ref, vectors_ref,
    up_e, down_e, up_d, down_d, grad_e, grad_d, after_e_grad, after_d_grad, gq_ref, gckv_ref, sems, out_sems,
):
    phase = lax.axis_index("phase")
    width = grad_low_ref.shape[1]
    wait_enc, wait_dec = load_sided(
        phase, (up_own, down_own), (up_other, down_other), (up_e, down_e), (up_d, down_d), sems
    )
    grad_out = grad_low_ref[...] + grad_token_ref[...]
    grad_res, gain_grad, bias_grad = norm_back(res_d_ref[...], norms_ref[2:3, :], grad_out)
    vectors_ref[2:3, :] = gain_grad
    vectors_ref[3:4, :] = bias_grad
    cres = cres_ref[...]
    middle_low = norm_forward(cres, cgain_ref[...], cbias_ref[...]).astype(BF16)
    wait_dec(0)
    wait_dec(1)
    grad_middle = feed_back(grad_res, middle_low, up_d, down_d, hid_d_ref, slope_d_ref, *feed_puts(grad_d, 4))
    move_d = [
        pltpu.make_async_copy(grad_d, own_ref, out_sems.at[0]),
        pltpu.make_async_copy(grad_d, other_ref, out_sems.at[0]),
    ]

    @pl.when(phase == 0)
    def _():
        move_d[1].start()

    @pl.when(phase != 0)
    def _():
        move_d[0].start()

    grad_res, gain_grad, bias_grad = norm_back(cres, cgain_ref[...], grad_middle)
    vectors_ref[4:5, :] = gain_grad
    vectors_ref[5:6, :] = bias_grad
    branch = grad_res.astype(BF16)
    after_low = after_d_ref[...].astype(BF16)
    rows = width // GROUPS
    put_shards(cross_ref, 3 * rows, mm_tn(cmixed_ref[...], branch))
    grad_mixed = mm_nt(branch, co_w_ref[...]).astype(BF16)

    def put_q(pair, value):
        gq_ref[:, column(pair)] = value

    def put_k(pair, value):
        gckv_ref[:, column(pair)] = value

    def put_v(pair, value):
        gckv_ref[:, column(pair, width)] = value

    attend_backward(
        lambda pair: cq_ref[:, column(pair)],
        lambda pair: ckv_ref[:, column(pair)],
        lambda pair: ckv_ref[:, column(pair, width)],
        lambda pair: grad_mixed[:, column(pair)],
        ids_e_ref[...] == ids_d_row_ref[...],
        ctotals_ref, put_q, put_k, put_v,
    )
    grad_q = gq_ref[...]
    grad_kv = gckv_ref[...]
    put_shards(cross_ref, 0, mm_tn(after_low, grad_q))
    put_shards(cross_ref, rows, mm_tn(src_ref[...], grad_kv))
    cross_ref[:, 4 * rows : 5 * rows, :] = grad_place_ref[...]
    after_d_grad[...] = grad_res + mm_nt(grad_q, cq_w_ref[...])
    grad_src = mm_nt(grad_kv, ckv_w_ref[...]).astype(BF16).astype(F32)
    grad_res, gain_grad, bias_grad = norm_back(res_e_ref[...], norms_ref[0:1, :], grad_src)
    vectors_ref[0:1, :] = gain_grad
    vectors_ref[1:2, :] = bias_grad
    vectors_ref[6:8, :] = jnp.zeros((2, width), F32)
    wait_enc(0)
    wait_enc(1)
    after_e_grad[...] = feed_back(
        grad_res, after_e_ref[...].astype(BF16), up_e, down_e, hid_e_ref, slope_e_ref,
        *feed_puts(grad_e, 4),
    )
    move_e = [
        pltpu.make_async_copy(grad_e, own_ref, out_sems.at[1]),
        pltpu.make_async_copy(grad_e, other_ref, out_sems.at[1]),
    ]

    @pl.when(phase == 0)
    def _():
        move_e[0].start()
        keep_ref[...] = after_e_grad[...]
        send_ref[...] = after_d_grad[...]

    @pl.when(phase != 0)
    def _():
        move_e[1].start()
        keep_ref[...] = after_d_grad[...]
        send_ref[...] = after_e_grad[...]

    move_d[0].wait()
    move_e[0].wait()


def self_backward(
    keep_ref, recv_ref, x_ref, ids_ref, ids_row_ref, qkv_w_ref, mix_w_ref, gain_ref,
    qkv_ref, mixed_ref, res_ref, totals_ref,
    grad_x_ref, shards_ref, vectors_ref,
    after_grad, grad_qkv,
):
    phase = lax.axis_index("phase")
    count, length = ids_ref.shape[0], ids_ref.shape[1]
    width = x_ref.shape[1]
    for row in range(count):
        rows = slice(row * length, (row + 1) * length)

        @pl.when(phase == row)
        def _():
            after_grad[rows, :] = keep_ref[...]

        @pl.when(phase != row)
        def _():
            after_grad[rows, :] = recv_ref[...]

    grad_res, gain_grad, bias_grad = norm_back(res_ref[...], gain_ref[0:1, :], after_grad[...])
    vectors_ref[0:1, :] = gain_grad
    vectors_ref[1:2, :] = bias_grad
    vectors_ref[2:8, :] = jnp.zeros((6, width), F32)
    grad_x_ref[...] = grad_res
    branch = grad_res.astype(BF16)
    rows_each = width // GROUPS
    put_shards(shards_ref, 3 * rows_each, mm_tn(mixed_ref[...], branch))
    grad_mixed = mm_nt(branch, mix_w_ref[...]).astype(BF16)
    for row in range(count):
        rows = slice(row * length, (row + 1) * length)

        def put(offset):
            def store(pair, value):
                grad_qkv[rows, column(pair, offset)] = value

            return store

        attend_backward(
            lambda pair: qkv_ref[rows, column(pair)],
            lambda pair: qkv_ref[rows, column(pair, width)],
            lambda pair: qkv_ref[rows, column(pair, 2 * width)],
            lambda pair: grad_mixed[rows, column(pair)],
            ids_ref[row] == ids_row_ref[row],
            totals_ref.at[row], put(0), put(width), put(2 * width),
        )
    for part in range(3):
        cols = slice(part * width, (part + 1) * width)
        put_shards(shards_ref, part * rows_each, mm_tn(x_ref[...], grad_qkv[:, cols]))
    grad_x_ref[...] += mm_nt(grad_qkv[...], qkv_w_ref[...])


def token_forward(low_ref, weight_ref, probs_ref, totals_ref):
    logits = mm_nt(weight_ref[...], low_ref[...])
    top = jnp.max(logits, axis=0, keepdims=True)
    weights = jnp.exp(logits - top)
    summed = jnp.sum(weights, axis=0, keepdims=True)
    probs_ref[0] = (weights * (1.0 / summed)).astype(BF16)
    totals_ref[0] = top + jnp.log(summed)


def token_backward(
    scale, probs_ref, share_ref, label_ref, low_ref, weight_ref, grad_low_ref, grad_weight_ref, total
):
    step = pl.program_id(0)
    labels = label_ref[0]
    shape = probs_ref.shape[1:]
    offset = (lax.axis_index("dp") * 2 + lax.axis_index("phase")) * shape[0]
    chosen = lax.broadcasted_iota(jnp.int32, shape, 0) == labels - offset
    grads = probs_ref[0].astype(F32) * share_ref[0] - chosen.astype(F32)
    grads = (grads * jnp.where(labels >= 0, scale, 0.0)).astype(BF16)
    grad_low = mm_tn(grads, weight_ref[...]).astype(BF16)
    cap = grad_low_ref.shape[1]
    for block in range(grad_low_ref.shape[0]):
        grad_low_ref[block] = grad_low[block * cap : (block + 1) * cap]
    part = mm(grads, low_ref[...])

    @pl.when(step == 0)
    def _():
        total[...] = part

    @pl.when(step != 0)
    def _():
        total[...] += part

    @pl.when(step == pl.num_programs(0) - 1)
    def _():
        grad_weight_ref[...] = total[...].T


def place_of(dp):
    return lax.rem(dp, 2), lax.rem(dp // 2, 2), dp // 4


def index_of(x, y, z):
    return (z * 2 + y) * 2 + x


def greet(devices):
    barrier = pltpu.get_barrier_semaphore()
    for dp, phase in devices:
        pl.semaphore_signal(barrier, inc=1, device_id=(dp, phase), device_id_type=MESH)
    pl.semaphore_wait(barrier, len(devices))


def remote(src, dst, send, recv, device):
    return pltpu.make_async_remote_copy(
        src_ref=src, dst_ref=dst, send_sem=send, recv_sem=recv, device_id=device, device_id_type=MESH
    )


def gather_kernel(block_ref, out_ref, send, recv, local):
    dp, phase = lax.axis_index("dp"), lax.axis_index("phase")
    x, y, z = place_of(dp)
    x_first = phase == 0
    zs = [lax.rem(z + k, 4) for k in (1, 2, 3)]
    second = index_of(jnp.where(x_first, 1 - x, x), jnp.where(x_first, y, 1 - y), z)
    third = index_of(jnp.where(x_first, x, 1 - x), jnp.where(x_first, 1 - y, y), z)
    greet([(index_of(x, y, k), phase) for k in zs] + [(second, phase), (third, phase), (dp, 1 - phase)])
    own = pltpu.make_async_copy(block_ref, out_ref.at[phase, z, y, x], local.at[0])
    own.start()
    started = []
    first = []
    for k in range(3):
        copy = remote(
            block_ref, out_ref.at[phase, z, y, x], send.at[k], recv.at[k], (index_of(x, y, zs[k]), phase)
        )
        copy.start()
        first.append(copy)
    cross = []

    def to_core(slot, src):
        copy = remote(src, src, send.at[slot], recv.at[slot], (dp, 1 - phase))
        copy.start()
        cross.append(copy)

    mine = remote(block_ref, out_ref.at[phase, z, y, x], send.at[3], recv.at[3], (dp, 1 - phase))
    mine.start()
    cross.append(mine)
    own.wait()
    seconds = []
    x2 = jnp.where(x_first, 1 - x, x)
    y2 = jnp.where(x_first, y, 1 - y)
    x3 = jnp.where(x_first, x, 1 - x)
    y3 = jnp.where(x_first, 1 - y, y)

    def relay(slot, zz, yy, xx, device, into):
        src = out_ref.at[phase, zz, yy, xx]
        copy = remote(src, src, send.at[slot], recv.at[slot], (device, phase))
        copy.start()
        into.append(copy)

    thirds = []
    relay(4, z, y, x, second, seconds)
    relay(8, z, y, x, third, thirds)
    sources = [lax.rem(z + 4 - k, 4) for k in (1, 2, 3)]
    for k in range(3):
        first[k].wait_recv()
        relay(5 + k, sources[k], y, x, second, seconds)
        relay(9 + k, sources[k], y, x, third, thirds)
        to_core(16 + k, out_ref.at[phase, sources[k], y, x])
    order = [z] + sources
    for k in range(4):
        seconds[k].wait_recv()
        relay(12 + k, order[k], y2, x2, third, thirds)
        to_core(19 + k, out_ref.at[phase, order[k], y2, x2])
    for k in range(8):
        thirds_k = thirds[k]
        thirds_k.wait_recv()
        where_y, where_x = (y3, x3) if k < 4 else (1 - y, 1 - x)
        to_core(23 + k, out_ref.at[phase, order[k % 4], where_y, where_x])
    for copy in cross:
        copy.wait_recv()
    for copy in first + seconds + thirds + cross:
        copy.wait_send()


def gather_blocks(block, number):
    dp = lax.axis_size("dp")
    if dp != GROUPS:
        return lax.all_gather(lax.all_gather(block, "dp"), "phase")
    rows, width = block.shape
    out = pl.pallas_call(
        gather_kernel,
        out_shape=jax.ShapeDtypeStruct((2, 4, 2, 2, rows, width), block.dtype),
        in_specs=[pl.BlockSpec(memory_space=pl.ANY)],
        out_specs=pl.BlockSpec(memory_space=pl.ANY),
        scratch_shapes=[
            pltpu.SemaphoreType.DMA((31,)), pltpu.SemaphoreType.DMA((31,)), pltpu.SemaphoreType.DMA((1,)),
        ],
        compiler_params=pltpu.CompilerParams(collective_id=number, has_side_effects=True),
        name="gather_blocks",
    )(block)
    return out.reshape(2, dp, rows, width)


def scatter_kernel(part_ref, out_ref, core_in, third_out, third_in, second_out, second_in, z_out, z_in, send, recv):
    dp, phase = lax.axis_index("dp"), lax.axis_index("phase")
    x, y, z = place_of(dp)
    x_first = phase == 0
    x2 = jnp.where(x_first, 1 - x, x)
    y2 = jnp.where(x_first, y, 1 - y)
    x3 = jnp.where(x_first, x, 1 - x)
    y3 = jnp.where(x_first, 1 - y, y)
    second, third = index_of(x2, y2, z), index_of(x3, y3, z)
    zs = [lax.rem(z + k, 4) for k in (1, 2, 3)]
    greet([(index_of(x, y, k), phase) for k in zs] + [(second, phase), (third, phase), (dp, 1 - phase)])
    order = [lax.rem(z + k, 4) for k in (1, 2, 3, 0)]
    spots = (
        [(zz, 1 - y, 1 - x) for zz in order]
        + [(zz, y3, x3) for zz in order]
        + [(zz, y2, x2) for zz in order]
        + [(zz, y, x) for zz in order]
    )
    theirs = (
        [(zz, 1 - y, 1 - x) for zz in order]
        + [(zz, y2, x2) for zz in order]
        + [(zz, y3, x3) for zz in order]
        + [(zz, y, x) for zz in order]
    )
    cores = []
    for j in range(16):
        zz, yy, xx = theirs[j]
        copy = remote(part_ref.at[1 - phase, zz, yy, xx], core_in.at[j], send.at[j], recv.at[j], (dp, 1 - phase))
        copy.start()
        cores.append(copy)

    def both(j):
        zz, yy, xx = spots[j]
        cores[j].wait_recv()
        return part_ref[phase, zz, yy, xx].astype(F32) + core_in[j].astype(F32)

    thirds = []
    for j in range(8):
        third_out[j] = both(j).astype(BF16)
        copy = remote(third_out.at[j], third_in.at[j], send.at[16 + j], recv.at[16 + j], (third, phase))
        copy.start()
        thirds.append(copy)
    seconds = []
    for j in range(4):
        total = both(8 + j)
        thirds[j].wait_recv()
        second_out[j] = (total + third_in[j].astype(F32)).astype(BF16)
        copy = remote(second_out.at[j], second_in.at[j], send.at[24 + j], recv.at[24 + j], (second, phase))
        copy.start()
        seconds.append(copy)
    along = []
    for j in range(4):
        total = both(12 + j)
        thirds[4 + j].wait_recv()
        total = total + third_in[4 + j].astype(F32)
        seconds[j].wait_recv()
        total = total + second_in[j].astype(F32)
        if j < 3:
            z_out[j] = total.astype(BF16)
            copy = remote(z_out.at[j], z_in.at[j], send.at[28 + j], recv.at[28 + j], (index_of(x, y, zs[j]), phase))
            copy.start()
            along.append(copy)
        else:
            for copy in along:
                copy.wait_recv()
            out_ref[...] = total + z_in[0].astype(F32) + z_in[1].astype(F32) + z_in[2].astype(F32)
    for copy in cores + thirds + seconds + along:
        copy.wait_send()


def scatter_blocks(part, number):
    dp = lax.axis_size("dp")
    if dp != GROUPS:
        part = lax.psum_scatter(part.astype(F32), "phase", scatter_dimension=0, tiled=False)
        return lax.psum_scatter(part, "dp", scatter_dimension=0, tiled=False)
    rows, width = part.shape[2:]
    return pl.pallas_call(
        scatter_kernel,
        out_shape=jax.ShapeDtypeStruct((rows, width), F32),
        in_specs=[pl.BlockSpec(memory_space=VMEM)],
        out_specs=pl.BlockSpec(memory_space=VMEM),
        scratch_shapes=[VMEM((n, rows, width), BF16) for n in (16, 8, 8, 4, 4, 3, 3)]
        + [pltpu.SemaphoreType.DMA((31,)), pltpu.SemaphoreType.DMA((31,))],
        compiler_params=pltpu.CompilerParams(
            collective_id=number, has_side_effects=True, vmem_limit_bytes=48 * 1024 * 1024
        ),
        name="scatter_blocks",
    )(part.reshape(2, 4, 2, 2, rows, width))


def share_kernel(totals_ref, share_ref, near_in, joined, far_in, send, recv):
    dp, phase = lax.axis_index("dp"), lax.axis_index("phase")
    x, y, z = place_of(dp)
    near = [
        (index_of(lax.rem(x + a, 2), lax.rem(y + b, 2), z), lax.rem(phase + c, 2))
        for a in range(2) for b in range(2) for c in range(2) if a + b + c
    ]
    far = [(index_of(x, y, lax.rem(z + k, 4)), phase) for k in (1, 2, 3)]
    greet(near + far)

    def join(parts):
        top = parts[0]
        for part in parts[1:]:
            top = jnp.maximum(top, part)
        summed = jnp.exp(parts[0] - top)
        for part in parts[1:]:
            summed = summed + jnp.exp(part - top)
        return top + jnp.log(summed)

    copies = []
    for j, device in enumerate(near):
        copies.append(remote(totals_ref, near_in.at[j], send.at[j], recv.at[j], device))
        copies[-1].start()
    for copy in copies:
        copy.wait_recv()
    total = join([totals_ref[...]] + [near_in[j] for j in range(7)])
    joined[...] = total
    for j, device in enumerate(far):
        copies.append(remote(joined, far_in.at[j], send.at[7 + j], recv.at[7 + j], device))
        copies[-1].start()
    for copy in copies[7:]:
        copy.wait_recv()
    share_ref[...] = jnp.exp(totals_ref[...] - join([total] + [far_in[j] for j in range(3)]))
    for copy in copies:
        copy.wait_send()


def token_shares(totals, number):
    if lax.axis_size("dp") != GROUPS:
        top = lax.pmax(totals, ("dp", "phase"))
        return jnp.exp(totals - top) / lax.psum(jnp.exp(totals - top), ("dp", "phase"))
    flat = totals.reshape(-1, 128)
    rows = flat.shape[0]
    share = pl.pallas_call(
        share_kernel,
        out_shape=jax.ShapeDtypeStruct((rows, 128), F32),
        in_specs=[pl.BlockSpec(memory_space=VMEM)],
        out_specs=pl.BlockSpec(memory_space=VMEM),
        scratch_shapes=[
            VMEM((7, rows, 128), F32), VMEM((rows, 128), F32), VMEM((3, rows, 128), F32),
            pltpu.SemaphoreType.DMA((10,)), pltpu.SemaphoreType.DMA((10,)),
        ],
        compiler_params=pltpu.CompilerParams(collective_id=number, has_side_effects=True),
        name="token_shares",
    )(flat)
    return share.reshape(totals.shape)


def pack_labels(labels, flags, out_ref):
    count, length = labels.shape
    before = lax.broadcasted_iota(jnp.int32, (length, length), 0)
    after = lax.broadcasted_iota(jnp.int32, (length, length), 1)
    upto = jnp.where(before <= after, 1.0, 0.0).astype(BF16)
    rows = jnp.concatenate([flags.astype(F32)] + [jnp.zeros((8 - count, length), F32)], axis=0)
    place = mm(rows.astype(BF16), upto)
    for row in range(count):
        flag = rows[row : row + 1]
        chosen = (before.astype(F32) == place[row : row + 1] - 1.0) & (flag > 0.0)
        label = labels[row : row + 1]
        high = lax.shift_right_logical(label, 8)
        parts = [high.astype(F32), (label - high * 256).astype(F32), flag, jnp.zeros((5, length), F32)]
        found = mm_nt(
            jnp.concatenate(parts, axis=0).astype(BF16), jnp.where(chosen, 1.0, 0.0).astype(BF16)
        )
        packed = jnp.where(found[2:3] > 0.5, found[0:1] * 256.0 + found[1:2], -1.0)
        out_ref[row : row + 1, :] = packed.astype(jnp.int32)


FORWARD = (
    "qkv", "mixed", "res", "after", "res_e", "ckv", "cq", "cmixed", "cres",
    "hid_e", "slope_e", "hid_d", "slope_d", "res_d", "src", "low", "grad_low", "grad_place",
)


def forward_kernel(
    scale, x_ref, segments_ref, delete_ref, place_ref, token_ref, mask_ref,
    qkv_w_ref, mix_w_ref, gain_ref, bias_ref, up_own, down_own,
    cq_w_any, ckv_w_any, co_w_any, cgain_ref, cbias_ref, delete_w_ref, place_w_any,
    rows_ref, cols_ref, labels_small_ref, labels_large_ref, most_ref, norms_ref, up_other, down_other,
    totals_ref, ctotals_ref, grad_delete_ref, *rest,
):
    outs, rest = dict(zip(FORWARD, rest)), rest[len(FORWARD) :]
    held, rest = dict(zip(FORWARD, rest)), rest[len(FORWARD) :]
    up, down, cq_w, ckv_w, co_w, place_w, send_after, own_labels, all_labels, turned, load, store, send, recv = rest
    dp, phase = lax.axis_index("dp"), lax.axis_index("phase")
    x, y, z = place_of(dp)
    chips = [
        (lax.rem(x + a, 2), lax.rem(y + b, 2), lax.rem(z + c, 4))
        for c in range(4) for b in range(2) for a in range(2) if a + b + c
    ]
    core = (dp, 1 - phase)
    greet([(index_of(*chip), phase) for chip in chips] + [core])
    copies, stores = [], []

    def remote_to(src, dst, device):
        i = len(copies)
        copy = remote(src, dst, send.at[i], recv.at[i], device)
        copy.start()
        copies.append(copy)
        return copy

    def save(*names):
        for name in names:
            copy = pltpu.make_async_copy(held[name], outs[name], store.at[len(stores)])
            copy.start()
            stores.append(copy)

    norms_ref[phase, 0:1, :] = gain_ref[1:2, :]
    norms_ref[phase, 1:2, :] = bias_ref[1:2, :]
    from_norms = remote_to(norms_ref.at[phase], norms_ref.at[phase], core)
    from_up = remote_to(up_own, up.at[phase], core)
    from_down = remote_to(down_own, down.at[phase], core)
    loads = [
        pltpu.make_async_copy(src, dst, load.at[i])
        for i, (src, dst) in enumerate((
            (up_own, up.at[phase]), (down_own, down.at[phase]), (ckv_w_any, ckv_w), (cq_w_any, cq_w),
            (co_w_any, co_w), (place_w_any, place_w),
        ))
    ]
    for copy in loads:
        copy.start()
    pack_labels(token_ref[...], mask_ref[...], own_labels)
    for chip in chips:
        remote_to(own_labels, all_labels.at[z, y, x], (index_of(*chip), phase))
    label_copies = copies[3:]
    all_labels[z, y, x] = own_labels[...]
    is_enc = phase == 0
    segments = segments_ref[...].astype(F32)
    length = segments.shape[2]

    def pick(first, second):
        return jnp.where(is_enc, first, second)

    def own_row(ref):
        value = ref[...].astype(F32)
        return pick(value[0:1], value[1:2])

    ids_e = pick(segments[0, 0:1], segments[1, 0:1])
    ids_d = pick(segments[0, 1:2], segments[1, 1:2])
    own_ids = [pick(segments[r, 0:1], segments[r, 1:2]) for r in range(2)]
    block = jnp.concatenate([ids_d] * 8, axis=0)
    later = pltpu.roll(block, length - 1, 1)
    lane = lax.broadcasted_iota(jnp.int32, (8, length), 1)
    valid = jnp.where((block == later) & (lane < length - 1), 1.0, 0.0)[0:1]
    rows = jnp.concatenate(
        own_ids + [ids_e, ids_d, own_row(delete_ref), own_row(place_ref), valid, own_row(mask_ref)], axis=0
    )
    rows_ref[...] = rows
    turned[...] = jnp.zeros(turned.shape, F32)
    turned[0:8, :] = rows
    cols = turned[...].T
    cols_ref[...] = cols
    width = x_ref.shape[1]
    qkv, mixed, res = held["qkv"], held["mixed"], held["res"]
    for part in range(3):
        span = slice(part * width, (part + 1) * width)
        qkv[:, span] = mm(x_ref[...], qkv_w_ref[:, span]).astype(BF16)
    save("qkv")
    for turn in range(2):
        row = 1 - phase if turn == 0 else phase
        span = pl.ds(pl.multiple_of(row * length, length), length)
        allowed = jnp.where(row == 0, cols[:, 0:1], cols[:, 1:2]) == jnp.where(
            row == 0, own_ids[0], own_ids[1]
        )
        attend_forward(
            lambda pair: qkv[span, column(pair)],
            lambda pair: qkv[span, column(pair, width)],
            lambda pair: qkv[span, column(pair, 2 * width)],
            allowed, mixed, totals_ref.at[row], span,
        )
        residual = x_ref[span, :].astype(F32) + mm(mixed[span, :], mix_w_ref[...])
        res[span, :] = residual
        after = norm_forward(residual, gain_ref[0:1, :], bias_ref[0:1, :])
        if turn == 0:
            send_after[...] = after
            from_after = remote_to(send_after, held["after"].at[phase], core)
        else:
            held["after"][phase] = after
    save("mixed", "res")
    from_after.wait_recv()
    save("after")
    from_norms.wait_recv()
    from_up.wait_recv()
    from_down.wait_recv()
    for copy in loads:
        copy.wait()
    for i, (src, dst) in enumerate(((up, up_other), (down, down_other))):
        copy = pltpu.make_async_copy(src.at[1 - phase], dst, store.at[len(stores)])
        copy.start()
        stores.append(copy)
    encoder_rows(
        held["after"].at[0], up.at[0], down.at[0], norms_ref[0, 0:1, :], norms_ref[0, 1:2, :], ckv_w,
        held["hid_e"], held["slope_e"], held["res_e"], held["src"], held["ckv"],
    )
    save("hid_e", "slope_e", "res_e", "src", "ckv")
    middle = cross_rows(
        held["after"].at[1], cols[:, 2:3] == rows[3:4], cq_w, co_w, cgain_ref, cbias_ref,
        held["cq"], held["ckv"], held["cmixed"], held["cres"], ctotals_ref,
    )
    save("cq", "cmixed", "cres")
    decoder_rows(
        scale, middle, up.at[1], down.at[1], norms_ref[1, 0:1, :], norms_ref[1, 1:2, :],
        cols[:, 4:5].astype(jnp.int32), cols[:, 5:6].astype(jnp.int32), cols[:, 6:7], delete_w_ref, place_w,
        held["hid_d"], held["slope_d"], held["res_d"], held["low"], held["grad_low"],
        grad_delete_ref, held["grad_place"],
    )
    save("hid_d", "slope_d", "res_d", "low", "grad_low", "grad_place")
    for copy in label_copies:
        copy.wait_recv()
    small = length // 2
    for at, (p, yy, xx, zz) in enumerate(
        (p, yy, xx, zz) for p in range(2) for yy in range(2) for xx in range(2) for zz in range(4)
    ):
        line = all_labels[zz, yy, xx, p : p + 1, :]
        labels_small_ref[:, at * small : (at + 1) * small] = line[:, :small]
        labels_large_ref[:, at * length : (at + 1) * length] = line
    beyond = jnp.max(all_labels[:, :, :, :, small:].astype(F32).reshape(2 * GROUPS, length - small))
    most_ref[...] = jnp.full(most_ref.shape, beyond, F32)
    for copy in copies:
        copy.wait_send()
    for copy in stores:
        copy.wait()


def token_kernel(
    scale, cap, low_ref, rows_ref, cols_ref, labels_ref, head_any,
    grad_ref, grad_weight_ref,
    weight, weight_t, every, probs, totals, near_in, joined, far_in, shares,
    part, core_in, third_in, second_in, z_in, load, send, recv,
):
    dp, phase = lax.axis_index("dp"), lax.axis_index("phase")
    x, y, z = place_of(dp)
    x_first = phase == 0
    x2, y2 = jnp.where(x_first, 1 - x, x), jnp.where(x_first, y, 1 - y)
    x3, y3 = jnp.where(x_first, x, 1 - x), jnp.where(x_first, 1 - y, y)
    second, third, core = (index_of(x2, y2, z), phase), (index_of(x3, y3, z), phase), (dp, 1 - phase)
    zs = [lax.rem(z + k, 4) for k in (1, 2, 3)]
    along = [(index_of(x, y, k), phase) for k in zs]
    shard, length = weight_t.shape[0], low_ref.shape[0]
    near = [
        (index_of(lax.rem(x + a, 2), lax.rem(y + b, 2), z), lax.rem(phase + c, 2))
        for a in range(2) for b in range(2) for c in range(2) if a + b + c
    ]
    greet(near + along)
    offset = pl.multiple_of((dp * 2 + phase) * shard, shard)
    weight_copy = pltpu.make_async_copy(head_any.at[:, pl.ds(offset, shard)], weight, load.at[0])
    weight_copy.start()
    copies = []

    def remote_to(src, dst, device):
        i = len(copies)
        copy = remote(src, dst, send.at[i], recv.at[i], device)
        copy.start()
        copies.append(copy)
        return copy

    def unit(p, yy, xx):
        return (p * 2 + yy) * 2 + xx

    def block(u, zz):
        return pl.ds(pl.multiple_of((u * 4 + zz) * cap, cap), cap)

    before = lax.broadcasted_iota(jnp.int32, (length, length), 0)
    after = lax.broadcasted_iota(jnp.int32, (length, length), 1)
    rows = rows_ref[...]
    place = mm(rows.astype(BF16), jnp.where(before <= after, 1.0, 0.0).astype(BF16))[7:8]
    slot = lax.broadcasted_iota(jnp.int32, (cap, length), 0).astype(F32)
    chosen = jnp.where((slot == place - 1.0) & (rows[7:8] > 0.0), 1.0, 0.0).astype(BF16)
    own = unit(phase, y, x)
    every[block(own, z), :] = mm(chosen, low_ref[...]).astype(BF16)
    def relay(u, zz, device):
        here = every.at[block(u, zz), :]
        return remote_to(here, here, device)

    firsts = [relay(own, z, device) for device in along]
    cross = [relay(own, z, core)]
    seconds = [relay(own, z, second)]
    thirds = [relay(own, z, third)]
    weight_copy.wait()
    weight_t[...] = weight[...].T
    sources = [lax.rem(z + 4 - k, 4) for k in (1, 2, 3)]
    order = [z] + sources
    for k in range(3):
        firsts[k].wait_recv()
        seconds.append(relay(own, sources[k], second))
        thirds.append(relay(own, sources[k], third))
        cross.append(relay(own, sources[k], core))
    tall = 256
    chunks = 4 * cap // tall

    def look(u):
        def step(j, _):
            span = pl.ds(pl.multiple_of((u * chunks + j) * tall, tall), tall)
            logits = mm_nt(weight_t[...], every[span, :])
            top = jnp.max(logits, axis=0, keepdims=True)
            weights = jnp.exp(logits - top)
            summed = jnp.sum(weights, axis=0, keepdims=True)
            probs[:, span] = (weights * (1.0 / summed)).astype(BF16)
            totals[:, span] = top + jnp.log(summed)
            return 0

        lax.fori_loop(0, chunks, step, 0)

    def arrived(some):
        for copy in some:
            copy.wait_recv()

    look(own)
    for k in range(4):
        seconds[k].wait_recv()
        thirds.append(relay(unit(phase, y2, x2), order[k], third))
        cross.append(relay(unit(phase, y2, x2), order[k], core))
    arrived(cross[0:4])
    look(unit(1 - phase, y, x))
    look(unit(phase, y2, x2))
    for k in range(4):
        thirds[k].wait_recv()
        cross.append(relay(unit(phase, y3, x3), order[k], core))
    arrived(cross[4:8])
    look(unit(1 - phase, y3, x3))
    for k in range(4):
        thirds[4 + k].wait_recv()
        cross.append(relay(unit(phase, 1 - y, 1 - x), order[k], core))
    look(unit(phase, y3, x3))
    arrived(cross[8:12])
    look(unit(1 - phase, y2, x2))
    look(unit(phase, 1 - y, 1 - x))
    arrived(cross[12:16])
    look(unit(1 - phase, 1 - y, 1 - x))

    def join(parts):
        top = parts[0]
        for piece in parts[1:]:
            top = jnp.maximum(top, piece)
        summed = jnp.exp(parts[0] - top)
        for piece in parts[1:]:
            summed = summed + jnp.exp(piece - top)
        return top + jnp.log(summed)

    near_copies = [remote_to(totals, near_in.at[j], device) for j, device in enumerate(near)]
    arrived(near_copies)
    total = join([totals[...]] + [near_in[j] for j in range(7)])
    joined[...] = total
    far_copies = [remote_to(joined, far_in.at[j], device) for j, device in enumerate(along)]
    arrived(far_copies)
    shares[...] = jnp.exp(totals[...] - join([total] + [far_in[j] for j in range(3)]))

    per = tall // cap

    def learn(u):
        def step(j, _):
            span = pl.ds(pl.multiple_of((u * chunks + j) * tall, tall), tall)
            labels = labels_ref[:, span]
            hit = lax.broadcasted_iota(jnp.int32, (shard, tall), 0) == labels - offset
            grads = probs[:, span].astype(F32) * shares[:, span] - jnp.where(hit, 1.0, 0.0)
            grads = (grads * jnp.where(labels >= 0, scale, 0.0)).astype(BF16)
            probs[:, span] = grads
            back = mm(weight[...], grads).astype(BF16)
            for k in range(per):
                part[u, j * per + k] = back[:, k * cap : (k + 1) * cap]
            return 0

        lax.fori_loop(0, chunks, step, 0)

    def add(u, *others):
        def step(zz, _):
            value = part[u, zz].astype(F32)
            for other in others:
                value = value + other[zz].astype(F32)
            part[u, zz] = value.astype(BF16)
            return 0

        lax.fori_loop(0, 4, step, 0)

    mine = [unit(phase, 1 - y, 1 - x), unit(phase, y3, x3), unit(phase, y2, x2), own]
    theirs = [
        unit(1 - phase, 1 - y, 1 - x), unit(1 - phase, y2, x2), unit(1 - phase, y3, x3), unit(1 - phase, y, x)
    ]
    core_copies, third_copies = [], []
    for k in range(4):
        learn(theirs[k])
        core_copies.append(remote_to(part.at[theirs[k]], core_in.at[k], core))
        if 1 <= k <= 2:
            core_copies[k - 1].wait_recv()
            add(mine[k - 1], core_in.at[k - 1])
            third_copies.append(remote_to(part.at[mine[k - 1]], third_in.at[k - 1], third))
        learn(mine[k])
    core_copies[2].wait_recv()
    third_copies[0].wait_recv()
    add(mine[2], core_in.at[2], third_in.at[0])
    second_copy = remote_to(part.at[mine[2]], second_in, second)

    slab = min(256, shard)

    def weigh(k):
        value = mm(probs[k * slab : (k + 1) * slab, :], every[...])
        grad_weight_ref[:, k * slab : (k + 1) * slab] = value.T

    slabs = shard // slab
    for k in range((slabs + 1) // 2):
        weigh(k)
    core_copies[3].wait_recv()
    third_copies[1].wait_recv()
    add(own, core_in.at[3], third_in.at[1])
    second_copy.wait_recv()
    add(own, second_in)
    z_copies = [remote_to(part.at[own, zz], z_in.at[j], along[j]) for j, zz in enumerate(zs)]
    for k in range((slabs + 1) // 2, slabs):
        weigh(k)
    arrived(z_copies)
    back = part[own, z].astype(F32)
    for j in range(3):
        back = back + z_in[j].astype(F32)
    place = mm(jnp.where(after <= before, 1.0, 0.0).astype(BF16), cols_ref[...].astype(BF16))[:, 7:8]
    slot = lax.broadcasted_iota(jnp.int32, (length, cap), 1).astype(F32)
    spread = jnp.where((slot == place - 1.0) & (cols_ref[:, 7:8] > 0.0), 1.0, 0.0).astype(BF16)
    grad_ref[...] = mm_nt(spread, back.astype(BF16))
    for copy in copies:
        copy.wait_send()


def token_chips(number, cap, low, rows, cols, labels, head):
    length, width = low.shape
    shard = head.shape[1] // (2 * GROUPS)
    count = 2 * GROUPS * cap
    scale = float(2 * length * GROUPS) ** (-0.5)
    copies = 48
    return pl.pallas_call(
        partial(token_kernel, scale, cap),
        out_shape=(whole((length, width), F32), whole((width, shard), F32)),
        in_specs=in_vmem(4) + [pl.BlockSpec(memory_space=pl.ANY)],
        out_specs=tuple(in_vmem(2)),
        scratch_shapes=[
            VMEM((width, shard), BF16), VMEM((shard, width), BF16), VMEM((count, width), BF16),
            VMEM((shard, count), BF16), VMEM((1, count), F32), VMEM((7, 1, count), F32), VMEM((1, count), F32),
            VMEM((3, 1, count), F32), VMEM((1, count), F32),
            VMEM((8, 4, width, cap), BF16), VMEM((4, 4, width, cap), BF16), VMEM((2, 4, width, cap), BF16),
            VMEM((4, width, cap), BF16), VMEM((3, width, cap), BF16),
            pltpu.SemaphoreType.DMA((1,)), pltpu.SemaphoreType.DMA((copies + 8,)), pltpu.SemaphoreType.DMA((copies + 8,)),
        ],
        compiler_params=pltpu.CompilerParams(
            collective_id=number, has_side_effects=True, vmem_limit_bytes=60 * 1024 * 1024
        ),
        name="token_head",
    )(low, rows, cols, labels, head)


class Exchange:
    def __init__(self, send, recv):
        self.dp, self.phase = lax.axis_index("dp"), lax.axis_index("phase")
        self.x, self.y, self.z = place_of(self.dp)
        x, y, z = self.x, self.y, self.z
        self.along_x, self.along_y = index_of(1 - x, y, z), index_of(x, 1 - y, z)
        self.zs = [lax.rem(z + k, 4) for k in (1, 2, 3)]
        self.send, self.recv, self.used, self.copies = send, recv, 0, []

    def greet(self):
        devices = [(index_of(self.x, self.y, k), self.phase) for k in self.zs]
        greet(devices + [(self.along_x, self.phase), (self.along_y, self.phase), (self.dp, 1 - self.phase)])

    def copy(self, src, dst, device):
        copy = remote(src, dst, self.send.at[self.used], self.recv.at[self.used], device)
        self.used += 1
        copy.start()
        self.copies.append(copy)
        return copy

    def to_core(self, src, dst):
        return self.copy(src, dst, (self.dp, 1 - self.phase))

    def first(self, batch, part):
        start, size, x_first = part
        rows = pl.ds(start, size)
        if x_first:
            src, device = batch.shards.at[:, :, 1 - self.x, rows], self.along_x
        else:
            src, device = batch.shards.at[:, 1 - self.y, :, rows], self.along_y
        return self.copy(src, batch.in1.at[:, :, rows], (device, self.phase))

    def second(self, batch, part):
        start, size, x_first = part
        rows = pl.ds(start, size)
        x, y, in1 = self.x, self.y, batch.in1
        other, device = (1 - y, self.along_y) if x_first else (1 - x, self.along_x)

        def add(i, _):
            zz, which = i // 2, lax.rem(i, 2)
            mine = batch.shards[zz, which, x, rows] if x_first else batch.shards[zz, y, which, rows]
            in1[zz, which, rows] = (in1[zz, which, rows].astype(F32) + mine.astype(F32)).astype(BF16)
            return 0

        lax.fori_loop(0, 8, add, 0)
        return self.copy(in1.at[:, other, rows], batch.in2.at[:, rows], (device, self.phase))

    def third(self, batch, part):
        start, size, x_first = part
        rows = pl.ds(start, size)
        own = self.y if x_first else self.x
        in1, in2 = batch.in1, batch.in2

        def add(zz, _):
            in2[zz, rows] = (in2[zz, rows].astype(F32) + in1[zz, own, rows].astype(F32)).astype(BF16)
            return 0

        lax.fori_loop(0, 4, add, 0)
        return [
            self.copy(in2.at[zz, rows], batch.in3.at[j, rows], (index_of(self.x, self.y, zz), self.phase))
            for j, zz in enumerate(self.zs)
        ]

    def last(self, batch, part, put):
        start, size, _ = part
        rows = pl.ds(start, size)
        in3 = batch.in3
        total = batch.in2[self.z, rows].astype(F32) + in3[0, rows].astype(F32)
        put(rows, total + in3[1, rows].astype(F32) + in3[2, rows].astype(F32))

    def finish(self):
        for copy in self.copies:
            copy.wait_send()


class Batch:
    def __init__(self, exchange, shards, in1, in2, in3, put, parts):
        self.exchange, self.shards, self.in1, self.in2, self.in3 = exchange, shards, in1, in2, in3
        self.put, self.parts = put, parts
        self.waits = [None] * len(parts)

    def from_core(self, copy, own):
        copy.wait_recv()
        shards = self.shards
        for i, part in enumerate(self.parts):
            rows = pl.ds(part[0], part[1])

            def add(j, _):
                at = (j // 4, lax.rem(j // 2, 2), lax.rem(j, 2), rows)
                shards[at] = (shards[at].astype(F32) + own[at].astype(F32)).astype(BF16)
                return 0

            lax.fori_loop(0, GROUPS, add, 0)
            self.waits[i] = self.exchange.first(self, part)

    def start(self):
        for i, part in enumerate(self.parts):
            self.waits[i] = self.exchange.first(self, part)

    def second(self):
        for i, part in enumerate(self.parts):
            self.waits[i].wait_recv()
            self.waits[i] = self.exchange.second(self, part)

    def third(self):
        for i, part in enumerate(self.parts):
            self.waits[i].wait_recv()
            self.waits[i] = self.exchange.third(self, part)

    def last(self):
        for i, part in enumerate(self.parts):
            for copy in self.waits[i]:
                copy.wait_recv()
            self.exchange.last(self, part, self.put)


FF_PARTS = ((0, 64, True), (64, 64, False))
CROSS_PARTS = ((0, 48, False), (48, 32, True))


BACKWARD = (
    "co_w", "cmixed", "cq", "ckv", "grad_place", "after", "src", "cq_w", "ckv_w", "res_e",
    "res", "mix_w", "qkv", "mixed", "x", "qkv_w",
)


def backward_kernel(
    grad_low_ref, grad_token_ref, rows_ref, cols_ref, norms_ref, cgain_ref, cbias_ref, ctotals_ref, totals_ref,
    res_d_ref, cres_ref, grad_delete_ref, gain_ref,
    up_own, up_other, down_own, down_other, hid_e_any, slope_e_any, hid_d_any, slope_d_any, *rest,
):
    held_any, rest = dict(zip(BACKWARD, rest)), rest[len(BACKWARD) :]
    grad_x_any, red_ff_ref, red_attention_ref, red_cross_ref, vectors_ref = rest[:5]
    held, rest = dict(zip(BACKWARD, rest[5:])), rest[5 + len(BACKWARD) :]
    (
        up, down, hid, slope, grad_d, grad_e, grad_c, grad_a, core_d, core_e, core_c,
        in1_d, in1_e, in1_c, in1_a, in2_d, in2_e, in2_c, in2_a, in3_d, in3_e, in3_c, in3_a,
        after_grads, after_in, gq_ref, gckv_ref, grad_qkv, sums, grad_x_ref,
        vec_own, vec_core, vec_1, vec_2, vec_3, vec_in, sems, held_sems, send, recv,
    ) = rest
    phase = lax.axis_index("phase")
    ex = Exchange(send, recv)
    ex.greet()

    def moved(name):
        i = BACKWARD.index(name)
        return pltpu.make_async_copy(held_any[name], held[name], held_sems.at[i])

    waited = set()

    def get(name):
        if name not in waited:
            waited.add(name)
            moved(name).wait()
        return held[name]

    width = grad_low_ref.shape[1]
    each = width // GROUPS
    length = grad_low_ref.shape[0]

    def load(own_side, i):
        hidden, slopes = (hid_e_any, slope_e_any) if own_side == 0 else (hid_d_any, slope_d_any)

        @pl.when(phase == own_side)
        def _():
            pltpu.make_async_copy(up_own, up, sems.at[i]).start()
            pltpu.make_async_copy(down_own, down, sems.at[i + 1]).start()

        @pl.when(phase != own_side)
        def _():
            pltpu.make_async_copy(up_other, up, sems.at[i]).start()
            pltpu.make_async_copy(down_other, down, sems.at[i + 1]).start()

        pltpu.make_async_copy(hidden, hid, sems.at[i + 2]).start()
        pltpu.make_async_copy(slopes, slope, sems.at[i + 3]).start()

    def loaded(i):
        for k, (src, dst) in enumerate(
            ((up_own, up), (down_own, down), (hid_e_any, hid), (slope_e_any, slope))
        ):
            pltpu.make_async_copy(src, dst, sems.at[i + k]).wait()

    def puts(ref):
        def put_up(part, value):
            ref[0, :, :, :, part * each : (part + 1) * each, :] = value.astype(BF16).reshape(
                4, 2, 2, each, width
            )

        def put_down(part, value):
            ref[1, part] = value.astype(BF16).reshape(2, 2, width // 4, width)

        return put_up, put_down

    batch_d = Batch(ex, core_d, in1_d, in2_d, in3_d, None, FF_PARTS)
    batch_e = Batch(ex, core_e, in1_e, in2_e, in3_e, None, FF_PARTS)
    batch_c = Batch(ex, core_c, in1_c, in2_c, in3_c, None, CROSS_PARTS)
    batch_a = Batch(ex, grad_a, in1_a, in2_a, in3_a, None, FF_PARTS)

    load(1, 0)
    for name in BACKWARD:
        moved(name).start()
    grad_out = grad_low_ref[...] + grad_token_ref[...]
    grad_res, gain_grad, bias_grad = norm_back(res_d_ref[...], norms_ref[1, 0:1, :], grad_out)
    vec_own[2:3, :] = gain_grad
    vec_own[3:4, :] = bias_grad
    vec_own[6:8, :] = grad_delete_ref[0:2, :]
    cres = cres_ref[...]
    middle_low = norm_forward(cres, cgain_ref[...], cbias_ref[...]).astype(BF16)
    loaded(0)
    grad_middle = feed_back(grad_res, middle_low, up, down, hid, slope, *puts(grad_d))
    from_d = ex.to_core(grad_d.at[1 - phase], core_d)
    load(0, 4)
    grad_res, gain_grad, bias_grad = norm_back(cres, cgain_ref[...], grad_middle)
    vec_own[4:5, :] = gain_grad
    vec_own[5:6, :] = bias_grad
    branch = grad_res.astype(BF16)

    def put_cross(first, value):
        half_rows = grad_c.shape[4]
        value = value.astype(BF16).reshape(4, 2, 2, each, width)
        for at in range(0, each, 16):
            half, row = divmod(first + at, half_rows)
            grad_c[half, :, :, :, row : row + 16, :] = value[:, :, :, at : at + 16, :]

    put_cross(3 * each, mm_tn(get("cmixed")[...], branch))
    put_cross(4 * each, get("grad_place")[...])
    grad_mixed = mm_nt(branch, get("co_w")[...]).astype(BF16)
    cq_ref, ckv_ref = get("cq"), get("ckv")

    def put_q(pair, value):
        gq_ref[:, column(pair)] = value

    def put_k(pair, value):
        gckv_ref[:, column(pair)] = value

    def put_v(pair, value):
        gckv_ref[:, column(pair, width)] = value

    def between(pair):
        if pair == 2:
            batch_d.from_core(from_d, grad_d.at[phase])

    attend_backward(
        lambda pair: cq_ref[:, column(pair)],
        lambda pair: ckv_ref[:, column(pair)],
        lambda pair: ckv_ref[:, column(pair, width)],
        lambda pair: grad_mixed[:, column(pair)],
        cols_ref[:, 2:3] == rows_ref[3:4, :],
        ctotals_ref, put_q, put_k, put_v, between,
    )
    grad_q = gq_ref[...]
    put_cross(0, mm_tn(get("after")[1].astype(BF16), grad_q))
    for part in range(2):
        put_cross((1 + part) * each, mm_tn(get("src")[...], gckv_ref[:, part * width : (part + 1) * width]))
    from_c = ex.to_core(grad_c.at[1 - phase], core_c)
    after_grads[1] = grad_res + mm_nt(grad_q, get("cq_w")[...])
    grad_src = mm_nt(gckv_ref[...], get("ckv_w")[...]).astype(BF16).astype(F32)
    grad_res, gain_grad, bias_grad = norm_back(get("res_e")[...], norms_ref[0, 0:1, :], grad_src)
    vec_own[0:1, :] = gain_grad
    vec_own[1:2, :] = bias_grad
    from_v = ex.to_core(vec_own, vec_core)
    loaded(4)
    after_grads[0] = feed_back(
        grad_res, get("after")[0].astype(BF16), up, down, hid, slope, *puts(grad_e)
    )
    from_e = ex.to_core(grad_e.at[1 - phase], core_e)
    from_after = ex.to_core(after_grads.at[1 - phase], after_in)
    batch_c.from_core(from_c, grad_c.at[phase])
    res_ref, mix_w_ref, qkv_ref, mixed_ref, x_ref = [get(n) for n in ("res", "mix_w", "qkv", "mixed", "x")]
    first_vectors = []
    for turn in range(2):
        row = phase if turn == 0 else 1 - phase
        rows = pl.ds(pl.multiple_of(row * length, length), length)
        if turn == 0:
            grad_after = after_grads[phase]
        else:
            from_after.wait_recv()
            grad_after = after_in[...]
        grad_res, gain_grad, bias_grad = norm_back(res_ref[rows, :], gain_ref[0:1, :], grad_after)
        first_vectors.append((gain_grad, bias_grad))
        grad_x_ref[rows, :] = grad_res
        branch = grad_res.astype(BF16)
        if turn == 0:
            first_branch, first_rows = branch, rows
        grad_mixed = mm_nt(branch, mix_w_ref[...]).astype(BF16)

        def put(offset):
            def store(pair, value):
                grad_qkv[rows, column(pair, offset)] = value

            return store

        def between(pair):
            if turn == 0 and pair == 1:
                batch_e.from_core(from_e, grad_e.at[phase])
            if turn == 0 and pair == 3:
                batch_d.second()

        attend_backward(
            lambda pair: qkv_ref[rows, column(pair)],
            lambda pair: qkv_ref[rows, column(pair, width)],
            lambda pair: qkv_ref[rows, column(pair, 2 * width)],
            lambda pair: grad_mixed[:, column(pair)],
            jnp.where(row == 0, cols_ref[:, 0:1], cols_ref[:, 1:2])
            == jnp.where(row == 0, rows_ref[0:1, :], rows_ref[1:2, :]),
            totals_ref.at[row], put(0), put(width), put(2 * width), between,
        )
    shape = (4, 2, 2, each, width)
    grad_mix = mm_tn(mixed_ref[first_rows, :], first_branch) + mm_tn(mixed_ref[rows, :], branch)
    grad_a[:, :, :, 3 * each :, :] = grad_mix.astype(BF16).reshape(shape)
    for part in range(3):
        cols = slice(part * width, (part + 1) * width)
        value = mm_tn(x_ref[...], grad_qkv[:, cols])
        grad_a[:, :, :, part * each : (part + 1) * each, :] = value.astype(BF16).reshape(shape)
    batch_a.start()
    batch_c.second()
    grad_x_ref[...] += mm_nt(grad_qkv[...], get("qkv_w")[...])
    grad_x_copy = pltpu.make_async_copy(grad_x_ref, grad_x_any, held_sems.at[len(BACKWARD)])
    grad_x_copy.start()
    from_v.wait_recv()
    vec_1[0:8, :] = vec_own[...] + vec_core[...]
    vec_1[8:9, :] = first_vectors[0][0] + first_vectors[1][0]
    vec_1[9:10, :] = first_vectors[0][1] + first_vectors[1][1]
    vec_1[10:16, :] = jnp.zeros((6, width), F32)
    vec_x = ex.copy(vec_1, vec_in.at[0], (ex.along_x, phase))

    def put_ff(half):
        def put(rows, value):
            sums[half, rows, :] = value

        return put

    def put_attention(rows, value):
        red_attention_ref[rows, :] = value

    cross_sum = red_cross_ref.at[phase]

    def put_cross_sum(rows, value):
        cross_sum[rows, :] = value

    batch_d.put, batch_e.put, batch_c.put, batch_a.put = put_ff(1), put_ff(0), put_cross_sum, put_attention
    batch_e.second()
    batch_d.third()
    vec_x.wait_recv()
    vec_2[...] = vec_1[...] + vec_in[0]
    vec_y = ex.copy(vec_2, vec_in.at[1], (ex.along_y, phase))
    batch_c.third()
    batch_a.second()
    vec_y.wait_recv()
    vec_3[...] = vec_2[...] + vec_in[1]
    vec_z = [
        ex.copy(vec_3, vec_in.at[2 + j], (index_of(ex.x, ex.y, zz), phase)) for j, zz in enumerate(ex.zs)
    ]
    batch_e.third()
    batch_d.last()
    batch_c.last()
    cross_copy = ex.to_core(cross_sum, red_cross_ref.at[phase])
    batch_a.third()
    batch_e.last()
    ff_copy = ex.to_core(sums.at[1 - phase], red_ff_ref.at[phase])
    red_ff_ref[phase] = sums[phase]
    for copy in vec_z:
        copy.wait_recv()
    vectors_ref[...] = vec_3[...] + vec_in[2] + vec_in[3] + vec_in[4]
    batch_a.last()
    cross_copy.wait_recv()
    ff_copy.wait_recv()
    grad_x_copy.wait()
    ex.finish()


def unpack_kernel(ff_ref, attention_ref, cross_halves_ref, qkv_ref, mix_ref, up_ref, down_ref, cq_ref, ckv_ref, co_ref, place_ref):
    width = mix_ref.shape[1]
    high = mix_ref.shape[0]
    for block in range(up_ref.shape[1] // width):
        up_ref[:, block * width : (block + 1) * width] = ff_ref[0, block * high : (block + 1) * high, :]
    down_ref[...] = ff_ref[1]
    for block in range(3):
        qkv_ref[:, block * width : (block + 1) * width] = attention_ref[block * high : (block + 1) * high, :]
    mix_ref[...] = attention_ref[3 * high :, :]
    half_rows = cross_halves_ref.shape[1]

    def cross(start):
        half, row = divmod(start, half_rows)
        return cross_halves_ref[half, row : row + 16, :]

    for start in range(0, 5 * high, 16):
        part, inner = start // high, slice(start % high, start % high + 16)
        if part == 0:
            cq_ref[inner, :] = cross(start)
        elif part < 3:
            ckv_ref[inner, (part - 1) * width : part * width] = cross(start)
        elif part == 3:
            co_ref[inner, :] = cross(start)
        else:
            value = cross(start)
            cols = place_ref.shape[1]
            at = start % high
            place_ref[at : at + 16, :] = value[:, :cols]
            place_ref[high + at : high + at + 16, :] = value[:, cols:]


def whole(shape, dtype):
    return jax.ShapeDtypeStruct(shape, dtype)


def in_vmem(count):
    return [pl.BlockSpec(memory_space=VMEM)] * count


def swap(value):
    return lax.ppermute(value, "phase", [(0, 1), (1, 0)])


def unpacked(shards, height, columns):
    groups, rows, width = shards.shape
    blocks = columns // width
    parts = shards.reshape(groups, blocks, rows // blocks, width)
    return parts.transpose(0, 2, 1, 3).reshape(height, columns)


def token_head(numbers, cap, block_rows, low, flags, labels_all, flags_all, weight, weight_t, scale):
    length, width = low.shape
    dp = lax.axis_size("dp")
    shard = weight_t.shape[0]

    def choice(flags):
        place = jnp.cumsum(flags, axis=-1) - 1
        places = lax.broadcasted_iota(jnp.int32, flags.shape[:-1] + (cap, flags.shape[-1]), flags.ndim - 1)
        return (places == place[..., None, :]) & (flags[..., None, :] > 0)

    chosen = choice(flags)
    packed = mm(chosen.astype(BF16), low).astype(BF16)
    every = gather_blocks(packed, numbers[0]).reshape(2 * dp * cap, width)
    labels = jnp.max(jnp.where(choice(flags_all), labels_all[:, None, :], -1), axis=-1)
    labels = labels.reshape(dp, 2, cap).transpose(1, 0, 2).reshape(2 * dp * cap)
    tall = block_rows
    count = 2 * dp * cap // tall
    probs, totals = pl.pallas_call(
        token_forward,
        grid=(count,),
        out_shape=(whole((count, shard, tall), BF16), whole((count, 1, tall), F32)),
        in_specs=[
            pl.BlockSpec((tall, width), lambda i: (i, 0)),
            pl.BlockSpec((shard, width), lambda i: (0, 0)),
        ],
        out_specs=(
            pl.BlockSpec((1, shard, tall), lambda i: (i, 0, 0)),
            pl.BlockSpec((1, 1, tall), lambda i: (i, 0, 0)),
        ),
        compiler_params=pltpu.CompilerParams(vmem_limit_bytes=48 * 1024 * 1024),
        name="token_forward",
    )(every, weight_t)
    shares = token_shares(totals, numbers[1])
    each = tall // cap
    grad_low, grad_weight = pl.pallas_call(
        partial(token_backward, scale),
        grid=(count,),
        out_shape=(whole((2 * dp, cap, width), BF16), whole((width, shard), F32)),
        in_specs=[
            pl.BlockSpec((1, shard, tall), lambda i: (i, 0, 0)),
            pl.BlockSpec((1, 1, tall), lambda i: (i, 0, 0)),
            pl.BlockSpec((1, 1, tall), lambda i: (i, 0, 0)),
            pl.BlockSpec((tall, width), lambda i: (i, 0)),
            pl.BlockSpec((shard, width), lambda i: (0, 0)),
        ],
        out_specs=(
            pl.BlockSpec((each, cap, width), lambda i: (i, 0, 0)),
            pl.BlockSpec((width, shard), lambda i: (0, 0)),
        ),
        scratch_shapes=[VMEM((shard, width), F32)],
        compiler_params=pltpu.CompilerParams(vmem_limit_bytes=48 * 1024 * 1024),
        name="token_backward",
    )(probs, shares, labels.reshape(count, 1, tall), every, weight_t)
    back = scatter_blocks(grad_low.reshape(2, dp, cap, width), numbers[2])
    return mm_tn(chosen.astype(BF16), back.astype(BF16)), grad_weight


def on_chips(
    inputs, segments, delete_target, place_target, token_target, token_mask,
    attention_in, attention_out, feedforward_in, feedforward_out, norm_gain, norm_bias,
    cross_query, cross_keyvalue, cross_out, cross_gain, cross_bias,
    head_delete, head_place, head_token,
):
    phase, dp_index = lax.axis_index("phase"), lax.axis_index("dp")
    count, length, width = inputs.shape[1:]
    hidden, classes = feedforward_in.shape[2], head_place.shape[1]
    each = width // GROUPS
    scale = float(count * length * GROUPS) ** (-0.5)
    any_space = pl.BlockSpec(memory_space=pl.ANY)
    is_enc = phase == 0
    states = inputs[0].reshape(count * length, width)
    up_own, down_own = feedforward_in[0], feedforward_out[0]
    qkv_w, mix_w = attention_in[0], attention_out[0]
    delete_weight = jnp.pad(head_delete, ((0, 0), (0, 126)))
    gain_row, bias_row = cross_gain[None, :], cross_bias[None, :]
    shapes = {
        "qkv": ((count * length, 3 * width), BF16), "mixed": ((count * length, width), BF16),
        "res": ((count * length, width), F32), "after": ((2, length, width), F32),
        "res_e": ((length, width), F32), "ckv": ((length, 2 * width), BF16), "cq": ((length, width), BF16),
        "cmixed": ((length, width), BF16), "cres": ((length, width), F32),
        "hid_e": ((length, hidden), BF16), "slope_e": ((length, hidden), BF16),
        "hid_d": ((length, hidden), BF16), "slope_d": ((length, hidden), BF16),
        "res_d": ((length, width), F32), "src": ((length, width), BF16), "low": ((length, width), BF16),
        "grad_low": ((length, width), F32), "grad_place": ((GROUPS, each, 2 * classes), BF16),
        "co_w": ((width, width), BF16), "cq_w": ((width, width), BF16), "ckv_w": ((width, 2 * width), BF16),
        "mix_w": ((width, width), BF16), "qkv_w": ((width, 3 * width), BF16), "x": ((count * length, width), BF16),
    }
    outs = pl.pallas_call(
        partial(forward_kernel, scale),
        out_shape=(
            whole((8, length), F32), whole((length, 128), F32),
            whole((1, GROUPS * length), jnp.int32), whole((1, 2 * GROUPS * length), jnp.int32), whole((8, 128), F32),
            whole((2, 2, width), F32), whole((width, hidden), BF16), whole((hidden, width), BF16),
            whole((count, HEADS, length), F32), whole((HEADS, length), F32), whole((8, width), F32),
            *[whole(*shapes[name]) for name in FORWARD],
        ),
        in_specs=in_vmem(10) + [any_space] * 5 + in_vmem(3) + [any_space],
        out_specs=tuple(in_vmem(6) + [any_space] * 2 + in_vmem(3) + [any_space] * len(FORWARD)),
        scratch_shapes=[
            *[VMEM(*shapes[name]) for name in FORWARD],
            VMEM((2, width, hidden), BF16), VMEM((2, hidden, width), BF16),
            VMEM((width, width), BF16), VMEM((width, 2 * width), BF16), VMEM((width, width), BF16),
            VMEM((2 * width, classes), BF16), VMEM((length, width), F32),
            VMEM((2, length), jnp.int32), VMEM((4, 2, 2, 2, length), jnp.int32), VMEM((128, length), F32),
            pltpu.SemaphoreType.DMA((6,)), pltpu.SemaphoreType.DMA((len(FORWARD) + 2,)),
            pltpu.SemaphoreType.DMA((20,)), pltpu.SemaphoreType.DMA((20,)),
        ],
        compiler_params=pltpu.CompilerParams(
            collective_id=1, has_side_effects=True, vmem_limit_bytes=56 * 1024 * 1024
        ),
        name="forward",
    )(
        states, segments, delete_target, place_target, token_target, token_mask,
        qkv_w, mix_w, norm_gain[0], norm_bias[0], up_own, down_own,
        cross_query, cross_keyvalue, cross_out, gain_row, bias_row, delete_weight, head_place,
    )
    rows, cols, labels_small, labels_large, most, norms, up_other, down_other, totals, ctotals, grad_delete = outs[:11]
    saved = dict(zip(FORWARD, outs[11:]))
    grad_token, grad_weight = lax.cond(
        most[0, 0] < 0.0,
        lambda: token_chips(2, length // 2, saved["low"], rows, cols, labels_small, head_token),
        lambda: token_chips(3, length, saved["low"], rows, cols, labels_large, head_token),
    )
    other_weight = swap(grad_weight)
    grad_head_token = jnp.concatenate(
        [jnp.where(is_enc, grad_weight, other_weight), jnp.where(is_enc, other_weight, grad_weight)], axis=1
    )
    saved.update(co_w=cross_out, cq_w=cross_query, ckv_w=cross_keyvalue, mix_w=mix_w, qkv_w=qkv_w, x=states)
    half_rows, ff_half, attention_rows = 5 * each // 2, hidden // GROUPS, 4 * each
    rows_of = (ff_half, ff_half, half_rows, attention_rows)

    def shards(tall, *lead):
        return VMEM(lead + (tall, width), BF16)

    grad_states, red_ff, red_attention, red_cross, vectors = pl.pallas_call(
        backward_kernel,
        out_shape=(
            whole((count * length, width), F32), whole((2, ff_half, width), F32),
            whole((attention_rows, width), F32), whole((2, half_rows, width), F32), whole((16, width), F32),
        ),
        in_specs=in_vmem(13) + [any_space] * (8 + len(BACKWARD)),
        out_specs=tuple([any_space] + in_vmem(4)),
        scratch_shapes=[
            *[VMEM(*shapes[name]) for name in BACKWARD],
            VMEM((width, hidden), BF16), VMEM((hidden, width), BF16),
            VMEM((length, hidden), BF16), VMEM((length, hidden), BF16),
            shards(ff_half, 2, 4, 2, 2), shards(ff_half, 2, 4, 2, 2), shards(half_rows, 2, 4, 2, 2),
            shards(attention_rows, 4, 2, 2),
            shards(ff_half, 4, 2, 2), shards(ff_half, 4, 2, 2), shards(half_rows, 4, 2, 2),
            *[shards(tall, 4, 2) for tall in rows_of],
            *[shards(tall, 4) for tall in rows_of],
            *[shards(tall, 3) for tall in rows_of],
            VMEM((2, length, width), F32), VMEM((length, width), F32),
            VMEM((length, width), BF16), VMEM((length, 2 * width), BF16), VMEM((count * length, 3 * width), BF16),
            VMEM((2, ff_half, width), F32), VMEM((count * length, width), F32),
            VMEM((8, width), F32), VMEM((8, width), F32),
            VMEM((16, width), F32), VMEM((16, width), F32), VMEM((16, width), F32), VMEM((5, 16, width), F32),
            pltpu.SemaphoreType.DMA((8,)), pltpu.SemaphoreType.DMA((len(BACKWARD) + 1,)),
            pltpu.SemaphoreType.DMA((56,)), pltpu.SemaphoreType.DMA((56,)),
        ],
        compiler_params=pltpu.CompilerParams(
            collective_id=0, has_side_effects=True, vmem_limit_bytes=62 * 1024 * 1024
        ),
        name="backward",
    )(
        saved["grad_low"], grad_token, rows, cols, norms, gain_row, bias_row, ctotals, totals,
        saved["res_d"], saved["cres"], grad_delete, norm_gain[0],
        up_own, up_other, down_own, down_other,
        saved["hid_e"], saved["slope_e"], saved["hid_d"], saved["slope_d"],
        *[saved[name] for name in BACKWARD],
    )
    grads = pl.pallas_call(
        unpack_kernel,
        out_shape=(
            whole((each, 3 * width), F32), whole((each, width), F32), whole((each, hidden), F32),
            whole((hidden // GROUPS, width), F32), whole((each, width), F32), whole((each, 2 * width), F32),
            whole((each, width), F32), whole((2 * each, classes), F32),
        ),
        in_specs=in_vmem(3),
        out_specs=tuple(in_vmem(8)),
        compiler_params=pltpu.CompilerParams(vmem_limit_bytes=32 * 1024 * 1024),
        name="unpack",
    )(red_ff, red_attention, red_cross)
    g_qkv, g_mix, g_up, g_down, g_cq, g_ckv, g_co, g_place = grads
    vectors = lax.dynamic_slice_in_dim(vectors, dp_index * each, each, 1)
    second = jnp.where(is_enc, vectors[0:2], vectors[2:4])
    vector_out = jnp.concatenate([vectors[8:9], second[0:1], vectors[9:10], second[1:2], vectors[4:8]])
    return (
        grad_states.reshape(1, count, length, width),
        g_qkv[None], g_mix[None], g_up[None], g_down[None],
        vector_out[None, 0:2], vector_out[None, 2:4],
        g_cq, g_ckv, g_co, vector_out[4], vector_out[5], vector_out[6:8].T, g_place, grad_head_token,
    )


def on_any(
    inputs, segments, delete_target, place_target, token_target, token_mask,
    attention_in, attention_out, feedforward_in, feedforward_out, norm_gain, norm_bias,
    cross_query, cross_keyvalue, cross_out, cross_gain, cross_bias,
    head_delete, head_place, head_token,
):
    phase = lax.axis_index("phase")
    dp_index, dp = lax.axis_index("dp"), lax.axis_size("dp")
    count, length, width = inputs.shape[1:]
    assert count == 2
    hidden = feedforward_in.shape[2]
    scale = float(count * length * dp) ** (-0.5)
    any_space = pl.BlockSpec(memory_space=pl.ANY)
    params = pltpu.CompilerParams(vmem_limit_bytes=56 * 1024 * 1024)

    coded = jnp.where(token_mask == 1, token_target, -1)
    labels_all = lax.all_gather(coded, "dp", tiled=True)
    flags_all = (labels_all >= 0).astype(jnp.int32)

    def row_of(value):
        return lax.dynamic_index_in_dim(value, phase, 0, keepdims=False)

    own_norms = jnp.stack([norm_gain[0, 1], norm_bias[0, 1]])
    up_other, down_other = swap(feedforward_in[0]), swap(feedforward_out[0])
    other_norms = swap(own_norms)
    is_enc = phase == 0
    norms = jnp.concatenate(
        [jnp.where(is_enc, own_norms, other_norms), jnp.where(is_enc, other_norms, own_norms)]
    )
    ids = row_of(segments)
    own_ids = lax.dynamic_index_in_dim(segments, phase, 1, keepdims=False)
    states = inputs[0].reshape(count * length, width)

    qkv, mixed, res, totals, keep, send = pl.pallas_call(
        self_forward,
        out_shape=(
            whole((count * length, 3 * width), BF16),
            whole((count * length, width), BF16),
            whole((count * length, width), F32),
            whole((count, HEADS, length), F32),
            whole((length, width), F32),
            whole((length, width), F32),
        ),
        in_specs=in_vmem(7),
        out_specs=tuple(in_vmem(6)),
        compiler_params=params,
        name="self_forward",
    )(states, own_ids[:, :, None], own_ids[:, None, :], attention_in[0], attention_out[0], norm_gain[0], norm_bias[0])
    received = swap(send)

    ids_e, ids_d_row = ids[0][:, None], ids[1][None, :]
    pair_valid = jnp.concatenate([ids[1, :-1] == ids[1, 1:], jnp.zeros((1,), bool)])
    targets = jnp.stack(
        [row_of(delete_target), row_of(place_target), pair_valid.astype(jnp.int32)], axis=1
    )
    delete_weight = jnp.pad(head_delete, ((0, 0), (0, 126)))
    gain_row, bias_row = cross_gain[None, :], cross_bias[None, :]
    ff_scratch = [
        VMEM((width, hidden), BF16), VMEM((hidden, width), BF16),
        VMEM((width, hidden), BF16), VMEM((hidden, width), BF16),
    ]
    saved_shapes = (
        whole((length, width), F32),
        whole((length, width), F32),
        whole((length, width), F32),
        whole((length, 2 * width), BF16),
        whole((length, width), BF16),
        whole((length, width), BF16),
        whole((length, width), F32),
        whole((HEADS, length), F32),
        whole((length, hidden), BF16), whole((length, hidden), BF16),
        whole((length, hidden), BF16), whole((length, hidden), BF16),
        whole((length, width), F32),
        whole((length, width), BF16),
    )
    classes = head_place.shape[1]
    each = width // GROUPS
    outs = pl.pallas_call(
        partial(rows_forward, scale),
        out_shape=saved_shapes + (
            whole((length, width), BF16),
            whole((length, width), F32),
            whole((8, width), F32),
            whole((GROUPS, each, 2 * classes), BF16),
        ),
        in_specs=in_vmem(5) + [any_space] * 4 + in_vmem(8),
        out_specs=tuple(in_vmem(18)),
        scratch_shapes=ff_scratch + [pltpu.SemaphoreType.DMA((2, 2))],
        compiler_params=params,
        name="rows_forward",
    )(
        keep, received, ids_e, ids_d_row, targets,
        feedforward_in[0], up_other, feedforward_out[0], down_other, norms,
        cross_query, cross_keyvalue, cross_out, gain_row, bias_row, delete_weight, head_place,
    )
    saved = outs[:14]
    low, grad_low, grad_delete, grad_place = outs[14:]

    shard = head_token.shape[1] // (2 * dp)
    weight = lax.dynamic_slice_in_dim(head_token, (dp_index * 2 + phase) * shard, shard, 1)
    weight_t = weight.T
    flags = row_of(token_mask)

    def run_head(numbers, cap, block_rows):
        return token_head(numbers, cap, block_rows, low, flags, labels_all, flags_all, weight, weight_t, scale)

    small = length // 2
    fits = jnp.max(jnp.sum(flags_all, axis=1)) <= small
    grad_token, grad_weight = lax.cond(
        fits, lambda: run_head((1, 2, 3), small, 4 * small), lambda: run_head((4, 5, 6), length, 2 * length)
    )
    other_weight = swap(grad_weight)
    grad_head_token = jnp.concatenate(
        [jnp.where(is_enc, grad_weight, other_weight), jnp.where(is_enc, other_weight, grad_weight)], axis=1
    )

    each = width // GROUPS
    ff_rows = 2 * hidden // GROUPS
    keep, send, ff_own, ff_other, cross_shards, vectors = pl.pallas_call(
        rows_backward,
        out_shape=(
            whole((length, width), F32), whole((length, width), F32),
            whole((GROUPS, ff_rows, width), BF16), whole((GROUPS, ff_rows, width), BF16),
            whole((GROUPS, 5 * each, width), BF16), whole((8, width), F32),
        ),
        in_specs=in_vmem(4) + [any_space] * 4 + in_vmem(6 + 14 + 1),
        out_specs=(in_vmem(2) + [any_space] * 2 + in_vmem(2)),
        scratch_shapes=ff_scratch + [
            VMEM((GROUPS, ff_rows, width), BF16), VMEM((GROUPS, ff_rows, width), BF16),
            VMEM((length, width), F32), VMEM((length, width), F32),
            VMEM((length, width), BF16), VMEM((length, 2 * width), BF16),
            pltpu.SemaphoreType.DMA((2, 2)), pltpu.SemaphoreType.DMA((2,)),
        ],
        compiler_params=params,
        name="rows_backward",
    )(
        grad_low, grad_token, ids_e, ids_d_row,
        feedforward_in[0], up_other, feedforward_out[0], down_other, norms,
        cross_query, cross_keyvalue, cross_out, gain_row, bias_row, *saved, grad_place,
    )
    received = swap(send)
    ff_received = swap(ff_other)
    half_rows = 5 * each // 2
    cross_keep = lax.dynamic_slice_in_dim(cross_shards, phase * half_rows, half_rows, 1)
    cross_received = swap(lax.dynamic_slice_in_dim(cross_shards, (1 - phase) * half_rows, half_rows, 1))
    shared = jnp.concatenate([vectors[4:6], grad_delete[:2]])
    norm_own = jnp.where(is_enc, vectors[0:2], vectors[2:4])
    norm_other = jnp.where(is_enc, vectors[2:4], vectors[0:2])
    vector_received = swap(jnp.concatenate([norm_other, shared]))
    vector_sums = jnp.concatenate([norm_own, shared]) + vector_received

    grad_states, attention_shards, first_vectors = pl.pallas_call(
        self_backward,
        out_shape=(
            whole((count * length, width), F32), whole((GROUPS, 4 * each, width), BF16), whole((8, width), F32),
        ),
        in_specs=in_vmem(12),
        out_specs=tuple(in_vmem(3)),
        scratch_shapes=[VMEM((count * length, width), F32), VMEM((count * length, 3 * width), BF16)],
        compiler_params=params,
        name="self_backward",
    )(
        keep, received, states, own_ids[:, :, None], own_ids[:, None, :], attention_in[0], attention_out[0],
        norm_gain[0], qkv, mixed, res, totals,
    )

    all_vectors = jnp.stack([
        first_vectors[0], vector_sums[0], first_vectors[1], vector_sums[1],
        vector_sums[2], vector_sums[3], vector_sums[4], vector_sums[5],
    ])
    ff_sum = (ff_own.astype(F32) + ff_received.astype(F32)).astype(BF16)
    cross_sum = (cross_keep.astype(F32) + cross_received.astype(F32)).astype(BF16)
    cross_other = swap(cross_sum)
    cross_all = jnp.concatenate(
        [jnp.where(is_enc, cross_sum, cross_other), jnp.where(is_enc, cross_other, cross_sum)], axis=1
    )
    ff_up = hidden // width * each

    def spread(value):
        return lax.psum_scatter(value.astype(F32), "dp", scatter_dimension=0, tiled=True)

    g_qkv = spread(unpacked(attention_shards[:, : 3 * each], width, 3 * width))
    g_mix = spread(unpacked(attention_shards[:, 3 * each :], width, width))
    g_up = spread(unpacked(ff_sum[:, :ff_up], width, hidden))
    g_down = spread(unpacked(ff_sum[:, ff_up:], hidden, width))
    g_cq = spread(unpacked(cross_all[:, :each], width, width))
    g_ckv = spread(unpacked(cross_all[:, each : 3 * each], width, 2 * width))
    g_co = spread(unpacked(cross_all[:, 3 * each : 4 * each], width, width))
    place = cross_all[:, 4 * each :].reshape(GROUPS, each, 2, classes)
    g_place = spread(place.transpose(0, 2, 1, 3).reshape(2 * width, classes))
    vector_out = lax.psum_scatter(all_vectors, "dp", scatter_dimension=1, tiled=True)
    return (
        grad_states.reshape(1, count, length, width),
        g_qkv[None], g_mix[None], g_up[None], g_down[None],
        vector_out[None, 0:2], vector_out[None, 2:4],
        g_cq, g_ckv, g_co, vector_out[4], vector_out[5], vector_out[6:8].T, g_place, grad_head_token,
    )


def on_device(*args):
    chips = lax.axis_size("dp") == GROUPS and args[0].shape[1] == 2
    return on_chips(*args) if chips else on_any(*args)


def solution(mesh):
    layer, row = P("phase", None, None), P("dp", None)
    return jax.shard_map(
        on_device,
        mesh=mesh,
        in_specs=(P("phase", "dp", None, None), P("dp", None, None), row, row, row, row)
        + (layer,) * 6 + (P(),) * 8,
        out_specs=(P("phase", "dp", None, None),) + (P("phase", "dp", None),) * 4
        + (P("phase", None, "dp"),) * 2 + (row,) * 3 + (P("dp"),) * 2 + (row,) * 2 + (P(None, "dp"),),
        check_vma=False,
    )
```

```python
from functools import partial

import jax
import jax.numpy as jnp
from jax import lax
from jax.experimental import pallas as pl
from jax.experimental.pallas import tpu as pltpu
from jax.sharding import PartitionSpec as P

HEADS = 8
HEAD = 64
PAIR = 2 * HEAD
MASKED_SCORE = -1e30
NORM_EPSILON = 1e-05
GROUPS = 16
F32 = jnp.float32
BF16 = jnp.bfloat16
MESH = pl.DeviceIdType.MESH
VMEM = pltpu.VMEM
GELU_C = 0.7978845608028654
GELU_A = 0.044715


def mm(left, right):
    return jnp.dot(left, right, preferred_element_type=F32)


def mm_nt(left, right):
    return lax.dot_general(left, right, (((1,), (1,)), ((), ())), preferred_element_type=F32)


def mm_tn(left, right):
    return lax.dot_general(left, right, (((0,), (0,)), ((), ())), preferred_element_type=F32)


def norm_forward(residual, gain, bias):
    centered = residual - jnp.mean(residual, axis=-1, keepdims=True)
    variance = jnp.mean(centered * centered, axis=-1, keepdims=True)
    return centered * lax.rsqrt(variance + NORM_EPSILON) * gain + bias


def norm_back(residual, gain, grad_out):
    centered = residual - jnp.mean(residual, axis=-1, keepdims=True)
    variance = jnp.mean(centered * centered, axis=-1, keepdims=True)
    scale = lax.rsqrt(variance + NORM_EPSILON)
    unit = centered * scale
    grad_unit = grad_out * gain
    grad_gain = jnp.sum(grad_out * unit, axis=0, keepdims=True)
    grad_bias = jnp.sum(grad_out, axis=0, keepdims=True)
    grad_res = scale * (
        grad_unit
        - jnp.mean(grad_unit, axis=-1, keepdims=True)
        - unit * jnp.mean(grad_unit * unit, axis=-1, keepdims=True)
    )
    return grad_res, grad_gain, grad_bias


def gelu_both(pre):
    square = pre * pre
    bent = jnp.tanh(GELU_C * pre * (1.0 + GELU_A * square))
    half = 0.5 * (1.0 + bent)
    slope = half + (0.5 * GELU_C) * pre * (1.0 - bent * bent) * (1.0 + 3.0 * GELU_A * square)
    return pre * half, slope


def attend_forward(queries, keys, values, allowed, out_ref, totals_ref, rows):
    lane = lax.broadcasted_iota(jnp.int32, (1, PAIR), 1)
    for pair in range(HEADS // 2):
        q, k, v = queries(pair), keys(pair), values(pair)
        mixed = None
        for side in range(2):
            own = (lane < HEAD) if side == 0 else (lane >= HEAD)
            scores = mm_nt(k, jnp.where(own, q * HEAD ** (-0.5), 0))
            scores = jnp.where(allowed, scores, MASKED_SCORE)
            top = jnp.max(scores, axis=0, keepdims=True)
            weights = jnp.exp(scores - top)
            summed = jnp.sum(weights, axis=0, keepdims=True)
            probs = (weights * (1.0 / summed)).astype(BF16)
            totals_ref[2 * pair + side : 2 * pair + side + 1, :] = top + jnp.log(summed)
            part = mm_tn(probs, jnp.where(own, v, 0))
            mixed = part if mixed is None else mixed + part
        out_ref[rows, pair * PAIR : (pair + 1) * PAIR] = mixed.astype(BF16)


def attend_backward(
    queries, keys, values, grads, allowed, totals_ref, put_q, put_k, put_v, between=None
):
    lane = lax.broadcasted_iota(jnp.int32, (1, PAIR), 1)
    for pair in range(HEADS // 2):
        q, k, v, da = queries(pair), keys(pair), values(pair), grads(pair)
        grad_q = grad_k = grad_v = None
        for side in range(2):
            own = (lane < HEAD) if side == 0 else (lane >= HEAD)
            q_own = jnp.where(own, q * HEAD ** (-0.5), 0)
            da_own = jnp.where(own, da, 0)
            scores = jnp.where(allowed, mm_nt(k, q_own), MASKED_SCORE)
            probs = jnp.exp(scores - totals_ref[2 * pair + side : 2 * pair + side + 1, :])
            grad_probs = mm_nt(v, da_own)
            part_v = mm(probs.astype(BF16), da_own)
            shared = jnp.sum(probs * grad_probs, axis=0, keepdims=True)
            grad_scores = (probs * (grad_probs - shared)).astype(BF16)
            part_k = mm(grad_scores, q_own)
            part_q = mm_tn(grad_scores, jnp.where(own, k, 0))
            grad_q = part_q if grad_q is None else grad_q + part_q
            grad_k = part_k if grad_k is None else grad_k + part_k
            grad_v = part_v if grad_v is None else grad_v + part_v
        put_q(pair, (grad_q * HEAD ** (-0.5)).astype(BF16))
        put_k(pair, grad_k.astype(BF16))
        put_v(pair, grad_v.astype(BF16))
        if between is not None:
            between(pair)


def column(pair, offset=0):
    return slice(offset + pair * PAIR, offset + (pair + 1) * PAIR)


def put_shards(ref, first, grad):
    height = grad.shape[0] // GROUPS
    width = ref.shape[2]
    for block in range(grad.shape[1] // width):
        piece = grad[:, block * width : (block + 1) * width].astype(BF16)
        ref[:, first + block * height : first + (block + 1) * height, :] = piece.reshape(
            GROUPS, height, width
        )


def self_forward(
    x_ref, ids_ref, ids_row_ref, qkv_w_ref, mix_w_ref, gain_ref, bias_ref,
    qkv_ref, mixed_ref, res_ref, totals_ref, keep_ref, send_ref,
):
    phase = lax.axis_index("phase")
    count, length = ids_ref.shape[0], ids_ref.shape[1]
    width = x_ref.shape[1]
    for part in range(3):
        cols = slice(part * width, (part + 1) * width)
        qkv_ref[:, cols] = mm(x_ref[...], qkv_w_ref[:, cols]).astype(BF16)
    for row in range(count):
        rows = slice(row * length, (row + 1) * length)
        attend_forward(
            lambda pair: qkv_ref[rows, column(pair)],
            lambda pair: qkv_ref[rows, column(pair, width)],
            lambda pair: qkv_ref[rows, column(pair, 2 * width)],
            ids_ref[row] == ids_row_ref[row],
            mixed_ref, totals_ref.at[row], rows,
        )
    for row in range(count):
        rows = slice(row * length, (row + 1) * length)
        residual = x_ref[rows, :].astype(F32) + mm(mixed_ref[rows, :], mix_w_ref[...])
        res_ref[rows, :] = residual
        after = norm_forward(residual, gain_ref[0:1, :], bias_ref[0:1, :])

        @pl.when(phase == row)
        def _():
            keep_ref[...] = after

        @pl.when(phase != row)
        def _():
            send_ref[...] = after


def load_sided(phase, own_refs, other_refs, enc_refs, dec_refs, sems):
    for i, (own, other, enc, dec) in enumerate(zip(own_refs, other_refs, enc_refs, dec_refs)):
        @pl.when(phase == 0)
        def _():
            pltpu.make_async_copy(own, enc, sems.at[0, i]).start()
            pltpu.make_async_copy(other, dec, sems.at[1, i]).start()

        @pl.when(phase != 0)
        def _():
            pltpu.make_async_copy(other, enc, sems.at[0, i]).start()
            pltpu.make_async_copy(own, dec, sems.at[1, i]).start()

    def wait_enc(i):
        pltpu.make_async_copy(own_refs[i], enc_refs[i], sems.at[0, i]).wait()

    def wait_dec(i):
        pltpu.make_async_copy(own_refs[i], dec_refs[i], sems.at[1, i]).wait()

    return wait_enc, wait_dec


def feed_forward(middle, up_ref, down_ref, hidden_ref, slope_ref):
    width = middle.shape[1]
    low = middle.astype(BF16)
    total = middle
    for part in range(up_ref.shape[1] // width):
        cols = slice(part * width, (part + 1) * width)
        hidden, slope = gelu_both(mm(low, up_ref[:, cols]))
        hidden = hidden.astype(BF16)
        hidden_ref[:, cols] = hidden
        slope_ref[:, cols] = slope.astype(BF16)
        total = total + mm(hidden, down_ref[cols, :])
    return total


def feed_back(grad_res, middle_low, up_ref, down_ref, hidden_ref, slope_ref, put_up, put_down, between=None):
    width = grad_res.shape[1]
    branch = grad_res.astype(BF16)
    total = grad_res
    for part in range(up_ref.shape[1] // width):
        cols = slice(part * width, (part + 1) * width)
        put_down(part, mm_tn(hidden_ref[:, cols], branch))
        grad_hidden = mm_nt(branch, down_ref[cols, :])
        grad_pre = (grad_hidden * slope_ref[:, cols].astype(F32)).astype(BF16)
        put_up(part, mm_tn(middle_low, grad_pre))
        total = total + mm_nt(grad_pre, up_ref[:, cols])
        if between is not None:
            between(part)
    return total


def feed_puts(ref, parts):
    width = ref.shape[2]
    rows = width // GROUPS
    per, tall = GROUPS // parts, parts * rows

    def put_up(part, value):
        put_shards(ref, part * rows, value)

    def put_down(part, value):
        ref[part * per : (part + 1) * per, tall : 2 * tall, :] = value.astype(BF16).reshape(
            per, tall, width
        )

    return put_up, put_down


def class_grads(logits, labels, row_weight, valid):
    lane = lax.broadcasted_iota(jnp.int32, logits.shape, 1)
    logits = jnp.where(lane < valid, logits, -jnp.inf) if valid < logits.shape[1] else logits
    top = jnp.max(logits, axis=-1, keepdims=True)
    weights = jnp.exp(logits - top)
    probs = weights * (1.0 / jnp.sum(weights, axis=-1, keepdims=True))
    return (probs - (lane == labels).astype(F32)) * row_weight


def rows_forward(
    scale, keep_ref, recv_ref, ids_e_ref, ids_d_row_ref, targets_ref,
    up_own, up_other, down_own, down_other, norms_ref,
    cq_w_ref, ckv_w_ref, co_w_ref, cgain_ref, cbias_ref, delete_w_ref, place_w_ref,
    after_e_ref, res_e_ref, after_d_ref, ckv_ref, cq_ref, cmixed_ref, cres_ref, ctotals_ref,
    hid_e_ref, slope_e_ref, hid_d_ref, slope_d_ref, res_d_ref, src_ref,
    low_ref, grad_ref, grad_delete_ref, grad_place_ref,
    up_e, down_e, up_d, down_d, sems,
):
    phase = lax.axis_index("phase")
    width = keep_ref.shape[1]
    wait_enc, wait_dec = load_sided(
        phase, (up_own, down_own), (up_other, down_other), (up_e, down_e), (up_d, down_d), sems
    )

    @pl.when(phase == 0)
    def _():
        after_e_ref[...] = keep_ref[...]
        after_d_ref[...] = recv_ref[...]

    @pl.when(phase != 0)
    def _():
        after_e_ref[...] = recv_ref[...]
        after_d_ref[...] = keep_ref[...]

    wait_enc(0)
    wait_enc(1)
    encoder_rows(
        after_e_ref, up_e, down_e, norms_ref[0:1, :], norms_ref[1:2, :], ckv_w_ref,
        hid_e_ref, slope_e_ref, res_e_ref, src_ref, ckv_ref,
    )
    middle = cross_rows(
        after_d_ref, ids_e_ref[...] == ids_d_row_ref[...], cq_w_ref, co_w_ref, cgain_ref, cbias_ref,
        cq_ref, ckv_ref, cmixed_ref, cres_ref, ctotals_ref,
    )
    wait_dec(0)
    wait_dec(1)
    targets = targets_ref[...]
    decoder_rows(
        scale, middle, up_d, down_d, norms_ref[2:3, :], norms_ref[3:4, :],
        targets[:, 0:1], targets[:, 1:2], targets[:, 2:3], delete_w_ref, place_w_ref,
        hid_d_ref, slope_d_ref, res_d_ref, low_ref, grad_ref, grad_delete_ref, grad_place_ref,
    )


def encoder_rows(
    after_ref, up, down, gain, bias, ckv_w_ref, hid_ref, slope_ref, res_ref, src_ref, ckv_ref
):
    residual = feed_forward(after_ref[...], up, down, hid_ref, slope_ref)
    res_ref[...] = residual
    src = norm_forward(residual, gain, bias).astype(BF16)
    src_ref[...] = src
    width = src.shape[1]
    for part in range(2):
        cols = slice(part * width, (part + 1) * width)
        ckv_ref[:, cols] = mm(src, ckv_w_ref[:, cols]).astype(BF16)


def cross_rows(
    after_ref, allowed, cq_w_ref, co_w_ref, cgain_ref, cbias_ref, cq_ref, ckv_ref, cmixed_ref, cres_ref, ctotals_ref
):
    width = after_ref.shape[1]
    cq_ref[...] = mm(after_ref[...].astype(BF16), cq_w_ref[...]).astype(BF16)
    attend_forward(
        lambda pair: cq_ref[:, column(pair)],
        lambda pair: ckv_ref[:, column(pair)],
        lambda pair: ckv_ref[:, column(pair, width)],
        allowed, cmixed_ref, ctotals_ref, slice(None),
    )
    residual = after_ref[...] + mm(cmixed_ref[...], co_w_ref[...])
    cres_ref[...] = residual
    return norm_forward(residual, cgain_ref[...], cbias_ref[...])


def decoder_rows(
    scale, middle, up, down, gain, bias, delete_label, place_label, pair_valid, delete_w_ref, place_w_ref,
    hid_ref, slope_ref, res_ref, low_ref, grad_ref, grad_delete_ref, grad_place_ref,
):
    residual = feed_forward(middle, up, down, hid_ref, slope_ref)
    res_ref[...] = residual
    low = norm_forward(residual, gain, bias).astype(BF16)
    low_ref[...] = low
    length, width = low.shape
    valid = delete_w_ref.shape[0]
    weight = jnp.concatenate([delete_w_ref[...], jnp.zeros((128 - valid, width), BF16)], axis=0)
    grads = class_grads(mm_nt(low, weight), delete_label, scale, valid).astype(BF16)
    grad_delete_ref[...] = mm_tn(grads, low)[:8]
    grad_low = mm(grads, weight)
    logits = mm(low, place_w_ref[:width, :]) + pltpu.roll(
        mm(low, place_w_ref[width:, :]), length - 1, 0
    )
    weight = pair_valid.astype(F32) * scale
    grads = class_grads(logits, place_label, weight, logits.shape[1])
    later = pltpu.roll(grads, 1, 0).astype(BF16)
    grads = grads.astype(BF16)
    classes = grads.shape[1]
    for top, part in enumerate((grads, later)):
        part = mm_tn(low, part).astype(BF16).reshape(GROUPS // 2, 2, width // GROUPS, classes)
        at = slice(top * GROUPS // 2, (top + 1) * GROUPS // 2)
        for half in range(2):
            grad_place_ref[at, :, half * classes : (half + 1) * classes] = part[:, half]
    grad_low = grad_low + mm_nt(grads, place_w_ref[:width, :]) + mm_nt(later, place_w_ref[width:, :])
    grad_ref[...] = grad_low


def rows_backward(
    grad_low_ref, grad_token_ref, ids_e_ref, ids_d_row_ref,
    up_own, up_other, down_own, down_other, norms_ref,
    cq_w_ref, ckv_w_ref, co_w_ref, cgain_ref, cbias_ref,
    after_e_ref, res_e_ref, after_d_ref, ckv_ref, cq_ref, cmixed_ref, cres_ref, ctotals_ref,
    hid_e_ref, slope_e_ref, hid_d_ref, slope_d_ref, res_d_ref, src_ref, grad_place_ref,
    keep_ref, send_ref, own_ref, other_ref, cross_ref, vectors_ref,
    up_e, down_e, up_d, down_d, grad_e, grad_d, after_e_grad, after_d_grad, gq_ref, gckv_ref, sems, out_sems,
):
    phase = lax.axis_index("phase")
    width = grad_low_ref.shape[1]
    wait_enc, wait_dec = load_sided(
        phase, (up_own, down_own), (up_other, down_other), (up_e, down_e), (up_d, down_d), sems
    )
    grad_out = grad_low_ref[...] + grad_token_ref[...]
    grad_res, gain_grad, bias_grad = norm_back(res_d_ref[...], norms_ref[2:3, :], grad_out)
    vectors_ref[2:3, :] = gain_grad
    vectors_ref[3:4, :] = bias_grad
    cres = cres_ref[...]
    middle_low = norm_forward(cres, cgain_ref[...], cbias_ref[...]).astype(BF16)
    wait_dec(0)
    wait_dec(1)
    grad_middle = feed_back(grad_res, middle_low, up_d, down_d, hid_d_ref, slope_d_ref, *feed_puts(grad_d, 4))
    move_d = [
        pltpu.make_async_copy(grad_d, own_ref, out_sems.at[0]),
        pltpu.make_async_copy(grad_d, other_ref, out_sems.at[0]),
    ]

    @pl.when(phase == 0)
    def _():
        move_d[1].start()

    @pl.when(phase != 0)
    def _():
        move_d[0].start()

    grad_res, gain_grad, bias_grad = norm_back(cres, cgain_ref[...], grad_middle)
    vectors_ref[4:5, :] = gain_grad
    vectors_ref[5:6, :] = bias_grad
    branch = grad_res.astype(BF16)
    after_low = after_d_ref[...].astype(BF16)
    rows = width // GROUPS
    put_shards(cross_ref, 3 * rows, mm_tn(cmixed_ref[...], branch))
    grad_mixed = mm_nt(branch, co_w_ref[...]).astype(BF16)

    def put_q(pair, value):
        gq_ref[:, column(pair)] = value

    def put_k(pair, value):
        gckv_ref[:, column(pair)] = value

    def put_v(pair, value):
        gckv_ref[:, column(pair, width)] = value

    attend_backward(
        lambda pair: cq_ref[:, column(pair)],
        lambda pair: ckv_ref[:, column(pair)],
        lambda pair: ckv_ref[:, column(pair, width)],
        lambda pair: grad_mixed[:, column(pair)],
        ids_e_ref[...] == ids_d_row_ref[...],
        ctotals_ref, put_q, put_k, put_v,
    )
    grad_q = gq_ref[...]
    grad_kv = gckv_ref[...]
    put_shards(cross_ref, 0, mm_tn(after_low, grad_q))
    put_shards(cross_ref, rows, mm_tn(src_ref[...], grad_kv))
    cross_ref[:, 4 * rows : 5 * rows, :] = grad_place_ref[...]
    after_d_grad[...] = grad_res + mm_nt(grad_q, cq_w_ref[...])
    grad_src = mm_nt(grad_kv, ckv_w_ref[...]).astype(BF16).astype(F32)
    grad_res, gain_grad, bias_grad = norm_back(res_e_ref[...], norms_ref[0:1, :], grad_src)
    vectors_ref[0:1, :] = gain_grad
    vectors_ref[1:2, :] = bias_grad
    vectors_ref[6:8, :] = jnp.zeros((2, width), F32)
    wait_enc(0)
    wait_enc(1)
    after_e_grad[...] = feed_back(
        grad_res, after_e_ref[...].astype(BF16), up_e, down_e, hid_e_ref, slope_e_ref,
        *feed_puts(grad_e, 4),
    )
    move_e = [
        pltpu.make_async_copy(grad_e, own_ref, out_sems.at[1]),
        pltpu.make_async_copy(grad_e, other_ref, out_sems.at[1]),
    ]

    @pl.when(phase == 0)
    def _():
        move_e[0].start()
        keep_ref[...] = after_e_grad[...]
        send_ref[...] = after_d_grad[...]

    @pl.when(phase != 0)
    def _():
        move_e[1].start()
        keep_ref[...] = after_d_grad[...]
        send_ref[...] = after_e_grad[...]

    move_d[0].wait()
    move_e[0].wait()


def self_backward(
    keep_ref, recv_ref, x_ref, ids_ref, ids_row_ref, qkv_w_ref, mix_w_ref, gain_ref,
    qkv_ref, mixed_ref, res_ref, totals_ref,
    grad_x_ref, shards_ref, vectors_ref,
    after_grad, grad_qkv,
):
    phase = lax.axis_index("phase")
    count, length = ids_ref.shape[0], ids_ref.shape[1]
    width = x_ref.shape[1]
    for row in range(count):
        rows = slice(row * length, (row + 1) * length)

        @pl.when(phase == row)
        def _():
            after_grad[rows, :] = keep_ref[...]

        @pl.when(phase != row)
        def _():
            after_grad[rows, :] = recv_ref[...]

    grad_res, gain_grad, bias_grad = norm_back(res_ref[...], gain_ref[0:1, :], after_grad[...])
    vectors_ref[0:1, :] = gain_grad
    vectors_ref[1:2, :] = bias_grad
    vectors_ref[2:8, :] = jnp.zeros((6, width), F32)
    grad_x_ref[...] = grad_res
    branch = grad_res.astype(BF16)
    rows_each = width // GROUPS
    put_shards(shards_ref, 3 * rows_each, mm_tn(mixed_ref[...], branch))
    grad_mixed = mm_nt(branch, mix_w_ref[...]).astype(BF16)
    for row in range(count):
        rows = slice(row * length, (row + 1) * length)

        def put(offset):
            def store(pair, value):
                grad_qkv[rows, column(pair, offset)] = value

            return store

        attend_backward(
            lambda pair: qkv_ref[rows, column(pair)],
            lambda pair: qkv_ref[rows, column(pair, width)],
            lambda pair: qkv_ref[rows, column(pair, 2 * width)],
            lambda pair: grad_mixed[rows, column(pair)],
            ids_ref[row] == ids_row_ref[row],
            totals_ref.at[row], put(0), put(width), put(2 * width),
        )
    for part in range(3):
        cols = slice(part * width, (part + 1) * width)
        put_shards(shards_ref, part * rows_each, mm_tn(x_ref[...], grad_qkv[:, cols]))
    grad_x_ref[...] += mm_nt(grad_qkv[...], qkv_w_ref[...])


def token_forward(low_ref, weight_ref, probs_ref, totals_ref):
    logits = mm_nt(weight_ref[...], low_ref[...])
    top = jnp.max(logits, axis=0, keepdims=True)
    weights = jnp.exp(logits - top)
    summed = jnp.sum(weights, axis=0, keepdims=True)
    probs_ref[0] = (weights * (1.0 / summed)).astype(BF16)
    totals_ref[0] = top + jnp.log(summed)


def token_backward(
    scale, probs_ref, share_ref, label_ref, low_ref, weight_ref, grad_low_ref, grad_weight_ref, total
):
    step = pl.program_id(0)
    labels = label_ref[0]
    shape = probs_ref.shape[1:]
    offset = (lax.axis_index("dp") * 2 + lax.axis_index("phase")) * shape[0]
    chosen = lax.broadcasted_iota(jnp.int32, shape, 0) == labels - offset
    grads = probs_ref[0].astype(F32) * share_ref[0] - chosen.astype(F32)
    grads = (grads * jnp.where(labels >= 0, scale, 0.0)).astype(BF16)
    grad_low = mm_tn(grads, weight_ref[...]).astype(BF16)
    cap = grad_low_ref.shape[1]
    for block in range(grad_low_ref.shape[0]):
        grad_low_ref[block] = grad_low[block * cap : (block + 1) * cap]
    part = mm(grads, low_ref[...])

    @pl.when(step == 0)
    def _():
        total[...] = part

    @pl.when(step != 0)
    def _():
        total[...] += part

    @pl.when(step == pl.num_programs(0) - 1)
    def _():
        grad_weight_ref[...] = total[...].T


def place_of(dp):
    return lax.rem(dp, 2), lax.rem(dp // 2, 2), dp // 4


def index_of(x, y, z):
    return (z * 2 + y) * 2 + x


def greet(devices):
    barrier = pltpu.get_barrier_semaphore()
    for dp, phase in devices:
        pl.semaphore_signal(barrier, inc=1, device_id=(dp, phase), device_id_type=MESH)
    pl.semaphore_wait(barrier, len(devices))


def remote(src, dst, send, recv, device):
    return pltpu.make_async_remote_copy(
        src_ref=src, dst_ref=dst, send_sem=send, recv_sem=recv, device_id=device, device_id_type=MESH
    )


def gather_kernel(block_ref, out_ref, send, recv, local):
    dp, phase = lax.axis_index("dp"), lax.axis_index("phase")
    x, y, z = place_of(dp)
    x_first = phase == 0
    zs = [lax.rem(z + k, 4) for k in (1, 2, 3)]
    second = index_of(jnp.where(x_first, 1 - x, x), jnp.where(x_first, y, 1 - y), z)
    third = index_of(jnp.where(x_first, x, 1 - x), jnp.where(x_first, 1 - y, y), z)
    greet([(index_of(x, y, k), phase) for k in zs] + [(second, phase), (third, phase), (dp, 1 - phase)])
    own = pltpu.make_async_copy(block_ref, out_ref.at[phase, z, y, x], local.at[0])
    own.start()
    started = []
    first = []
    for k in range(3):
        copy = remote(
            block_ref, out_ref.at[phase, z, y, x], send.at[k], recv.at[k], (index_of(x, y, zs[k]), phase)
        )
        copy.start()
        first.append(copy)
    cross = []

    def to_core(slot, src):
        copy = remote(src, src, send.at[slot], recv.at[slot], (dp, 1 - phase))
        copy.start()
        cross.append(copy)

    mine = remote(block_ref, out_ref.at[phase, z, y, x], send.at[3], recv.at[3], (dp, 1 - phase))
    mine.start()
    cross.append(mine)
    own.wait()
    seconds = []
    x2 = jnp.where(x_first, 1 - x, x)
    y2 = jnp.where(x_first, y, 1 - y)
    x3 = jnp.where(x_first, x, 1 - x)
    y3 = jnp.where(x_first, 1 - y, y)

    def relay(slot, zz, yy, xx, device, into):
        src = out_ref.at[phase, zz, yy, xx]
        copy = remote(src, src, send.at[slot], recv.at[slot], (device, phase))
        copy.start()
        into.append(copy)

    thirds = []
    relay(4, z, y, x, second, seconds)
    relay(8, z, y, x, third, thirds)
    sources = [lax.rem(z + 4 - k, 4) for k in (1, 2, 3)]
    for k in range(3):
        first[k].wait_recv()
        relay(5 + k, sources[k], y, x, second, seconds)
        relay(9 + k, sources[k], y, x, third, thirds)
        to_core(16 + k, out_ref.at[phase, sources[k], y, x])
    order = [z] + sources
    for k in range(4):
        seconds[k].wait_recv()
        relay(12 + k, order[k], y2, x2, third, thirds)
        to_core(19 + k, out_ref.at[phase, order[k], y2, x2])
    for k in range(8):
        thirds_k = thirds[k]
        thirds_k.wait_recv()
        where_y, where_x = (y3, x3) if k < 4 else (1 - y, 1 - x)
        to_core(23 + k, out_ref.at[phase, order[k % 4], where_y, where_x])
    for copy in cross:
        copy.wait_recv()
    for copy in first + seconds + thirds + cross:
        copy.wait_send()


def gather_blocks(block, number):
    dp = lax.axis_size("dp")
    if dp != GROUPS:
        return lax.all_gather(lax.all_gather(block, "dp"), "phase")
    rows, width = block.shape
    out = pl.pallas_call(
        gather_kernel,
        out_shape=jax.ShapeDtypeStruct((2, 4, 2, 2, rows, width), block.dtype),
        in_specs=[pl.BlockSpec(memory_space=pl.ANY)],
        out_specs=pl.BlockSpec(memory_space=pl.ANY),
        scratch_shapes=[
            pltpu.SemaphoreType.DMA((31,)), pltpu.SemaphoreType.DMA((31,)), pltpu.SemaphoreType.DMA((1,)),
        ],
        compiler_params=pltpu.CompilerParams(collective_id=number, has_side_effects=True),
        name="gather_blocks",
    )(block)
    return out.reshape(2, dp, rows, width)


def scatter_kernel(part_ref, out_ref, core_in, third_out, third_in, second_out, second_in, z_out, z_in, send, recv):
    dp, phase = lax.axis_index("dp"), lax.axis_index("phase")
    x, y, z = place_of(dp)
    x_first = phase == 0
    x2 = jnp.where(x_first, 1 - x, x)
    y2 = jnp.where(x_first, y, 1 - y)
    x3 = jnp.where(x_first, x, 1 - x)
    y3 = jnp.where(x_first, 1 - y, y)
    second, third = index_of(x2, y2, z), index_of(x3, y3, z)
    zs = [lax.rem(z + k, 4) for k in (1, 2, 3)]
    greet([(index_of(x, y, k), phase) for k in zs] + [(second, phase), (third, phase), (dp, 1 - phase)])
    order = [lax.rem(z + k, 4) for k in (1, 2, 3, 0)]
    spots = (
        [(zz, 1 - y, 1 - x) for zz in order]
        + [(zz, y3, x3) for zz in order]
        + [(zz, y2, x2) for zz in order]
        + [(zz, y, x) for zz in order]
    )
    theirs = (
        [(zz, 1 - y, 1 - x) for zz in order]
        + [(zz, y2, x2) for zz in order]
        + [(zz, y3, x3) for zz in order]
        + [(zz, y, x) for zz in order]
    )
    cores = []
    for j in range(16):
        zz, yy, xx = theirs[j]
        copy = remote(part_ref.at[1 - phase, zz, yy, xx], core_in.at[j], send.at[j], recv.at[j], (dp, 1 - phase))
        copy.start()
        cores.append(copy)

    def both(j):
        zz, yy, xx = spots[j]
        cores[j].wait_recv()
        return part_ref[phase, zz, yy, xx].astype(F32) + core_in[j].astype(F32)

    thirds = []
    for j in range(8):
        third_out[j] = both(j).astype(BF16)
        copy = remote(third_out.at[j], third_in.at[j], send.at[16 + j], recv.at[16 + j], (third, phase))
        copy.start()
        thirds.append(copy)
    seconds = []
    for j in range(4):
        total = both(8 + j)
        thirds[j].wait_recv()
        second_out[j] = (total + third_in[j].astype(F32)).astype(BF16)
        copy = remote(second_out.at[j], second_in.at[j], send.at[24 + j], recv.at[24 + j], (second, phase))
        copy.start()
        seconds.append(copy)
    along = []
    for j in range(4):
        total = both(12 + j)
        thirds[4 + j].wait_recv()
        total = total + third_in[4 + j].astype(F32)
        seconds[j].wait_recv()
        total = total + second_in[j].astype(F32)
        if j < 3:
            z_out[j] = total.astype(BF16)
            copy = remote(z_out.at[j], z_in.at[j], send.at[28 + j], recv.at[28 + j], (index_of(x, y, zs[j]), phase))
            copy.start()
            along.append(copy)
        else:
            for copy in along:
                copy.wait_recv()
            out_ref[...] = total + z_in[0].astype(F32) + z_in[1].astype(F32) + z_in[2].astype(F32)
    for copy in cores + thirds + seconds + along:
        copy.wait_send()


def scatter_blocks(part, number):
    dp = lax.axis_size("dp")
    if dp != GROUPS:
        part = lax.psum_scatter(part.astype(F32), "phase", scatter_dimension=0, tiled=False)
        return lax.psum_scatter(part, "dp", scatter_dimension=0, tiled=False)
    rows, width = part.shape[2:]
    return pl.pallas_call(
        scatter_kernel,
        out_shape=jax.ShapeDtypeStruct((rows, width), F32),
        in_specs=[pl.BlockSpec(memory_space=VMEM)],
        out_specs=pl.BlockSpec(memory_space=VMEM),
        scratch_shapes=[VMEM((n, rows, width), BF16) for n in (16, 8, 8, 4, 4, 3, 3)]
        + [pltpu.SemaphoreType.DMA((31,)), pltpu.SemaphoreType.DMA((31,))],
        compiler_params=pltpu.CompilerParams(
            collective_id=number, has_side_effects=True, vmem_limit_bytes=48 * 1024 * 1024
        ),
        name="scatter_blocks",
    )(part.reshape(2, 4, 2, 2, rows, width))


def share_kernel(totals_ref, share_ref, near_in, joined, far_in, send, recv):
    dp, phase = lax.axis_index("dp"), lax.axis_index("phase")
    x, y, z = place_of(dp)
    near = [
        (index_of(lax.rem(x + a, 2), lax.rem(y + b, 2), z), lax.rem(phase + c, 2))
        for a in range(2) for b in range(2) for c in range(2) if a + b + c
    ]
    far = [(index_of(x, y, lax.rem(z + k, 4)), phase) for k in (1, 2, 3)]
    greet(near + far)

    def join(parts):
        top = parts[0]
        for part in parts[1:]:
            top = jnp.maximum(top, part)
        summed = jnp.exp(parts[0] - top)
        for part in parts[1:]:
            summed = summed + jnp.exp(part - top)
        return top + jnp.log(summed)

    copies = []
    for j, device in enumerate(near):
        copies.append(remote(totals_ref, near_in.at[j], send.at[j], recv.at[j], device))
        copies[-1].start()
    for copy in copies:
        copy.wait_recv()
    total = join([totals_ref[...]] + [near_in[j] for j in range(7)])
    joined[...] = total
    for j, device in enumerate(far):
        copies.append(remote(joined, far_in.at[j], send.at[7 + j], recv.at[7 + j], device))
        copies[-1].start()
    for copy in copies[7:]:
        copy.wait_recv()
    share_ref[...] = jnp.exp(totals_ref[...] - join([total] + [far_in[j] for j in range(3)]))
    for copy in copies:
        copy.wait_send()


def token_shares(totals, number):
    if lax.axis_size("dp") != GROUPS:
        top = lax.pmax(totals, ("dp", "phase"))
        return jnp.exp(totals - top) / lax.psum(jnp.exp(totals - top), ("dp", "phase"))
    flat = totals.reshape(-1, 128)
    rows = flat.shape[0]
    share = pl.pallas_call(
        share_kernel,
        out_shape=jax.ShapeDtypeStruct((rows, 128), F32),
        in_specs=[pl.BlockSpec(memory_space=VMEM)],
        out_specs=pl.BlockSpec(memory_space=VMEM),
        scratch_shapes=[
            VMEM((7, rows, 128), F32), VMEM((rows, 128), F32), VMEM((3, rows, 128), F32),
            pltpu.SemaphoreType.DMA((10,)), pltpu.SemaphoreType.DMA((10,)),
        ],
        compiler_params=pltpu.CompilerParams(collective_id=number, has_side_effects=True),
        name="token_shares",
    )(flat)
    return share.reshape(totals.shape)


def pack_labels(labels, flags, out_ref):
    count, length = labels.shape
    before = lax.broadcasted_iota(jnp.int32, (length, length), 0)
    after = lax.broadcasted_iota(jnp.int32, (length, length), 1)
    upto = jnp.where(before <= after, 1.0, 0.0).astype(BF16)
    rows = jnp.concatenate([flags.astype(F32)] + [jnp.zeros((8 - count, length), F32)], axis=0)
    place = mm(rows.astype(BF16), upto)
    for row in range(count):
        flag = rows[row : row + 1]
        chosen = (before.astype(F32) == place[row : row + 1] - 1.0) & (flag > 0.0)
        label = labels[row : row + 1]
        high = lax.shift_right_logical(label, 8)
        parts = [high.astype(F32), (label - high * 256).astype(F32), flag, jnp.zeros((5, length), F32)]
        found = mm_nt(
            jnp.concatenate(parts, axis=0).astype(BF16), jnp.where(chosen, 1.0, 0.0).astype(BF16)
        )
        packed = jnp.where(found[2:3] > 0.5, found[0:1] * 256.0 + found[1:2], -1.0)
        out_ref[row : row + 1, :] = packed.astype(jnp.int32)


FORWARD = (
    "qkv", "mixed", "res", "after", "res_e", "ckv", "cq", "cmixed", "cres",
    "hid_e", "slope_e", "hid_d", "slope_d", "res_d", "src", "low", "grad_low", "grad_place",
)


def forward_kernel(
    scale, x_ref, segments_ref, delete_ref, place_ref, token_ref, mask_ref,
    qkv_w_ref, mix_w_ref, gain_ref, bias_ref, up_own, down_own,
    cq_w_any, ckv_w_any, co_w_any, cgain_ref, cbias_ref, delete_w_ref, place_w_any,
    rows_ref, cols_ref, labels_small_ref, labels_large_ref, most_ref, norms_ref, up_other, down_other,
    totals_ref, ctotals_ref, grad_delete_ref, *rest,
):
    outs, rest = dict(zip(FORWARD, rest)), rest[len(FORWARD) :]
    held, rest = dict(zip(FORWARD, rest)), rest[len(FORWARD) :]
    up, down, cq_w, ckv_w, co_w, place_w, send_after, own_labels, all_labels, turned, load, store, send, recv = rest
    dp, phase = lax.axis_index("dp"), lax.axis_index("phase")
    x, y, z = place_of(dp)
    chips = [
        (lax.rem(x + a, 2), lax.rem(y + b, 2), lax.rem(z + c, 4))
        for c in range(4) for b in range(2) for a in range(2) if a + b + c
    ]
    core = (dp, 1 - phase)
    greet([(index_of(*chip), phase) for chip in chips] + [core])
    copies, stores = [], []

    def remote_to(src, dst, device):
        i = len(copies)
        copy = remote(src, dst, send.at[i], recv.at[i], device)
        copy.start()
        copies.append(copy)
        return copy

    def save(*names):
        for name in names:
            copy = pltpu.make_async_copy(held[name], outs[name], store.at[len(stores)])
            copy.start()
            stores.append(copy)

    norms_ref[phase, 0:1, :] = gain_ref[1:2, :]
    norms_ref[phase, 1:2, :] = bias_ref[1:2, :]
    from_norms = remote_to(norms_ref.at[phase], norms_ref.at[phase], core)
    from_up = remote_to(up_own, up.at[phase], core)
    from_down = remote_to(down_own, down.at[phase], core)
    loads = [
        pltpu.make_async_copy(src, dst, load.at[i])
        for i, (src, dst) in enumerate((
            (up_own, up.at[phase]), (down_own, down.at[phase]), (ckv_w_any, ckv_w), (cq_w_any, cq_w),
            (co_w_any, co_w), (place_w_any, place_w),
        ))
    ]
    for copy in loads:
        copy.start()
    pack_labels(token_ref[...], mask_ref[...], own_labels)
    for chip in chips:
        remote_to(own_labels, all_labels.at[z, y, x], (index_of(*chip), phase))
    label_copies = copies[3:]
    all_labels[z, y, x] = own_labels[...]
    is_enc = phase == 0
    segments = segments_ref[...].astype(F32)
    length = segments.shape[2]

    def pick(first, second):
        return jnp.where(is_enc, first, second)

    def own_row(ref):
        value = ref[...].astype(F32)
        return pick(value[0:1], value[1:2])

    ids_e = pick(segments[0, 0:1], segments[1, 0:1])
    ids_d = pick(segments[0, 1:2], segments[1, 1:2])
    own_ids = [pick(segments[r, 0:1], segments[r, 1:2]) for r in range(2)]
    block = jnp.concatenate([ids_d] * 8, axis=0)
    later = pltpu.roll(block, length - 1, 1)
    lane = lax.broadcasted_iota(jnp.int32, (8, length), 1)
    valid = jnp.where((block == later) & (lane < length - 1), 1.0, 0.0)[0:1]
    rows = jnp.concatenate(
        own_ids + [ids_e, ids_d, own_row(delete_ref), own_row(place_ref), valid, own_row(mask_ref)], axis=0
    )
    rows_ref[...] = rows
    turned[...] = jnp.zeros(turned.shape, F32)
    turned[0:8, :] = rows
    cols = turned[...].T
    cols_ref[...] = cols
    width = x_ref.shape[1]
    qkv, mixed, res = held["qkv"], held["mixed"], held["res"]
    for part in range(3):
        span = slice(part * width, (part + 1) * width)
        qkv[:, span] = mm(x_ref[...], qkv_w_ref[:, span]).astype(BF16)
    save("qkv")
    for turn in range(2):
        row = 1 - phase if turn == 0 else phase
        span = pl.ds(pl.multiple_of(row * length, length), length)
        allowed = jnp.where(row == 0, cols[:, 0:1], cols[:, 1:2]) == jnp.where(
            row == 0, own_ids[0], own_ids[1]
        )
        attend_forward(
            lambda pair: qkv[span, column(pair)],
            lambda pair: qkv[span, column(pair, width)],
            lambda pair: qkv[span, column(pair, 2 * width)],
            allowed, mixed, totals_ref.at[row], span,
        )
        residual = x_ref[span, :].astype(F32) + mm(mixed[span, :], mix_w_ref[...])
        res[span, :] = residual
        after = norm_forward(residual, gain_ref[0:1, :], bias_ref[0:1, :])
        if turn == 0:
            send_after[...] = after
            from_after = remote_to(send_after, held["after"].at[phase], core)
        else:
            held["after"][phase] = after
    save("mixed", "res")
    from_after.wait_recv()
    save("after")
    from_norms.wait_recv()
    from_up.wait_recv()
    from_down.wait_recv()
    for copy in loads:
        copy.wait()
    for i, (src, dst) in enumerate(((up, up_other), (down, down_other))):
        copy = pltpu.make_async_copy(src.at[1 - phase], dst, store.at[len(stores)])
        copy.start()
        stores.append(copy)
    encoder_rows(
        held["after"].at[0], up.at[0], down.at[0], norms_ref[0, 0:1, :], norms_ref[0, 1:2, :], ckv_w,
        held["hid_e"], held["slope_e"], held["res_e"], held["src"], held["ckv"],
    )
    save("hid_e", "slope_e", "res_e", "src", "ckv")
    middle = cross_rows(
        held["after"].at[1], cols[:, 2:3] == rows[3:4], cq_w, co_w, cgain_ref, cbias_ref,
        held["cq"], held["ckv"], held["cmixed"], held["cres"], ctotals_ref,
    )
    save("cq", "cmixed", "cres")
    decoder_rows(
        scale, middle, up.at[1], down.at[1], norms_ref[1, 0:1, :], norms_ref[1, 1:2, :],
        cols[:, 4:5].astype(jnp.int32), cols[:, 5:6].astype(jnp.int32), cols[:, 6:7], delete_w_ref, place_w,
        held["hid_d"], held["slope_d"], held["res_d"], held["low"], held["grad_low"],
        grad_delete_ref, held["grad_place"],
    )
    save("hid_d", "slope_d", "res_d", "low", "grad_low", "grad_place")
    for copy in label_copies:
        copy.wait_recv()
    small = length // 2
    for at, (p, yy, xx, zz) in enumerate(
        (p, yy, xx, zz) for p in range(2) for yy in range(2) for xx in range(2) for zz in range(4)
    ):
        line = all_labels[zz, yy, xx, p : p + 1, :]
        labels_small_ref[:, at * small : (at + 1) * small] = line[:, :small]
        labels_large_ref[:, at * length : (at + 1) * length] = line
    beyond = jnp.max(all_labels[:, :, :, :, small:].astype(F32).reshape(2 * GROUPS, length - small))
    most_ref[...] = jnp.full(most_ref.shape, beyond, F32)
    for copy in copies:
        copy.wait_send()
    for copy in stores:
        copy.wait()


def token_kernel(
    scale, cap, low_ref, rows_ref, cols_ref, labels_ref, head_any,
    grad_ref, grad_weight_ref,
    weight, weight_t, every, probs, totals, near_in, joined, far_in, shares,
    part, core_in, third_in, second_in, z_in, load, send, recv,
):
    dp, phase = lax.axis_index("dp"), lax.axis_index("phase")
    x, y, z = place_of(dp)
    x_first = phase == 0
    x2, y2 = jnp.where(x_first, 1 - x, x), jnp.where(x_first, y, 1 - y)
    x3, y3 = jnp.where(x_first, x, 1 - x), jnp.where(x_first, 1 - y, y)
    second, third, core = (index_of(x2, y2, z), phase), (index_of(x3, y3, z), phase), (dp, 1 - phase)
    zs = [lax.rem(z + k, 4) for k in (1, 2, 3)]
    along = [(index_of(x, y, k), phase) for k in zs]
    shard, length = weight_t.shape[0], low_ref.shape[0]
    near = [
        (index_of(lax.rem(x + a, 2), lax.rem(y + b, 2), z), lax.rem(phase + c, 2))
        for a in range(2) for b in range(2) for c in range(2) if a + b + c
    ]
    greet(near + along)
    offset = pl.multiple_of((dp * 2 + phase) * shard, shard)
    weight_copy = pltpu.make_async_copy(head_any.at[:, pl.ds(offset, shard)], weight, load.at[0])
    weight_copy.start()
    copies = []

    def remote_to(src, dst, device):
        i = len(copies)
        copy = remote(src, dst, send.at[i], recv.at[i], device)
        copy.start()
        copies.append(copy)
        return copy

    def unit(p, yy, xx):
        return (p * 2 + yy) * 2 + xx

    def block(u, zz):
        return pl.ds(pl.multiple_of((u * 4 + zz) * cap, cap), cap)

    before = lax.broadcasted_iota(jnp.int32, (length, length), 0)
    after = lax.broadcasted_iota(jnp.int32, (length, length), 1)
    rows = rows_ref[...]
    place = mm(rows.astype(BF16), jnp.where(before <= after, 1.0, 0.0).astype(BF16))[7:8]
    slot = lax.broadcasted_iota(jnp.int32, (cap, length), 0).astype(F32)
    chosen = jnp.where((slot == place - 1.0) & (rows[7:8] > 0.0), 1.0, 0.0).astype(BF16)
    own = unit(phase, y, x)
    every[block(own, z), :] = mm(chosen, low_ref[...]).astype(BF16)
    def relay(u, zz, device):
        here = every.at[block(u, zz), :]
        return remote_to(here, here, device)

    firsts = [relay(own, z, device) for device in along]
    cross = [relay(own, z, core)]
    seconds = [relay(own, z, second)]
    thirds = [relay(own, z, third)]
    weight_copy.wait()
    weight_t[...] = weight[...].T
    sources = [lax.rem(z + 4 - k, 4) for k in (1, 2, 3)]
    order = [z] + sources
    for k in range(3):
        firsts[k].wait_recv()
        seconds.append(relay(own, sources[k], second))
        thirds.append(relay(own, sources[k], third))
        cross.append(relay(own, sources[k], core))
    tall = 256
    chunks = 4 * cap // tall

    def look(u):
        def step(j, _):
            span = pl.ds(pl.multiple_of((u * chunks + j) * tall, tall), tall)
            logits = mm_nt(weight_t[...], every[span, :])
            top = jnp.max(logits, axis=0, keepdims=True)
            weights = jnp.exp(logits - top)
            summed = jnp.sum(weights, axis=0, keepdims=True)
            probs[:, span] = (weights * (1.0 / summed)).astype(BF16)
            totals[:, span] = top + jnp.log(summed)
            return 0

        lax.fori_loop(0, chunks, step, 0)

    def arrived(some):
        for copy in some:
            copy.wait_recv()

    look(own)
    for k in range(4):
        seconds[k].wait_recv()
        thirds.append(relay(unit(phase, y2, x2), order[k], third))
        cross.append(relay(unit(phase, y2, x2), order[k], core))
    arrived(cross[0:4])
    look(unit(1 - phase, y, x))
    look(unit(phase, y2, x2))
    for k in range(4):
        thirds[k].wait_recv()
        cross.append(relay(unit(phase, y3, x3), order[k], core))
    arrived(cross[4:8])
    look(unit(1 - phase, y3, x3))
    for k in range(4):
        thirds[4 + k].wait_recv()
        cross.append(relay(unit(phase, 1 - y, 1 - x), order[k], core))
    look(unit(phase, y3, x3))
    arrived(cross[8:12])
    look(unit(1 - phase, y2, x2))
    look(unit(phase, 1 - y, 1 - x))
    arrived(cross[12:16])
    look(unit(1 - phase, 1 - y, 1 - x))

    def join(parts):
        top = parts[0]
        for piece in parts[1:]:
            top = jnp.maximum(top, piece)
        summed = jnp.exp(parts[0] - top)
        for piece in parts[1:]:
            summed = summed + jnp.exp(piece - top)
        return top + jnp.log(summed)

    near_copies = [remote_to(totals, near_in.at[j], device) for j, device in enumerate(near)]
    arrived(near_copies)
    total = join([totals[...]] + [near_in[j] for j in range(7)])
    joined[...] = total
    far_copies = [remote_to(joined, far_in.at[j], device) for j, device in enumerate(along)]
    arrived(far_copies)
    shares[...] = jnp.exp(totals[...] - join([total] + [far_in[j] for j in range(3)]))

    per = tall // cap

    def learn(u):
        def step(j, _):
            span = pl.ds(pl.multiple_of((u * chunks + j) * tall, tall), tall)
            labels = labels_ref[:, span]
            hit = lax.broadcasted_iota(jnp.int32, (shard, tall), 0) == labels - offset
            grads = probs[:, span].astype(F32) * shares[:, span] - jnp.where(hit, 1.0, 0.0)
            grads = (grads * jnp.where(labels >= 0, scale, 0.0)).astype(BF16)
            probs[:, span] = grads
            back = mm(weight[...], grads).astype(BF16)
            for k in range(per):
                part[u, j * per + k] = back[:, k * cap : (k + 1) * cap]
            return 0

        lax.fori_loop(0, chunks, step, 0)

    def add(u, zz, *others):
        value = part[u, zz].astype(F32)
        for other in others:
            value = value + other.astype(F32)
        part[u, zz] = value.astype(BF16)

    mine = [unit(phase, 1 - y, 1 - x), unit(phase, y3, x3), unit(phase, y2, x2), own]
    theirs = [
        unit(1 - phase, 1 - y, 1 - x), unit(1 - phase, y2, x2), unit(1 - phase, y3, x3), unit(1 - phase, y, x)
    ]
    route = zs + [z]
    core_copies, third_copies = [], []

    def to_third(k):
        core_copies[k].wait_recv()
        for j, zz in enumerate(route):
            add(mine[k], zz, core_in[k, zz])
            third_copies.append(remote_to(part.at[mine[k], zz], third_in.at[k, j], third))

    for k in range(4):
        learn(theirs[k])
        core_copies.append(remote_to(part.at[theirs[k]], core_in.at[k], core))
        if 1 <= k <= 2:
            to_third(k - 1)
        learn(mine[k])
    core_copies[2].wait_recv()
    second_copies = []
    for j, zz in enumerate(route):
        third_copies[j].wait_recv()
        add(mine[2], zz, core_in[2, zz], third_in[0, j])
        second_copies.append(remote_to(part.at[mine[2], zz], second_in.at[j], second))

    slab = min(256, shard)

    def weigh(k):
        value = mm(probs[k * slab : (k + 1) * slab, :], every[...])
        grad_weight_ref[:, k * slab : (k + 1) * slab] = value.T

    slabs = shard // slab
    for k in range((slabs + 1) // 2):
        weigh(k)
    core_copies[3].wait_recv()
    z_copies = []
    for j, zz in enumerate(route):
        third_copies[4 + j].wait_recv()
        second_copies[j].wait_recv()
        add(own, zz, core_in[3, zz], third_in[1, j], second_in[j])
        if j < 3:
            z_copies.append(remote_to(part.at[own, zz], z_in.at[j], along[j]))
    for k in range((slabs + 1) // 2, slabs):
        weigh(k)
    arrived(z_copies)
    back = part[own, z].astype(F32)
    for j in range(3):
        back = back + z_in[j].astype(F32)
    place = mm(jnp.where(after <= before, 1.0, 0.0).astype(BF16), cols_ref[...].astype(BF16))[:, 7:8]
    slot = lax.broadcasted_iota(jnp.int32, (length, cap), 1).astype(F32)
    spread = jnp.where((slot == place - 1.0) & (cols_ref[:, 7:8] > 0.0), 1.0, 0.0).astype(BF16)
    grad_ref[...] = mm_nt(spread, back.astype(BF16))
    for copy in copies:
        copy.wait_send()


def token_chips(number, cap, low, rows, cols, labels, head):
    length, width = low.shape
    shard = head.shape[1] // (2 * GROUPS)
    count = 2 * GROUPS * cap
    scale = float(2 * length * GROUPS) ** (-0.5)
    copies = 64
    return pl.pallas_call(
        partial(token_kernel, scale, cap),
        out_shape=(whole((length, width), F32), whole((width, shard), F32)),
        in_specs=in_vmem(4) + [pl.BlockSpec(memory_space=pl.ANY)],
        out_specs=tuple(in_vmem(2)),
        scratch_shapes=[
            VMEM((width, shard), BF16), VMEM((shard, width), BF16), VMEM((count, width), BF16),
            VMEM((shard, count), BF16), VMEM((1, count), F32), VMEM((7, 1, count), F32), VMEM((1, count), F32),
            VMEM((3, 1, count), F32), VMEM((1, count), F32),
            VMEM((8, 4, width, cap), BF16), VMEM((4, 4, width, cap), BF16), VMEM((2, 4, width, cap), BF16),
            VMEM((4, width, cap), BF16), VMEM((3, width, cap), BF16),
            pltpu.SemaphoreType.DMA((1,)), pltpu.SemaphoreType.DMA((copies + 8,)), pltpu.SemaphoreType.DMA((copies + 8,)),
        ],
        compiler_params=pltpu.CompilerParams(
            collective_id=number, has_side_effects=True, vmem_limit_bytes=60 * 1024 * 1024
        ),
        name="token_head",
    )(low, rows, cols, labels, head)


class Exchange:
    def __init__(self, send, recv):
        self.dp, self.phase = lax.axis_index("dp"), lax.axis_index("phase")
        self.x, self.y, self.z = place_of(self.dp)
        x, y, z = self.x, self.y, self.z
        self.along_x, self.along_y = index_of(1 - x, y, z), index_of(x, 1 - y, z)
        self.zs = [lax.rem(z + k, 4) for k in (1, 2, 3)]
        self.send, self.recv, self.used, self.copies = send, recv, 0, []

    def greet(self):
        devices = [(index_of(self.x, self.y, k), self.phase) for k in self.zs]
        greet(devices + [(self.along_x, self.phase), (self.along_y, self.phase), (self.dp, 1 - self.phase)])

    def copy(self, src, dst, device):
        copy = remote(src, dst, self.send.at[self.used], self.recv.at[self.used], device)
        self.used += 1
        copy.start()
        self.copies.append(copy)
        return copy

    def to_core(self, src, dst):
        return self.copy(src, dst, (self.dp, 1 - self.phase))

    def first(self, batch, part):
        start, size, x_first = part
        rows = pl.ds(start, size)
        if x_first:
            src, device = batch.shards.at[:, :, 1 - self.x, rows], self.along_x
        else:
            src, device = batch.shards.at[:, 1 - self.y, :, rows], self.along_y
        return self.copy(src, batch.in1.at[:, :, rows], (device, self.phase))

    def second(self, batch, part):
        start, size, x_first = part
        rows = pl.ds(start, size)
        x, y, in1 = self.x, self.y, batch.in1
        other, device = (1 - y, self.along_y) if x_first else (1 - x, self.along_x)

        def add(i, _):
            zz, which = i // 2, lax.rem(i, 2)
            mine = batch.shards[zz, which, x, rows] if x_first else batch.shards[zz, y, which, rows]
            in1[zz, which, rows] = (in1[zz, which, rows].astype(F32) + mine.astype(F32)).astype(BF16)
            return 0

        lax.fori_loop(0, 8, add, 0)
        return self.copy(in1.at[:, other, rows], batch.in2.at[:, rows], (device, self.phase))

    def third(self, batch, part):
        start, size, x_first = part
        rows = pl.ds(start, size)
        own = self.y if x_first else self.x
        in1, in2 = batch.in1, batch.in2

        def add(zz, _):
            in2[zz, rows] = (in2[zz, rows].astype(F32) + in1[zz, own, rows].astype(F32)).astype(BF16)
            return 0

        lax.fori_loop(0, 4, add, 0)
        return [
            self.copy(in2.at[zz, rows], batch.in3.at[j, rows], (index_of(self.x, self.y, zz), self.phase))
            for j, zz in enumerate(self.zs)
        ]

    def last(self, batch, part, put):
        start, size, _ = part
        rows = pl.ds(start, size)
        in3 = batch.in3
        total = batch.in2[self.z, rows].astype(F32) + in3[0, rows].astype(F32)
        put(rows, total + in3[1, rows].astype(F32) + in3[2, rows].astype(F32))

    def finish(self):
        for copy in self.copies:
            copy.wait_send()


class Batch:
    def __init__(self, exchange, shards, in1, in2, in3, put, parts):
        self.exchange, self.shards, self.in1, self.in2, self.in3 = exchange, shards, in1, in2, in3
        self.put, self.parts = put, parts
        self.waits = [None] * len(parts)

    def join(self, own, *some):
        shards = self.shards
        for i in some:
            rows = pl.ds(self.parts[i][0], self.parts[i][1])

            def add(j, _):
                at = (j // 4, lax.rem(j // 2, 2), lax.rem(j, 2), rows)
                shards[at] = (shards[at].astype(F32) + own[at].astype(F32)).astype(BF16)
                return 0

            lax.fori_loop(0, GROUPS, add, 0)
            self.start(i)

    def start(self, *some):
        for i in some:
            self.waits[i] = self.exchange.first(self, self.parts[i])

    def second(self, *some):
        for i in some:
            self.waits[i].wait_recv()
            self.waits[i] = self.exchange.second(self, self.parts[i])

    def third(self, *some):
        for i in some:
            self.waits[i].wait_recv()
            self.waits[i] = self.exchange.third(self, self.parts[i])

    def last(self, *some):
        for i in some:
            for copy in self.waits[i]:
                copy.wait_recv()
            self.exchange.last(self, self.parts[i], self.put)


FF_PARTS = ((0, 32, True), (32, 32, False), (64, 32, True), (96, 32, False))
CROSS_PARTS = ((0, 32, True), (32, 32, False), (64, 16, False))


BACKWARD = (
    "co_w", "cmixed", "cq", "ckv", "grad_place", "after", "src", "cq_w", "ckv_w", "res_e",
    "res", "mix_w", "qkv", "mixed", "x", "qkv_w",
)


def backward_kernel(
    grad_low_ref, grad_token_ref, rows_ref, cols_ref, norms_ref, cgain_ref, cbias_ref, ctotals_ref, totals_ref,
    res_d_ref, cres_ref, grad_delete_ref, gain_ref,
    up_own, up_other, down_own, down_other, hid_e_any, slope_e_any, hid_d_any, slope_d_any, *rest,
):
    held_any, rest = dict(zip(BACKWARD, rest)), rest[len(BACKWARD) :]
    grad_x_any, red_ff_ref, red_attention_ref, red_cross_ref, vectors_ref = rest[:5]
    held, rest = dict(zip(BACKWARD, rest[5:])), rest[5 + len(BACKWARD) :]
    (
        up, down, hid, slope, grad_d, grad_e, grad_c, grad_a, core_d, core_e, core_c,
        in1_d, in1_e, in1_c, in1_a, in2_d, in2_e, in2_c, in2_a, in3_d, in3_e, in3_c, in3_a,
        after_grads, after_in, gq_ref, gckv_ref, grad_qkv, sums, grad_x_ref,
        vec_own, vec_core, vec_1, vec_2, vec_3, vec_in, sems, held_sems, send, recv,
    ) = rest
    phase = lax.axis_index("phase")
    ex = Exchange(send, recv)
    ex.greet()

    def moved(name):
        i = BACKWARD.index(name)
        return pltpu.make_async_copy(held_any[name], held[name], held_sems.at[i])

    waited = set()

    def get(name):
        if name not in waited:
            waited.add(name)
            moved(name).wait()
        return held[name]

    width = grad_low_ref.shape[1]
    each = width // GROUPS
    length = grad_low_ref.shape[0]

    def load(own_side, i):
        hidden, slopes = (hid_e_any, slope_e_any) if own_side == 0 else (hid_d_any, slope_d_any)

        @pl.when(phase == own_side)
        def _():
            pltpu.make_async_copy(up_own, up, sems.at[i]).start()
            pltpu.make_async_copy(down_own, down, sems.at[i + 1]).start()

        @pl.when(phase != own_side)
        def _():
            pltpu.make_async_copy(up_other, up, sems.at[i]).start()
            pltpu.make_async_copy(down_other, down, sems.at[i + 1]).start()

        pltpu.make_async_copy(hidden, hid, sems.at[i + 2]).start()
        pltpu.make_async_copy(slopes, slope, sems.at[i + 3]).start()

    def loaded(i):
        for k, (src, dst) in enumerate(
            ((up_own, up), (down_own, down), (hid_e_any, hid), (slope_e_any, slope))
        ):
            pltpu.make_async_copy(src, dst, sems.at[i + k]).wait()

    def puts(ref):
        def put_up(part, value):
            ref[0, :, :, :, part * each : (part + 1) * each, :] = value.astype(BF16).reshape(
                4, 2, 2, each, width
            )

        def put_down(part, value):
            ref[1, part] = value.astype(BF16).reshape(2, 2, width // 4, width)

        return put_up, put_down

    def put_ff(half):
        def put(rows, value):
            sums[half, rows, :] = value

        return put

    def put_attention(rows, value):
        red_attention_ref[rows, :] = value

    cross_sum = red_cross_ref.at[phase]

    def put_cross_sum(rows, value):
        cross_sum[rows, :] = value

    batch_d = Batch(ex, core_d, in1_d, in2_d, in3_d, put_ff(1), FF_PARTS)
    batch_e = Batch(ex, core_e, in1_e, in2_e, in3_e, put_ff(0), FF_PARTS)
    batch_c = Batch(ex, core_c, in1_c, in2_c, in3_c, put_cross_sum, CROSS_PARTS)
    batch_a = Batch(ex, grad_a, in1_a, in2_a, in3_a, put_attention, FF_PARTS)

    load(1, 0)
    for name in BACKWARD:
        moved(name).start()
    grad_out = grad_low_ref[...] + grad_token_ref[...]
    grad_res, gain_grad, bias_grad = norm_back(res_d_ref[...], norms_ref[1, 0:1, :], grad_out)
    vec_own[2:3, :] = gain_grad
    vec_own[3:4, :] = bias_grad
    vec_own[6:8, :] = grad_delete_ref[0:2, :]
    cres = cres_ref[...]
    middle_low = norm_forward(cres, cgain_ref[...], cbias_ref[...]).astype(BF16)
    loaded(0)
    grad_middle = feed_back(grad_res, middle_low, up, down, hid, slope, *puts(grad_d))
    from_d = ex.to_core(grad_d.at[1 - phase], core_d)
    load(0, 4)
    grad_res, gain_grad, bias_grad = norm_back(cres, cgain_ref[...], grad_middle)
    vec_own[4:5, :] = gain_grad
    vec_own[5:6, :] = bias_grad
    branch = grad_res.astype(BF16)

    def put_cross(first, value):
        half_rows = grad_c.shape[4]
        value = value.astype(BF16).reshape(4, 2, 2, each, width)
        for at in range(0, each, 16):
            half, row = divmod(first + at, half_rows)
            grad_c[half, :, :, :, row : row + 16, :] = value[:, :, :, at : at + 16, :]

    put_cross(3 * each, mm_tn(get("cmixed")[...], branch))
    put_cross(4 * each, get("grad_place")[...])
    grad_mixed = mm_nt(branch, get("co_w")[...]).astype(BF16)
    cq_ref, ckv_ref = get("cq"), get("ckv")

    def put_q(pair, value):
        gq_ref[:, column(pair)] = value

    def put_k(pair, value):
        gckv_ref[:, column(pair)] = value

    def put_v(pair, value):
        gckv_ref[:, column(pair, width)] = value

    def between(pair):
        if pair == 1:
            from_d.wait_recv()
            batch_d.join(grad_d.at[phase], 0, 1)
        if pair == 2:
            batch_d.join(grad_d.at[phase], 2, 3)

    attend_backward(
        lambda pair: cq_ref[:, column(pair)],
        lambda pair: ckv_ref[:, column(pair)],
        lambda pair: ckv_ref[:, column(pair, width)],
        lambda pair: grad_mixed[:, column(pair)],
        cols_ref[:, 2:3] == rows_ref[3:4, :],
        ctotals_ref, put_q, put_k, put_v, between,
    )
    grad_q = gq_ref[...]
    put_cross(0, mm_tn(get("after")[1].astype(BF16), grad_q))
    for part in range(2):
        put_cross((1 + part) * each, mm_tn(get("src")[...], gckv_ref[:, part * width : (part + 1) * width]))
    from_c = ex.to_core(grad_c.at[1 - phase], core_c)
    after_grads[1] = grad_res + mm_nt(grad_q, get("cq_w")[...])
    grad_src = mm_nt(gckv_ref[...], get("ckv_w")[...]).astype(BF16).astype(F32)
    grad_res, gain_grad, bias_grad = norm_back(get("res_e")[...], norms_ref[0, 0:1, :], grad_src)
    vec_own[0:1, :] = gain_grad
    vec_own[1:2, :] = bias_grad
    from_v = ex.to_core(vec_own, vec_core)
    loaded(4)

    def between(part):
        if part == 1:
            batch_d.second(0, 1)
        if part == 2:
            from_c.wait_recv()
            batch_c.join(grad_c.at[phase], 0, 1, 2)

    after_grads[0] = feed_back(
        grad_res, get("after")[0].astype(BF16), up, down, hid, slope, *puts(grad_e), between
    )
    from_e = ex.to_core(grad_e.at[1 - phase], core_e)
    from_after = ex.to_core(after_grads.at[1 - phase], after_in)
    res_ref, mix_w_ref, qkv_ref, mixed_ref, x_ref = [get(n) for n in ("res", "mix_w", "qkv", "mixed", "x")]
    first_vectors = []
    for turn in range(2):
        row = phase if turn == 0 else 1 - phase
        rows = pl.ds(pl.multiple_of(row * length, length), length)
        if turn == 0:
            grad_after = after_grads[phase]
        else:
            from_after.wait_recv()
            grad_after = after_in[...]
        grad_res, gain_grad, bias_grad = norm_back(res_ref[rows, :], gain_ref[0:1, :], grad_after)
        first_vectors.append((gain_grad, bias_grad))
        grad_x_ref[rows, :] = grad_res
        branch = grad_res.astype(BF16)
        if turn == 0:
            first_branch, first_rows = branch, rows
        grad_mixed = mm_nt(branch, mix_w_ref[...]).astype(BF16)

        def put(offset):
            def store(pair, value):
                grad_qkv[rows, column(pair, offset)] = value

            return store

        def between(pair):
            at = turn * 4 + pair
            if at == 0:
                batch_d.second(2, 3)
            if at == 1:
                from_e.wait_recv()
                batch_e.join(grad_e.at[phase], 0, 1)
                batch_d.third(0, 1)
            if at == 3:
                batch_e.join(grad_e.at[phase], 2, 3)
                batch_d.third(2, 3)
            if at == 5:
                batch_c.second(0, 1, 2)
            if at == 6:
                batch_d.last(0, 1)
            if at == 7:
                batch_e.second(0, 1)

        attend_backward(
            lambda pair: qkv_ref[rows, column(pair)],
            lambda pair: qkv_ref[rows, column(pair, width)],
            lambda pair: qkv_ref[rows, column(pair, 2 * width)],
            lambda pair: grad_mixed[:, column(pair)],
            jnp.where(row == 0, cols_ref[:, 0:1], cols_ref[:, 1:2])
            == jnp.where(row == 0, rows_ref[0:1, :], rows_ref[1:2, :]),
            totals_ref.at[row], put(0), put(width), put(2 * width), between,
        )
    shape = (4, 2, 2, each, width)
    grad_mix = mm_tn(mixed_ref[first_rows, :], first_branch) + mm_tn(mixed_ref[rows, :], branch)
    grad_a[:, :, :, 3 * each :, :] = grad_mix.astype(BF16).reshape(shape)
    for part in range(3):
        cols = slice(part * width, (part + 1) * width)
        value = mm_tn(x_ref[...], grad_qkv[:, cols])
        grad_a[:, :, :, part * each : (part + 1) * each, :] = value.astype(BF16).reshape(shape)
    batch_a.start(0, 1, 2, 3)
    grad_x_ref[...] += mm_nt(grad_qkv[...], get("qkv_w")[...])
    grad_x_copy = pltpu.make_async_copy(grad_x_ref, grad_x_any, held_sems.at[len(BACKWARD)])
    grad_x_copy.start()
    from_v.wait_recv()
    vec_1[0:8, :] = vec_own[...] + vec_core[...]
    vec_1[8:9, :] = first_vectors[0][0] + first_vectors[1][0]
    vec_1[9:10, :] = first_vectors[0][1] + first_vectors[1][1]
    vec_1[10:16, :] = jnp.zeros((6, width), F32)
    vec_x = ex.copy(vec_1, vec_in.at[0], (ex.along_x, phase))

    batch_c.third(0, 1, 2)
    batch_d.last(2, 3)
    batch_e.second(2, 3)
    batch_e.third(0, 1)
    vec_x.wait_recv()
    vec_2[...] = vec_1[...] + vec_in[0]
    vec_y = ex.copy(vec_2, vec_in.at[1], (ex.along_y, phase))
    batch_a.second(0, 1)
    batch_c.last(0, 1, 2)
    cross_copy = ex.to_core(cross_sum, red_cross_ref.at[phase])
    batch_e.third(2, 3)
    vec_y.wait_recv()
    vec_3[...] = vec_2[...] + vec_in[1]
    vec_z = [
        ex.copy(vec_3, vec_in.at[2 + j], (index_of(ex.x, ex.y, zz), phase)) for j, zz in enumerate(ex.zs)
    ]
    batch_e.last(0, 1)
    batch_a.second(2, 3)
    batch_a.third(0, 1)
    batch_e.last(2, 3)
    ff_copy = ex.to_core(sums.at[1 - phase], red_ff_ref.at[phase])
    red_ff_ref[phase] = sums[phase]
    batch_a.third(2, 3)
    for copy in vec_z:
        copy.wait_recv()
    vectors_ref[...] = vec_3[...] + vec_in[2] + vec_in[3] + vec_in[4]
    batch_a.last(0, 1, 2, 3)
    cross_copy.wait_recv()
    ff_copy.wait_recv()
    grad_x_copy.wait()
    ex.finish()


def unpack_kernel(
    ff_ref, attention_ref, cross_halves_ref, vectors_ref, own_ref, other_ref,
    qkv_ref, mix_ref, up_ref, down_ref, cq_ref, ckv_ref, co_ref, place_ref,
    gain_ref, bias_ref, cgain_ref, cbias_ref, delete_ref, token_ref,
):
    phase, dp = lax.axis_index("phase"), lax.axis_index("dp")
    shard = own_ref.shape[1]

    @pl.when(phase == 0)
    def _():
        token_ref[:, :shard] = own_ref[...]
        token_ref[:, shard:] = other_ref[...]

    @pl.when(phase != 0)
    def _():
        token_ref[:, :shard] = other_ref[...]
        token_ref[:, shard:] = own_ref[...]

    each = gain_ref.shape[2]
    vectors = vectors_ref[...]
    whole_width = vectors.shape[1]
    vectors = pltpu.roll(vectors, lax.rem(whole_width - dp * each, whole_width), 1)[:, :each]
    gain_ref[0, 0:1, :] = vectors[8:9]
    gain_ref[0, 1:2, :] = jnp.where(phase == 0, vectors[0:1], vectors[2:3])
    bias_ref[0, 0:1, :] = vectors[9:10]
    bias_ref[0, 1:2, :] = jnp.where(phase == 0, vectors[1:2], vectors[3:4])
    cgain_ref[...] = vectors[4:5]
    cbias_ref[...] = vectors[5:6]
    delete_ref[...] = vectors[6:8]
    width = mix_ref.shape[1]
    high = mix_ref.shape[0]
    for block in range(up_ref.shape[1] // width):
        up_ref[:, block * width : (block + 1) * width] = ff_ref[0, block * high : (block + 1) * high, :]
    down_ref[...] = ff_ref[1]
    for block in range(3):
        qkv_ref[:, block * width : (block + 1) * width] = attention_ref[block * high : (block + 1) * high, :]
    mix_ref[...] = attention_ref[3 * high :, :]
    half_rows = cross_halves_ref.shape[1]

    def cross(start):
        half, row = divmod(start, half_rows)
        return cross_halves_ref[half, row : row + 16, :]

    for start in range(0, 5 * high, 16):
        part, inner = start // high, slice(start % high, start % high + 16)
        if part == 0:
            cq_ref[inner, :] = cross(start)
        elif part < 3:
            ckv_ref[inner, (part - 1) * width : part * width] = cross(start)
        elif part == 3:
            co_ref[inner, :] = cross(start)
        else:
            value = cross(start)
            cols = place_ref.shape[1]
            at = start % high
            place_ref[at : at + 16, :] = value[:, :cols]
            place_ref[high + at : high + at + 16, :] = value[:, cols:]


def whole(shape, dtype):
    return jax.ShapeDtypeStruct(shape, dtype)


def in_vmem(count):
    return [pl.BlockSpec(memory_space=VMEM)] * count


def swap(value):
    return lax.ppermute(value, "phase", [(0, 1), (1, 0)])


def unpacked(shards, height, columns):
    groups, rows, width = shards.shape
    blocks = columns // width
    parts = shards.reshape(groups, blocks, rows // blocks, width)
    return parts.transpose(0, 2, 1, 3).reshape(height, columns)


def token_head(numbers, cap, block_rows, low, flags, labels_all, flags_all, weight, weight_t, scale):
    length, width = low.shape
    dp = lax.axis_size("dp")
    shard = weight_t.shape[0]

    def choice(flags):
        place = jnp.cumsum(flags, axis=-1) - 1
        places = lax.broadcasted_iota(jnp.int32, flags.shape[:-1] + (cap, flags.shape[-1]), flags.ndim - 1)
        return (places == place[..., None, :]) & (flags[..., None, :] > 0)

    chosen = choice(flags)
    packed = mm(chosen.astype(BF16), low).astype(BF16)
    every = gather_blocks(packed, numbers[0]).reshape(2 * dp * cap, width)
    labels = jnp.max(jnp.where(choice(flags_all), labels_all[:, None, :], -1), axis=-1)
    labels = labels.reshape(dp, 2, cap).transpose(1, 0, 2).reshape(2 * dp * cap)
    tall = block_rows
    count = 2 * dp * cap // tall
    probs, totals = pl.pallas_call(
        token_forward,
        grid=(count,),
        out_shape=(whole((count, shard, tall), BF16), whole((count, 1, tall), F32)),
        in_specs=[
            pl.BlockSpec((tall, width), lambda i: (i, 0)),
            pl.BlockSpec((shard, width), lambda i: (0, 0)),
        ],
        out_specs=(
            pl.BlockSpec((1, shard, tall), lambda i: (i, 0, 0)),
            pl.BlockSpec((1, 1, tall), lambda i: (i, 0, 0)),
        ),
        compiler_params=pltpu.CompilerParams(vmem_limit_bytes=48 * 1024 * 1024),
        name="token_forward",
    )(every, weight_t)
    shares = token_shares(totals, numbers[1])
    each = tall // cap
    grad_low, grad_weight = pl.pallas_call(
        partial(token_backward, scale),
        grid=(count,),
        out_shape=(whole((2 * dp, cap, width), BF16), whole((width, shard), F32)),
        in_specs=[
            pl.BlockSpec((1, shard, tall), lambda i: (i, 0, 0)),
            pl.BlockSpec((1, 1, tall), lambda i: (i, 0, 0)),
            pl.BlockSpec((1, 1, tall), lambda i: (i, 0, 0)),
            pl.BlockSpec((tall, width), lambda i: (i, 0)),
            pl.BlockSpec((shard, width), lambda i: (0, 0)),
        ],
        out_specs=(
            pl.BlockSpec((each, cap, width), lambda i: (i, 0, 0)),
            pl.BlockSpec((width, shard), lambda i: (0, 0)),
        ),
        scratch_shapes=[VMEM((shard, width), F32)],
        compiler_params=pltpu.CompilerParams(vmem_limit_bytes=48 * 1024 * 1024),
        name="token_backward",
    )(probs, shares, labels.reshape(count, 1, tall), every, weight_t)
    back = scatter_blocks(grad_low.reshape(2, dp, cap, width), numbers[2])
    return mm_tn(chosen.astype(BF16), back.astype(BF16)), grad_weight


def on_chips(
    inputs, segments, delete_target, place_target, token_target, token_mask,
    attention_in, attention_out, feedforward_in, feedforward_out, norm_gain, norm_bias,
    cross_query, cross_keyvalue, cross_out, cross_gain, cross_bias,
    head_delete, head_place, head_token,
):
    phase, dp_index = lax.axis_index("phase"), lax.axis_index("dp")
    count, length, width = inputs.shape[1:]
    hidden, classes = feedforward_in.shape[2], head_place.shape[1]
    each = width // GROUPS
    scale = float(count * length * GROUPS) ** (-0.5)
    any_space = pl.BlockSpec(memory_space=pl.ANY)
    is_enc = phase == 0
    states = inputs[0].reshape(count * length, width)
    up_own, down_own = feedforward_in[0], feedforward_out[0]
    qkv_w, mix_w = attention_in[0], attention_out[0]
    delete_weight = head_delete.T
    gain_row, bias_row = cross_gain[None, :], cross_bias[None, :]
    shapes = {
        "qkv": ((count * length, 3 * width), BF16), "mixed": ((count * length, width), BF16),
        "res": ((count * length, width), F32), "after": ((2, length, width), F32),
        "res_e": ((length, width), F32), "ckv": ((length, 2 * width), BF16), "cq": ((length, width), BF16),
        "cmixed": ((length, width), BF16), "cres": ((length, width), F32),
        "hid_e": ((length, hidden), BF16), "slope_e": ((length, hidden), BF16),
        "hid_d": ((length, hidden), BF16), "slope_d": ((length, hidden), BF16),
        "res_d": ((length, width), F32), "src": ((length, width), BF16), "low": ((length, width), BF16),
        "grad_low": ((length, width), F32), "grad_place": ((GROUPS, each, 2 * classes), BF16),
        "co_w": ((width, width), BF16), "cq_w": ((width, width), BF16), "ckv_w": ((width, 2 * width), BF16),
        "mix_w": ((width, width), BF16), "qkv_w": ((width, 3 * width), BF16), "x": ((count * length, width), BF16),
    }
    outs = pl.pallas_call(
        partial(forward_kernel, scale),
        out_shape=(
            whole((8, length), F32), whole((length, 128), F32),
            whole((1, GROUPS * length), jnp.int32), whole((1, 2 * GROUPS * length), jnp.int32), whole((1, 1), F32),
            whole((2, 2, width), F32), whole((width, hidden), BF16), whole((hidden, width), BF16),
            whole((count, HEADS, length), F32), whole((HEADS, length), F32), whole((8, width), F32),
            *[whole(*shapes[name]) for name in FORWARD],
        ),
        in_specs=in_vmem(10) + [any_space] * 5 + in_vmem(3) + [any_space],
        out_specs=tuple(in_vmem(6) + [any_space] * 2 + in_vmem(3) + [any_space] * len(FORWARD)),
        scratch_shapes=[
            *[VMEM(*shapes[name]) for name in FORWARD],
            VMEM((2, width, hidden), BF16), VMEM((2, hidden, width), BF16),
            VMEM((width, width), BF16), VMEM((width, 2 * width), BF16), VMEM((width, width), BF16),
            VMEM((2 * width, classes), BF16), VMEM((length, width), F32),
            VMEM((2, length), jnp.int32), VMEM((4, 2, 2, 2, length), jnp.int32), VMEM((128, length), F32),
            pltpu.SemaphoreType.DMA((6,)), pltpu.SemaphoreType.DMA((len(FORWARD) + 2,)),
            pltpu.SemaphoreType.DMA((20,)), pltpu.SemaphoreType.DMA((20,)),
        ],
        compiler_params=pltpu.CompilerParams(
            collective_id=1, has_side_effects=True, vmem_limit_bytes=56 * 1024 * 1024
        ),
        name="forward",
    )(
        states, segments, delete_target, place_target, token_target, token_mask,
        qkv_w, mix_w, norm_gain[0], norm_bias[0], up_own, down_own,
        cross_query, cross_keyvalue, cross_out, gain_row, bias_row, delete_weight, head_place,
    )
    rows, cols, labels_small, labels_large, most, norms, up_other, down_other, totals, ctotals, grad_delete = outs[:11]
    saved = dict(zip(FORWARD, outs[11:]))
    grad_token, grad_weight = lax.cond(
        most[0, 0] < 0.0,
        lambda: token_chips(2, length // 2, saved["low"], rows, cols, labels_small, head_token),
        lambda: token_chips(3, length, saved["low"], rows, cols, labels_large, head_token),
    )
    other_weight = swap(grad_weight)
    saved.update(co_w=cross_out, cq_w=cross_query, ckv_w=cross_keyvalue, mix_w=mix_w, qkv_w=qkv_w, x=states)
    half_rows, ff_half, attention_rows = 5 * each // 2, hidden // GROUPS, 4 * each
    rows_of = (ff_half, ff_half, half_rows, attention_rows)

    def shards(tall, *lead):
        return VMEM(lead + (tall, width), BF16)

    grad_states, red_ff, red_attention, red_cross, vectors = pl.pallas_call(
        backward_kernel,
        out_shape=(
            whole((count * length, width), F32), whole((2, ff_half, width), F32),
            whole((attention_rows, width), F32), whole((2, half_rows, width), F32), whole((16, width), F32),
        ),
        in_specs=in_vmem(13) + [any_space] * (8 + len(BACKWARD)),
        out_specs=tuple([any_space] + in_vmem(4)),
        scratch_shapes=[
            *[VMEM(*shapes[name]) for name in BACKWARD],
            VMEM((width, hidden), BF16), VMEM((hidden, width), BF16),
            VMEM((length, hidden), BF16), VMEM((length, hidden), BF16),
            shards(ff_half, 2, 4, 2, 2), shards(ff_half, 2, 4, 2, 2), shards(half_rows, 2, 4, 2, 2),
            shards(attention_rows, 4, 2, 2),
            shards(ff_half, 4, 2, 2), shards(ff_half, 4, 2, 2), shards(half_rows, 4, 2, 2),
            *[shards(tall, 4, 2) for tall in rows_of],
            *[shards(tall, 4) for tall in rows_of],
            *[shards(tall, 3) for tall in rows_of],
            VMEM((2, length, width), F32), VMEM((length, width), F32),
            VMEM((length, width), BF16), VMEM((length, 2 * width), BF16), VMEM((count * length, 3 * width), BF16),
            VMEM((2, ff_half, width), F32), VMEM((count * length, width), F32),
            VMEM((8, width), F32), VMEM((8, width), F32),
            VMEM((16, width), F32), VMEM((16, width), F32), VMEM((16, width), F32), VMEM((5, 16, width), F32),
            pltpu.SemaphoreType.DMA((8,)), pltpu.SemaphoreType.DMA((len(BACKWARD) + 1,)),
            pltpu.SemaphoreType.DMA((90,)), pltpu.SemaphoreType.DMA((90,)),
        ],
        compiler_params=pltpu.CompilerParams(
            collective_id=0, has_side_effects=True, vmem_limit_bytes=62 * 1024 * 1024
        ),
        name="backward",
    )(
        saved["grad_low"], grad_token, rows, cols, norms, gain_row, bias_row, ctotals, totals,
        saved["res_d"], saved["cres"], grad_delete, norm_gain[0],
        up_own, up_other, down_own, down_other,
        saved["hid_e"], saved["slope_e"], saved["hid_d"], saved["slope_d"],
        *[saved[name] for name in BACKWARD],
    )
    vocabulary = head_token.shape[1]
    g_qkv, g_mix, g_up, g_down, g_cq, g_ckv, g_co, g_place, g_gain, g_bias, g_cgain, g_cbias, g_delete, g_token = (
        pl.pallas_call(
            unpack_kernel,
            out_shape=(
                whole((each, 3 * width), F32), whole((each, width), F32), whole((each, hidden), F32),
                whole((hidden // GROUPS, width), F32), whole((each, width), F32), whole((each, 2 * width), F32),
                whole((each, width), F32), whole((2 * each, classes), F32),
                whole((1, 2, each), F32), whole((1, 2, each), F32), whole((1, each), F32), whole((1, each), F32),
                whole((2, each), F32), whole((width, vocabulary // GROUPS), F32),
            ),
            in_specs=in_vmem(6),
            out_specs=tuple(in_vmem(14)),
            compiler_params=pltpu.CompilerParams(vmem_limit_bytes=32 * 1024 * 1024),
            name="unpack",
        )(red_ff, red_attention, red_cross, vectors, grad_weight, other_weight)
    )
    return (
        grad_states.reshape(1, count, length, width),
        g_qkv[None], g_mix[None], g_up[None], g_down[None], g_gain, g_bias,
        g_cq, g_ckv, g_co, g_cgain[0], g_cbias[0], g_delete.T, g_place, g_token,
    )


def on_any(
    inputs, segments, delete_target, place_target, token_target, token_mask,
    attention_in, attention_out, feedforward_in, feedforward_out, norm_gain, norm_bias,
    cross_query, cross_keyvalue, cross_out, cross_gain, cross_bias,
    head_delete, head_place, head_token,
):
    phase = lax.axis_index("phase")
    dp_index, dp = lax.axis_index("dp"), lax.axis_size("dp")
    count, length, width = inputs.shape[1:]
    assert count == 2
    hidden = feedforward_in.shape[2]
    scale = float(count * length * dp) ** (-0.5)
    any_space = pl.BlockSpec(memory_space=pl.ANY)
    params = pltpu.CompilerParams(vmem_limit_bytes=56 * 1024 * 1024)

    coded = jnp.where(token_mask == 1, token_target, -1)
    labels_all = lax.all_gather(coded, "dp", tiled=True)
    flags_all = (labels_all >= 0).astype(jnp.int32)

    def row_of(value):
        return lax.dynamic_index_in_dim(value, phase, 0, keepdims=False)

    own_norms = jnp.stack([norm_gain[0, 1], norm_bias[0, 1]])
    up_other, down_other = swap(feedforward_in[0]), swap(feedforward_out[0])
    other_norms = swap(own_norms)
    is_enc = phase == 0
    norms = jnp.concatenate(
        [jnp.where(is_enc, own_norms, other_norms), jnp.where(is_enc, other_norms, own_norms)]
    )
    ids = row_of(segments)
    own_ids = lax.dynamic_index_in_dim(segments, phase, 1, keepdims=False)
    states = inputs[0].reshape(count * length, width)

    qkv, mixed, res, totals, keep, send = pl.pallas_call(
        self_forward,
        out_shape=(
            whole((count * length, 3 * width), BF16),
            whole((count * length, width), BF16),
            whole((count * length, width), F32),
            whole((count, HEADS, length), F32),
            whole((length, width), F32),
            whole((length, width), F32),
        ),
        in_specs=in_vmem(7),
        out_specs=tuple(in_vmem(6)),
        compiler_params=params,
        name="self_forward",
    )(states, own_ids[:, :, None], own_ids[:, None, :], attention_in[0], attention_out[0], norm_gain[0], norm_bias[0])
    received = swap(send)

    ids_e, ids_d_row = ids[0][:, None], ids[1][None, :]
    pair_valid = jnp.concatenate([ids[1, :-1] == ids[1, 1:], jnp.zeros((1,), bool)])
    targets = jnp.stack(
        [row_of(delete_target), row_of(place_target), pair_valid.astype(jnp.int32)], axis=1
    )
    delete_weight = head_delete.T
    gain_row, bias_row = cross_gain[None, :], cross_bias[None, :]
    ff_scratch = [
        VMEM((width, hidden), BF16), VMEM((hidden, width), BF16),
        VMEM((width, hidden), BF16), VMEM((hidden, width), BF16),
    ]
    saved_shapes = (
        whole((length, width), F32),
        whole((length, width), F32),
        whole((length, width), F32),
        whole((length, 2 * width), BF16),
        whole((length, width), BF16),
        whole((length, width), BF16),
        whole((length, width), F32),
        whole((HEADS, length), F32),
        whole((length, hidden), BF16), whole((length, hidden), BF16),
        whole((length, hidden), BF16), whole((length, hidden), BF16),
        whole((length, width), F32),
        whole((length, width), BF16),
    )
    classes = head_place.shape[1]
    each = width // GROUPS
    outs = pl.pallas_call(
        partial(rows_forward, scale),
        out_shape=saved_shapes + (
            whole((length, width), BF16),
            whole((length, width), F32),
            whole((8, width), F32),
            whole((GROUPS, each, 2 * classes), BF16),
        ),
        in_specs=in_vmem(5) + [any_space] * 4 + in_vmem(8),
        out_specs=tuple(in_vmem(18)),
        scratch_shapes=ff_scratch + [pltpu.SemaphoreType.DMA((2, 2))],
        compiler_params=params,
        name="rows_forward",
    )(
        keep, received, ids_e, ids_d_row, targets,
        feedforward_in[0], up_other, feedforward_out[0], down_other, norms,
        cross_query, cross_keyvalue, cross_out, gain_row, bias_row, delete_weight, head_place,
    )
    saved = outs[:14]
    low, grad_low, grad_delete, grad_place = outs[14:]

    shard = head_token.shape[1] // (2 * dp)
    weight = lax.dynamic_slice_in_dim(head_token, (dp_index * 2 + phase) * shard, shard, 1)
    weight_t = weight.T
    flags = row_of(token_mask)

    def run_head(numbers, cap, block_rows):
        return token_head(numbers, cap, block_rows, low, flags, labels_all, flags_all, weight, weight_t, scale)

    small = length // 2
    fits = jnp.max(jnp.sum(flags_all, axis=1)) <= small
    grad_token, grad_weight = lax.cond(
        fits, lambda: run_head((1, 2, 3), small, 4 * small), lambda: run_head((4, 5, 6), length, 2 * length)
    )
    other_weight = swap(grad_weight)
    grad_head_token = jnp.concatenate(
        [jnp.where(is_enc, grad_weight, other_weight), jnp.where(is_enc, other_weight, grad_weight)], axis=1
    )

    each = width // GROUPS
    ff_rows = 2 * hidden // GROUPS
    keep, send, ff_own, ff_other, cross_shards, vectors = pl.pallas_call(
        rows_backward,
        out_shape=(
            whole((length, width), F32), whole((length, width), F32),
            whole((GROUPS, ff_rows, width), BF16), whole((GROUPS, ff_rows, width), BF16),
            whole((GROUPS, 5 * each, width), BF16), whole((8, width), F32),
        ),
        in_specs=in_vmem(4) + [any_space] * 4 + in_vmem(6 + 14 + 1),
        out_specs=(in_vmem(2) + [any_space] * 2 + in_vmem(2)),
        scratch_shapes=ff_scratch + [
            VMEM((GROUPS, ff_rows, width), BF16), VMEM((GROUPS, ff_rows, width), BF16),
            VMEM((length, width), F32), VMEM((length, width), F32),
            VMEM((length, width), BF16), VMEM((length, 2 * width), BF16),
            pltpu.SemaphoreType.DMA((2, 2)), pltpu.SemaphoreType.DMA((2,)),
        ],
        compiler_params=params,
        name="rows_backward",
    )(
        grad_low, grad_token, ids_e, ids_d_row,
        feedforward_in[0], up_other, feedforward_out[0], down_other, norms,
        cross_query, cross_keyvalue, cross_out, gain_row, bias_row, *saved, grad_place,
    )
    received = swap(send)
    ff_received = swap(ff_other)
    half_rows = 5 * each // 2
    cross_keep = lax.dynamic_slice_in_dim(cross_shards, phase * half_rows, half_rows, 1)
    cross_received = swap(lax.dynamic_slice_in_dim(cross_shards, (1 - phase) * half_rows, half_rows, 1))
    shared = jnp.concatenate([vectors[4:6], grad_delete[:2]])
    norm_own = jnp.where(is_enc, vectors[0:2], vectors[2:4])
    norm_other = jnp.where(is_enc, vectors[2:4], vectors[0:2])
    vector_received = swap(jnp.concatenate([norm_other, shared]))
    vector_sums = jnp.concatenate([norm_own, shared]) + vector_received

    grad_states, attention_shards, first_vectors = pl.pallas_call(
        self_backward,
        out_shape=(
            whole((count * length, width), F32), whole((GROUPS, 4 * each, width), BF16), whole((8, width), F32),
        ),
        in_specs=in_vmem(12),
        out_specs=tuple(in_vmem(3)),
        scratch_shapes=[VMEM((count * length, width), F32), VMEM((count * length, 3 * width), BF16)],
        compiler_params=params,
        name="self_backward",
    )(
        keep, received, states, own_ids[:, :, None], own_ids[:, None, :], attention_in[0], attention_out[0],
        norm_gain[0], qkv, mixed, res, totals,
    )

    all_vectors = jnp.stack([
        first_vectors[0], vector_sums[0], first_vectors[1], vector_sums[1],
        vector_sums[2], vector_sums[3], vector_sums[4], vector_sums[5],
    ])
    ff_sum = (ff_own.astype(F32) + ff_received.astype(F32)).astype(BF16)
    cross_sum = (cross_keep.astype(F32) + cross_received.astype(F32)).astype(BF16)
    cross_other = swap(cross_sum)
    cross_all = jnp.concatenate(
        [jnp.where(is_enc, cross_sum, cross_other), jnp.where(is_enc, cross_other, cross_sum)], axis=1
    )
    ff_up = hidden // width * each

    def spread(value):
        return lax.psum_scatter(value.astype(F32), "dp", scatter_dimension=0, tiled=True)

    g_qkv = spread(unpacked(attention_shards[:, : 3 * each], width, 3 * width))
    g_mix = spread(unpacked(attention_shards[:, 3 * each :], width, width))
    g_up = spread(unpacked(ff_sum[:, :ff_up], width, hidden))
    g_down = spread(unpacked(ff_sum[:, ff_up:], hidden, width))
    g_cq = spread(unpacked(cross_all[:, :each], width, width))
    g_ckv = spread(unpacked(cross_all[:, each : 3 * each], width, 2 * width))
    g_co = spread(unpacked(cross_all[:, 3 * each : 4 * each], width, width))
    place = cross_all[:, 4 * each :].reshape(GROUPS, each, 2, classes)
    g_place = spread(place.transpose(0, 2, 1, 3).reshape(2 * width, classes))
    vector_out = lax.psum_scatter(all_vectors, "dp", scatter_dimension=1, tiled=True)
    return (
        grad_states.reshape(1, count, length, width),
        g_qkv[None], g_mix[None], g_up[None], g_down[None],
        vector_out[None, 0:2], vector_out[None, 2:4],
        g_cq, g_ckv, g_co, vector_out[4], vector_out[5], vector_out[6:8].T, g_place, grad_head_token,
    )


def on_device(*args):
    chips = lax.axis_size("dp") == GROUPS and args[0].shape[1] == 2
    return on_chips(*args) if chips else on_any(*args)


def solution(mesh):
    layer, row = P("phase", None, None), P("dp", None)
    return jax.shard_map(
        on_device,
        mesh=mesh,
        in_specs=(P("phase", "dp", None, None), P("dp", None, None), row, row, row, row)
        + (layer,) * 6 + (P(),) * 8,
        out_specs=(P("phase", "dp", None, None),) + (P("phase", "dp", None),) * 4
        + (P("phase", None, "dp"),) * 2 + (row,) * 3 + (P("dp"),) * 2 + (row,) * 2 + (P(None, "dp"),),
        check_vma=False,
    )
```

```python
from functools import partial

import jax
import jax.numpy as jnp
from jax import lax
from jax.experimental import pallas as pl
from jax.experimental.pallas import tpu as pltpu
from jax.sharding import PartitionSpec as P

HEADS = 8
HEAD = 64
PAIR = 2 * HEAD
MASKED_SCORE = -1e30
NORM_EPSILON = 1e-05
GROUPS = 16
F32 = jnp.float32
BF16 = jnp.bfloat16
MESH = pl.DeviceIdType.MESH
VMEM = pltpu.VMEM
GELU_C = 0.7978845608028654
GELU_A = 0.044715


def mm(left, right):
    return jnp.dot(left, right, preferred_element_type=F32)


def mm_nt(left, right):
    return lax.dot_general(left, right, (((1,), (1,)), ((), ())), preferred_element_type=F32)


def mm_tn(left, right):
    return lax.dot_general(left, right, (((0,), (0,)), ((), ())), preferred_element_type=F32)


def norm_forward(residual, gain, bias):
    centered = residual - jnp.mean(residual, axis=-1, keepdims=True)
    variance = jnp.mean(centered * centered, axis=-1, keepdims=True)
    return centered * lax.rsqrt(variance + NORM_EPSILON) * gain + bias


def norm_back(residual, gain, grad_out):
    centered = residual - jnp.mean(residual, axis=-1, keepdims=True)
    variance = jnp.mean(centered * centered, axis=-1, keepdims=True)
    scale = lax.rsqrt(variance + NORM_EPSILON)
    unit = centered * scale
    grad_unit = grad_out * gain
    grad_gain = jnp.sum(grad_out * unit, axis=0, keepdims=True)
    grad_bias = jnp.sum(grad_out, axis=0, keepdims=True)
    grad_res = scale * (
        grad_unit
        - jnp.mean(grad_unit, axis=-1, keepdims=True)
        - unit * jnp.mean(grad_unit * unit, axis=-1, keepdims=True)
    )
    return grad_res, grad_gain, grad_bias


def gelu_both(pre):
    square = pre * pre
    bent = jnp.tanh(GELU_C * pre * (1.0 + GELU_A * square))
    half = 0.5 * (1.0 + bent)
    slope = half + (0.5 * GELU_C) * pre * (1.0 - bent * bent) * (1.0 + 3.0 * GELU_A * square)
    return pre * half, slope


def attend_forward(queries, keys, values, allowed, out_ref, totals_ref, rows):
    lane = lax.broadcasted_iota(jnp.int32, (1, PAIR), 1)
    for pair in range(HEADS // 2):
        q, k, v = queries(pair), keys(pair), values(pair)
        mixed = None
        for side in range(2):
            own = (lane < HEAD) if side == 0 else (lane >= HEAD)
            scores = mm_nt(k, jnp.where(own, q * HEAD ** (-0.5), 0))
            scores = jnp.where(allowed, scores, MASKED_SCORE)
            top = jnp.max(scores, axis=0, keepdims=True)
            weights = jnp.exp(scores - top)
            summed = jnp.sum(weights, axis=0, keepdims=True)
            probs = (weights * (1.0 / summed)).astype(BF16)
            totals_ref[2 * pair + side : 2 * pair + side + 1, :] = top + jnp.log(summed)
            part = mm_tn(probs, jnp.where(own, v, 0))
            mixed = part if mixed is None else mixed + part
        out_ref[rows, pair * PAIR : (pair + 1) * PAIR] = mixed.astype(BF16)


def attend_backward(
    queries, keys, values, grads, allowed, totals_ref, put_q, put_k, put_v, between=None
):
    lane = lax.broadcasted_iota(jnp.int32, (1, PAIR), 1)
    for pair in range(HEADS // 2):
        q, k, v, da = queries(pair), keys(pair), values(pair), grads(pair)
        grad_q = grad_k = grad_v = None
        for side in range(2):
            own = (lane < HEAD) if side == 0 else (lane >= HEAD)
            q_own = jnp.where(own, q * HEAD ** (-0.5), 0)
            da_own = jnp.where(own, da, 0)
            scores = jnp.where(allowed, mm_nt(k, q_own), MASKED_SCORE)
            probs = jnp.exp(scores - totals_ref[2 * pair + side : 2 * pair + side + 1, :])
            grad_probs = mm_nt(v, da_own)
            part_v = mm(probs.astype(BF16), da_own)
            shared = jnp.sum(probs * grad_probs, axis=0, keepdims=True)
            grad_scores = (probs * (grad_probs - shared)).astype(BF16)
            part_k = mm(grad_scores, q_own)
            part_q = mm_tn(grad_scores, jnp.where(own, k, 0))
            grad_q = part_q if grad_q is None else grad_q + part_q
            grad_k = part_k if grad_k is None else grad_k + part_k
            grad_v = part_v if grad_v is None else grad_v + part_v
        put_q(pair, (grad_q * HEAD ** (-0.5)).astype(BF16))
        put_k(pair, grad_k.astype(BF16))
        put_v(pair, grad_v.astype(BF16))
        if between is not None:
            between(pair)


def column(pair, offset=0):
    return slice(offset + pair * PAIR, offset + (pair + 1) * PAIR)


def put_shards(ref, first, grad):
    height = grad.shape[0] // GROUPS
    width = ref.shape[2]
    for block in range(grad.shape[1] // width):
        piece = grad[:, block * width : (block + 1) * width].astype(BF16)
        ref[:, first + block * height : first + (block + 1) * height, :] = piece.reshape(
            GROUPS, height, width
        )


def self_forward(
    x_ref, ids_ref, ids_row_ref, qkv_w_ref, mix_w_ref, gain_ref, bias_ref,
    qkv_ref, mixed_ref, res_ref, totals_ref, keep_ref, send_ref,
):
    phase = lax.axis_index("phase")
    count, length = ids_ref.shape[0], ids_ref.shape[1]
    width = x_ref.shape[1]
    for part in range(3):
        cols = slice(part * width, (part + 1) * width)
        qkv_ref[:, cols] = mm(x_ref[...], qkv_w_ref[:, cols]).astype(BF16)
    for row in range(count):
        rows = slice(row * length, (row + 1) * length)
        attend_forward(
            lambda pair: qkv_ref[rows, column(pair)],
            lambda pair: qkv_ref[rows, column(pair, width)],
            lambda pair: qkv_ref[rows, column(pair, 2 * width)],
            ids_ref[row] == ids_row_ref[row],
            mixed_ref, totals_ref.at[row], rows,
        )
    for row in range(count):
        rows = slice(row * length, (row + 1) * length)
        residual = x_ref[rows, :].astype(F32) + mm(mixed_ref[rows, :], mix_w_ref[...])
        res_ref[rows, :] = residual
        after = norm_forward(residual, gain_ref[0:1, :], bias_ref[0:1, :])

        @pl.when(phase == row)
        def _():
            keep_ref[...] = after

        @pl.when(phase != row)
        def _():
            send_ref[...] = after


def load_sided(phase, own_refs, other_refs, enc_refs, dec_refs, sems):
    for i, (own, other, enc, dec) in enumerate(zip(own_refs, other_refs, enc_refs, dec_refs)):
        @pl.when(phase == 0)
        def _():
            pltpu.make_async_copy(own, enc, sems.at[0, i]).start()
            pltpu.make_async_copy(other, dec, sems.at[1, i]).start()

        @pl.when(phase != 0)
        def _():
            pltpu.make_async_copy(other, enc, sems.at[0, i]).start()
            pltpu.make_async_copy(own, dec, sems.at[1, i]).start()

    def wait_enc(i):
        pltpu.make_async_copy(own_refs[i], enc_refs[i], sems.at[0, i]).wait()

    def wait_dec(i):
        pltpu.make_async_copy(own_refs[i], dec_refs[i], sems.at[1, i]).wait()

    return wait_enc, wait_dec


def feed_forward(middle, up_ref, down_ref, hidden_ref, slope_ref):
    width = middle.shape[1]
    low = middle.astype(BF16)
    total = middle
    for part in range(up_ref.shape[1] // width):
        cols = slice(part * width, (part + 1) * width)
        hidden, slope = gelu_both(mm(low, up_ref[:, cols]))
        hidden = hidden.astype(BF16)
        hidden_ref[:, cols] = hidden
        slope_ref[:, cols] = slope.astype(BF16)
        total = total + mm(hidden, down_ref[cols, :])
    return total


def feed_back(grad_res, middle_low, up_ref, down_ref, hidden_ref, slope_ref, put_up, put_down, between=None):
    width = grad_res.shape[1]
    branch = grad_res.astype(BF16)
    total = grad_res
    for part in range(up_ref.shape[1] // width):
        cols = slice(part * width, (part + 1) * width)
        put_down(part, mm_tn(hidden_ref[:, cols], branch))
        grad_hidden = mm_nt(branch, down_ref[cols, :])
        grad_pre = (grad_hidden * slope_ref[:, cols].astype(F32)).astype(BF16)
        put_up(part, mm_tn(middle_low, grad_pre))
        total = total + mm_nt(grad_pre, up_ref[:, cols])
        if between is not None:
            between(part)
    return total


def feed_puts(ref, parts):
    width = ref.shape[2]
    rows = width // GROUPS
    per, tall = GROUPS // parts, parts * rows

    def put_up(part, value):
        put_shards(ref, part * rows, value)

    def put_down(part, value):
        ref[part * per : (part + 1) * per, tall : 2 * tall, :] = value.astype(BF16).reshape(
            per, tall, width
        )

    return put_up, put_down


def class_grads(logits, labels, row_weight, valid):
    lane = lax.broadcasted_iota(jnp.int32, logits.shape, 1)
    logits = jnp.where(lane < valid, logits, -jnp.inf) if valid < logits.shape[1] else logits
    top = jnp.max(logits, axis=-1, keepdims=True)
    weights = jnp.exp(logits - top)
    probs = weights * (1.0 / jnp.sum(weights, axis=-1, keepdims=True))
    return (probs - (lane == labels).astype(F32)) * row_weight


def rows_forward(
    scale, keep_ref, recv_ref, ids_e_ref, ids_d_row_ref, targets_ref,
    up_own, up_other, down_own, down_other, norms_ref,
    cq_w_ref, ckv_w_ref, co_w_ref, cgain_ref, cbias_ref, delete_w_ref, place_w_ref,
    after_e_ref, res_e_ref, after_d_ref, ckv_ref, cq_ref, cmixed_ref, cres_ref, ctotals_ref,
    hid_e_ref, slope_e_ref, hid_d_ref, slope_d_ref, res_d_ref, src_ref,
    low_ref, grad_ref, grad_delete_ref, grad_place_ref,
    up_e, down_e, up_d, down_d, sems,
):
    phase = lax.axis_index("phase")
    width = keep_ref.shape[1]
    wait_enc, wait_dec = load_sided(
        phase, (up_own, down_own), (up_other, down_other), (up_e, down_e), (up_d, down_d), sems
    )

    @pl.when(phase == 0)
    def _():
        after_e_ref[...] = keep_ref[...]
        after_d_ref[...] = recv_ref[...]

    @pl.when(phase != 0)
    def _():
        after_e_ref[...] = recv_ref[...]
        after_d_ref[...] = keep_ref[...]

    wait_enc(0)
    wait_enc(1)
    encoder_rows(
        after_e_ref, up_e, down_e, norms_ref[0:1, :], norms_ref[1:2, :], ckv_w_ref,
        hid_e_ref, slope_e_ref, res_e_ref, src_ref, ckv_ref,
    )
    middle = cross_rows(
        after_d_ref, ids_e_ref[...] == ids_d_row_ref[...], cq_w_ref, co_w_ref, cgain_ref, cbias_ref,
        cq_ref, ckv_ref, cmixed_ref, cres_ref, ctotals_ref,
    )
    wait_dec(0)
    wait_dec(1)
    targets = targets_ref[...]
    decoder_rows(
        scale, middle, up_d, down_d, norms_ref[2:3, :], norms_ref[3:4, :],
        targets[:, 0:1], targets[:, 1:2], targets[:, 2:3], delete_w_ref, place_w_ref,
        hid_d_ref, slope_d_ref, res_d_ref, low_ref, grad_ref, grad_delete_ref, grad_place_ref,
    )


def encoder_rows(
    after_ref, up, down, gain, bias, ckv_w_ref, hid_ref, slope_ref, res_ref, src_ref, ckv_ref
):
    residual = feed_forward(after_ref[...], up, down, hid_ref, slope_ref)
    res_ref[...] = residual
    src = norm_forward(residual, gain, bias).astype(BF16)
    src_ref[...] = src
    width = src.shape[1]
    for part in range(2):
        cols = slice(part * width, (part + 1) * width)
        ckv_ref[:, cols] = mm(src, ckv_w_ref[:, cols]).astype(BF16)


def cross_rows(
    after_ref, allowed, cq_w_ref, co_w_ref, cgain_ref, cbias_ref, cq_ref, ckv_ref, cmixed_ref, cres_ref, ctotals_ref
):
    width = after_ref.shape[1]
    cq_ref[...] = mm(after_ref[...].astype(BF16), cq_w_ref[...]).astype(BF16)
    attend_forward(
        lambda pair: cq_ref[:, column(pair)],
        lambda pair: ckv_ref[:, column(pair)],
        lambda pair: ckv_ref[:, column(pair, width)],
        allowed, cmixed_ref, ctotals_ref, slice(None),
    )
    residual = after_ref[...] + mm(cmixed_ref[...], co_w_ref[...])
    cres_ref[...] = residual
    return norm_forward(residual, cgain_ref[...], cbias_ref[...])


def decoder_rows(
    scale, middle, up, down, gain, bias, delete_label, place_label, pair_valid, delete_w_ref, place_w_ref,
    hid_ref, slope_ref, res_ref, low_ref, grad_ref, grad_delete_ref, grad_place_ref,
):
    residual = feed_forward(middle, up, down, hid_ref, slope_ref)
    res_ref[...] = residual
    low = norm_forward(residual, gain, bias).astype(BF16)
    low_ref[...] = low
    length, width = low.shape
    valid = delete_w_ref.shape[0]
    weight = jnp.concatenate([delete_w_ref[...], jnp.zeros((128 - valid, width), BF16)], axis=0)
    grads = class_grads(mm_nt(low, weight), delete_label, scale, valid).astype(BF16)
    grad_delete_ref[...] = mm_tn(grads, low)[:8]
    grad_low = mm(grads, weight)
    logits = mm(low, place_w_ref[:width, :]) + pltpu.roll(
        mm(low, place_w_ref[width:, :]), length - 1, 0
    )
    weight = pair_valid.astype(F32) * scale
    grads = class_grads(logits, place_label, weight, logits.shape[1])
    later = pltpu.roll(grads, 1, 0).astype(BF16)
    grads = grads.astype(BF16)
    classes = grads.shape[1]
    for top, part in enumerate((grads, later)):
        part = mm_tn(low, part).astype(BF16).reshape(GROUPS // 2, 2, width // GROUPS, classes)
        at = slice(top * GROUPS // 2, (top + 1) * GROUPS // 2)
        for half in range(2):
            grad_place_ref[at, :, half * classes : (half + 1) * classes] = part[:, half]
    grad_low = grad_low + mm_nt(grads, place_w_ref[:width, :]) + mm_nt(later, place_w_ref[width:, :])
    grad_ref[...] = grad_low


def rows_backward(
    grad_low_ref, grad_token_ref, ids_e_ref, ids_d_row_ref,
    up_own, up_other, down_own, down_other, norms_ref,
    cq_w_ref, ckv_w_ref, co_w_ref, cgain_ref, cbias_ref,
    after_e_ref, res_e_ref, after_d_ref, ckv_ref, cq_ref, cmixed_ref, cres_ref, ctotals_ref,
    hid_e_ref, slope_e_ref, hid_d_ref, slope_d_ref, res_d_ref, src_ref, grad_place_ref,
    keep_ref, send_ref, own_ref, other_ref, cross_ref, vectors_ref,
    up_e, down_e, up_d, down_d, grad_e, grad_d, after_e_grad, after_d_grad, gq_ref, gckv_ref, sems, out_sems,
):
    phase = lax.axis_index("phase")
    width = grad_low_ref.shape[1]
    wait_enc, wait_dec = load_sided(
        phase, (up_own, down_own), (up_other, down_other), (up_e, down_e), (up_d, down_d), sems
    )
    grad_out = grad_low_ref[...] + grad_token_ref[...]
    grad_res, gain_grad, bias_grad = norm_back(res_d_ref[...], norms_ref[2:3, :], grad_out)
    vectors_ref[2:3, :] = gain_grad
    vectors_ref[3:4, :] = bias_grad
    cres = cres_ref[...]
    middle_low = norm_forward(cres, cgain_ref[...], cbias_ref[...]).astype(BF16)
    wait_dec(0)
    wait_dec(1)
    grad_middle = feed_back(grad_res, middle_low, up_d, down_d, hid_d_ref, slope_d_ref, *feed_puts(grad_d, 4))
    move_d = [
        pltpu.make_async_copy(grad_d, own_ref, out_sems.at[0]),
        pltpu.make_async_copy(grad_d, other_ref, out_sems.at[0]),
    ]

    @pl.when(phase == 0)
    def _():
        move_d[1].start()

    @pl.when(phase != 0)
    def _():
        move_d[0].start()

    grad_res, gain_grad, bias_grad = norm_back(cres, cgain_ref[...], grad_middle)
    vectors_ref[4:5, :] = gain_grad
    vectors_ref[5:6, :] = bias_grad
    branch = grad_res.astype(BF16)
    after_low = after_d_ref[...].astype(BF16)
    rows = width // GROUPS
    put_shards(cross_ref, 3 * rows, mm_tn(cmixed_ref[...], branch))
    grad_mixed = mm_nt(branch, co_w_ref[...]).astype(BF16)

    def put_q(pair, value):
        gq_ref[:, column(pair)] = value

    def put_k(pair, value):
        gckv_ref[:, column(pair)] = value

    def put_v(pair, value):
        gckv_ref[:, column(pair, width)] = value

    attend_backward(
        lambda pair: cq_ref[:, column(pair)],
        lambda pair: ckv_ref[:, column(pair)],
        lambda pair: ckv_ref[:, column(pair, width)],
        lambda pair: grad_mixed[:, column(pair)],
        ids_e_ref[...] == ids_d_row_ref[...],
        ctotals_ref, put_q, put_k, put_v,
    )
    grad_q = gq_ref[...]
    grad_kv = gckv_ref[...]
    put_shards(cross_ref, 0, mm_tn(after_low, grad_q))
    put_shards(cross_ref, rows, mm_tn(src_ref[...], grad_kv))
    cross_ref[:, 4 * rows : 5 * rows, :] = grad_place_ref[...]
    after_d_grad[...] = grad_res + mm_nt(grad_q, cq_w_ref[...])
    grad_src = mm_nt(grad_kv, ckv_w_ref[...]).astype(BF16).astype(F32)
    grad_res, gain_grad, bias_grad = norm_back(res_e_ref[...], norms_ref[0:1, :], grad_src)
    vectors_ref[0:1, :] = gain_grad
    vectors_ref[1:2, :] = bias_grad
    vectors_ref[6:8, :] = jnp.zeros((2, width), F32)
    wait_enc(0)
    wait_enc(1)
    after_e_grad[...] = feed_back(
        grad_res, after_e_ref[...].astype(BF16), up_e, down_e, hid_e_ref, slope_e_ref,
        *feed_puts(grad_e, 4),
    )
    move_e = [
        pltpu.make_async_copy(grad_e, own_ref, out_sems.at[1]),
        pltpu.make_async_copy(grad_e, other_ref, out_sems.at[1]),
    ]

    @pl.when(phase == 0)
    def _():
        move_e[0].start()
        keep_ref[...] = after_e_grad[...]
        send_ref[...] = after_d_grad[...]

    @pl.when(phase != 0)
    def _():
        move_e[1].start()
        keep_ref[...] = after_d_grad[...]
        send_ref[...] = after_e_grad[...]

    move_d[0].wait()
    move_e[0].wait()


def self_backward(
    keep_ref, recv_ref, x_ref, ids_ref, ids_row_ref, qkv_w_ref, mix_w_ref, gain_ref,
    qkv_ref, mixed_ref, res_ref, totals_ref,
    grad_x_ref, shards_ref, vectors_ref,
    after_grad, grad_qkv,
):
    phase = lax.axis_index("phase")
    count, length = ids_ref.shape[0], ids_ref.shape[1]
    width = x_ref.shape[1]
    for row in range(count):
        rows = slice(row * length, (row + 1) * length)

        @pl.when(phase == row)
        def _():
            after_grad[rows, :] = keep_ref[...]

        @pl.when(phase != row)
        def _():
            after_grad[rows, :] = recv_ref[...]

    grad_res, gain_grad, bias_grad = norm_back(res_ref[...], gain_ref[0:1, :], after_grad[...])
    vectors_ref[0:1, :] = gain_grad
    vectors_ref[1:2, :] = bias_grad
    vectors_ref[2:8, :] = jnp.zeros((6, width), F32)
    grad_x_ref[...] = grad_res
    branch = grad_res.astype(BF16)
    rows_each = width // GROUPS
    put_shards(shards_ref, 3 * rows_each, mm_tn(mixed_ref[...], branch))
    grad_mixed = mm_nt(branch, mix_w_ref[...]).astype(BF16)
    for row in range(count):
        rows = slice(row * length, (row + 1) * length)

        def put(offset):
            def store(pair, value):
                grad_qkv[rows, column(pair, offset)] = value

            return store

        attend_backward(
            lambda pair: qkv_ref[rows, column(pair)],
            lambda pair: qkv_ref[rows, column(pair, width)],
            lambda pair: qkv_ref[rows, column(pair, 2 * width)],
            lambda pair: grad_mixed[rows, column(pair)],
            ids_ref[row] == ids_row_ref[row],
            totals_ref.at[row], put(0), put(width), put(2 * width),
        )
    for part in range(3):
        cols = slice(part * width, (part + 1) * width)
        put_shards(shards_ref, part * rows_each, mm_tn(x_ref[...], grad_qkv[:, cols]))
    grad_x_ref[...] += mm_nt(grad_qkv[...], qkv_w_ref[...])


def token_forward(low_ref, weight_ref, probs_ref, totals_ref):
    logits = mm_nt(weight_ref[...], low_ref[...])
    top = jnp.max(logits, axis=0, keepdims=True)
    weights = jnp.exp(logits - top)
    summed = jnp.sum(weights, axis=0, keepdims=True)
    probs_ref[0] = (weights * (1.0 / summed)).astype(BF16)
    totals_ref[0] = top + jnp.log(summed)


def token_backward(
    scale, probs_ref, share_ref, label_ref, low_ref, weight_ref, grad_low_ref, grad_weight_ref, total
):
    step = pl.program_id(0)
    labels = label_ref[0]
    shape = probs_ref.shape[1:]
    offset = (lax.axis_index("dp") * 2 + lax.axis_index("phase")) * shape[0]
    chosen = lax.broadcasted_iota(jnp.int32, shape, 0) == labels - offset
    grads = probs_ref[0].astype(F32) * share_ref[0] - chosen.astype(F32)
    grads = (grads * jnp.where(labels >= 0, scale, 0.0)).astype(BF16)
    grad_low = mm_tn(grads, weight_ref[...]).astype(BF16)
    cap = grad_low_ref.shape[1]
    for block in range(grad_low_ref.shape[0]):
        grad_low_ref[block] = grad_low[block * cap : (block + 1) * cap]
    part = mm(grads, low_ref[...])

    @pl.when(step == 0)
    def _():
        total[...] = part

    @pl.when(step != 0)
    def _():
        total[...] += part

    @pl.when(step == pl.num_programs(0) - 1)
    def _():
        grad_weight_ref[...] = total[...].T


def place_of(dp):
    return lax.rem(dp, 2), lax.rem(dp // 2, 2), dp // 4


def index_of(x, y, z):
    return (z * 2 + y) * 2 + x


def greet(devices):
    barrier = pltpu.get_barrier_semaphore()
    for dp, phase in devices:
        pl.semaphore_signal(barrier, inc=1, device_id=(dp, phase), device_id_type=MESH)
    pl.semaphore_wait(barrier, len(devices))


def remote(src, dst, send, recv, device):
    return pltpu.make_async_remote_copy(
        src_ref=src, dst_ref=dst, send_sem=send, recv_sem=recv, device_id=device, device_id_type=MESH
    )


def gather_blocks(block):
    return lax.all_gather(lax.all_gather(block, "dp"), "phase")


def scatter_blocks(part):
    part = lax.psum_scatter(part.astype(F32), "phase", scatter_dimension=0, tiled=False)
    return lax.psum_scatter(part, "dp", scatter_dimension=0, tiled=False)


def token_shares(totals):
    top = lax.pmax(totals, ("dp", "phase"))
    return jnp.exp(totals - top) / lax.psum(jnp.exp(totals - top), ("dp", "phase"))


def pack_labels(labels, flags, out_ref):
    count, length = labels.shape
    before = lax.broadcasted_iota(jnp.int32, (length, length), 0)
    after = lax.broadcasted_iota(jnp.int32, (length, length), 1)
    upto = jnp.where(before <= after, 1.0, 0.0).astype(BF16)
    rows = jnp.concatenate([flags.astype(F32)] + [jnp.zeros((8 - count, length), F32)], axis=0)
    place = mm(rows.astype(BF16), upto)
    for row in range(count):
        flag = rows[row : row + 1]
        chosen = (before.astype(F32) == place[row : row + 1] - 1.0) & (flag > 0.0)
        label = labels[row : row + 1]
        high = lax.shift_right_logical(label, 8)
        parts = [high.astype(F32), (label - high * 256).astype(F32), flag, jnp.zeros((5, length), F32)]
        found = mm_nt(
            jnp.concatenate(parts, axis=0).astype(BF16), jnp.where(chosen, 1.0, 0.0).astype(BF16)
        )
        packed = jnp.where(found[2:3] > 0.5, found[0:1] * 256.0 + found[1:2], -1.0)
        out_ref[row : row + 1, :] = packed.astype(jnp.int32)


FORWARD = (
    "qkv", "mixed", "res", "after", "res_e", "ckv", "cq", "cmixed", "cres",
    "hid_e", "slope_e", "hid_d", "slope_d", "res_d", "src", "low", "grad_low", "grad_place",
)


def forward_kernel(
    scale, x_ref, segments_ref, delete_ref, place_ref, token_ref, mask_ref,
    qkv_w_ref, mix_w_ref, gain_ref, bias_ref, up_own, down_own,
    cq_w_any, ckv_w_any, co_w_any, cgain_ref, cbias_ref, delete_w_ref, place_w_any,
    rows_ref, cols_ref, labels_small_ref, labels_large_ref, most_ref, norms_ref, up_other, down_other,
    totals_ref, ctotals_ref, grad_delete_ref, *rest,
):
    outs, rest = dict(zip(FORWARD, rest)), rest[len(FORWARD) :]
    held, rest = dict(zip(FORWARD, rest)), rest[len(FORWARD) :]
    up, down, cq_w, ckv_w, co_w, place_w, send_after, own_labels, all_labels, turned, load, store, send, recv = rest
    dp, phase = lax.axis_index("dp"), lax.axis_index("phase")
    x, y, z = place_of(dp)
    chips = [
        (lax.rem(x + a, 2), lax.rem(y + b, 2), lax.rem(z + c, 4))
        for c in range(4) for b in range(2) for a in range(2) if a + b + c
    ]
    core = (dp, 1 - phase)
    greet([(index_of(*chip), phase) for chip in chips] + [core])
    copies, stores = [], []

    def remote_to(src, dst, device):
        i = len(copies)
        copy = remote(src, dst, send.at[i], recv.at[i], device)
        copy.start()
        copies.append(copy)
        return copy

    def save(*names):
        for name in names:
            copy = pltpu.make_async_copy(held[name], outs[name], store.at[len(stores)])
            copy.start()
            stores.append(copy)

    norms_ref[phase, 0:1, :] = gain_ref[1:2, :]
    norms_ref[phase, 1:2, :] = bias_ref[1:2, :]
    from_norms = remote_to(norms_ref.at[phase], norms_ref.at[phase], core)
    from_up = remote_to(up_own, up.at[phase], core)
    from_down = remote_to(down_own, down.at[phase], core)
    loads = [
        pltpu.make_async_copy(src, dst, load.at[i])
        for i, (src, dst) in enumerate((
            (up_own, up.at[phase]), (down_own, down.at[phase]), (ckv_w_any, ckv_w), (cq_w_any, cq_w),
            (co_w_any, co_w), (place_w_any, place_w),
        ))
    ]
    for copy in loads:
        copy.start()
    pack_labels(token_ref[...], mask_ref[...], own_labels)
    for chip in chips:
        remote_to(own_labels, all_labels.at[z, y, x], (index_of(*chip), phase))
    label_copies = copies[3:]
    all_labels[z, y, x] = own_labels[...]
    is_enc = phase == 0
    segments = segments_ref[...].astype(F32)
    length = segments.shape[2]

    def pick(first, second):
        return jnp.where(is_enc, first, second)

    def own_row(ref):
        value = ref[...].astype(F32)
        return pick(value[0:1], value[1:2])

    ids_e = pick(segments[0, 0:1], segments[1, 0:1])
    ids_d = pick(segments[0, 1:2], segments[1, 1:2])
    own_ids = [pick(segments[r, 0:1], segments[r, 1:2]) for r in range(2)]
    block = jnp.concatenate([ids_d] * 8, axis=0)
    later = pltpu.roll(block, length - 1, 1)
    lane = lax.broadcasted_iota(jnp.int32, (8, length), 1)
    valid = jnp.where((block == later) & (lane < length - 1), 1.0, 0.0)[0:1]
    rows = jnp.concatenate(
        own_ids + [ids_e, ids_d, own_row(delete_ref), own_row(place_ref), valid, own_row(mask_ref)], axis=0
    )
    rows_ref[...] = rows
    turned[...] = jnp.zeros(turned.shape, F32)
    turned[0:8, :] = rows
    cols = turned[...].T
    cols_ref[...] = cols
    width = x_ref.shape[1]
    qkv, mixed, res = held["qkv"], held["mixed"], held["res"]
    for part in range(3):
        span = slice(part * width, (part + 1) * width)
        qkv[:, span] = mm(x_ref[...], qkv_w_ref[:, span]).astype(BF16)
    save("qkv")
    for turn in range(2):
        row = 1 - phase if turn == 0 else phase
        span = pl.ds(pl.multiple_of(row * length, length), length)
        allowed = jnp.where(row == 0, cols[:, 0:1], cols[:, 1:2]) == jnp.where(
            row == 0, own_ids[0], own_ids[1]
        )
        attend_forward(
            lambda pair: qkv[span, column(pair)],
            lambda pair: qkv[span, column(pair, width)],
            lambda pair: qkv[span, column(pair, 2 * width)],
            allowed, mixed, totals_ref.at[row], span,
        )
        residual = x_ref[span, :].astype(F32) + mm(mixed[span, :], mix_w_ref[...])
        res[span, :] = residual
        after = norm_forward(residual, gain_ref[0:1, :], bias_ref[0:1, :])
        if turn == 0:
            send_after[...] = after
            from_after = remote_to(send_after, held["after"].at[phase], core)
        else:
            held["after"][phase] = after
    save("mixed", "res")
    from_after.wait_recv()
    save("after")
    from_norms.wait_recv()
    from_up.wait_recv()
    from_down.wait_recv()
    for copy in loads:
        copy.wait()
    for i, (src, dst) in enumerate(((up, up_other), (down, down_other))):
        copy = pltpu.make_async_copy(src.at[1 - phase], dst, store.at[len(stores)])
        copy.start()
        stores.append(copy)
    encoder_rows(
        held["after"].at[0], up.at[0], down.at[0], norms_ref[0, 0:1, :], norms_ref[0, 1:2, :], ckv_w,
        held["hid_e"], held["slope_e"], held["res_e"], held["src"], held["ckv"],
    )
    save("hid_e", "slope_e", "res_e", "src", "ckv")
    middle = cross_rows(
        held["after"].at[1], cols[:, 2:3] == rows[3:4], cq_w, co_w, cgain_ref, cbias_ref,
        held["cq"], held["ckv"], held["cmixed"], held["cres"], ctotals_ref,
    )
    save("cq", "cmixed", "cres")
    decoder_rows(
        scale, middle, up.at[1], down.at[1], norms_ref[1, 0:1, :], norms_ref[1, 1:2, :],
        cols[:, 4:5].astype(jnp.int32), cols[:, 5:6].astype(jnp.int32), cols[:, 6:7], delete_w_ref, place_w,
        held["hid_d"], held["slope_d"], held["res_d"], held["low"], held["grad_low"],
        grad_delete_ref, held["grad_place"],
    )
    save("hid_d", "slope_d", "res_d", "low", "grad_low", "grad_place")
    for copy in label_copies:
        copy.wait_recv()
    small = length // 2
    for at, (p, yy, xx, zz) in enumerate(
        (p, yy, xx, zz) for p in range(2) for yy in range(2) for xx in range(2) for zz in range(4)
    ):
        line = all_labels[zz, yy, xx, p : p + 1, :]
        labels_small_ref[:, at * small : (at + 1) * small] = line[:, :small]
        labels_large_ref[:, at * length : (at + 1) * length] = line
    beyond = jnp.max(all_labels[:, :, :, :, small:].astype(F32).reshape(2 * GROUPS, length - small))
    most_ref[...] = jnp.full(most_ref.shape, beyond, F32)
    for copy in copies:
        copy.wait_send()
    for copy in stores:
        copy.wait()


def token_kernel(
    scale, cap, low_ref, rows_ref, cols_ref, labels_ref, head_any,
    grad_ref, grad_weight_ref,
    weight, weight_t, every, probs, totals, near_in, joined, far_in, shares,
    part, core_in, third_in, second_in, z_in, load, send, recv,
):
    dp, phase = lax.axis_index("dp"), lax.axis_index("phase")
    x, y, z = place_of(dp)
    x_first = phase == 0
    x2, y2 = jnp.where(x_first, 1 - x, x), jnp.where(x_first, y, 1 - y)
    x3, y3 = jnp.where(x_first, x, 1 - x), jnp.where(x_first, 1 - y, y)
    second, third, core = (index_of(x2, y2, z), phase), (index_of(x3, y3, z), phase), (dp, 1 - phase)
    zs = [lax.rem(z + k, 4) for k in (1, 2, 3)]
    along = [(index_of(x, y, k), phase) for k in zs]
    shard, length = weight_t.shape[0], low_ref.shape[0]
    near = [
        (index_of(lax.rem(x + a, 2), lax.rem(y + b, 2), z), lax.rem(phase + c, 2))
        for a in range(2) for b in range(2) for c in range(2) if a + b + c
    ]
    greet(near + along)
    offset = pl.multiple_of((dp * 2 + phase) * shard, shard)
    weight_copy = pltpu.make_async_copy(head_any.at[:, pl.ds(offset, shard)], weight, load.at[0])
    weight_copy.start()
    copies = []

    def remote_to(src, dst, device):
        i = len(copies)
        copy = remote(src, dst, send.at[i], recv.at[i], device)
        copy.start()
        copies.append(copy)
        return copy

    def unit(p, yy, xx):
        return (p * 2 + yy) * 2 + xx

    def block(u, zz):
        return pl.ds(pl.multiple_of((u * 4 + zz) * cap, cap), cap)

    before = lax.broadcasted_iota(jnp.int32, (length, length), 0)
    after = lax.broadcasted_iota(jnp.int32, (length, length), 1)
    rows = rows_ref[...]
    place = mm(rows.astype(BF16), jnp.where(before <= after, 1.0, 0.0).astype(BF16))[7:8]
    slot = lax.broadcasted_iota(jnp.int32, (cap, length), 0).astype(F32)
    chosen = jnp.where((slot == place - 1.0) & (rows[7:8] > 0.0), 1.0, 0.0).astype(BF16)
    own = unit(phase, y, x)
    every[block(own, z), :] = mm(chosen, low_ref[...]).astype(BF16)
    def relay(u, zz, device):
        here = every.at[block(u, zz), :]
        return remote_to(here, here, device)

    firsts = [relay(own, z, device) for device in along]
    cross = [relay(own, z, core)]
    seconds = [relay(own, z, second)]
    thirds = [relay(own, z, third)]
    weight_copy.wait()
    weight_t[...] = weight[...].T
    sources = [lax.rem(z + 4 - k, 4) for k in (1, 2, 3)]
    order = [z] + sources
    for k in range(3):
        firsts[k].wait_recv()
        seconds.append(relay(own, sources[k], second))
        thirds.append(relay(own, sources[k], third))
        cross.append(relay(own, sources[k], core))
    tall = 256
    chunks = 4 * cap // tall

    def look(u):
        def step(j, _):
            span = pl.ds(pl.multiple_of((u * chunks + j) * tall, tall), tall)
            logits = mm_nt(weight_t[...], every[span, :])
            top = jnp.max(logits, axis=0, keepdims=True)
            weights = jnp.exp(logits - top)
            summed = jnp.sum(weights, axis=0, keepdims=True)
            probs[:, span] = (weights * (1.0 / summed)).astype(BF16)
            totals[:, span] = top + jnp.log(summed)
            return 0

        lax.fori_loop(0, chunks, step, 0)

    def arrived(some):
        for copy in some:
            copy.wait_recv()

    look(own)
    for k in range(4):
        seconds[k].wait_recv()
        thirds.append(relay(unit(phase, y2, x2), order[k], third))
        cross.append(relay(unit(phase, y2, x2), order[k], core))
    arrived(cross[0:4])
    look(unit(1 - phase, y, x))
    look(unit(phase, y2, x2))
    for k in range(4):
        thirds[k].wait_recv()
        cross.append(relay(unit(phase, y3, x3), order[k], core))
    arrived(cross[4:8])
    look(unit(1 - phase, y3, x3))
    for k in range(4):
        thirds[4 + k].wait_recv()
        cross.append(relay(unit(phase, 1 - y, 1 - x), order[k], core))
    look(unit(phase, y3, x3))
    arrived(cross[8:12])
    look(unit(1 - phase, y2, x2))
    look(unit(phase, 1 - y, 1 - x))
    arrived(cross[12:16])
    look(unit(1 - phase, 1 - y, 1 - x))

    def join(parts):
        top = parts[0]
        for piece in parts[1:]:
            top = jnp.maximum(top, piece)
        summed = jnp.exp(parts[0] - top)
        for piece in parts[1:]:
            summed = summed + jnp.exp(piece - top)
        return top + jnp.log(summed)

    near_copies = [remote_to(totals, near_in.at[j], device) for j, device in enumerate(near)]
    arrived(near_copies)
    total = join([totals[...]] + [near_in[j] for j in range(7)])
    joined[...] = total
    far_copies = [remote_to(joined, far_in.at[j], device) for j, device in enumerate(along)]
    arrived(far_copies)
    shares[...] = jnp.exp(totals[...] - join([total] + [far_in[j] for j in range(3)]))

    per = tall // cap

    def learn(u):
        def step(j, _):
            span = pl.ds(pl.multiple_of((u * chunks + j) * tall, tall), tall)
            labels = labels_ref[:, span]
            hit = lax.broadcasted_iota(jnp.int32, (shard, tall), 0) == labels - offset
            grads = probs[:, span].astype(F32) * shares[:, span] - jnp.where(hit, 1.0, 0.0)
            grads = (grads * jnp.where(labels >= 0, scale, 0.0)).astype(BF16)
            probs[:, span] = grads
            back = mm(weight[...], grads).astype(BF16)
            for k in range(per):
                part[u, j * per + k] = back[:, k * cap : (k + 1) * cap]
            return 0

        lax.fori_loop(0, chunks, step, 0)

    def add(u, zz, *others):
        value = part[u, zz].astype(F32)
        for other in others:
            value = value + other.astype(F32)
        part[u, zz] = value.astype(BF16)

    mine = [unit(phase, 1 - y, 1 - x), unit(phase, y3, x3), unit(phase, y2, x2), own]
    theirs = [
        unit(1 - phase, 1 - y, 1 - x), unit(1 - phase, y2, x2), unit(1 - phase, y3, x3), unit(1 - phase, y, x)
    ]
    route = zs + [z]
    core_copies, third_copies = [], []

    def to_third(k):
        core_copies[k].wait_recv()
        for j, zz in enumerate(route):
            add(mine[k], zz, core_in[k, zz])
            third_copies.append(remote_to(part.at[mine[k], zz], third_in.at[k, j], third))

    for k in range(4):
        learn(theirs[k])
        core_copies.append(remote_to(part.at[theirs[k]], core_in.at[k], core))
        if 1 <= k <= 2:
            to_third(k - 1)
        learn(mine[k])
    core_copies[2].wait_recv()
    second_copies = []
    for j, zz in enumerate(route):
        third_copies[j].wait_recv()
        add(mine[2], zz, core_in[2, zz], third_in[0, j])
        second_copies.append(remote_to(part.at[mine[2], zz], second_in.at[j], second))

    slab = min(256, shard)

    def weigh(k):
        value = mm(probs[k * slab : (k + 1) * slab, :], every[...])
        grad_weight_ref[:, k * slab : (k + 1) * slab] = value.T

    slabs = shard // slab
    for k in range((slabs + 1) // 2):
        weigh(k)
    core_copies[3].wait_recv()
    z_copies = []
    for j, zz in enumerate(route):
        third_copies[4 + j].wait_recv()
        second_copies[j].wait_recv()
        add(own, zz, core_in[3, zz], third_in[1, j], second_in[j])
        if j < 3:
            z_copies.append(remote_to(part.at[own, zz], z_in.at[j], along[j]))
    for k in range((slabs + 1) // 2, slabs):
        weigh(k)
    arrived(z_copies)
    back = part[own, z].astype(F32)
    for j in range(3):
        back = back + z_in[j].astype(F32)
    place = mm(jnp.where(after <= before, 1.0, 0.0).astype(BF16), cols_ref[...].astype(BF16))[:, 7:8]
    slot = lax.broadcasted_iota(jnp.int32, (length, cap), 1).astype(F32)
    spread = jnp.where((slot == place - 1.0) & (cols_ref[:, 7:8] > 0.0), 1.0, 0.0).astype(BF16)
    grad_ref[...] = mm_nt(spread, back.astype(BF16))
    for copy in copies:
        copy.wait_send()


def token_chips(number, cap, low, rows, cols, labels, head):
    length, width = low.shape
    shard = head.shape[1] // (2 * GROUPS)
    count = 2 * GROUPS * cap
    scale = float(2 * length * GROUPS) ** (-0.5)
    copies = 64
    return pl.pallas_call(
        partial(token_kernel, scale, cap),
        out_shape=(whole((length, width), F32), whole((width, shard), F32)),
        in_specs=in_vmem(4) + [pl.BlockSpec(memory_space=pl.ANY)],
        out_specs=tuple(in_vmem(2)),
        scratch_shapes=[
            VMEM((width, shard), BF16), VMEM((shard, width), BF16), VMEM((count, width), BF16),
            VMEM((shard, count), BF16), VMEM((1, count), F32), VMEM((7, 1, count), F32), VMEM((1, count), F32),
            VMEM((3, 1, count), F32), VMEM((1, count), F32),
            VMEM((8, 4, width, cap), BF16), VMEM((4, 4, width, cap), BF16), VMEM((2, 4, width, cap), BF16),
            VMEM((4, width, cap), BF16), VMEM((3, width, cap), BF16),
            pltpu.SemaphoreType.DMA((1,)), pltpu.SemaphoreType.DMA((copies + 8,)), pltpu.SemaphoreType.DMA((copies + 8,)),
        ],
        compiler_params=pltpu.CompilerParams(
            collective_id=number, has_side_effects=True, vmem_limit_bytes=60 * 1024 * 1024
        ),
        name="token_head",
    )(low, rows, cols, labels, head)


class Exchange:
    def __init__(self, send, recv):
        self.dp, self.phase = lax.axis_index("dp"), lax.axis_index("phase")
        self.x, self.y, self.z = place_of(self.dp)
        x, y, z = self.x, self.y, self.z
        low, high = lax.rem(z, 2), z // 2
        self.own = {"b": high, "a": low, "y": y, "x": x}
        self.partner = {
            "b": index_of(x, y, (1 - high) * 2 + low), "a": index_of(x, y, high * 2 + 1 - low),
            "y": index_of(x, 1 - y, z), "x": index_of(1 - x, y, z),
        }
        self.send, self.recv, self.used, self.copies = send, recv, 0, []

    def greet(self):
        greet([(self.partner[step], self.phase) for step in "bayx"] + [(self.dp, 1 - self.phase)])

    def copy(self, src, dst, device):
        copy = remote(src, dst, self.send.at[self.used], self.recv.at[self.used], device)
        self.used += 1
        copy.start()
        self.copies.append(copy)
        return copy

    def to_core(self, src, dst):
        return self.copy(src, dst, (self.dp, 1 - self.phase))

    def to_core_either(self, first, second):
        i = self.used
        self.used += 1
        made = [remote(*pair, self.send.at[i], self.recv.at[i], (self.dp, 1 - self.phase)) for pair in (first, second)]

        @pl.when(self.phase == 0)
        def _():
            made[0].start()

        @pl.when(self.phase != 0)
        def _():
            made[1].start()

        self.copies.append(made[0])
        return made[0]

    def finish(self):
        for copy in self.copies:
            copy.wait_send()


class Batch:
    def __init__(self, shards, ins, put, own=None):
        self.shards, self.ins, self.put, self.own, self.arriving = shards, ins, put, own, []


class Chunk:
    def __init__(self, exchange, batch, start, size, order):
        self.exchange, self.batch, self.order = exchange, batch, order
        self.rows, self.step, self.fixed = pl.ds(start, size), -1, {}

    def at(self, fixed, free):
        free = list(free)
        return tuple(fixed[name] if name in fixed else free.pop(0) for name in "bayx") + (self.rows,)

    def advance(self):
        batch, ex, rows = self.batch, self.exchange, self.rows
        shards = batch.shards
        if self.step < 0 and batch.own is not None:
            for copy in batch.arriving:
                copy.wait_recv()
            batch.arriving = []
            own = batch.own

            def join(i, _):
                at = (i // 8, lax.rem(i // 4, 2), lax.rem(i // 2, 2), lax.rem(i, 2), rows)
                shards[at] = (shards[at].astype(F32) + own[at].astype(F32)).astype(BF16)
                return 0

            lax.fori_loop(0, GROUPS, join, 0)
        elif self.step >= 0:
            self.arriving.wait_recv()
            name = self.order[self.step]
            self.fixed[name] = ex.own[name]
            free = 3 - self.step
            arrived = batch.ins[self.step]
            if free == 0:
                batch.put(rows, shards[self.at(self.fixed, ())].astype(F32) + arrived[rows].astype(F32))
            else:

                def add(i, _):
                    spot = tuple(lax.rem(i // 2 ** (free - 1 - k), 2) for k in range(free))
                    at = self.at(self.fixed, spot)
                    shards[at] = (shards[at].astype(F32) + arrived[spot + (rows,)].astype(F32)).astype(BF16)
                    return 0

                lax.fori_loop(0, 2**free, add, 0)
        self.step += 1
        if self.step < 4:
            name = self.order[self.step]
            free = (slice(None),) * (3 - self.step)
            src = shards.at[self.at({**self.fixed, name: 1 - ex.own[name]}, free)]
            dst = batch.ins[self.step].at[free + (rows,)]
            self.arriving = ex.copy(src, dst, (ex.partner[name], ex.phase))


PARTS = (
    (
        (0, 32, "abxy"), (32, 16, "axby"), (48, 16, "axby"), (64, 16, "xyab"), (80, 32, "yxab"), (112, 16,
        "xyab"),
    ),
    ((0, 48, "ybxa"), (48, 32, "axby"),),
    ((0, 16, "xbya"), (16, 32, "yxab"), (48, 32, "xyab"), (80, 32, "abyx"), (112, 16, "xyab"),),
    (
        (0, 16, "xyab"), (16, 16, "yxab"), (32, 16, "xyab"), (48, 16, "yxab"), (64, 16, "yxab"), (80, 16,
        "abxy"), (96, 16, "xyab"), (112, 16, "byxa"),
    ),
)
SCHEDULE = (
    (),
    (0, 3, 4),
    (5, 1),
    (),
    (),
    (2, 3),
    (),
    (4, 5, 6),
    (3, 0, 1),
    (5, 4, 2),
    (3, 7, 1),
    (),
    (5, 2, 8),
    (9, 4, 6),
    (0, 10, 1),
    (),
    (2, 8),
    (),
    (12, 0, 11),
    (),
    (9,),
    (),
    (7,),
    (8,),
    (10, 13, 14, 18, 20, 6),
    (
        8, 12, 11, 16, 15, 0, 1, 2, 9, 3, 4, 5, 17, 19, 8, 7, 10, 14, 6, 12, 18, 13, 20, 9, 16, 15, 17, 19, 14, 13,
        20, 7, 12, 10, 16, 15, 6, 17, 11, 9, 14, 13, 20, 18, 19, 7, 12, 10, 16, 11, 15, 14, 17, 18, 13, 19, 20, 16,
        11, 15, 18, 17, 19,
    ),
)
CROSS, CROSS_END, ENCODER, SELF, WEIGHTS, TAIL = 0, 5, 6, 11, 21, 25


BACKWARD = (
    "co_w", "cmixed", "cq", "ckv", "grad_place", "after", "src", "cq_w", "ckv_w", "res_e",
    "res", "mix_w", "qkv", "mixed", "x", "qkv_w",
)


def backward_kernel(
    grad_low_ref, grad_token_ref, rows_ref, cols_ref, norms_ref, cgain_ref, cbias_ref, ctotals_ref, totals_ref,
    res_d_ref, cres_ref, grad_delete_ref, gain_ref,
    up_own, up_other, down_own, down_other, hid_e_any, slope_e_any, hid_d_any, slope_d_any, *rest,
):
    held_any, rest = dict(zip(BACKWARD, rest)), rest[len(BACKWARD) :]
    grad_x_any, red_ff_ref, red_attention_ref, red_cross_ref, vectors_ref = rest[:5]
    held, rest = dict(zip(BACKWARD, rest[5:])), rest[5 + len(BACKWARD) :]
    (
        up, down, hid, slope, grad_d, grad_e, grad_c, grad_a, core_d, core_e, core_c,
        in0_d, in0_e, in0_c, in0_a, in1_d, in1_e, in1_c, in1_a,
        in2_d, in2_e, in2_c, in2_a, in3_d, in3_e, in3_c, in3_a,
        after_grads, after_in, gq_ref, gckv_ref, grad_qkv, sums, grad_x_ref,
        vec_own, vec_core, vec_sums, vec_in, sems, held_sems, send, recv,
    ) = rest
    phase = lax.axis_index("phase")
    ex = Exchange(send, recv)
    ex.greet()

    def moved(name):
        i = BACKWARD.index(name)
        return pltpu.make_async_copy(held_any[name], held[name], held_sems.at[i])

    waited = set()

    def get(name):
        if name not in waited:
            waited.add(name)
            moved(name).wait()
        return held[name]

    width = grad_low_ref.shape[1]
    each = width // GROUPS
    length = grad_low_ref.shape[0]

    def load(own_side, i):
        hidden, slopes = (hid_e_any, slope_e_any) if own_side == 0 else (hid_d_any, slope_d_any)

        @pl.when(phase == own_side)
        def _():
            pltpu.make_async_copy(up_own, up, sems.at[i]).start()
            pltpu.make_async_copy(down_own, down, sems.at[i + 1]).start()

        @pl.when(phase != own_side)
        def _():
            pltpu.make_async_copy(up_other, up, sems.at[i]).start()
            pltpu.make_async_copy(down_other, down, sems.at[i + 1]).start()

        pltpu.make_async_copy(hidden, hid, sems.at[i + 2]).start()
        pltpu.make_async_copy(slopes, slope, sems.at[i + 3]).start()

    def loaded(i):
        for k, (src, dst) in enumerate(
            ((up_own, up), (down_own, down), (hid_e_any, hid), (slope_e_any, slope))
        ):
            pltpu.make_async_copy(src, dst, sems.at[i + k]).wait()

    def puts(ref):
        def put_up(part, value):
            ref[0, :, :, :, :, part * each : (part + 1) * each, :] = value.astype(BF16).reshape(
                2, 2, 2, 2, each, width
            )

        def put_down(part, value):
            ref[1, part // 2, part % 2] = value.astype(BF16).reshape(2, 2, width // 4, width)

        return put_up, put_down

    def put_ff(half):
        def put(rows, value):
            sums[half, rows, :] = value

        return put

    def put_attention(rows, value):
        red_attention_ref[rows, :] = value

    cross_sum = red_cross_ref.at[phase]

    def put_cross_sum(rows, value):
        cross_sum[rows, :] = value

    batch_d = Batch(core_d, (in0_d, in1_d, in2_d, in3_d), put_ff(1), grad_d.at[phase])
    batch_c = Batch(core_c, (in0_c, in1_c, in2_c, in3_c), put_cross_sum, grad_c.at[phase])
    batch_e = Batch(core_e, (in0_e, in1_e, in2_e, in3_e), put_ff(0), grad_e.at[phase])
    batch_a = Batch(grad_a, (in0_a, in1_a, in2_a, in3_a), put_attention)
    chunks = [
        Chunk(ex, batch, *part)
        for batch, parts in zip((batch_d, batch_c, batch_e, batch_a), PARTS) for part in parts
    ]

    def go_on(place):
        for name in SCHEDULE[place]:
            chunks[name].advance()

    def halves_to_core(batch, ref, core_ref, part):
        rows = pl.ds(part * each, each)
        batch.arriving.append(ex.to_core_either(
            (ref.at[1, part // 2, part % 2], core_ref.at[part // 2, part % 2]),
            (ref.at[0, :, :, :, :, rows], core_ref.at[:, :, :, :, rows]),
        ))

    load(1, 0)
    for name in BACKWARD:
        moved(name).start()
    grad_out = grad_low_ref[...] + grad_token_ref[...]
    grad_res, gain_grad, bias_grad = norm_back(res_d_ref[...], norms_ref[1, 0:1, :], grad_out)
    vec_own[2:3, :] = gain_grad
    vec_own[3:4, :] = bias_grad
    vec_own[6:8, :] = grad_delete_ref[0:2, :]
    cres = cres_ref[...]
    middle_low = norm_forward(cres, cgain_ref[...], cbias_ref[...]).astype(BF16)
    loaded(0)
    grad_middle = feed_back(
        grad_res, middle_low, up, down, hid, slope, *puts(grad_d),
        lambda part: halves_to_core(batch_d, grad_d, core_d, part),
    )
    load(0, 4)
    grad_res, gain_grad, bias_grad = norm_back(cres, cgain_ref[...], grad_middle)
    vec_own[4:5, :] = gain_grad
    vec_own[5:6, :] = bias_grad
    branch = grad_res.astype(BF16)

    def put_cross(first, value):
        half_rows = grad_c.shape[5]
        value = value.astype(BF16).reshape(2, 2, 2, 2, each, width)
        for at in range(0, each, 16):
            half, row = divmod(first + at, half_rows)
            grad_c[half, :, :, :, :, row : row + 16, :] = value[:, :, :, :, at : at + 16, :]

    put_cross(3 * each, mm_tn(get("cmixed")[...], branch))
    put_cross(4 * each, get("grad_place")[...])
    grad_mixed = mm_nt(branch, get("co_w")[...]).astype(BF16)
    cq_ref, ckv_ref = get("cq"), get("ckv")

    def put_q(pair, value):
        gq_ref[:, column(pair)] = value

    def put_k(pair, value):
        gckv_ref[:, column(pair)] = value

    def put_v(pair, value):
        gckv_ref[:, column(pair, width)] = value

    go_on(CROSS)

    def between(pair):
        go_on(CROSS + 1 + pair)

    attend_backward(
        lambda pair: cq_ref[:, column(pair)],
        lambda pair: ckv_ref[:, column(pair)],
        lambda pair: ckv_ref[:, column(pair, width)],
        lambda pair: grad_mixed[:, column(pair)],
        cols_ref[:, 2:3] == rows_ref[3:4, :],
        ctotals_ref, put_q, put_k, put_v, between,
    )
    grad_q = gq_ref[...]
    put_cross(0, mm_tn(get("after")[1].astype(BF16), grad_q))
    for part in range(2):
        put_cross((1 + part) * each, mm_tn(get("src")[...], gckv_ref[:, part * width : (part + 1) * width]))
    batch_c.arriving.append(ex.to_core(grad_c.at[1 - phase], core_c))
    after_grads[1] = grad_res + mm_nt(grad_q, get("cq_w")[...])
    go_on(CROSS_END)
    grad_src = mm_nt(gckv_ref[...], get("ckv_w")[...]).astype(BF16).astype(F32)
    grad_res, gain_grad, bias_grad = norm_back(get("res_e")[...], norms_ref[0, 0:1, :], grad_src)
    vec_own[0:1, :] = gain_grad
    vec_own[1:2, :] = bias_grad
    from_v = ex.to_core(vec_own, vec_core)
    loaded(4)

    go_on(ENCODER)

    def between(part):
        halves_to_core(batch_e, grad_e, core_e, part)
        go_on(ENCODER + 1 + part)

    after_grads[0] = feed_back(
        grad_res, get("after")[0].astype(BF16), up, down, hid, slope, *puts(grad_e), between
    )
    from_after = ex.to_core(after_grads.at[1 - phase], after_in)
    res_ref, mix_w_ref, qkv_ref, mixed_ref, x_ref = [get(n) for n in ("res", "mix_w", "qkv", "mixed", "x")]
    first_vectors = []
    for turn in range(2):
        row = phase if turn == 0 else 1 - phase
        rows = pl.ds(pl.multiple_of(row * length, length), length)
        if turn == 0:
            grad_after = after_grads[phase]
        else:
            from_after.wait_recv()
            grad_after = after_in[...]
        grad_res, gain_grad, bias_grad = norm_back(res_ref[rows, :], gain_ref[0:1, :], grad_after)
        first_vectors.append((gain_grad, bias_grad))
        grad_x_ref[rows, :] = grad_res
        branch = grad_res.astype(BF16)
        if turn == 0:
            first_branch, first_rows = branch, rows
        grad_mixed = mm_nt(branch, mix_w_ref[...]).astype(BF16)

        def put(offset):
            def store(pair, value):
                grad_qkv[rows, column(pair, offset)] = value

            return store

        go_on(SELF + 5 * turn)

        def between(pair):
            go_on(SELF + 5 * turn + 1 + pair)

        attend_backward(
            lambda pair: qkv_ref[rows, column(pair)],
            lambda pair: qkv_ref[rows, column(pair, width)],
            lambda pair: qkv_ref[rows, column(pair, 2 * width)],
            lambda pair: grad_mixed[:, column(pair)],
            jnp.where(row == 0, cols_ref[:, 0:1], cols_ref[:, 1:2])
            == jnp.where(row == 0, rows_ref[0:1, :], rows_ref[1:2, :]),
            totals_ref.at[row], put(0), put(width), put(2 * width), between,
        )
    shape = (2, 2, 2, 2, each, width)
    grad_mix = mm_tn(mixed_ref[first_rows, :], first_branch) + mm_tn(mixed_ref[rows, :], branch)
    grad_a[:, :, :, :, 3 * each :, :] = grad_mix.astype(BF16).reshape(shape)
    go_on(WEIGHTS)
    for part in range(3):
        cols = slice(part * width, (part + 1) * width)
        value = mm_tn(x_ref[...], grad_qkv[:, cols])
        grad_a[:, :, :, :, part * each : (part + 1) * each, :] = value.astype(BF16).reshape(shape)
        go_on(WEIGHTS + 1 + part)
    grad_x_ref[...] += mm_nt(grad_qkv[...], get("qkv_w")[...])
    grad_x_copy = pltpu.make_async_copy(grad_x_ref, grad_x_any, held_sems.at[len(BACKWARD)])
    grad_x_copy.start()
    from_v.wait_recv()
    vec_sums[0, 0:8, :] = vec_own[...] + vec_core[...]
    vec_sums[0, 8:9, :] = first_vectors[0][0] + first_vectors[1][0]
    vec_sums[0, 9:10, :] = first_vectors[0][1] + first_vectors[1][1]
    vec_sums[0, 10:16, :] = jnp.zeros((6, width), F32)
    tail = SCHEDULE[TAIL]
    left = [sum(chunks[item].batch is batch for item in tail) for batch in (batch_d, batch_c, batch_e)]
    vector_copies = []

    def vector_step(stage):
        if stage > 0:
            vector_copies[-1].wait_recv()
            vec_sums[stage] = vec_sums[stage - 1] + vec_in[stage - 1]
        if stage < 4:
            step = "xyab"[stage]
            vector_copies.append(ex.copy(vec_sums.at[stage], vec_in.at[stage], (ex.partner[step], phase)))

    vector_step(0)
    after_each = len(tail) // 5
    for at, name in enumerate(tail):
        chunks[name].advance()
        if at % after_each == after_each - 1 and len(vector_copies) < 4:
            vector_step(len(vector_copies))
        for i, batch in enumerate((batch_d, batch_c, batch_e)):
            left[i] -= chunks[name].batch is batch
        if chunks[name].batch is batch_c and left[1] == 0:
            cross_copy = ex.to_core(cross_sum, red_cross_ref.at[phase])
        if chunks[name].batch in (batch_d, batch_e) and left[0] + left[2] == 0:
            ff_copy = ex.to_core(sums.at[1 - phase], red_ff_ref.at[phase])
            red_ff_ref[phase] = sums[phase]
    vector_step(4)
    vectors_ref[...] = vec_sums[4]
    cross_copy.wait_recv()
    ff_copy.wait_recv()
    grad_x_copy.wait()
    ex.finish()


def unpack_kernel(
    ff_any, attention_any, cross_any, vectors_any, own_any, other_any,
    qkv_ref, mix_ref, up_ref, down_any, cq_ref, ckv_ref, co_ref, place_ref,
    gain_ref, bias_ref, cgain_ref, cbias_ref, delete_ref, token_any,
    ff_ref, attention_ref, cross_halves_ref, vectors_ref, halves, sems, token_sems,
):
    phase, dp = lax.axis_index("phase"), lax.axis_index("dp")
    shard, pieces = own_any.shape[1], token_sems.shape[1]
    tall = own_any.shape[0] // pieces
    arrive, leave = [], []
    for i in range(pieces):
        rows = pl.ds(i * tall, tall)
        for side, (src, at) in enumerate(((own_any, phase), (other_any, 1 - phase))):
            arrive.append(pltpu.make_async_copy(src.at[rows], halves.at[side, rows], token_sems.at[side, i]))
            cols = pl.ds(pl.multiple_of(at * shard, shard), shard)
            leave.append(pltpu.make_async_copy(halves.at[side, rows], token_any.at[rows, cols], token_sems.at[side, i]))
    moves = [
        pltpu.make_async_copy(src, dst, sems.at[i])
        for i, (src, dst) in enumerate((
            (vectors_any, vectors_ref), (ff_any, ff_ref), (attention_any, attention_ref), (cross_any, cross_halves_ref),
        ))
    ]
    for move in arrive[:2] + moves + arrive[2:]:
        move.start()
    for i in range(2 * pieces):
        arrive[i].wait()
        leave[i].start()
    for move in moves:
        move.wait()
    down_move = pltpu.make_async_copy(ff_ref.at[1], down_any, sems.at[4])
    down_move.start()
    each = gain_ref.shape[2]
    vectors = vectors_ref[...]
    whole_width = vectors.shape[1]
    vectors = pltpu.roll(vectors, lax.rem(whole_width - dp * each, whole_width), 1)[:, :each]
    gain_ref[0, 0:1, :] = vectors[8:9]
    gain_ref[0, 1:2, :] = jnp.where(phase == 0, vectors[0:1], vectors[2:3])
    bias_ref[0, 0:1, :] = vectors[9:10]
    bias_ref[0, 1:2, :] = jnp.where(phase == 0, vectors[1:2], vectors[3:4])
    cgain_ref[...] = vectors[4:5]
    cbias_ref[...] = vectors[5:6]
    delete_ref[...] = vectors[6:8]
    width = mix_ref.shape[1]
    high = mix_ref.shape[0]
    for block in range(up_ref.shape[1] // width):
        up_ref[:, block * width : (block + 1) * width] = ff_ref[0, block * high : (block + 1) * high, :]
    for block in range(3):
        qkv_ref[:, block * width : (block + 1) * width] = attention_ref[block * high : (block + 1) * high, :]
    mix_ref[...] = attention_ref[3 * high :, :]
    half_rows = cross_halves_ref.shape[1]

    def cross(start):
        half, row = divmod(start, half_rows)
        return cross_halves_ref[half, row : row + 16, :]

    for start in range(0, 5 * high, 16):
        part, inner = start // high, slice(start % high, start % high + 16)
        if part == 0:
            cq_ref[inner, :] = cross(start)
        elif part < 3:
            ckv_ref[inner, (part - 1) * width : part * width] = cross(start)
        elif part == 3:
            co_ref[inner, :] = cross(start)
        else:
            value = cross(start)
            cols = place_ref.shape[1]
            at = start % high
            place_ref[at : at + 16, :] = value[:, :cols]
            place_ref[high + at : high + at + 16, :] = value[:, cols:]
    down_move.wait()
    for move in leave:
        move.wait()


def whole(shape, dtype):
    return jax.ShapeDtypeStruct(shape, dtype)


def in_vmem(count):
    return [pl.BlockSpec(memory_space=VMEM)] * count


def swap(value):
    return lax.ppermute(value, "phase", [(0, 1), (1, 0)])


def unpacked(shards, height, columns):
    groups, rows, width = shards.shape
    blocks = columns // width
    parts = shards.reshape(groups, blocks, rows // blocks, width)
    return parts.transpose(0, 2, 1, 3).reshape(height, columns)


def token_head(cap, block_rows, low, flags, labels_all, flags_all, weight, weight_t, scale):
    length, width = low.shape
    dp = lax.axis_size("dp")
    shard = weight_t.shape[0]

    def choice(flags):
        place = jnp.cumsum(flags, axis=-1) - 1
        places = lax.broadcasted_iota(jnp.int32, flags.shape[:-1] + (cap, flags.shape[-1]), flags.ndim - 1)
        return (places == place[..., None, :]) & (flags[..., None, :] > 0)

    chosen = choice(flags)
    packed = mm(chosen.astype(BF16), low).astype(BF16)
    every = gather_blocks(packed).reshape(2 * dp * cap, width)
    labels = jnp.max(jnp.where(choice(flags_all), labels_all[:, None, :], -1), axis=-1)
    labels = labels.reshape(dp, 2, cap).transpose(1, 0, 2).reshape(2 * dp * cap)
    tall = block_rows
    count = 2 * dp * cap // tall
    probs, totals = pl.pallas_call(
        token_forward,
        grid=(count,),
        out_shape=(whole((count, shard, tall), BF16), whole((count, 1, tall), F32)),
        in_specs=[
            pl.BlockSpec((tall, width), lambda i: (i, 0)),
            pl.BlockSpec((shard, width), lambda i: (0, 0)),
        ],
        out_specs=(
            pl.BlockSpec((1, shard, tall), lambda i: (i, 0, 0)),
            pl.BlockSpec((1, 1, tall), lambda i: (i, 0, 0)),
        ),
        compiler_params=pltpu.CompilerParams(vmem_limit_bytes=48 * 1024 * 1024),
        name="token_forward",
    )(every, weight_t)
    shares = token_shares(totals)
    each = tall // cap
    grad_low, grad_weight = pl.pallas_call(
        partial(token_backward, scale),
        grid=(count,),
        out_shape=(whole((2 * dp, cap, width), BF16), whole((width, shard), F32)),
        in_specs=[
            pl.BlockSpec((1, shard, tall), lambda i: (i, 0, 0)),
            pl.BlockSpec((1, 1, tall), lambda i: (i, 0, 0)),
            pl.BlockSpec((1, 1, tall), lambda i: (i, 0, 0)),
            pl.BlockSpec((tall, width), lambda i: (i, 0)),
            pl.BlockSpec((shard, width), lambda i: (0, 0)),
        ],
        out_specs=(
            pl.BlockSpec((each, cap, width), lambda i: (i, 0, 0)),
            pl.BlockSpec((width, shard), lambda i: (0, 0)),
        ),
        scratch_shapes=[VMEM((shard, width), F32)],
        compiler_params=pltpu.CompilerParams(vmem_limit_bytes=48 * 1024 * 1024),
        name="token_backward",
    )(probs, shares, labels.reshape(count, 1, tall), every, weight_t)
    back = scatter_blocks(grad_low.reshape(2, dp, cap, width))
    return mm_tn(chosen.astype(BF16), back.astype(BF16)), grad_weight


def on_chips(
    inputs, segments, delete_target, place_target, token_target, token_mask,
    attention_in, attention_out, feedforward_in, feedforward_out, norm_gain, norm_bias,
    cross_query, cross_keyvalue, cross_out, cross_gain, cross_bias,
    head_delete, head_place, head_token,
):
    phase, dp_index = lax.axis_index("phase"), lax.axis_index("dp")
    count, length, width = inputs.shape[1:]
    hidden, classes = feedforward_in.shape[2], head_place.shape[1]
    each = width // GROUPS
    scale = float(count * length * GROUPS) ** (-0.5)
    any_space = pl.BlockSpec(memory_space=pl.ANY)
    is_enc = phase == 0
    states = inputs[0].reshape(count * length, width)
    up_own, down_own = feedforward_in[0], feedforward_out[0]
    qkv_w, mix_w = attention_in[0], attention_out[0]
    delete_weight = head_delete.T
    gain_row, bias_row = cross_gain[None, :], cross_bias[None, :]
    shapes = {
        "qkv": ((count * length, 3 * width), BF16), "mixed": ((count * length, width), BF16),
        "res": ((count * length, width), F32), "after": ((2, length, width), F32),
        "res_e": ((length, width), F32), "ckv": ((length, 2 * width), BF16), "cq": ((length, width), BF16),
        "cmixed": ((length, width), BF16), "cres": ((length, width), F32),
        "hid_e": ((length, hidden), BF16), "slope_e": ((length, hidden), BF16),
        "hid_d": ((length, hidden), BF16), "slope_d": ((length, hidden), BF16),
        "res_d": ((length, width), F32), "src": ((length, width), BF16), "low": ((length, width), BF16),
        "grad_low": ((length, width), F32), "grad_place": ((GROUPS, each, 2 * classes), BF16),
        "co_w": ((width, width), BF16), "cq_w": ((width, width), BF16), "ckv_w": ((width, 2 * width), BF16),
        "mix_w": ((width, width), BF16), "qkv_w": ((width, 3 * width), BF16), "x": ((count * length, width), BF16),
    }
    outs = pl.pallas_call(
        partial(forward_kernel, scale),
        out_shape=(
            whole((8, length), F32), whole((length, 128), F32),
            whole((1, GROUPS * length), jnp.int32), whole((1, 2 * GROUPS * length), jnp.int32), whole((1, 1), F32),
            whole((2, 2, width), F32), whole((width, hidden), BF16), whole((hidden, width), BF16),
            whole((count, HEADS, length), F32), whole((HEADS, length), F32), whole((8, width), F32),
            *[whole(*shapes[name]) for name in FORWARD],
        ),
        in_specs=in_vmem(10) + [any_space] * 5 + in_vmem(3) + [any_space],
        out_specs=tuple(in_vmem(6) + [any_space] * 2 + in_vmem(3) + [any_space] * len(FORWARD)),
        scratch_shapes=[
            *[VMEM(*shapes[name]) for name in FORWARD],
            VMEM((2, width, hidden), BF16), VMEM((2, hidden, width), BF16),
            VMEM((width, width), BF16), VMEM((width, 2 * width), BF16), VMEM((width, width), BF16),
            VMEM((2 * width, classes), BF16), VMEM((length, width), F32),
            VMEM((2, length), jnp.int32), VMEM((4, 2, 2, 2, length), jnp.int32), VMEM((128, length), F32),
            pltpu.SemaphoreType.DMA((6,)), pltpu.SemaphoreType.DMA((len(FORWARD) + 2,)),
            pltpu.SemaphoreType.DMA((20,)), pltpu.SemaphoreType.DMA((20,)),
        ],
        compiler_params=pltpu.CompilerParams(
            collective_id=1, has_side_effects=True, vmem_limit_bytes=56 * 1024 * 1024
        ),
        name="forward",
    )(
        states, segments, delete_target, place_target, token_target, token_mask,
        qkv_w, mix_w, norm_gain[0], norm_bias[0], up_own, down_own,
        cross_query, cross_keyvalue, cross_out, gain_row, bias_row, delete_weight, head_place,
    )
    rows, cols, labels_small, labels_large, most, norms, up_other, down_other, totals, ctotals, grad_delete = outs[:11]
    saved = dict(zip(FORWARD, outs[11:]))
    grad_token, grad_weight = lax.cond(
        most[0, 0] < 0.0,
        lambda: token_chips(2, length // 2, saved["low"], rows, cols, labels_small, head_token),
        lambda: token_chips(3, length, saved["low"], rows, cols, labels_large, head_token),
    )
    other_weight = swap(grad_weight)
    saved.update(co_w=cross_out, cq_w=cross_query, ckv_w=cross_keyvalue, mix_w=mix_w, qkv_w=qkv_w, x=states)
    half_rows, ff_half, attention_rows = 5 * each // 2, hidden // GROUPS, 4 * each
    rows_of = (ff_half, ff_half, half_rows, attention_rows)

    def shards(tall, *lead):
        return VMEM(lead + (tall, width), BF16)

    grad_states, red_ff, red_attention, red_cross, vectors = pl.pallas_call(
        backward_kernel,
        out_shape=(
            whole((count * length, width), F32), whole((2, ff_half, width), F32),
            whole((attention_rows, width), F32), whole((2, half_rows, width), F32), whole((16, width), F32),
        ),
        in_specs=in_vmem(13) + [any_space] * (8 + len(BACKWARD)),
        out_specs=tuple([any_space] + in_vmem(4)),
        scratch_shapes=[
            *[VMEM(*shapes[name]) for name in BACKWARD],
            VMEM((width, hidden), BF16), VMEM((hidden, width), BF16),
            VMEM((length, hidden), BF16), VMEM((length, hidden), BF16),
            shards(ff_half, 2, 2, 2, 2, 2), shards(ff_half, 2, 2, 2, 2, 2), shards(half_rows, 2, 2, 2, 2, 2),
            shards(attention_rows, 2, 2, 2, 2),
            shards(ff_half, 2, 2, 2, 2), shards(ff_half, 2, 2, 2, 2), shards(half_rows, 2, 2, 2, 2),
            *[shards(tall, 2, 2, 2) for tall in rows_of],
            *[shards(tall, 2, 2) for tall in rows_of],
            *[shards(tall, 2) for tall in rows_of],
            *[shards(tall) for tall in rows_of],
            VMEM((2, length, width), F32), VMEM((length, width), F32),
            VMEM((length, width), BF16), VMEM((length, 2 * width), BF16), VMEM((count * length, 3 * width), BF16),
            VMEM((2, ff_half, width), F32), VMEM((count * length, width), F32),
            VMEM((8, width), F32), VMEM((8, width), F32),
            VMEM((5, 16, width), F32), VMEM((4, 16, width), F32),
            pltpu.SemaphoreType.DMA((8,)), pltpu.SemaphoreType.DMA((len(BACKWARD) + 1,)),
            pltpu.SemaphoreType.DMA((128,)), pltpu.SemaphoreType.DMA((128,)),
        ],
        compiler_params=pltpu.CompilerParams(
            collective_id=0, has_side_effects=True, vmem_limit_bytes=62 * 1024 * 1024
        ),
        name="backward",
    )(
        saved["grad_low"], grad_token, rows, cols, norms, gain_row, bias_row, ctotals, totals,
        saved["res_d"], saved["cres"], grad_delete, norm_gain[0],
        up_own, up_other, down_own, down_other,
        saved["hid_e"], saved["slope_e"], saved["hid_d"], saved["slope_d"],
        *[saved[name] for name in BACKWARD],
    )
    vocabulary = head_token.shape[1]
    g_qkv, g_mix, g_up, g_down, g_cq, g_ckv, g_co, g_place, g_gain, g_bias, g_cgain, g_cbias, g_delete, g_token = (
        pl.pallas_call(
            unpack_kernel,
            out_shape=(
                whole((each, 3 * width), F32), whole((each, width), F32), whole((each, hidden), F32),
                whole((hidden // GROUPS, width), F32), whole((each, width), F32), whole((each, 2 * width), F32),
                whole((each, width), F32), whole((2 * each, classes), F32),
                whole((1, 2, each), F32), whole((1, 2, each), F32), whole((1, each), F32), whole((1, each), F32),
                whole((2, each), F32), whole((width, vocabulary // GROUPS), F32),
            ),
            in_specs=[any_space] * 6,
            out_specs=tuple(in_vmem(3) + [any_space] + in_vmem(9) + [any_space]),
            scratch_shapes=[
                VMEM(red_ff.shape, F32), VMEM(red_attention.shape, F32), VMEM(red_cross.shape, F32),
                VMEM(vectors.shape, F32), VMEM((2,) + grad_weight.shape, F32),
                pltpu.SemaphoreType.DMA((5,)), pltpu.SemaphoreType.DMA((2, 4)),
            ],
            compiler_params=pltpu.CompilerParams(vmem_limit_bytes=60 * 1024 * 1024),
            name="unpack",
        )(red_ff, red_attention, red_cross, vectors, grad_weight, other_weight)
    )
    return (
        grad_states.reshape(1, count, length, width),
        g_qkv[None], g_mix[None], g_up[None], g_down[None], g_gain, g_bias,
        g_cq, g_ckv, g_co, g_cgain[0], g_cbias[0], g_delete.T, g_place, g_token,
    )


def on_any(
    inputs, segments, delete_target, place_target, token_target, token_mask,
    attention_in, attention_out, feedforward_in, feedforward_out, norm_gain, norm_bias,
    cross_query, cross_keyvalue, cross_out, cross_gain, cross_bias,
    head_delete, head_place, head_token,
):
    phase = lax.axis_index("phase")
    dp_index, dp = lax.axis_index("dp"), lax.axis_size("dp")
    count, length, width = inputs.shape[1:]
    assert count == 2
    hidden = feedforward_in.shape[2]
    scale = float(count * length * dp) ** (-0.5)
    any_space = pl.BlockSpec(memory_space=pl.ANY)
    params = pltpu.CompilerParams(vmem_limit_bytes=56 * 1024 * 1024)

    coded = jnp.where(token_mask == 1, token_target, -1)
    labels_all = lax.all_gather(coded, "dp", tiled=True)
    flags_all = (labels_all >= 0).astype(jnp.int32)

    def row_of(value):
        return lax.dynamic_index_in_dim(value, phase, 0, keepdims=False)

    own_norms = jnp.stack([norm_gain[0, 1], norm_bias[0, 1]])
    up_other, down_other = swap(feedforward_in[0]), swap(feedforward_out[0])
    other_norms = swap(own_norms)
    is_enc = phase == 0
    norms = jnp.concatenate(
        [jnp.where(is_enc, own_norms, other_norms), jnp.where(is_enc, other_norms, own_norms)]
    )
    ids = row_of(segments)
    own_ids = lax.dynamic_index_in_dim(segments, phase, 1, keepdims=False)
    states = inputs[0].reshape(count * length, width)

    qkv, mixed, res, totals, keep, send = pl.pallas_call(
        self_forward,
        out_shape=(
            whole((count * length, 3 * width), BF16),
            whole((count * length, width), BF16),
            whole((count * length, width), F32),
            whole((count, HEADS, length), F32),
            whole((length, width), F32),
            whole((length, width), F32),
        ),
        in_specs=in_vmem(7),
        out_specs=tuple(in_vmem(6)),
        compiler_params=params,
        name="self_forward",
    )(states, own_ids[:, :, None], own_ids[:, None, :], attention_in[0], attention_out[0], norm_gain[0], norm_bias[0])
    received = swap(send)

    ids_e, ids_d_row = ids[0][:, None], ids[1][None, :]
    pair_valid = jnp.concatenate([ids[1, :-1] == ids[1, 1:], jnp.zeros((1,), bool)])
    targets = jnp.stack(
        [row_of(delete_target), row_of(place_target), pair_valid.astype(jnp.int32)], axis=1
    )
    delete_weight = head_delete.T
    gain_row, bias_row = cross_gain[None, :], cross_bias[None, :]
    ff_scratch = [
        VMEM((width, hidden), BF16), VMEM((hidden, width), BF16),
        VMEM((width, hidden), BF16), VMEM((hidden, width), BF16),
    ]
    saved_shapes = (
        whole((length, width), F32),
        whole((length, width), F32),
        whole((length, width), F32),
        whole((length, 2 * width), BF16),
        whole((length, width), BF16),
        whole((length, width), BF16),
        whole((length, width), F32),
        whole((HEADS, length), F32),
        whole((length, hidden), BF16), whole((length, hidden), BF16),
        whole((length, hidden), BF16), whole((length, hidden), BF16),
        whole((length, width), F32),
        whole((length, width), BF16),
    )
    classes = head_place.shape[1]
    each = width // GROUPS
    outs = pl.pallas_call(
        partial(rows_forward, scale),
        out_shape=saved_shapes + (
            whole((length, width), BF16),
            whole((length, width), F32),
            whole((8, width), F32),
            whole((GROUPS, each, 2 * classes), BF16),
        ),
        in_specs=in_vmem(5) + [any_space] * 4 + in_vmem(8),
        out_specs=tuple(in_vmem(18)),
        scratch_shapes=ff_scratch + [pltpu.SemaphoreType.DMA((2, 2))],
        compiler_params=params,
        name="rows_forward",
    )(
        keep, received, ids_e, ids_d_row, targets,
        feedforward_in[0], up_other, feedforward_out[0], down_other, norms,
        cross_query, cross_keyvalue, cross_out, gain_row, bias_row, delete_weight, head_place,
    )
    saved = outs[:14]
    low, grad_low, grad_delete, grad_place = outs[14:]

    shard = head_token.shape[1] // (2 * dp)
    weight = lax.dynamic_slice_in_dim(head_token, (dp_index * 2 + phase) * shard, shard, 1)
    weight_t = weight.T
    flags = row_of(token_mask)

    def run_head(cap, block_rows):
        return token_head(cap, block_rows, low, flags, labels_all, flags_all, weight, weight_t, scale)

    small = length // 2
    fits = jnp.max(jnp.sum(flags_all, axis=1)) <= small
    grad_token, grad_weight = lax.cond(
        fits, lambda: run_head(small, 4 * small), lambda: run_head(length, 2 * length)
    )
    other_weight = swap(grad_weight)
    grad_head_token = jnp.concatenate(
        [jnp.where(is_enc, grad_weight, other_weight), jnp.where(is_enc, other_weight, grad_weight)], axis=1
    )

    each = width // GROUPS
    ff_rows = 2 * hidden // GROUPS
    keep, send, ff_own, ff_other, cross_shards, vectors = pl.pallas_call(
        rows_backward,
        out_shape=(
            whole((length, width), F32), whole((length, width), F32),
            whole((GROUPS, ff_rows, width), BF16), whole((GROUPS, ff_rows, width), BF16),
            whole((GROUPS, 5 * each, width), BF16), whole((8, width), F32),
        ),
        in_specs=in_vmem(4) + [any_space] * 4 + in_vmem(6 + 14 + 1),
        out_specs=(in_vmem(2) + [any_space] * 2 + in_vmem(2)),
        scratch_shapes=ff_scratch + [
            VMEM((GROUPS, ff_rows, width), BF16), VMEM((GROUPS, ff_rows, width), BF16),
            VMEM((length, width), F32), VMEM((length, width), F32),
            VMEM((length, width), BF16), VMEM((length, 2 * width), BF16),
            pltpu.SemaphoreType.DMA((2, 2)), pltpu.SemaphoreType.DMA((2,)),
        ],
        compiler_params=params,
        name="rows_backward",
    )(
        grad_low, grad_token, ids_e, ids_d_row,
        feedforward_in[0], up_other, feedforward_out[0], down_other, norms,
        cross_query, cross_keyvalue, cross_out, gain_row, bias_row, *saved, grad_place,
    )
    received = swap(send)
    ff_received = swap(ff_other)
    half_rows = 5 * each // 2
    cross_keep = lax.dynamic_slice_in_dim(cross_shards, phase * half_rows, half_rows, 1)
    cross_received = swap(lax.dynamic_slice_in_dim(cross_shards, (1 - phase) * half_rows, half_rows, 1))
    shared = jnp.concatenate([vectors[4:6], grad_delete[:2]])
    norm_own = jnp.where(is_enc, vectors[0:2], vectors[2:4])
    norm_other = jnp.where(is_enc, vectors[2:4], vectors[0:2])
    vector_received = swap(jnp.concatenate([norm_other, shared]))
    vector_sums = jnp.concatenate([norm_own, shared]) + vector_received

    grad_states, attention_shards, first_vectors = pl.pallas_call(
        self_backward,
        out_shape=(
            whole((count * length, width), F32), whole((GROUPS, 4 * each, width), BF16), whole((8, width), F32),
        ),
        in_specs=in_vmem(12),
        out_specs=tuple(in_vmem(3)),
        scratch_shapes=[VMEM((count * length, width), F32), VMEM((count * length, 3 * width), BF16)],
        compiler_params=params,
        name="self_backward",
    )(
        keep, received, states, own_ids[:, :, None], own_ids[:, None, :], attention_in[0], attention_out[0],
        norm_gain[0], qkv, mixed, res, totals,
    )

    all_vectors = jnp.stack([
        first_vectors[0], vector_sums[0], first_vectors[1], vector_sums[1],
        vector_sums[2], vector_sums[3], vector_sums[4], vector_sums[5],
    ])
    ff_sum = (ff_own.astype(F32) + ff_received.astype(F32)).astype(BF16)
    cross_sum = (cross_keep.astype(F32) + cross_received.astype(F32)).astype(BF16)
    cross_other = swap(cross_sum)
    cross_all = jnp.concatenate(
        [jnp.where(is_enc, cross_sum, cross_other), jnp.where(is_enc, cross_other, cross_sum)], axis=1
    )
    ff_up = hidden // width * each

    def spread(value):
        return lax.psum_scatter(value.astype(F32), "dp", scatter_dimension=0, tiled=True)

    g_qkv = spread(unpacked(attention_shards[:, : 3 * each], width, 3 * width))
    g_mix = spread(unpacked(attention_shards[:, 3 * each :], width, width))
    g_up = spread(unpacked(ff_sum[:, :ff_up], width, hidden))
    g_down = spread(unpacked(ff_sum[:, ff_up:], hidden, width))
    g_cq = spread(unpacked(cross_all[:, :each], width, width))
    g_ckv = spread(unpacked(cross_all[:, each : 3 * each], width, 2 * width))
    g_co = spread(unpacked(cross_all[:, 3 * each : 4 * each], width, width))
    place = cross_all[:, 4 * each :].reshape(GROUPS, each, 2, classes)
    g_place = spread(place.transpose(0, 2, 1, 3).reshape(2 * width, classes))
    vector_out = lax.psum_scatter(all_vectors, "dp", scatter_dimension=1, tiled=True)
    return (
        grad_states.reshape(1, count, length, width),
        g_qkv[None], g_mix[None], g_up[None], g_down[None],
        vector_out[None, 0:2], vector_out[None, 2:4],
        g_cq, g_ckv, g_co, vector_out[4], vector_out[5], vector_out[6:8].T, g_place, grad_head_token,
    )


def on_device(*args):
    chips = lax.axis_size("dp") == GROUPS and args[0].shape[1] == 2
    return on_chips(*args) if chips else on_any(*args)


def solution(mesh):
    layer, row = P("phase", None, None), P("dp", None)
    return jax.shard_map(
        on_device,
        mesh=mesh,
        in_specs=(P("phase", "dp", None, None), P("dp", None, None), row, row, row, row)
        + (layer,) * 6 + (P(),) * 8,
        out_specs=(P("phase", "dp", None, None),) + (P("phase", "dp", None),) * 4
        + (P("phase", None, "dp"),) * 2 + (row,) * 3 + (P("dp"),) * 2 + (row,) * 2 + (P(None, "dp"),),
        check_vma=False,
    )
```

```python
from functools import partial

import jax
import jax.numpy as jnp
from jax import lax
from jax.experimental import pallas as pl
from jax.experimental.pallas import tpu as pltpu
from jax.sharding import PartitionSpec as P

HEADS = 8
HEAD = 64
PAIR = 2 * HEAD
MASKED_SCORE = -1e30
NORM_EPSILON = 1e-05
GROUPS = 16
F32 = jnp.float32
BF16 = jnp.bfloat16
MESH = pl.DeviceIdType.MESH
VMEM = pltpu.VMEM
GELU_C = 0.7978845608028654
GELU_A = 0.044715


def mm(left, right):
    return jnp.dot(left, right, preferred_element_type=F32)


def mm_nt(left, right):
    return lax.dot_general(left, right, (((1,), (1,)), ((), ())), preferred_element_type=F32)


def mm_tn(left, right):
    return lax.dot_general(left, right, (((0,), (0,)), ((), ())), preferred_element_type=F32)


def norm_forward(residual, gain, bias):
    centered = residual - jnp.mean(residual, axis=-1, keepdims=True)
    variance = jnp.mean(centered * centered, axis=-1, keepdims=True)
    return centered * lax.rsqrt(variance + NORM_EPSILON) * gain + bias


def norm_back(residual, gain, grad_out):
    centered = residual - jnp.mean(residual, axis=-1, keepdims=True)
    variance = jnp.mean(centered * centered, axis=-1, keepdims=True)
    scale = lax.rsqrt(variance + NORM_EPSILON)
    unit = centered * scale
    grad_unit = grad_out * gain
    grad_gain = jnp.sum(grad_out * unit, axis=0, keepdims=True)
    grad_bias = jnp.sum(grad_out, axis=0, keepdims=True)
    grad_res = scale * (
        grad_unit
        - jnp.mean(grad_unit, axis=-1, keepdims=True)
        - unit * jnp.mean(grad_unit * unit, axis=-1, keepdims=True)
    )
    return grad_res, grad_gain, grad_bias


def gelu_both(pre):
    square = pre * pre
    bent = jnp.tanh(GELU_C * pre * (1.0 + GELU_A * square))
    half = 0.5 * (1.0 + bent)
    slope = half + (0.5 * GELU_C) * pre * (1.0 - bent * bent) * (1.0 + 3.0 * GELU_A * square)
    return pre * half, slope


def attend_forward(queries, keys, values, allowed, out_ref, totals_ref, rows):
    lane = lax.broadcasted_iota(jnp.int32, (1, PAIR), 1)
    for pair in range(HEADS // 2):
        q, k, v = queries(pair), keys(pair), values(pair)
        mixed = None
        for side in range(2):
            own = (lane < HEAD) if side == 0 else (lane >= HEAD)
            scores = mm_nt(k, jnp.where(own, q * HEAD ** (-0.5), 0))
            scores = jnp.where(allowed, scores, MASKED_SCORE)
            top = jnp.max(scores, axis=0, keepdims=True)
            weights = jnp.exp(scores - top)
            summed = jnp.sum(weights, axis=0, keepdims=True)
            probs = (weights * (1.0 / summed)).astype(BF16)
            totals_ref[2 * pair + side : 2 * pair + side + 1, :] = top + jnp.log(summed)
            part = mm_tn(probs, jnp.where(own, v, 0))
            mixed = part if mixed is None else mixed + part
        out_ref[rows, pair * PAIR : (pair + 1) * PAIR] = mixed.astype(BF16)


def attend_backward(
    queries, keys, values, grads, allowed, totals_ref, put_q, put_k, put_v, between=None
):
    lane = lax.broadcasted_iota(jnp.int32, (1, PAIR), 1)
    for pair in range(HEADS // 2):
        q, k, v, da = queries(pair), keys(pair), values(pair), grads(pair)
        grad_q = grad_k = grad_v = None
        for side in range(2):
            own = (lane < HEAD) if side == 0 else (lane >= HEAD)
            q_own = jnp.where(own, q * HEAD ** (-0.5), 0)
            da_own = jnp.where(own, da, 0)
            scores = jnp.where(allowed, mm_nt(k, q_own), MASKED_SCORE)
            probs = jnp.exp(scores - totals_ref[2 * pair + side : 2 * pair + side + 1, :])
            grad_probs = mm_nt(v, da_own)
            part_v = mm(probs.astype(BF16), da_own)
            shared = jnp.sum(probs * grad_probs, axis=0, keepdims=True)
            grad_scores = (probs * (grad_probs - shared)).astype(BF16)
            part_k = mm(grad_scores, q_own)
            part_q = mm_tn(grad_scores, jnp.where(own, k, 0))
            grad_q = part_q if grad_q is None else grad_q + part_q
            grad_k = part_k if grad_k is None else grad_k + part_k
            grad_v = part_v if grad_v is None else grad_v + part_v
        put_q(pair, (grad_q * HEAD ** (-0.5)).astype(BF16))
        put_k(pair, grad_k.astype(BF16))
        put_v(pair, grad_v.astype(BF16))
        if between is not None:
            between(pair)


def column(pair, offset=0):
    return slice(offset + pair * PAIR, offset + (pair + 1) * PAIR)


def put_shards(ref, first, grad):
    height = grad.shape[0] // GROUPS
    width = ref.shape[2]
    for block in range(grad.shape[1] // width):
        piece = grad[:, block * width : (block + 1) * width].astype(BF16)
        ref[:, first + block * height : first + (block + 1) * height, :] = piece.reshape(
            GROUPS, height, width
        )


def self_forward(
    x_ref, ids_ref, ids_row_ref, qkv_w_ref, mix_w_ref, gain_ref, bias_ref,
    qkv_ref, mixed_ref, res_ref, totals_ref, keep_ref, send_ref,
):
    phase = lax.axis_index("phase")
    count, length = ids_ref.shape[0], ids_ref.shape[1]
    width = x_ref.shape[1]
    for part in range(3):
        cols = slice(part * width, (part + 1) * width)
        qkv_ref[:, cols] = mm(x_ref[...], qkv_w_ref[:, cols]).astype(BF16)
    for row in range(count):
        rows = slice(row * length, (row + 1) * length)
        attend_forward(
            lambda pair: qkv_ref[rows, column(pair)],
            lambda pair: qkv_ref[rows, column(pair, width)],
            lambda pair: qkv_ref[rows, column(pair, 2 * width)],
            ids_ref[row] == ids_row_ref[row],
            mixed_ref, totals_ref.at[row], rows,
        )
    for row in range(count):
        rows = slice(row * length, (row + 1) * length)
        residual = x_ref[rows, :].astype(F32) + mm(mixed_ref[rows, :], mix_w_ref[...])
        res_ref[rows, :] = residual
        after = norm_forward(residual, gain_ref[0:1, :], bias_ref[0:1, :])

        @pl.when(phase == row)
        def _():
            keep_ref[...] = after

        @pl.when(phase != row)
        def _():
            send_ref[...] = after


def load_sided(phase, own_refs, other_refs, enc_refs, dec_refs, sems):
    for i, (own, other, enc, dec) in enumerate(zip(own_refs, other_refs, enc_refs, dec_refs)):
        @pl.when(phase == 0)
        def _():
            pltpu.make_async_copy(own, enc, sems.at[0, i]).start()
            pltpu.make_async_copy(other, dec, sems.at[1, i]).start()

        @pl.when(phase != 0)
        def _():
            pltpu.make_async_copy(other, enc, sems.at[0, i]).start()
            pltpu.make_async_copy(own, dec, sems.at[1, i]).start()

    def wait_enc(i):
        pltpu.make_async_copy(own_refs[i], enc_refs[i], sems.at[0, i]).wait()

    def wait_dec(i):
        pltpu.make_async_copy(own_refs[i], dec_refs[i], sems.at[1, i]).wait()

    return wait_enc, wait_dec


def feed_forward(middle, up_ref, down_ref, hidden_ref, slope_ref):
    width = middle.shape[1]
    low = middle.astype(BF16)
    total = middle
    for part in range(up_ref.shape[1] // width):
        cols = slice(part * width, (part + 1) * width)
        hidden, slope = gelu_both(mm(low, up_ref[:, cols]))
        hidden = hidden.astype(BF16)
        hidden_ref[:, cols] = hidden
        slope_ref[:, cols] = slope.astype(BF16)
        total = total + mm(hidden, down_ref[cols, :])
    return total


def feed_back(grad_res, middle_low, up_ref, down_ref, hidden_ref, slope_ref, put_up, put_down, between=None):
    width = grad_res.shape[1]
    branch = grad_res.astype(BF16)
    total = grad_res
    for part in range(up_ref.shape[1] // width):
        cols = slice(part * width, (part + 1) * width)
        put_down(part, mm_tn(hidden_ref[:, cols], branch))
        grad_hidden = mm_nt(branch, down_ref[cols, :])
        grad_pre = (grad_hidden * slope_ref[:, cols].astype(F32)).astype(BF16)
        put_up(part, mm_tn(middle_low, grad_pre))
        total = total + mm_nt(grad_pre, up_ref[:, cols])
        if between is not None:
            between(part)
    return total


def feed_puts(ref, parts):
    width = ref.shape[2]
    rows = width // GROUPS
    per, tall = GROUPS // parts, parts * rows

    def put_up(part, value):
        put_shards(ref, part * rows, value)

    def put_down(part, value):
        ref[part * per : (part + 1) * per, tall : 2 * tall, :] = value.astype(BF16).reshape(
            per, tall, width
        )

    return put_up, put_down


def class_grads(logits, labels, row_weight, valid):
    lane = lax.broadcasted_iota(jnp.int32, logits.shape, 1)
    logits = jnp.where(lane < valid, logits, -jnp.inf) if valid < logits.shape[1] else logits
    top = jnp.max(logits, axis=-1, keepdims=True)
    weights = jnp.exp(logits - top)
    probs = weights * (1.0 / jnp.sum(weights, axis=-1, keepdims=True))
    return (probs - (lane == labels).astype(F32)) * row_weight


def rows_forward(
    scale, keep_ref, recv_ref, ids_e_ref, ids_d_row_ref, targets_ref,
    up_own, up_other, down_own, down_other, norms_ref,
    cq_w_ref, ckv_w_ref, co_w_ref, cgain_ref, cbias_ref, delete_w_ref, place_w_ref,
    after_e_ref, res_e_ref, after_d_ref, ckv_ref, cq_ref, cmixed_ref, cres_ref, ctotals_ref,
    hid_e_ref, slope_e_ref, hid_d_ref, slope_d_ref, res_d_ref, src_ref,
    low_ref, grad_ref, grad_delete_ref, grad_place_ref,
    up_e, down_e, up_d, down_d, sems,
):
    phase = lax.axis_index("phase")
    width = keep_ref.shape[1]
    wait_enc, wait_dec = load_sided(
        phase, (up_own, down_own), (up_other, down_other), (up_e, down_e), (up_d, down_d), sems
    )

    @pl.when(phase == 0)
    def _():
        after_e_ref[...] = keep_ref[...]
        after_d_ref[...] = recv_ref[...]

    @pl.when(phase != 0)
    def _():
        after_e_ref[...] = recv_ref[...]
        after_d_ref[...] = keep_ref[...]

    wait_enc(0)
    wait_enc(1)
    encoder_rows(
        after_e_ref, up_e, down_e, norms_ref[0:1, :], norms_ref[1:2, :], ckv_w_ref,
        hid_e_ref, slope_e_ref, res_e_ref, src_ref, ckv_ref,
    )
    middle = cross_rows(
        after_d_ref, ids_e_ref[...] == ids_d_row_ref[...], cq_w_ref, co_w_ref, cgain_ref, cbias_ref,
        cq_ref, ckv_ref, cmixed_ref, cres_ref, ctotals_ref,
    )
    wait_dec(0)
    wait_dec(1)
    targets = targets_ref[...]
    decoder_rows(
        scale, middle, up_d, down_d, norms_ref[2:3, :], norms_ref[3:4, :],
        targets[:, 0:1], targets[:, 1:2], targets[:, 2:3], delete_w_ref, place_w_ref,
        hid_d_ref, slope_d_ref, res_d_ref, low_ref, grad_ref, grad_delete_ref, grad_place_ref,
    )


def encoder_rows(
    after_ref, up, down, gain, bias, ckv_w_ref, hid_ref, slope_ref, res_ref, src_ref, ckv_ref
):
    residual = feed_forward(after_ref[...], up, down, hid_ref, slope_ref)
    res_ref[...] = residual
    src = norm_forward(residual, gain, bias).astype(BF16)
    src_ref[...] = src
    width = src.shape[1]
    for part in range(2):
        cols = slice(part * width, (part + 1) * width)
        ckv_ref[:, cols] = mm(src, ckv_w_ref[:, cols]).astype(BF16)


def cross_rows(
    after_ref, allowed, cq_w_ref, co_w_ref, cgain_ref, cbias_ref, cq_ref, ckv_ref, cmixed_ref, cres_ref, ctotals_ref
):
    width = after_ref.shape[1]
    cq_ref[...] = mm(after_ref[...].astype(BF16), cq_w_ref[...]).astype(BF16)
    attend_forward(
        lambda pair: cq_ref[:, column(pair)],
        lambda pair: ckv_ref[:, column(pair)],
        lambda pair: ckv_ref[:, column(pair, width)],
        allowed, cmixed_ref, ctotals_ref, slice(None),
    )
    residual = after_ref[...] + mm(cmixed_ref[...], co_w_ref[...])
    cres_ref[...] = residual
    return norm_forward(residual, cgain_ref[...], cbias_ref[...])


def decoder_rows(
    scale, middle, up, down, gain, bias, delete_label, place_label, pair_valid, delete_w_ref, place_w_ref,
    hid_ref, slope_ref, res_ref, low_ref, grad_ref, grad_delete_ref, grad_place_ref,
):
    residual = feed_forward(middle, up, down, hid_ref, slope_ref)
    res_ref[...] = residual
    low = norm_forward(residual, gain, bias).astype(BF16)
    low_ref[...] = low
    length, width = low.shape
    valid = delete_w_ref.shape[0]
    weight = jnp.concatenate([delete_w_ref[...], jnp.zeros((128 - valid, width), BF16)], axis=0)
    grads = class_grads(mm_nt(low, weight), delete_label, scale, valid).astype(BF16)
    grad_delete_ref[...] = mm_tn(grads, low)[:8]
    grad_low = mm(grads, weight)
    logits = mm(low, place_w_ref[:width, :]) + pltpu.roll(
        mm(low, place_w_ref[width:, :]), length - 1, 0
    )
    weight = pair_valid.astype(F32) * scale
    grads = class_grads(logits, place_label, weight, logits.shape[1])
    later = pltpu.roll(grads, 1, 0).astype(BF16)
    grads = grads.astype(BF16)
    classes = grads.shape[1]
    for top, part in enumerate((grads, later)):
        part = mm_tn(low, part).astype(BF16).reshape(GROUPS // 2, 2, width // GROUPS, classes)
        at = slice(top * GROUPS // 2, (top + 1) * GROUPS // 2)
        for half in range(2):
            grad_place_ref[at, :, half * classes : (half + 1) * classes] = part[:, half]
    grad_low = grad_low + mm_nt(grads, place_w_ref[:width, :]) + mm_nt(later, place_w_ref[width:, :])
    grad_ref[...] = grad_low


def rows_backward(
    grad_low_ref, grad_token_ref, ids_e_ref, ids_d_row_ref,
    up_own, up_other, down_own, down_other, norms_ref,
    cq_w_ref, ckv_w_ref, co_w_ref, cgain_ref, cbias_ref,
    after_e_ref, res_e_ref, after_d_ref, ckv_ref, cq_ref, cmixed_ref, cres_ref, ctotals_ref,
    hid_e_ref, slope_e_ref, hid_d_ref, slope_d_ref, res_d_ref, src_ref, grad_place_ref,
    keep_ref, send_ref, own_ref, other_ref, cross_ref, vectors_ref,
    up_e, down_e, up_d, down_d, grad_e, grad_d, after_e_grad, after_d_grad, gq_ref, gckv_ref, sems, out_sems,
):
    phase = lax.axis_index("phase")
    width = grad_low_ref.shape[1]
    wait_enc, wait_dec = load_sided(
        phase, (up_own, down_own), (up_other, down_other), (up_e, down_e), (up_d, down_d), sems
    )
    grad_out = grad_low_ref[...] + grad_token_ref[...]
    grad_res, gain_grad, bias_grad = norm_back(res_d_ref[...], norms_ref[2:3, :], grad_out)
    vectors_ref[2:3, :] = gain_grad
    vectors_ref[3:4, :] = bias_grad
    cres = cres_ref[...]
    middle_low = norm_forward(cres, cgain_ref[...], cbias_ref[...]).astype(BF16)
    wait_dec(0)
    wait_dec(1)
    grad_middle = feed_back(grad_res, middle_low, up_d, down_d, hid_d_ref, slope_d_ref, *feed_puts(grad_d, 4))
    move_d = [
        pltpu.make_async_copy(grad_d, own_ref, out_sems.at[0]),
        pltpu.make_async_copy(grad_d, other_ref, out_sems.at[0]),
    ]

    @pl.when(phase == 0)
    def _():
        move_d[1].start()

    @pl.when(phase != 0)
    def _():
        move_d[0].start()

    grad_res, gain_grad, bias_grad = norm_back(cres, cgain_ref[...], grad_middle)
    vectors_ref[4:5, :] = gain_grad
    vectors_ref[5:6, :] = bias_grad
    branch = grad_res.astype(BF16)
    after_low = after_d_ref[...].astype(BF16)
    rows = width // GROUPS
    put_shards(cross_ref, 3 * rows, mm_tn(cmixed_ref[...], branch))
    grad_mixed = mm_nt(branch, co_w_ref[...]).astype(BF16)

    def put_q(pair, value):
        gq_ref[:, column(pair)] = value

    def put_k(pair, value):
        gckv_ref[:, column(pair)] = value

    def put_v(pair, value):
        gckv_ref[:, column(pair, width)] = value

    attend_backward(
        lambda pair: cq_ref[:, column(pair)],
        lambda pair: ckv_ref[:, column(pair)],
        lambda pair: ckv_ref[:, column(pair, width)],
        lambda pair: grad_mixed[:, column(pair)],
        ids_e_ref[...] == ids_d_row_ref[...],
        ctotals_ref, put_q, put_k, put_v,
    )
    grad_q = gq_ref[...]
    grad_kv = gckv_ref[...]
    put_shards(cross_ref, 0, mm_tn(after_low, grad_q))
    put_shards(cross_ref, rows, mm_tn(src_ref[...], grad_kv))
    cross_ref[:, 4 * rows : 5 * rows, :] = grad_place_ref[...]
    after_d_grad[...] = grad_res + mm_nt(grad_q, cq_w_ref[...])
    grad_src = mm_nt(grad_kv, ckv_w_ref[...]).astype(BF16).astype(F32)
    grad_res, gain_grad, bias_grad = norm_back(res_e_ref[...], norms_ref[0:1, :], grad_src)
    vectors_ref[0:1, :] = gain_grad
    vectors_ref[1:2, :] = bias_grad
    vectors_ref[6:8, :] = jnp.zeros((2, width), F32)
    wait_enc(0)
    wait_enc(1)
    after_e_grad[...] = feed_back(
        grad_res, after_e_ref[...].astype(BF16), up_e, down_e, hid_e_ref, slope_e_ref,
        *feed_puts(grad_e, 4),
    )
    move_e = [
        pltpu.make_async_copy(grad_e, own_ref, out_sems.at[1]),
        pltpu.make_async_copy(grad_e, other_ref, out_sems.at[1]),
    ]

    @pl.when(phase == 0)
    def _():
        move_e[0].start()
        keep_ref[...] = after_e_grad[...]
        send_ref[...] = after_d_grad[...]

    @pl.when(phase != 0)
    def _():
        move_e[1].start()
        keep_ref[...] = after_d_grad[...]
        send_ref[...] = after_e_grad[...]

    move_d[0].wait()
    move_e[0].wait()


def self_backward(
    keep_ref, recv_ref, x_ref, ids_ref, ids_row_ref, qkv_w_ref, mix_w_ref, gain_ref,
    qkv_ref, mixed_ref, res_ref, totals_ref,
    grad_x_ref, shards_ref, vectors_ref,
    after_grad, grad_qkv,
):
    phase = lax.axis_index("phase")
    count, length = ids_ref.shape[0], ids_ref.shape[1]
    width = x_ref.shape[1]
    for row in range(count):
        rows = slice(row * length, (row + 1) * length)

        @pl.when(phase == row)
        def _():
            after_grad[rows, :] = keep_ref[...]

        @pl.when(phase != row)
        def _():
            after_grad[rows, :] = recv_ref[...]

    grad_res, gain_grad, bias_grad = norm_back(res_ref[...], gain_ref[0:1, :], after_grad[...])
    vectors_ref[0:1, :] = gain_grad
    vectors_ref[1:2, :] = bias_grad
    vectors_ref[2:8, :] = jnp.zeros((6, width), F32)
    grad_x_ref[...] = grad_res
    branch = grad_res.astype(BF16)
    rows_each = width // GROUPS
    put_shards(shards_ref, 3 * rows_each, mm_tn(mixed_ref[...], branch))
    grad_mixed = mm_nt(branch, mix_w_ref[...]).astype(BF16)
    for row in range(count):
        rows = slice(row * length, (row + 1) * length)

        def put(offset):
            def store(pair, value):
                grad_qkv[rows, column(pair, offset)] = value

            return store

        attend_backward(
            lambda pair: qkv_ref[rows, column(pair)],
            lambda pair: qkv_ref[rows, column(pair, width)],
            lambda pair: qkv_ref[rows, column(pair, 2 * width)],
            lambda pair: grad_mixed[rows, column(pair)],
            ids_ref[row] == ids_row_ref[row],
            totals_ref.at[row], put(0), put(width), put(2 * width),
        )
    for part in range(3):
        cols = slice(part * width, (part + 1) * width)
        put_shards(shards_ref, part * rows_each, mm_tn(x_ref[...], grad_qkv[:, cols]))
    grad_x_ref[...] += mm_nt(grad_qkv[...], qkv_w_ref[...])


def token_forward(low_ref, weight_ref, probs_ref, totals_ref):
    logits = mm_nt(weight_ref[...], low_ref[...])
    top = jnp.max(logits, axis=0, keepdims=True)
    weights = jnp.exp(logits - top)
    summed = jnp.sum(weights, axis=0, keepdims=True)
    probs_ref[0] = (weights * (1.0 / summed)).astype(BF16)
    totals_ref[0] = top + jnp.log(summed)


def token_backward(
    scale, probs_ref, share_ref, label_ref, low_ref, weight_ref, grad_low_ref, grad_weight_ref, total
):
    step = pl.program_id(0)
    labels = label_ref[0]
    shape = probs_ref.shape[1:]
    offset = (lax.axis_index("dp") * 2 + lax.axis_index("phase")) * shape[0]
    chosen = lax.broadcasted_iota(jnp.int32, shape, 0) == labels - offset
    grads = probs_ref[0].astype(F32) * share_ref[0] - chosen.astype(F32)
    grads = (grads * jnp.where(labels >= 0, scale, 0.0)).astype(BF16)
    grad_low = mm_tn(grads, weight_ref[...]).astype(BF16)
    cap = grad_low_ref.shape[1]
    for block in range(grad_low_ref.shape[0]):
        grad_low_ref[block] = grad_low[block * cap : (block + 1) * cap]
    part = mm(grads, low_ref[...])

    @pl.when(step == 0)
    def _():
        total[...] = part

    @pl.when(step != 0)
    def _():
        total[...] += part

    @pl.when(step == pl.num_programs(0) - 1)
    def _():
        grad_weight_ref[...] = total[...].T


def place_of(dp):
    return lax.rem(dp, 2), lax.rem(dp // 2, 2), dp // 4


def index_of(x, y, z):
    return (z * 2 + y) * 2 + x


def greet(devices):
    barrier = pltpu.get_barrier_semaphore()
    for dp, phase in devices:
        pl.semaphore_signal(barrier, inc=1, device_id=(dp, phase), device_id_type=MESH)
    return lambda: pl.semaphore_wait(barrier, len(devices))


def remote(src, dst, send, recv, device):
    return pltpu.make_async_remote_copy(
        src_ref=src, dst_ref=dst, send_sem=send, recv_sem=recv, device_id=device, device_id_type=MESH
    )


def gather_blocks(block):
    return lax.all_gather(lax.all_gather(block, "dp"), "phase")


def scatter_blocks(part):
    part = lax.psum_scatter(part.astype(F32), "phase", scatter_dimension=0, tiled=False)
    return lax.psum_scatter(part, "dp", scatter_dimension=0, tiled=False)


def token_shares(totals):
    top = lax.pmax(totals, ("dp", "phase"))
    return jnp.exp(totals - top) / lax.psum(jnp.exp(totals - top), ("dp", "phase"))


def pack_labels(labels, flags, out_ref):
    count, length = labels.shape
    before = lax.broadcasted_iota(jnp.int32, (length, length), 0)
    after = lax.broadcasted_iota(jnp.int32, (length, length), 1)
    upto = jnp.where(before <= after, 1.0, 0.0).astype(BF16)
    rows = jnp.concatenate([flags.astype(F32)] + [jnp.zeros((8 - count, length), F32)], axis=0)
    place = mm(rows.astype(BF16), upto)
    for row in range(count):
        flag = rows[row : row + 1]
        chosen = (before.astype(F32) == place[row : row + 1] - 1.0) & (flag > 0.0)
        label = labels[row : row + 1]
        high = lax.shift_right_logical(label, 8)
        parts = [high.astype(F32), (label - high * 256).astype(F32), flag, jnp.zeros((5, length), F32)]
        found = mm_nt(
            jnp.concatenate(parts, axis=0).astype(BF16), jnp.where(chosen, 1.0, 0.0).astype(BF16)
        )
        packed = jnp.where(found[2:3] > 0.5, found[0:1] * 256.0 + found[1:2], -1.0)
        out_ref[row : row + 1, :] = packed.astype(jnp.int32)


FORWARD = (
    "qkv", "mixed", "res", "after", "res_e", "ckv", "cq", "cmixed", "cres",
    "hid_e", "slope_e", "hid_d", "slope_d", "res_d", "src", "low", "grad_low", "grad_place",
)


def forward_kernel(
    scale, x_ref, segments_ref, delete_ref, place_ref, token_ref, mask_ref,
    qkv_w_ref, mix_w_ref, gain_ref, bias_ref, up_own, down_own,
    cq_w_any, ckv_w_any, co_w_any, cgain_ref, cbias_ref, delete_w_ref, place_w_any,
    rows_ref, cols_ref, labels_small_ref, labels_large_ref, most_ref, norms_ref, up_other, down_other,
    totals_ref, ctotals_ref, grad_delete_ref, *rest,
):
    outs, rest = dict(zip(FORWARD, rest)), rest[len(FORWARD) :]
    held, rest = dict(zip(FORWARD, rest)), rest[len(FORWARD) :]
    up, down, cq_w, ckv_w, co_w, place_w, send_after, own_labels, all_labels, turned, load, store, send, recv = rest
    dp, phase = lax.axis_index("dp"), lax.axis_index("phase")
    x, y, z = place_of(dp)
    chips = [
        (lax.rem(x + a, 2), lax.rem(y + b, 2), lax.rem(z + c, 4))
        for c in range(4) for b in range(2) for a in range(2) if a + b + c
    ]
    core = (dp, 1 - phase)
    met = greet([(index_of(*chip), phase) for chip in chips] + [core])
    copies, stores = [], []

    def remote_to(src, dst, device):
        i = len(copies)
        copy = remote(src, dst, send.at[i], recv.at[i], device)
        copy.start()
        copies.append(copy)
        return copy

    def save(*names):
        for name in names:
            copy = pltpu.make_async_copy(held[name], outs[name], store.at[len(stores)])
            copy.start()
            stores.append(copy)

    loads = [
        pltpu.make_async_copy(src, dst, load.at[i])
        for i, (src, dst) in enumerate((
            (up_own, up.at[phase]), (down_own, down.at[phase]), (ckv_w_any, ckv_w), (cq_w_any, cq_w),
            (co_w_any, co_w), (place_w_any, place_w),
        ))
    ]
    for copy in loads:
        copy.start()
    norms_ref[phase, 0:1, :] = gain_ref[1:2, :]
    norms_ref[phase, 1:2, :] = bias_ref[1:2, :]
    pack_labels(token_ref[...], mask_ref[...], own_labels)
    all_labels[z, y, x] = own_labels[...]
    width = x_ref.shape[1]
    qkv, mixed, res = held["qkv"], held["mixed"], held["res"]
    for part in range(3):
        span = slice(part * width, (part + 1) * width)
        qkv[:, span] = mm(x_ref[...], qkv_w_ref[:, span]).astype(BF16)
    save("qkv")
    met()
    from_norms = remote_to(norms_ref.at[phase], norms_ref.at[phase], core)
    from_up = remote_to(up_own, up.at[phase], core)
    from_down = remote_to(down_own, down.at[phase], core)
    for chip in chips:
        remote_to(own_labels, all_labels.at[z, y, x], (index_of(*chip), phase))
    label_copies = copies[3:]
    is_enc = phase == 0
    segments = segments_ref[...].astype(F32)
    length = segments.shape[2]

    def pick(first, second):
        return jnp.where(is_enc, first, second)

    def own_row(ref):
        value = ref[...].astype(F32)
        return pick(value[0:1], value[1:2])

    ids_e = pick(segments[0, 0:1], segments[1, 0:1])
    ids_d = pick(segments[0, 1:2], segments[1, 1:2])
    own_ids = [pick(segments[r, 0:1], segments[r, 1:2]) for r in range(2)]
    block = jnp.concatenate([ids_d] * 8, axis=0)
    later = pltpu.roll(block, length - 1, 1)
    lane = lax.broadcasted_iota(jnp.int32, (8, length), 1)
    valid = jnp.where((block == later) & (lane < length - 1), 1.0, 0.0)[0:1]
    rows = jnp.concatenate(
        own_ids + [ids_e, ids_d, own_row(delete_ref), own_row(place_ref), valid, own_row(mask_ref)], axis=0
    )
    rows_ref[...] = rows
    turned[...] = jnp.zeros(turned.shape, F32)
    turned[0:8, :] = rows
    cols = turned[...].T
    cols_ref[...] = cols
    for turn in range(2):
        row = 1 - phase if turn == 0 else phase
        span = pl.ds(pl.multiple_of(row * length, length), length)
        allowed = jnp.where(row == 0, cols[:, 0:1], cols[:, 1:2]) == jnp.where(
            row == 0, own_ids[0], own_ids[1]
        )
        attend_forward(
            lambda pair: qkv[span, column(pair)],
            lambda pair: qkv[span, column(pair, width)],
            lambda pair: qkv[span, column(pair, 2 * width)],
            allowed, mixed, totals_ref.at[row], span,
        )
        residual = x_ref[span, :].astype(F32) + mm(mixed[span, :], mix_w_ref[...])
        res[span, :] = residual
        after = norm_forward(residual, gain_ref[0:1, :], bias_ref[0:1, :])
        if turn == 0:
            send_after[...] = after
            from_after = remote_to(send_after, held["after"].at[phase], core)
        else:
            held["after"][phase] = after
    save("mixed", "res")
    from_after.wait_recv()
    save("after")
    from_norms.wait_recv()
    from_up.wait_recv()
    from_down.wait_recv()
    for copy in loads:
        copy.wait()
    for i, (src, dst) in enumerate(((up, up_other), (down, down_other))):
        copy = pltpu.make_async_copy(src.at[1 - phase], dst, store.at[len(stores)])
        copy.start()
        stores.append(copy)
    encoder_rows(
        held["after"].at[0], up.at[0], down.at[0], norms_ref[0, 0:1, :], norms_ref[0, 1:2, :], ckv_w,
        held["hid_e"], held["slope_e"], held["res_e"], held["src"], held["ckv"],
    )
    save("hid_e", "slope_e", "res_e", "src", "ckv")
    middle = cross_rows(
        held["after"].at[1], cols[:, 2:3] == rows[3:4], cq_w, co_w, cgain_ref, cbias_ref,
        held["cq"], held["ckv"], held["cmixed"], held["cres"], ctotals_ref,
    )
    save("cq", "cmixed", "cres")
    decoder_rows(
        scale, middle, up.at[1], down.at[1], norms_ref[1, 0:1, :], norms_ref[1, 1:2, :],
        cols[:, 4:5].astype(jnp.int32), cols[:, 5:6].astype(jnp.int32), cols[:, 6:7], delete_w_ref, place_w,
        held["hid_d"], held["slope_d"], held["res_d"], held["low"], held["grad_low"],
        grad_delete_ref, held["grad_place"],
    )
    save("hid_d", "slope_d", "res_d", "low", "grad_low", "grad_place")
    for copy in label_copies:
        copy.wait_recv()
    small = length // 2
    for at, (p, yy, xx, zz) in enumerate(
        (p, yy, xx, zz) for p in range(2) for yy in range(2) for xx in range(2) for zz in range(4)
    ):
        line = all_labels[zz, yy, xx, p : p + 1, :]
        labels_small_ref[:, at * small : (at + 1) * small] = line[:, :small]
        labels_large_ref[:, at * length : (at + 1) * length] = line
    beyond = jnp.max(all_labels[:, :, :, :, small:].astype(F32).reshape(2 * GROUPS, length - small))
    most_ref[...] = jnp.full(most_ref.shape, beyond, F32)
    for copy in copies:
        copy.wait_send()
    for copy in stores:
        copy.wait()


def token_kernel(
    scale, cap, low_ref, rows_ref, cols_ref, labels_ref, head_any,
    grad_ref, grad_weight_ref,
    weight, weight_t, every, probs, totals, near_in, joined, far_in, shares,
    part, core_in, third_in, second_in, z_in, load, send, recv,
):
    dp, phase = lax.axis_index("dp"), lax.axis_index("phase")
    x, y, z = place_of(dp)
    x_first = phase == 0
    x2, y2 = jnp.where(x_first, 1 - x, x), jnp.where(x_first, y, 1 - y)
    x3, y3 = jnp.where(x_first, x, 1 - x), jnp.where(x_first, 1 - y, y)
    second, third, core = (index_of(x2, y2, z), phase), (index_of(x3, y3, z), phase), (dp, 1 - phase)
    zs = [lax.rem(z + k, 4) for k in (1, 2, 3)]
    along = [(index_of(x, y, k), phase) for k in zs]
    shard, length = weight_t.shape[0], low_ref.shape[0]
    near = [
        (index_of(lax.rem(x + a, 2), lax.rem(y + b, 2), z), lax.rem(phase + c, 2))
        for a in range(2) for b in range(2) for c in range(2) if a + b + c
    ]
    met = greet(near + along)
    offset = pl.multiple_of((dp * 2 + phase) * shard, shard)
    weight_copy = pltpu.make_async_copy(head_any.at[:, pl.ds(offset, shard)], weight, load.at[0])
    weight_copy.start()
    copies = []

    def remote_to(src, dst, device):
        i = len(copies)
        copy = remote(src, dst, send.at[i], recv.at[i], device)
        copy.start()
        copies.append(copy)
        return copy

    def unit(p, yy, xx):
        return (p * 2 + yy) * 2 + xx

    def block(u, zz):
        return pl.ds(pl.multiple_of((u * 4 + zz) * cap, cap), cap)

    before = lax.broadcasted_iota(jnp.int32, (length, length), 0)
    after = lax.broadcasted_iota(jnp.int32, (length, length), 1)
    rows = rows_ref[...]
    place = mm(rows.astype(BF16), jnp.where(before <= after, 1.0, 0.0).astype(BF16))[7:8]
    slot = lax.broadcasted_iota(jnp.int32, (cap, length), 0).astype(F32)
    chosen = jnp.where((slot == place - 1.0) & (rows[7:8] > 0.0), 1.0, 0.0).astype(BF16)
    own = unit(phase, y, x)
    every[block(own, z), :] = mm(chosen, low_ref[...]).astype(BF16)
    def relay(u, zz, device):
        here = every.at[block(u, zz), :]
        return remote_to(here, here, device)

    beside, across = (index_of(x, y, z + 1 - 2 * lax.rem(z, 2)), phase), (index_of(x, y, lax.rem(z + 2, 4)), phase)
    met()
    firsts = [relay(own, z, beside), relay(own, z, across)]
    cross = [relay(own, z, core)]
    seconds = [relay(own, z, second)]
    thirds = [relay(own, z, third)]
    weight_copy.wait()
    weight_t[...] = weight[...].T
    near_z = z + 1 - 2 * lax.rem(z, 2)
    sources = [near_z, lax.rem(z + 2, 4), lax.rem(near_z + 2, 4)]
    order = [z] + sources
    for k in range(3):
        firsts[k].wait_recv()
        if k == 0:
            firsts.append(relay(own, near_z, across))
        seconds.append(relay(own, sources[k], second))
        thirds.append(relay(own, sources[k], third))
        cross.append(relay(own, sources[k], core))
    tall = 256
    chunks = 4 * cap // tall

    def look(u):
        def step(j, _):
            span = pl.ds(pl.multiple_of((u * chunks + j) * tall, tall), tall)
            logits = mm_nt(weight_t[...], every[span, :])
            top = jnp.max(logits, axis=0, keepdims=True)
            weights = jnp.exp(logits - top)
            summed = jnp.sum(weights, axis=0, keepdims=True)
            probs[:, span] = (weights * (1.0 / summed)).astype(BF16)
            totals[:, span] = top + jnp.log(summed)
            return 0

        lax.fori_loop(0, chunks, step, 0)

    def arrived(some):
        for copy in some:
            copy.wait_recv()

    look(own)
    for k in range(4):
        seconds[k].wait_recv()
        thirds.append(relay(unit(phase, y2, x2), order[k], third))
        cross.append(relay(unit(phase, y2, x2), order[k], core))
    arrived(cross[0:4])
    look(unit(1 - phase, y, x))
    look(unit(phase, y2, x2))
    for k in range(4):
        thirds[k].wait_recv()
        cross.append(relay(unit(phase, y3, x3), order[k], core))
    arrived(cross[4:8])
    look(unit(1 - phase, y3, x3))
    for k in range(4):
        thirds[4 + k].wait_recv()
        cross.append(relay(unit(phase, 1 - y, 1 - x), order[k], core))
    look(unit(phase, y3, x3))
    arrived(cross[8:12])
    look(unit(1 - phase, y2, x2))
    look(unit(phase, 1 - y, 1 - x))
    arrived(cross[12:16])
    look(unit(1 - phase, 1 - y, 1 - x))

    def join(parts):
        top = parts[0]
        for piece in parts[1:]:
            top = jnp.maximum(top, piece)
        summed = jnp.exp(parts[0] - top)
        for piece in parts[1:]:
            summed = summed + jnp.exp(piece - top)
        return top + jnp.log(summed)

    near_copies = [remote_to(totals, near_in.at[j], device) for j, device in enumerate(near)]
    arrived(near_copies)
    total = join([totals[...]] + [near_in[j] for j in range(7)])
    joined[...] = total
    far_copies = [remote_to(joined, far_in.at[j], device) for j, device in enumerate(along)]
    arrived(far_copies)
    shares[...] = jnp.exp(totals[...] - join([total] + [far_in[j] for j in range(3)]))

    per = tall // cap

    def learn(u):
        def step(j, _):
            span = pl.ds(pl.multiple_of((u * chunks + j) * tall, tall), tall)
            labels = labels_ref[:, span]
            hit = lax.broadcasted_iota(jnp.int32, (shard, tall), 0) == labels - offset
            grads = probs[:, span].astype(F32) * shares[:, span] - jnp.where(hit, 1.0, 0.0)
            grads = (grads * jnp.where(labels >= 0, scale, 0.0)).astype(BF16)
            probs[:, span] = grads
            back = mm(weight[...], grads).astype(BF16)
            for k in range(per):
                part[u, j * per + k] = back[:, k * cap : (k + 1) * cap]
            return 0

        lax.fori_loop(0, chunks, step, 0)

    def add(u, zz, *others):
        value = part[u, zz].astype(F32)
        for other in others:
            value = value + other.astype(F32)
        part[u, zz] = value.astype(BF16)

    mine = [unit(phase, 1 - y, 1 - x), unit(phase, y3, x3), unit(phase, y2, x2), own]
    theirs = [
        unit(1 - phase, 1 - y, 1 - x), unit(1 - phase, y2, x2), unit(1 - phase, y3, x3), unit(1 - phase, y, x)
    ]
    route = zs + [z]
    core_copies, third_copies = [], []

    def to_third(k):
        core_copies[k].wait_recv()
        for j, zz in enumerate(route):
            add(mine[k], zz, core_in[k, zz])
            third_copies.append(remote_to(part.at[mine[k], zz], third_in.at[k, j], third))

    for k in range(4):
        learn(theirs[k])
        core_copies.append(remote_to(part.at[theirs[k]], core_in.at[k], core))
        learn(mine[k])
        if k < 2:
            to_third(k)
    core_copies[2].wait_recv()
    second_copies = []
    for j, zz in enumerate(route):
        third_copies[j].wait_recv()
        add(mine[2], zz, core_in[2, zz], third_in[0, j])
        second_copies.append(remote_to(part.at[mine[2], zz], second_in.at[j], second))

    slab = min(256, shard)

    def weigh(k):
        value = mm(probs[k * slab : (k + 1) * slab, :], every[...])
        grad_weight_ref[:, k * slab : (k + 1) * slab] = value.T

    slabs = shard // slab
    for k in range((slabs + 1) // 2):
        weigh(k)
    core_copies[3].wait_recv()
    z_copies = []
    for j, zz in enumerate(route):
        third_copies[4 + j].wait_recv()
        second_copies[j].wait_recv()
        add(own, zz, core_in[3, zz], third_in[1, j], second_in[j])
        if j < 3:
            z_copies.append(remote_to(part.at[own, zz], z_in.at[j], along[j]))
    for k in range((slabs + 1) // 2, slabs):
        weigh(k)
    arrived(z_copies)
    back = part[own, z].astype(F32)
    for j in range(3):
        back = back + z_in[j].astype(F32)
    place = mm(jnp.where(after <= before, 1.0, 0.0).astype(BF16), cols_ref[...].astype(BF16))[:, 7:8]
    slot = lax.broadcasted_iota(jnp.int32, (length, cap), 1).astype(F32)
    spread = jnp.where((slot == place - 1.0) & (cols_ref[:, 7:8] > 0.0), 1.0, 0.0).astype(BF16)
    grad_ref[...] = mm_nt(spread, back.astype(BF16))
    for copy in copies:
        copy.wait_send()


def token_chips(number, cap, low, rows, cols, labels, head):
    length, width = low.shape
    shard = head.shape[1] // (2 * GROUPS)
    count = 2 * GROUPS * cap
    scale = float(2 * length * GROUPS) ** (-0.5)
    copies = 64
    return pl.pallas_call(
        partial(token_kernel, scale, cap),
        out_shape=(whole((length, width), F32), whole((width, shard), F32)),
        in_specs=in_vmem(4) + [pl.BlockSpec(memory_space=pl.ANY)],
        out_specs=tuple(in_vmem(2)),
        scratch_shapes=[
            VMEM((width, shard), BF16), VMEM((shard, width), BF16), VMEM((count, width), BF16),
            VMEM((shard, count), BF16), VMEM((1, count), F32), VMEM((7, 1, count), F32), VMEM((1, count), F32),
            VMEM((3, 1, count), F32), VMEM((1, count), F32),
            VMEM((8, 4, width, cap), BF16), VMEM((4, 4, width, cap), BF16), VMEM((2, 4, width, cap), BF16),
            VMEM((4, width, cap), BF16), VMEM((3, width, cap), BF16),
            pltpu.SemaphoreType.DMA((1,)), pltpu.SemaphoreType.DMA((copies + 8,)), pltpu.SemaphoreType.DMA((copies + 8,)),
        ],
        compiler_params=pltpu.CompilerParams(
            collective_id=number, has_side_effects=True, vmem_limit_bytes=60 * 1024 * 1024
        ),
        name="token_head",
    )(low, rows, cols, labels, head)


class Exchange:
    def __init__(self, send, recv):
        self.dp, self.phase = lax.axis_index("dp"), lax.axis_index("phase")
        self.x, self.y, self.z = place_of(self.dp)
        x, y, z = self.x, self.y, self.z
        low, high = lax.rem(z, 2), z // 2
        self.own = {"b": high, "a": low, "y": y, "x": x}
        self.partner = {
            "b": index_of(x, y, (1 - high) * 2 + low), "a": index_of(x, y, high * 2 + 1 - low),
            "y": index_of(x, 1 - y, z), "x": index_of(1 - x, y, z),
        }
        self.send, self.recv, self.used, self.copies = send, recv, 0, []

    def greet(self):
        return greet([(self.partner[step], self.phase) for step in "bayx"] + [(self.dp, 1 - self.phase)])

    def copy(self, src, dst, device):
        copy = remote(src, dst, self.send.at[self.used], self.recv.at[self.used], device)
        self.used += 1
        copy.start()
        self.copies.append(copy)
        return copy

    def to_core(self, src, dst):
        return self.copy(src, dst, (self.dp, 1 - self.phase))

    def to_core_either(self, first, second):
        i = self.used
        self.used += 1
        made = [remote(*pair, self.send.at[i], self.recv.at[i], (self.dp, 1 - self.phase)) for pair in (first, second)]

        @pl.when(self.phase == 0)
        def _():
            made[0].start()

        @pl.when(self.phase != 0)
        def _():
            made[1].start()

        self.copies.append(made[0])
        return made[0]

    def finish(self):
        for copy in self.copies:
            copy.wait_send()


class Batch:
    def __init__(self, shards, ins, put, own=None):
        self.shards, self.ins, self.put, self.own, self.arriving = shards, ins, put, own, []


class Chunk:
    def __init__(self, exchange, batch, start, size, order):
        self.exchange, self.batch, self.order = exchange, batch, order
        self.rows, self.step, self.fixed = pl.ds(start, size), -1, {}

    def at(self, fixed, free):
        free = list(free)
        return tuple(fixed[name] if name in fixed else free.pop(0) for name in "bayx") + (self.rows,)

    def advance(self):
        batch, ex, rows = self.batch, self.exchange, self.rows
        shards = batch.shards
        if self.step < 0 and batch.own is not None:
            for copy in batch.arriving:
                copy.wait_recv()
            batch.arriving = []
            own = batch.own

            def join(i, _):
                at = (i // 8, lax.rem(i // 4, 2), lax.rem(i // 2, 2), lax.rem(i, 2), rows)
                shards[at] = (shards[at].astype(F32) + own[at].astype(F32)).astype(BF16)
                return 0

            lax.fori_loop(0, GROUPS, join, 0)
        elif self.step >= 0:
            self.arriving.wait_recv()
            name = self.order[self.step]
            self.fixed[name] = ex.own[name]
            free = 3 - self.step
            arrived = batch.ins[self.step]
            if free == 0:
                batch.put(rows, shards[self.at(self.fixed, ())].astype(F32) + arrived[rows].astype(F32))
            else:

                def add(i, _):
                    spot = tuple(lax.rem(i // 2 ** (free - 1 - k), 2) for k in range(free))
                    at = self.at(self.fixed, spot)
                    shards[at] = (shards[at].astype(F32) + arrived[spot + (rows,)].astype(F32)).astype(BF16)
                    return 0

                lax.fori_loop(0, 2**free, add, 0)
        self.step += 1
        if self.step < 4:
            name = self.order[self.step]
            free = (slice(None),) * (3 - self.step)
            src = shards.at[self.at({**self.fixed, name: 1 - ex.own[name]}, free)]
            dst = batch.ins[self.step].at[free + (rows,)]
            self.arriving = ex.copy(src, dst, (ex.partner[name], ex.phase))


PARTS = (
    ((0, 32, "yxab"), (32, 32, "yabx"), (64, 16, "abxy"), (80, 16, "abxy"), (96, 32, "axyb"),),
    ((0, 48, "xyab"), (48, 32, "yabx"),),
    ((0, 32, "xyab"), (32, 32, "yxab"), (64, 32, "abyx"), (96, 16, "yxab"), (112, 16, "yxab"),),
    (
        (0, 16, "xyab"), (16, 16, "yxab"), (32, 16, "xyab"), (48, 16, "yxab"), (64, 16, "abxy"), (80, 16,
        "ayxb"), (96, 16, "xyab"), (112, 16, "yxab"),
    ),
)
SCHEDULE = (
    (),
    (0, 2, 3),
    (),
    (),
    (1, 4),
    (),
    (),
    (2,),
    (0, 6, 3),
    (5, 1, 2),
    (0, 4),
    (3,),
    (8, 9, 2),
    (1, 0, 6),
    (3, 10, 7),
    (),
    (11, 4),
    (),
    (),
    (1,),
    (),
    (),
    (5, 6, 8),
    (4, 10, 9),
    (7, 11, 16, 12, 13, 17),
    (
        14, 15, 5, 6, 8, 10, 0, 1, 18, 19, 2, 11, 3, 4, 7, 9, 6, 12, 13, 10, 14, 11, 16, 18, 15, 8, 17, 13, 10, 9,
        5, 19, 7, 11, 12, 15, 13, 9, 14, 18, 17, 19, 8, 12, 16, 15, 14, 18, 17, 7, 19, 5, 12, 13, 16, 15, 14, 18,
        17, 19, 16,
    ),
)
CROSS, CROSS_END, ENCODER, SELF, WEIGHTS, TAIL = 0, 5, 6, 11, 21, 25


BACKWARD = (
    "grad_low", "grad_token", "res_d", "cres", "co_w", "cmixed", "cq", "ckv", "grad_place", "after", "src", "cq_w", "ckv_w", "res_e",
    "res", "mix_w", "qkv", "mixed", "x", "qkv_w",
)


def backward_kernel(
    rows_ref, cols_ref, norms_ref, cgain_ref, cbias_ref, ctotals_ref, totals_ref, grad_delete_ref, gain_ref,
    up_own, up_other, down_own, down_other, hid_e_any, slope_e_any, hid_d_any, slope_d_any, *rest,
):
    held_any, rest = dict(zip(BACKWARD, rest)), rest[len(BACKWARD) :]
    grad_x_any, red_ff_ref, red_attention_ref, red_cross_ref, vectors_ref = rest[:5]
    held, rest = dict(zip(BACKWARD, rest[5:])), rest[5 + len(BACKWARD) :]
    (
        up, down, hid, slope, grad_d, grad_e, grad_c, grad_a, core_d, core_e, core_c,
        in0_d, in0_e, in0_c, in0_a, in1_d, in1_e, in1_c, in1_a,
        in2_d, in2_e, in2_c, in2_a, in3_d, in3_e, in3_c, in3_a,
        after_grads, after_in, gq_ref, gckv_ref, grad_qkv, sums, grad_x_ref,
        vec_own, vec_core, vec_sums, vec_in, sems, held_sems, send, recv,
    ) = rest
    phase = lax.axis_index("phase")
    ex = Exchange(send, recv)
    met = ex.greet()

    def moved(name):
        i = BACKWARD.index(name)
        return pltpu.make_async_copy(held_any[name], held[name], held_sems.at[i])

    waited = set()

    def get(name):
        if name not in waited:
            waited.add(name)
            moved(name).wait()
        return held[name]

    length, width = held["grad_low"].shape
    each = width // GROUPS

    def load(own_side, i):
        hidden, slopes = (hid_e_any, slope_e_any) if own_side == 0 else (hid_d_any, slope_d_any)

        @pl.when(phase == own_side)
        def _():
            pltpu.make_async_copy(up_own, up, sems.at[i]).start()
            pltpu.make_async_copy(down_own, down, sems.at[i + 1]).start()

        @pl.when(phase != own_side)
        def _():
            pltpu.make_async_copy(up_other, up, sems.at[i]).start()
            pltpu.make_async_copy(down_other, down, sems.at[i + 1]).start()

        pltpu.make_async_copy(hidden, hid, sems.at[i + 2]).start()
        pltpu.make_async_copy(slopes, slope, sems.at[i + 3]).start()

    def loaded(i):
        for k, (src, dst) in enumerate(
            ((up_own, up), (down_own, down), (hid_e_any, hid), (slope_e_any, slope))
        ):
            pltpu.make_async_copy(src, dst, sems.at[i + k]).wait()

    def puts(ref):
        def put_up(part, value):
            ref[0, :, :, :, :, part * each : (part + 1) * each, :] = value.astype(BF16).reshape(
                2, 2, 2, 2, each, width
            )

        def put_down(part, value):
            ref[1, part // 2, part % 2] = value.astype(BF16).reshape(2, 2, width // 4, width)

        return put_up, put_down

    def put_ff(half):
        def put(rows, value):
            sums[half, rows, :] = value

        return put

    def put_attention(rows, value):
        red_attention_ref[rows, :] = value

    cross_sum = red_cross_ref.at[phase]

    def put_cross_sum(rows, value):
        cross_sum[rows, :] = value

    batch_d = Batch(core_d, (in0_d, in1_d, in2_d, in3_d), put_ff(1), grad_d.at[phase])
    batch_c = Batch(core_c, (in0_c, in1_c, in2_c, in3_c), put_cross_sum, grad_c.at[phase])
    batch_e = Batch(core_e, (in0_e, in1_e, in2_e, in3_e), put_ff(0), grad_e.at[phase])
    batch_a = Batch(grad_a, (in0_a, in1_a, in2_a, in3_a), put_attention)
    chunks = [
        Chunk(ex, batch, *part)
        for batch, parts in zip((batch_d, batch_c, batch_e, batch_a), PARTS) for part in parts
    ]

    def go_on(place):
        for name in SCHEDULE[place]:
            chunks[name].advance()

    def halves_to_core(batch, ref, core_ref, part):
        rows = pl.ds(part * each, each)
        batch.arriving.append(ex.to_core_either(
            (ref.at[1, part // 2, part % 2], core_ref.at[part // 2, part % 2]),
            (ref.at[0, :, :, :, :, rows], core_ref.at[:, :, :, :, rows]),
        ))

    for name in BACKWARD[:4]:
        moved(name).start()
    load(1, 0)
    for name in BACKWARD[4:]:
        moved(name).start()
    grad_out = get("grad_low")[...] + get("grad_token")[...]
    grad_res, gain_grad, bias_grad = norm_back(get("res_d")[...], norms_ref[1, 0:1, :], grad_out)
    vec_own[2:3, :] = gain_grad
    vec_own[3:4, :] = bias_grad
    vec_own[6:8, :] = grad_delete_ref[0:2, :]
    cres = get("cres")[...]
    middle_low = norm_forward(cres, cgain_ref[...], cbias_ref[...]).astype(BF16)
    loaded(0)
    met()
    grad_middle = feed_back(
        grad_res, middle_low, up, down, hid, slope, *puts(grad_d),
        lambda part: halves_to_core(batch_d, grad_d, core_d, part),
    )
    load(0, 4)
    grad_res, gain_grad, bias_grad = norm_back(cres, cgain_ref[...], grad_middle)
    vec_own[4:5, :] = gain_grad
    vec_own[5:6, :] = bias_grad
    branch = grad_res.astype(BF16)

    def put_cross(first, value):
        half_rows = grad_c.shape[5]
        value = value.astype(BF16).reshape(2, 2, 2, 2, each, width)
        for at in range(0, each, 16):
            half, row = divmod(first + at, half_rows)
            grad_c[half, :, :, :, :, row : row + 16, :] = value[:, :, :, :, at : at + 16, :]

    put_cross(3 * each, mm_tn(get("cmixed")[...], branch))
    put_cross(4 * each, get("grad_place")[...])
    grad_mixed = mm_nt(branch, get("co_w")[...]).astype(BF16)
    cq_ref, ckv_ref = get("cq"), get("ckv")

    def put_q(pair, value):
        gq_ref[:, column(pair)] = value

    def put_k(pair, value):
        gckv_ref[:, column(pair)] = value

    def put_v(pair, value):
        gckv_ref[:, column(pair, width)] = value

    go_on(CROSS)

    def between(pair):
        go_on(CROSS + 1 + pair)

    attend_backward(
        lambda pair: cq_ref[:, column(pair)],
        lambda pair: ckv_ref[:, column(pair)],
        lambda pair: ckv_ref[:, column(pair, width)],
        lambda pair: grad_mixed[:, column(pair)],
        cols_ref[:, 2:3] == rows_ref[3:4, :],
        ctotals_ref, put_q, put_k, put_v, between,
    )
    grad_q = gq_ref[...]
    put_cross(0, mm_tn(get("after")[1].astype(BF16), grad_q))
    for part in range(2):
        put_cross((1 + part) * each, mm_tn(get("src")[...], gckv_ref[:, part * width : (part + 1) * width]))
    batch_c.arriving.append(ex.to_core(grad_c.at[1 - phase], core_c))
    after_grads[1] = grad_res + mm_nt(grad_q, get("cq_w")[...])
    go_on(CROSS_END)
    grad_src = mm_nt(gckv_ref[...], get("ckv_w")[...]).astype(BF16).astype(F32)
    grad_res, gain_grad, bias_grad = norm_back(get("res_e")[...], norms_ref[0, 0:1, :], grad_src)
    vec_own[0:1, :] = gain_grad
    vec_own[1:2, :] = bias_grad
    from_v = ex.to_core(vec_own, vec_core)
    loaded(4)

    go_on(ENCODER)

    def between(part):
        halves_to_core(batch_e, grad_e, core_e, part)
        go_on(ENCODER + 1 + part)

    after_grads[0] = feed_back(
        grad_res, get("after")[0].astype(BF16), up, down, hid, slope, *puts(grad_e), between
    )
    from_after = ex.to_core(after_grads.at[1 - phase], after_in)
    res_ref, mix_w_ref, qkv_ref, mixed_ref, x_ref = [get(n) for n in ("res", "mix_w", "qkv", "mixed", "x")]
    first_vectors = []
    for turn in range(2):
        row = phase if turn == 0 else 1 - phase
        rows = pl.ds(pl.multiple_of(row * length, length), length)
        if turn == 0:
            grad_after = after_grads[phase]
        else:
            from_after.wait_recv()
            grad_after = after_in[...]
        grad_res, gain_grad, bias_grad = norm_back(res_ref[rows, :], gain_ref[0:1, :], grad_after)
        first_vectors.append((gain_grad, bias_grad))
        grad_x_ref[rows, :] = grad_res
        branch = grad_res.astype(BF16)
        if turn == 0:
            first_branch, first_rows = branch, rows
        grad_mixed = mm_nt(branch, mix_w_ref[...]).astype(BF16)

        def put(offset):
            def store(pair, value):
                grad_qkv[rows, column(pair, offset)] = value

            return store

        go_on(SELF + 5 * turn)

        def between(pair):
            go_on(SELF + 5 * turn + 1 + pair)

        attend_backward(
            lambda pair: qkv_ref[rows, column(pair)],
            lambda pair: qkv_ref[rows, column(pair, width)],
            lambda pair: qkv_ref[rows, column(pair, 2 * width)],
            lambda pair: grad_mixed[:, column(pair)],
            jnp.where(row == 0, cols_ref[:, 0:1], cols_ref[:, 1:2])
            == jnp.where(row == 0, rows_ref[0:1, :], rows_ref[1:2, :]),
            totals_ref.at[row], put(0), put(width), put(2 * width), between,
        )
    shape = (2, 2, 2, 2, each, width)
    grad_mix = mm_tn(mixed_ref[first_rows, :], first_branch) + mm_tn(mixed_ref[rows, :], branch)
    grad_a[:, :, :, :, 3 * each :, :] = grad_mix.astype(BF16).reshape(shape)
    go_on(WEIGHTS)
    for part in range(3):
        cols = slice(part * width, (part + 1) * width)
        value = mm_tn(x_ref[...], grad_qkv[:, cols])
        grad_a[:, :, :, :, part * each : (part + 1) * each, :] = value.astype(BF16).reshape(shape)
        go_on(WEIGHTS + 1 + part)
    grad_x_ref[...] += mm_nt(grad_qkv[...], get("qkv_w")[...])
    grad_x_copy = pltpu.make_async_copy(grad_x_ref, grad_x_any, held_sems.at[len(BACKWARD)])
    grad_x_copy.start()
    from_v.wait_recv()
    vec_sums[0, 0:8, :] = vec_own[...] + vec_core[...]
    vec_sums[0, 8:9, :] = first_vectors[0][0] + first_vectors[1][0]
    vec_sums[0, 9:10, :] = first_vectors[0][1] + first_vectors[1][1]
    vec_sums[0, 10:16, :] = jnp.zeros((6, width), F32)
    tail = SCHEDULE[TAIL]
    left = [sum(chunks[item].batch is batch for item in tail) for batch in (batch_d, batch_c, batch_e)]
    vector_copies = []

    def vector_step(stage):
        if stage > 0:
            vector_copies[-1].wait_recv()
            vec_sums[stage] = vec_sums[stage - 1] + vec_in[stage - 1]
        if stage < 4:
            step = "xyab"[stage]
            vector_copies.append(ex.copy(vec_sums.at[stage], vec_in.at[stage], (ex.partner[step], phase)))

    vector_step(0)
    after_each = len(tail) // 5
    for at, name in enumerate(tail):
        chunks[name].advance()
        if at % after_each == after_each - 1 and len(vector_copies) < 4:
            vector_step(len(vector_copies))
        for i, batch in enumerate((batch_d, batch_c, batch_e)):
            left[i] -= chunks[name].batch is batch
        if chunks[name].batch is batch_c and left[1] == 0:
            cross_copy = ex.to_core(cross_sum, red_cross_ref.at[phase])
        if chunks[name].batch in (batch_d, batch_e) and left[0] + left[2] == 0:
            ff_copy = ex.to_core(sums.at[1 - phase], red_ff_ref.at[phase])
            red_ff_ref[phase] = sums[phase]
    vector_step(4)
    vectors_ref[...] = vec_sums[4]
    cross_copy.wait_recv()
    ff_copy.wait_recv()
    grad_x_copy.wait()
    ex.finish()


def unpack_kernel(
    ff_any, attention_any, cross_any, vectors_any, own_any, other_any,
    qkv_ref, mix_ref, up_ref, down_any, cq_ref, ckv_ref, co_ref, place_ref,
    gain_ref, bias_ref, cgain_ref, cbias_ref, delete_ref, token_any,
    ff_ref, attention_ref, cross_halves_ref, vectors_ref, halves, sems, token_sems,
):
    phase, dp = lax.axis_index("phase"), lax.axis_index("dp")
    shard, pieces = own_any.shape[1], token_sems.shape[1]
    tall = own_any.shape[0] // pieces
    arrive, leave = [], []
    for i in range(pieces):
        rows = pl.ds(i * tall, tall)
        for side, (src, at) in enumerate(((own_any, phase), (other_any, 1 - phase))):
            arrive.append(pltpu.make_async_copy(src.at[rows], halves.at[side, rows], token_sems.at[side, i]))
            cols = pl.ds(pl.multiple_of(at * shard, shard), shard)
            leave.append(pltpu.make_async_copy(halves.at[side, rows], token_any.at[rows, cols], token_sems.at[side, i]))
    moves = [
        pltpu.make_async_copy(src, dst, sems.at[i])
        for i, (src, dst) in enumerate((
            (vectors_any, vectors_ref), (ff_any, ff_ref), (attention_any, attention_ref), (cross_any, cross_halves_ref),
        ))
    ]
    for move in arrive[:2] + moves + arrive[2:]:
        move.start()
    for i in range(2 * pieces):
        arrive[i].wait()
        leave[i].start()
    for move in moves:
        move.wait()
    down_move = pltpu.make_async_copy(ff_ref.at[1], down_any, sems.at[4])
    down_move.start()
    each = gain_ref.shape[2]
    vectors = vectors_ref[...]
    whole_width = vectors.shape[1]
    vectors = pltpu.roll(vectors, lax.rem(whole_width - dp * each, whole_width), 1)[:, :each]
    gain_ref[0, 0:1, :] = vectors[8:9]
    gain_ref[0, 1:2, :] = jnp.where(phase == 0, vectors[0:1], vectors[2:3])
    bias_ref[0, 0:1, :] = vectors[9:10]
    bias_ref[0, 1:2, :] = jnp.where(phase == 0, vectors[1:2], vectors[3:4])
    cgain_ref[...] = vectors[4:5]
    cbias_ref[...] = vectors[5:6]
    delete_ref[...] = vectors[6:8]
    width = mix_ref.shape[1]
    high = mix_ref.shape[0]
    for block in range(up_ref.shape[1] // width):
        up_ref[:, block * width : (block + 1) * width] = ff_ref[0, block * high : (block + 1) * high, :]
    for block in range(3):
        qkv_ref[:, block * width : (block + 1) * width] = attention_ref[block * high : (block + 1) * high, :]
    mix_ref[...] = attention_ref[3 * high :, :]
    half_rows = cross_halves_ref.shape[1]

    def cross(start):
        half, row = divmod(start, half_rows)
        return cross_halves_ref[half, row : row + 16, :]

    for start in range(0, 5 * high, 16):
        part, inner = start // high, slice(start % high, start % high + 16)
        if part == 0:
            cq_ref[inner, :] = cross(start)
        elif part < 3:
            ckv_ref[inner, (part - 1) * width : part * width] = cross(start)
        elif part == 3:
            co_ref[inner, :] = cross(start)
        else:
            value = cross(start)
            cols = place_ref.shape[1]
            at = start % high
            place_ref[at : at + 16, :] = value[:, :cols]
            place_ref[high + at : high + at + 16, :] = value[:, cols:]
    down_move.wait()
    for move in leave:
        move.wait()


def whole(shape, dtype):
    return jax.ShapeDtypeStruct(shape, dtype)


def in_vmem(count):
    return [pl.BlockSpec(memory_space=VMEM)] * count


def swap(value):
    return lax.ppermute(value, "phase", [(0, 1), (1, 0)])


def unpacked(shards, height, columns):
    groups, rows, width = shards.shape
    blocks = columns // width
    parts = shards.reshape(groups, blocks, rows // blocks, width)
    return parts.transpose(0, 2, 1, 3).reshape(height, columns)


def token_head(cap, block_rows, low, flags, labels_all, flags_all, weight, weight_t, scale):
    length, width = low.shape
    dp = lax.axis_size("dp")
    shard = weight_t.shape[0]

    def choice(flags):
        place = jnp.cumsum(flags, axis=-1) - 1
        places = lax.broadcasted_iota(jnp.int32, flags.shape[:-1] + (cap, flags.shape[-1]), flags.ndim - 1)
        return (places == place[..., None, :]) & (flags[..., None, :] > 0)

    chosen = choice(flags)
    packed = mm(chosen.astype(BF16), low).astype(BF16)
    every = gather_blocks(packed).reshape(2 * dp * cap, width)
    labels = jnp.max(jnp.where(choice(flags_all), labels_all[:, None, :], -1), axis=-1)
    labels = labels.reshape(dp, 2, cap).transpose(1, 0, 2).reshape(2 * dp * cap)
    tall = block_rows
    count = 2 * dp * cap // tall
    probs, totals = pl.pallas_call(
        token_forward,
        grid=(count,),
        out_shape=(whole((count, shard, tall), BF16), whole((count, 1, tall), F32)),
        in_specs=[
            pl.BlockSpec((tall, width), lambda i: (i, 0)),
            pl.BlockSpec((shard, width), lambda i: (0, 0)),
        ],
        out_specs=(
            pl.BlockSpec((1, shard, tall), lambda i: (i, 0, 0)),
            pl.BlockSpec((1, 1, tall), lambda i: (i, 0, 0)),
        ),
        compiler_params=pltpu.CompilerParams(vmem_limit_bytes=48 * 1024 * 1024),
        name="token_forward",
    )(every, weight_t)
    shares = token_shares(totals)
    each = tall // cap
    grad_low, grad_weight = pl.pallas_call(
        partial(token_backward, scale),
        grid=(count,),
        out_shape=(whole((2 * dp, cap, width), BF16), whole((width, shard), F32)),
        in_specs=[
            pl.BlockSpec((1, shard, tall), lambda i: (i, 0, 0)),
            pl.BlockSpec((1, 1, tall), lambda i: (i, 0, 0)),
            pl.BlockSpec((1, 1, tall), lambda i: (i, 0, 0)),
            pl.BlockSpec((tall, width), lambda i: (i, 0)),
            pl.BlockSpec((shard, width), lambda i: (0, 0)),
        ],
        out_specs=(
            pl.BlockSpec((each, cap, width), lambda i: (i, 0, 0)),
            pl.BlockSpec((width, shard), lambda i: (0, 0)),
        ),
        scratch_shapes=[VMEM((shard, width), F32)],
        compiler_params=pltpu.CompilerParams(vmem_limit_bytes=48 * 1024 * 1024),
        name="token_backward",
    )(probs, shares, labels.reshape(count, 1, tall), every, weight_t)
    back = scatter_blocks(grad_low.reshape(2, dp, cap, width))
    return mm_tn(chosen.astype(BF16), back.astype(BF16)), grad_weight


def on_chips(
    inputs, segments, delete_target, place_target, token_target, token_mask,
    attention_in, attention_out, feedforward_in, feedforward_out, norm_gain, norm_bias,
    cross_query, cross_keyvalue, cross_out, cross_gain, cross_bias,
    head_delete, head_place, head_token,
):
    phase, dp_index = lax.axis_index("phase"), lax.axis_index("dp")
    count, length, width = inputs.shape[1:]
    hidden, classes = feedforward_in.shape[2], head_place.shape[1]
    each = width // GROUPS
    scale = float(count * length * GROUPS) ** (-0.5)
    any_space = pl.BlockSpec(memory_space=pl.ANY)
    is_enc = phase == 0
    states = inputs[0].reshape(count * length, width)
    up_own, down_own = feedforward_in[0], feedforward_out[0]
    qkv_w, mix_w = attention_in[0], attention_out[0]
    delete_weight = head_delete.T
    gain_row, bias_row = cross_gain[None, :], cross_bias[None, :]
    shapes = {
        "qkv": ((count * length, 3 * width), BF16), "mixed": ((count * length, width), BF16),
        "res": ((count * length, width), F32), "after": ((2, length, width), F32),
        "res_e": ((length, width), F32), "ckv": ((length, 2 * width), BF16), "cq": ((length, width), BF16),
        "cmixed": ((length, width), BF16), "cres": ((length, width), F32),
        "hid_e": ((length, hidden), BF16), "slope_e": ((length, hidden), BF16),
        "hid_d": ((length, hidden), BF16), "slope_d": ((length, hidden), BF16),
        "res_d": ((length, width), F32), "src": ((length, width), BF16), "low": ((length, width), BF16),
        "grad_low": ((length, width), F32), "grad_place": ((GROUPS, each, 2 * classes), BF16),
        "co_w": ((width, width), BF16), "cq_w": ((width, width), BF16), "ckv_w": ((width, 2 * width), BF16),
        "mix_w": ((width, width), BF16), "qkv_w": ((width, 3 * width), BF16), "x": ((count * length, width), BF16),
        "grad_token": ((length, width), F32),
    }
    outs = pl.pallas_call(
        partial(forward_kernel, scale),
        out_shape=(
            whole((8, length), F32), whole((length, 128), F32),
            whole((1, GROUPS * length), jnp.int32), whole((1, 2 * GROUPS * length), jnp.int32), whole((1, 1), F32),
            whole((2, 2, width), F32), whole((width, hidden), BF16), whole((hidden, width), BF16),
            whole((count, HEADS, length), F32), whole((HEADS, length), F32), whole((8, width), F32),
            *[whole(*shapes[name]) for name in FORWARD],
        ),
        in_specs=in_vmem(10) + [any_space] * 5 + in_vmem(3) + [any_space],
        out_specs=tuple(in_vmem(6) + [any_space] * 2 + in_vmem(3) + [any_space] * len(FORWARD)),
        scratch_shapes=[
            *[VMEM(*shapes[name]) for name in FORWARD],
            VMEM((2, width, hidden), BF16), VMEM((2, hidden, width), BF16),
            VMEM((width, width), BF16), VMEM((width, 2 * width), BF16), VMEM((width, width), BF16),
            VMEM((2 * width, classes), BF16), VMEM((length, width), F32),
            VMEM((2, length), jnp.int32), VMEM((4, 2, 2, 2, length), jnp.int32), VMEM((128, length), F32),
            pltpu.SemaphoreType.DMA((6,)), pltpu.SemaphoreType.DMA((len(FORWARD) + 2,)),
            pltpu.SemaphoreType.DMA((20,)), pltpu.SemaphoreType.DMA((20,)),
        ],
        compiler_params=pltpu.CompilerParams(
            collective_id=1, has_side_effects=True, vmem_limit_bytes=56 * 1024 * 1024
        ),
        name="forward",
    )(
        states, segments, delete_target, place_target, token_target, token_mask,
        qkv_w, mix_w, norm_gain[0], norm_bias[0], up_own, down_own,
        cross_query, cross_keyvalue, cross_out, gain_row, bias_row, delete_weight, head_place,
    )
    rows, cols, labels_small, labels_large, most, norms, up_other, down_other, totals, ctotals, grad_delete = outs[:11]
    saved = dict(zip(FORWARD, outs[11:]))
    grad_token, grad_weight = lax.cond(
        most[0, 0] < 0.0,
        lambda: token_chips(2, length // 2, saved["low"], rows, cols, labels_small, head_token),
        lambda: token_chips(3, length, saved["low"], rows, cols, labels_large, head_token),
    )
    other_weight = swap(grad_weight)
    saved.update(co_w=cross_out, cq_w=cross_query, ckv_w=cross_keyvalue, mix_w=mix_w, qkv_w=qkv_w, x=states, grad_token=grad_token)
    half_rows, ff_half, attention_rows = 5 * each // 2, hidden // GROUPS, 4 * each
    rows_of = (ff_half, ff_half, half_rows, attention_rows)

    def shards(tall, *lead):
        return VMEM(lead + (tall, width), BF16)

    grad_states, red_ff, red_attention, red_cross, vectors = pl.pallas_call(
        backward_kernel,
        out_shape=(
            whole((count * length, width), F32), whole((2, ff_half, width), F32),
            whole((attention_rows, width), F32), whole((2, half_rows, width), F32), whole((16, width), F32),
        ),
        in_specs=in_vmem(9) + [any_space] * (8 + len(BACKWARD)),
        out_specs=tuple([any_space] + in_vmem(4)),
        scratch_shapes=[
            *[VMEM(*shapes[name]) for name in BACKWARD],
            VMEM((width, hidden), BF16), VMEM((hidden, width), BF16),
            VMEM((length, hidden), BF16), VMEM((length, hidden), BF16),
            shards(ff_half, 2, 2, 2, 2, 2), shards(ff_half, 2, 2, 2, 2, 2), shards(half_rows, 2, 2, 2, 2, 2),
            shards(attention_rows, 2, 2, 2, 2),
            shards(ff_half, 2, 2, 2, 2), shards(ff_half, 2, 2, 2, 2), shards(half_rows, 2, 2, 2, 2),
            *[shards(tall, 2, 2, 2) for tall in rows_of],
            *[shards(tall, 2, 2) for tall in rows_of],
            *[shards(tall, 2) for tall in rows_of],
            *[shards(tall) for tall in rows_of],
            VMEM((2, length, width), F32), VMEM((length, width), F32),
            VMEM((length, width), BF16), VMEM((length, 2 * width), BF16), VMEM((count * length, 3 * width), BF16),
            VMEM((2, ff_half, width), F32), VMEM((count * length, width), F32),
            VMEM((8, width), F32), VMEM((8, width), F32),
            VMEM((5, 16, width), F32), VMEM((4, 16, width), F32),
            pltpu.SemaphoreType.DMA((8,)), pltpu.SemaphoreType.DMA((len(BACKWARD) + 1,)),
            pltpu.SemaphoreType.DMA((128,)), pltpu.SemaphoreType.DMA((128,)),
        ],
        compiler_params=pltpu.CompilerParams(
            collective_id=0, has_side_effects=True, vmem_limit_bytes=62 * 1024 * 1024
        ),
        name="backward",
    )(
        rows, cols, norms, gain_row, bias_row, ctotals, totals, grad_delete, norm_gain[0],
        up_own, up_other, down_own, down_other,
        saved["hid_e"], saved["slope_e"], saved["hid_d"], saved["slope_d"],
        *[saved[name] for name in BACKWARD],
    )
    vocabulary = head_token.shape[1]
    g_qkv, g_mix, g_up, g_down, g_cq, g_ckv, g_co, g_place, g_gain, g_bias, g_cgain, g_cbias, g_delete, g_token = (
        pl.pallas_call(
            unpack_kernel,
            out_shape=(
                whole((each, 3 * width), F32), whole((each, width), F32), whole((each, hidden), F32),
                whole((hidden // GROUPS, width), F32), whole((each, width), F32), whole((each, 2 * width), F32),
                whole((each, width), F32), whole((2 * each, classes), F32),
                whole((1, 2, each), F32), whole((1, 2, each), F32), whole((1, each), F32), whole((1, each), F32),
                whole((2, each), F32), whole((width, vocabulary // GROUPS), F32),
            ),
            in_specs=[any_space] * 6,
            out_specs=tuple(in_vmem(3) + [any_space] + in_vmem(9) + [any_space]),
            scratch_shapes=[
                VMEM(red_ff.shape, F32), VMEM(red_attention.shape, F32), VMEM(red_cross.shape, F32),
                VMEM(vectors.shape, F32), VMEM((2,) + grad_weight.shape, F32),
                pltpu.SemaphoreType.DMA((5,)), pltpu.SemaphoreType.DMA((2, 2)),
            ],
            compiler_params=pltpu.CompilerParams(vmem_limit_bytes=60 * 1024 * 1024),
            name="unpack",
        )(red_ff, red_attention, red_cross, vectors, grad_weight, other_weight)
    )
    return (
        grad_states.reshape(1, count, length, width),
        g_qkv[None], g_mix[None], g_up[None], g_down[None], g_gain, g_bias,
        g_cq, g_ckv, g_co, g_cgain[0], g_cbias[0], g_delete.T, g_place, g_token,
    )


def on_any(
    inputs, segments, delete_target, place_target, token_target, token_mask,
    attention_in, attention_out, feedforward_in, feedforward_out, norm_gain, norm_bias,
    cross_query, cross_keyvalue, cross_out, cross_gain, cross_bias,
    head_delete, head_place, head_token,
):
    phase = lax.axis_index("phase")
    dp_index, dp = lax.axis_index("dp"), lax.axis_size("dp")
    count, length, width = inputs.shape[1:]
    assert count == 2
    hidden = feedforward_in.shape[2]
    scale = float(count * length * dp) ** (-0.5)
    any_space = pl.BlockSpec(memory_space=pl.ANY)
    params = pltpu.CompilerParams(vmem_limit_bytes=56 * 1024 * 1024)

    coded = jnp.where(token_mask == 1, token_target, -1)
    labels_all = lax.all_gather(coded, "dp", tiled=True)
    flags_all = (labels_all >= 0).astype(jnp.int32)

    def row_of(value):
        return lax.dynamic_index_in_dim(value, phase, 0, keepdims=False)

    own_norms = jnp.stack([norm_gain[0, 1], norm_bias[0, 1]])
    up_other, down_other = swap(feedforward_in[0]), swap(feedforward_out[0])
    other_norms = swap(own_norms)
    is_enc = phase == 0
    norms = jnp.concatenate(
        [jnp.where(is_enc, own_norms, other_norms), jnp.where(is_enc, other_norms, own_norms)]
    )
    ids = row_of(segments)
    own_ids = lax.dynamic_index_in_dim(segments, phase, 1, keepdims=False)
    states = inputs[0].reshape(count * length, width)

    qkv, mixed, res, totals, keep, send = pl.pallas_call(
        self_forward,
        out_shape=(
            whole((count * length, 3 * width), BF16),
            whole((count * length, width), BF16),
            whole((count * length, width), F32),
            whole((count, HEADS, length), F32),
            whole((length, width), F32),
            whole((length, width), F32),
        ),
        in_specs=in_vmem(7),
        out_specs=tuple(in_vmem(6)),
        compiler_params=params,
        name="self_forward",
    )(states, own_ids[:, :, None], own_ids[:, None, :], attention_in[0], attention_out[0], norm_gain[0], norm_bias[0])
    received = swap(send)

    ids_e, ids_d_row = ids[0][:, None], ids[1][None, :]
    pair_valid = jnp.concatenate([ids[1, :-1] == ids[1, 1:], jnp.zeros((1,), bool)])
    targets = jnp.stack(
        [row_of(delete_target), row_of(place_target), pair_valid.astype(jnp.int32)], axis=1
    )
    delete_weight = head_delete.T
    gain_row, bias_row = cross_gain[None, :], cross_bias[None, :]
    ff_scratch = [
        VMEM((width, hidden), BF16), VMEM((hidden, width), BF16),
        VMEM((width, hidden), BF16), VMEM((hidden, width), BF16),
    ]
    saved_shapes = (
        whole((length, width), F32),
        whole((length, width), F32),
        whole((length, width), F32),
        whole((length, 2 * width), BF16),
        whole((length, width), BF16),
        whole((length, width), BF16),
        whole((length, width), F32),
        whole((HEADS, length), F32),
        whole((length, hidden), BF16), whole((length, hidden), BF16),
        whole((length, hidden), BF16), whole((length, hidden), BF16),
        whole((length, width), F32),
        whole((length, width), BF16),
    )
    classes = head_place.shape[1]
    each = width // GROUPS
    outs = pl.pallas_call(
        partial(rows_forward, scale),
        out_shape=saved_shapes + (
            whole((length, width), BF16),
            whole((length, width), F32),
            whole((8, width), F32),
            whole((GROUPS, each, 2 * classes), BF16),
        ),
        in_specs=in_vmem(5) + [any_space] * 4 + in_vmem(8),
        out_specs=tuple(in_vmem(18)),
        scratch_shapes=ff_scratch + [pltpu.SemaphoreType.DMA((2, 2))],
        compiler_params=params,
        name="rows_forward",
    )(
        keep, received, ids_e, ids_d_row, targets,
        feedforward_in[0], up_other, feedforward_out[0], down_other, norms,
        cross_query, cross_keyvalue, cross_out, gain_row, bias_row, delete_weight, head_place,
    )
    saved = outs[:14]
    low, grad_low, grad_delete, grad_place = outs[14:]

    shard = head_token.shape[1] // (2 * dp)
    weight = lax.dynamic_slice_in_dim(head_token, (dp_index * 2 + phase) * shard, shard, 1)
    weight_t = weight.T
    flags = row_of(token_mask)

    def run_head(cap, block_rows):
        return token_head(cap, block_rows, low, flags, labels_all, flags_all, weight, weight_t, scale)

    small = length // 2
    fits = jnp.max(jnp.sum(flags_all, axis=1)) <= small
    grad_token, grad_weight = lax.cond(
        fits, lambda: run_head(small, 4 * small), lambda: run_head(length, 2 * length)
    )
    other_weight = swap(grad_weight)
    grad_head_token = jnp.concatenate(
        [jnp.where(is_enc, grad_weight, other_weight), jnp.where(is_enc, other_weight, grad_weight)], axis=1
    )

    each = width // GROUPS
    ff_rows = 2 * hidden // GROUPS
    keep, send, ff_own, ff_other, cross_shards, vectors = pl.pallas_call(
        rows_backward,
        out_shape=(
            whole((length, width), F32), whole((length, width), F32),
            whole((GROUPS, ff_rows, width), BF16), whole((GROUPS, ff_rows, width), BF16),
            whole((GROUPS, 5 * each, width), BF16), whole((8, width), F32),
        ),
        in_specs=in_vmem(4) + [any_space] * 4 + in_vmem(6 + 14 + 1),
        out_specs=(in_vmem(2) + [any_space] * 2 + in_vmem(2)),
        scratch_shapes=ff_scratch + [
            VMEM((GROUPS, ff_rows, width), BF16), VMEM((GROUPS, ff_rows, width), BF16),
            VMEM((length, width), F32), VMEM((length, width), F32),
            VMEM((length, width), BF16), VMEM((length, 2 * width), BF16),
            pltpu.SemaphoreType.DMA((2, 2)), pltpu.SemaphoreType.DMA((2,)),
        ],
        compiler_params=params,
        name="rows_backward",
    )(
        grad_low, grad_token, ids_e, ids_d_row,
        feedforward_in[0], up_other, feedforward_out[0], down_other, norms,
        cross_query, cross_keyvalue, cross_out, gain_row, bias_row, *saved, grad_place,
    )
    received = swap(send)
    ff_received = swap(ff_other)
    half_rows = 5 * each // 2
    cross_keep = lax.dynamic_slice_in_dim(cross_shards, phase * half_rows, half_rows, 1)
    cross_received = swap(lax.dynamic_slice_in_dim(cross_shards, (1 - phase) * half_rows, half_rows, 1))
    shared = jnp.concatenate([vectors[4:6], grad_delete[:2]])
    norm_own = jnp.where(is_enc, vectors[0:2], vectors[2:4])
    norm_other = jnp.where(is_enc, vectors[2:4], vectors[0:2])
    vector_received = swap(jnp.concatenate([norm_other, shared]))
    vector_sums = jnp.concatenate([norm_own, shared]) + vector_received

    grad_states, attention_shards, first_vectors = pl.pallas_call(
        self_backward,
        out_shape=(
            whole((count * length, width), F32), whole((GROUPS, 4 * each, width), BF16), whole((8, width), F32),
        ),
        in_specs=in_vmem(12),
        out_specs=tuple(in_vmem(3)),
        scratch_shapes=[VMEM((count * length, width), F32), VMEM((count * length, 3 * width), BF16)],
        compiler_params=params,
        name="self_backward",
    )(
        keep, received, states, own_ids[:, :, None], own_ids[:, None, :], attention_in[0], attention_out[0],
        norm_gain[0], qkv, mixed, res, totals,
    )

    all_vectors = jnp.stack([
        first_vectors[0], vector_sums[0], first_vectors[1], vector_sums[1],
        vector_sums[2], vector_sums[3], vector_sums[4], vector_sums[5],
    ])
    ff_sum = (ff_own.astype(F32) + ff_received.astype(F32)).astype(BF16)
    cross_sum = (cross_keep.astype(F32) + cross_received.astype(F32)).astype(BF16)
    cross_other = swap(cross_sum)
    cross_all = jnp.concatenate(
        [jnp.where(is_enc, cross_sum, cross_other), jnp.where(is_enc, cross_other, cross_sum)], axis=1
    )
    ff_up = hidden // width * each

    def spread(value):
        return lax.psum_scatter(value.astype(F32), "dp", scatter_dimension=0, tiled=True)

    g_qkv = spread(unpacked(attention_shards[:, : 3 * each], width, 3 * width))
    g_mix = spread(unpacked(attention_shards[:, 3 * each :], width, width))
    g_up = spread(unpacked(ff_sum[:, :ff_up], width, hidden))
    g_down = spread(unpacked(ff_sum[:, ff_up:], hidden, width))
    g_cq = spread(unpacked(cross_all[:, :each], width, width))
    g_ckv = spread(unpacked(cross_all[:, each : 3 * each], width, 2 * width))
    g_co = spread(unpacked(cross_all[:, 3 * each : 4 * each], width, width))
    place = cross_all[:, 4 * each :].reshape(GROUPS, each, 2, classes)
    g_place = spread(place.transpose(0, 2, 1, 3).reshape(2 * width, classes))
    vector_out = lax.psum_scatter(all_vectors, "dp", scatter_dimension=1, tiled=True)
    return (
        grad_states.reshape(1, count, length, width),
        g_qkv[None], g_mix[None], g_up[None], g_down[None],
        vector_out[None, 0:2], vector_out[None, 2:4],
        g_cq, g_ckv, g_co, vector_out[4], vector_out[5], vector_out[6:8].T, g_place, grad_head_token,
    )


def on_device(*args):
    chips = lax.axis_size("dp") == GROUPS and args[0].shape[1] == 2
    return on_chips(*args) if chips else on_any(*args)


def solution(mesh):
    layer, row = P("phase", None, None), P("dp", None)
    return jax.shard_map(
        on_device,
        mesh=mesh,
        in_specs=(P("phase", "dp", None, None), P("dp", None, None), row, row, row, row)
        + (layer,) * 6 + (P(),) * 8,
        out_specs=(P("phase", "dp", None, None),) + (P("phase", "dp", None),) * 4
        + (P("phase", None, "dp"),) * 2 + (row,) * 3 + (P("dp"),) * 2 + (row,) * 2 + (P(None, "dp"),),
        check_vma=False,
    )
```

```python
from functools import partial

import jax
import jax.numpy as jnp
from jax import lax
from jax.experimental import pallas as pl
from jax.experimental.pallas import tpu as pltpu
from jax.sharding import PartitionSpec as P

HEADS = 8
HEAD = 64
PAIR = 2 * HEAD
MASKED_SCORE = -1e30
NORM_EPSILON = 1e-05
GROUPS = 16
F32 = jnp.float32
BF16 = jnp.bfloat16
MESH = pl.DeviceIdType.MESH
VMEM = pltpu.VMEM
GELU_C = 0.7978845608028654
GELU_A = 0.044715


def mm(left, right):
    return jnp.dot(left, right, preferred_element_type=F32)


def mm_nt(left, right):
    return lax.dot_general(left, right, (((1,), (1,)), ((), ())), preferred_element_type=F32)


def mm_tn(left, right):
    return lax.dot_general(left, right, (((0,), (0,)), ((), ())), preferred_element_type=F32)


def norm_forward(residual, gain, bias):
    centered = residual - jnp.mean(residual, axis=-1, keepdims=True)
    variance = jnp.mean(centered * centered, axis=-1, keepdims=True)
    return centered * lax.rsqrt(variance + NORM_EPSILON) * gain + bias


def norm_back(residual, gain, grad_out):
    centered = residual - jnp.mean(residual, axis=-1, keepdims=True)
    variance = jnp.mean(centered * centered, axis=-1, keepdims=True)
    scale = lax.rsqrt(variance + NORM_EPSILON)
    unit = centered * scale
    grad_unit = grad_out * gain
    grad_gain = jnp.sum(grad_out * unit, axis=0, keepdims=True)
    grad_bias = jnp.sum(grad_out, axis=0, keepdims=True)
    grad_res = scale * (
        grad_unit
        - jnp.mean(grad_unit, axis=-1, keepdims=True)
        - unit * jnp.mean(grad_unit * unit, axis=-1, keepdims=True)
    )
    return grad_res, grad_gain, grad_bias


def gelu_both(pre):
    square = pre * pre
    bent = jnp.tanh(GELU_C * pre * (1.0 + GELU_A * square))
    half = 0.5 * (1.0 + bent)
    slope = half + (0.5 * GELU_C) * pre * (1.0 - bent * bent) * (1.0 + 3.0 * GELU_A * square)
    return pre * half, slope


def attend_forward(queries, keys, values, allowed, out_ref, totals_ref, rows):
    lane = lax.broadcasted_iota(jnp.int32, (1, PAIR), 1)
    for pair in range(HEADS // 2):
        q, k, v = queries(pair), keys(pair), values(pair)
        mixed = None
        for side in range(2):
            own = (lane < HEAD) if side == 0 else (lane >= HEAD)
            scores = mm_nt(k, jnp.where(own, q * HEAD ** (-0.5), 0))
            scores = jnp.where(allowed, scores, MASKED_SCORE)
            top = jnp.max(scores, axis=0, keepdims=True)
            weights = jnp.exp(scores - top)
            summed = jnp.sum(weights, axis=0, keepdims=True)
            probs = (weights * (1.0 / summed)).astype(BF16)
            totals_ref[2 * pair + side : 2 * pair + side + 1, :] = top + jnp.log(summed)
            part = mm_tn(probs, jnp.where(own, v, 0))
            mixed = part if mixed is None else mixed + part
        out_ref[rows, pair * PAIR : (pair + 1) * PAIR] = mixed.astype(BF16)


def attend_backward(
    queries, keys, values, grads, allowed, totals_ref, put_q, put_k, put_v, between=None
):
    lane = lax.broadcasted_iota(jnp.int32, (1, PAIR), 1)
    for pair in range(HEADS // 2):
        q, k, v, da = queries(pair), keys(pair), values(pair), grads(pair)
        grad_q = grad_k = grad_v = None
        for side in range(2):
            own = (lane < HEAD) if side == 0 else (lane >= HEAD)
            q_own = jnp.where(own, q * HEAD ** (-0.5), 0)
            da_own = jnp.where(own, da, 0)
            scores = jnp.where(allowed, mm_nt(k, q_own), MASKED_SCORE)
            probs = jnp.exp(scores - totals_ref[2 * pair + side : 2 * pair + side + 1, :])
            grad_probs = mm_nt(v, da_own)
            part_v = mm(probs.astype(BF16), da_own)
            shared = jnp.sum(probs * grad_probs, axis=0, keepdims=True)
            grad_scores = (probs * (grad_probs - shared)).astype(BF16)
            part_k = mm(grad_scores, q_own)
            part_q = mm_tn(grad_scores, jnp.where(own, k, 0))
            grad_q = part_q if grad_q is None else grad_q + part_q
            grad_k = part_k if grad_k is None else grad_k + part_k
            grad_v = part_v if grad_v is None else grad_v + part_v
        put_q(pair, (grad_q * HEAD ** (-0.5)).astype(BF16))
        put_k(pair, grad_k.astype(BF16))
        put_v(pair, grad_v.astype(BF16))
        if between is not None:
            between(pair)


def column(pair, offset=0):
    return slice(offset + pair * PAIR, offset + (pair + 1) * PAIR)


def put_shards(ref, first, grad):
    height = grad.shape[0] // GROUPS
    width = ref.shape[2]
    for block in range(grad.shape[1] // width):
        piece = grad[:, block * width : (block + 1) * width].astype(BF16)
        ref[:, first + block * height : first + (block + 1) * height, :] = piece.reshape(
            GROUPS, height, width
        )


def self_forward(
    x_ref, ids_ref, ids_row_ref, qkv_w_ref, mix_w_ref, gain_ref, bias_ref,
    qkv_ref, mixed_ref, res_ref, totals_ref, keep_ref, send_ref,
):
    phase = lax.axis_index("phase")
    count, length = ids_ref.shape[0], ids_ref.shape[1]
    width = x_ref.shape[1]
    for part in range(3):
        cols = slice(part * width, (part + 1) * width)
        qkv_ref[:, cols] = mm(x_ref[...], qkv_w_ref[:, cols]).astype(BF16)
    for row in range(count):
        rows = slice(row * length, (row + 1) * length)
        attend_forward(
            lambda pair: qkv_ref[rows, column(pair)],
            lambda pair: qkv_ref[rows, column(pair, width)],
            lambda pair: qkv_ref[rows, column(pair, 2 * width)],
            ids_ref[row] == ids_row_ref[row],
            mixed_ref, totals_ref.at[row], rows,
        )
    for row in range(count):
        rows = slice(row * length, (row + 1) * length)
        residual = x_ref[rows, :].astype(F32) + mm(mixed_ref[rows, :], mix_w_ref[...])
        res_ref[rows, :] = residual
        after = norm_forward(residual, gain_ref[0:1, :], bias_ref[0:1, :])

        @pl.when(phase == row)
        def _():
            keep_ref[...] = after

        @pl.when(phase != row)
        def _():
            send_ref[...] = after


def load_sided(phase, own_refs, other_refs, enc_refs, dec_refs, sems):
    for i, (own, other, enc, dec) in enumerate(zip(own_refs, other_refs, enc_refs, dec_refs)):
        @pl.when(phase == 0)
        def _():
            pltpu.make_async_copy(own, enc, sems.at[0, i]).start()
            pltpu.make_async_copy(other, dec, sems.at[1, i]).start()

        @pl.when(phase != 0)
        def _():
            pltpu.make_async_copy(other, enc, sems.at[0, i]).start()
            pltpu.make_async_copy(own, dec, sems.at[1, i]).start()

    def wait_enc(i):
        pltpu.make_async_copy(own_refs[i], enc_refs[i], sems.at[0, i]).wait()

    def wait_dec(i):
        pltpu.make_async_copy(own_refs[i], dec_refs[i], sems.at[1, i]).wait()

    return wait_enc, wait_dec


def feed_forward(middle, up_ref, down_ref, hidden_ref, slope_ref):
    width = middle.shape[1]
    low = middle.astype(BF16)
    total = middle
    for part in range(up_ref.shape[1] // width):
        cols = slice(part * width, (part + 1) * width)
        hidden, slope = gelu_both(mm(low, up_ref[:, cols]))
        hidden = hidden.astype(BF16)
        hidden_ref[:, cols] = hidden
        slope_ref[:, cols] = slope.astype(BF16)
        total = total + mm(hidden, down_ref[cols, :])
    return total


def feed_back(grad_res, middle_low, up_ref, down_ref, hidden_ref, slope_ref, put_up, put_down, between=None):
    width = grad_res.shape[1]
    branch = grad_res.astype(BF16)
    total = grad_res
    for part in range(up_ref.shape[1] // width):
        cols = slice(part * width, (part + 1) * width)
        put_down(part, mm_tn(hidden_ref[:, cols], branch))
        grad_hidden = mm_nt(branch, down_ref[cols, :])
        grad_pre = (grad_hidden * slope_ref[:, cols].astype(F32)).astype(BF16)
        put_up(part, mm_tn(middle_low, grad_pre))
        total = total + mm_nt(grad_pre, up_ref[:, cols])
        if between is not None:
            between(part)
    return total


def feed_puts(ref, parts):
    width = ref.shape[2]
    rows = width // GROUPS
    per, tall = GROUPS // parts, parts * rows

    def put_up(part, value):
        put_shards(ref, part * rows, value)

    def put_down(part, value):
        ref[part * per : (part + 1) * per, tall : 2 * tall, :] = value.astype(BF16).reshape(
            per, tall, width
        )

    return put_up, put_down


def class_grads(logits, labels, row_weight, valid):
    lane = lax.broadcasted_iota(jnp.int32, logits.shape, 1)
    logits = jnp.where(lane < valid, logits, -jnp.inf) if valid < logits.shape[1] else logits
    top = jnp.max(logits, axis=-1, keepdims=True)
    weights = jnp.exp(logits - top)
    probs = weights * (1.0 / jnp.sum(weights, axis=-1, keepdims=True))
    return (probs - (lane == labels).astype(F32)) * row_weight


def rows_forward(
    scale, keep_ref, recv_ref, ids_e_ref, ids_d_row_ref, targets_ref,
    up_own, up_other, down_own, down_other, norms_ref,
    cq_w_ref, ckv_w_ref, co_w_ref, cgain_ref, cbias_ref, delete_w_ref, place_w_ref,
    after_e_ref, res_e_ref, after_d_ref, ckv_ref, cq_ref, cmixed_ref, cres_ref, ctotals_ref,
    hid_e_ref, slope_e_ref, hid_d_ref, slope_d_ref, res_d_ref, src_ref,
    low_ref, grad_ref, grad_delete_ref, grad_place_ref,
    up_e, down_e, up_d, down_d, sems,
):
    phase = lax.axis_index("phase")
    width = keep_ref.shape[1]
    wait_enc, wait_dec = load_sided(
        phase, (up_own, down_own), (up_other, down_other), (up_e, down_e), (up_d, down_d), sems
    )

    @pl.when(phase == 0)
    def _():
        after_e_ref[...] = keep_ref[...]
        after_d_ref[...] = recv_ref[...]

    @pl.when(phase != 0)
    def _():
        after_e_ref[...] = recv_ref[...]
        after_d_ref[...] = keep_ref[...]

    wait_enc(0)
    wait_enc(1)
    encoder_rows(
        after_e_ref, up_e, down_e, norms_ref[0:1, :], norms_ref[1:2, :], ckv_w_ref,
        hid_e_ref, slope_e_ref, res_e_ref, src_ref, ckv_ref,
    )
    middle = cross_rows(
        after_d_ref, ids_e_ref[...] == ids_d_row_ref[...], cq_w_ref, co_w_ref, cgain_ref, cbias_ref,
        cq_ref, ckv_ref, cmixed_ref, cres_ref, ctotals_ref,
    )
    wait_dec(0)
    wait_dec(1)
    targets = targets_ref[...]
    decoder_rows(
        scale, middle, up_d, down_d, norms_ref[2:3, :], norms_ref[3:4, :],
        targets[:, 0:1], targets[:, 1:2], targets[:, 2:3], delete_w_ref, place_w_ref,
        hid_d_ref, slope_d_ref, res_d_ref, low_ref, grad_ref, grad_delete_ref, grad_place_ref,
    )


def encoder_rows(
    after_ref, up, down, gain, bias, ckv_w_ref, hid_ref, slope_ref, res_ref, src_ref, ckv_ref
):
    residual = feed_forward(after_ref[...], up, down, hid_ref, slope_ref)
    res_ref[...] = residual
    src = norm_forward(residual, gain, bias).astype(BF16)
    src_ref[...] = src
    width = src.shape[1]
    for part in range(2):
        cols = slice(part * width, (part + 1) * width)
        ckv_ref[:, cols] = mm(src, ckv_w_ref[:, cols]).astype(BF16)


def cross_rows(
    after_ref, allowed, cq_w_ref, co_w_ref, cgain_ref, cbias_ref, cq_ref, ckv_ref, cmixed_ref, cres_ref, ctotals_ref
):
    width = after_ref.shape[1]
    cq_ref[...] = mm(after_ref[...].astype(BF16), cq_w_ref[...]).astype(BF16)
    attend_forward(
        lambda pair: cq_ref[:, column(pair)],
        lambda pair: ckv_ref[:, column(pair)],
        lambda pair: ckv_ref[:, column(pair, width)],
        allowed, cmixed_ref, ctotals_ref, slice(None),
    )
    residual = after_ref[...] + mm(cmixed_ref[...], co_w_ref[...])
    cres_ref[...] = residual
    return norm_forward(residual, cgain_ref[...], cbias_ref[...])


def decoder_rows(
    scale, middle, up, down, gain, bias, delete_label, place_label, pair_valid, delete_w_ref, place_w_ref,
    hid_ref, slope_ref, res_ref, low_ref, grad_ref, grad_delete_ref, grad_place_ref,
):
    residual = feed_forward(middle, up, down, hid_ref, slope_ref)
    res_ref[...] = residual
    low = norm_forward(residual, gain, bias).astype(BF16)
    low_ref[...] = low
    length, width = low.shape
    valid = delete_w_ref.shape[0]
    weight = jnp.concatenate([delete_w_ref[...], jnp.zeros((128 - valid, width), BF16)], axis=0)
    grads = class_grads(mm_nt(low, weight), delete_label, scale, valid).astype(BF16)
    grad_delete_ref[...] = mm_tn(grads, low)[:8]
    grad_low = mm(grads, weight)
    logits = mm(low, place_w_ref[:width, :]) + pltpu.roll(
        mm(low, place_w_ref[width:, :]), length - 1, 0
    )
    weight = pair_valid.astype(F32) * scale
    grads = class_grads(logits, place_label, weight, logits.shape[1])
    later = pltpu.roll(grads, 1, 0).astype(BF16)
    grads = grads.astype(BF16)
    classes = grads.shape[1]
    for top, part in enumerate((grads, later)):
        part = mm_tn(low, part).astype(BF16).reshape(GROUPS // 2, 2, width // GROUPS, classes)
        at = slice(top * GROUPS // 2, (top + 1) * GROUPS // 2)
        for half in range(2):
            grad_place_ref[at, :, half * classes : (half + 1) * classes] = part[:, half]
    grad_low = grad_low + mm_nt(grads, place_w_ref[:width, :]) + mm_nt(later, place_w_ref[width:, :])
    grad_ref[...] = grad_low


def rows_backward(
    grad_low_ref, grad_token_ref, ids_e_ref, ids_d_row_ref,
    up_own, up_other, down_own, down_other, norms_ref,
    cq_w_ref, ckv_w_ref, co_w_ref, cgain_ref, cbias_ref,
    after_e_ref, res_e_ref, after_d_ref, ckv_ref, cq_ref, cmixed_ref, cres_ref, ctotals_ref,
    hid_e_ref, slope_e_ref, hid_d_ref, slope_d_ref, res_d_ref, src_ref, grad_place_ref,
    keep_ref, send_ref, own_ref, other_ref, cross_ref, vectors_ref,
    up_e, down_e, up_d, down_d, grad_e, grad_d, after_e_grad, after_d_grad, gq_ref, gckv_ref, sems, out_sems,
):
    phase = lax.axis_index("phase")
    width = grad_low_ref.shape[1]
    wait_enc, wait_dec = load_sided(
        phase, (up_own, down_own), (up_other, down_other), (up_e, down_e), (up_d, down_d), sems
    )
    grad_out = grad_low_ref[...] + grad_token_ref[...]
    grad_res, gain_grad, bias_grad = norm_back(res_d_ref[...], norms_ref[2:3, :], grad_out)
    vectors_ref[2:3, :] = gain_grad
    vectors_ref[3:4, :] = bias_grad
    cres = cres_ref[...]
    middle_low = norm_forward(cres, cgain_ref[...], cbias_ref[...]).astype(BF16)
    wait_dec(0)
    wait_dec(1)
    grad_middle = feed_back(grad_res, middle_low, up_d, down_d, hid_d_ref, slope_d_ref, *feed_puts(grad_d, 4))
    move_d = [
        pltpu.make_async_copy(grad_d, own_ref, out_sems.at[0]),
        pltpu.make_async_copy(grad_d, other_ref, out_sems.at[0]),
    ]

    @pl.when(phase == 0)
    def _():
        move_d[1].start()

    @pl.when(phase != 0)
    def _():
        move_d[0].start()

    grad_res, gain_grad, bias_grad = norm_back(cres, cgain_ref[...], grad_middle)
    vectors_ref[4:5, :] = gain_grad
    vectors_ref[5:6, :] = bias_grad
    branch = grad_res.astype(BF16)
    after_low = after_d_ref[...].astype(BF16)
    rows = width // GROUPS
    put_shards(cross_ref, 3 * rows, mm_tn(cmixed_ref[...], branch))
    grad_mixed = mm_nt(branch, co_w_ref[...]).astype(BF16)

    def put_q(pair, value):
        gq_ref[:, column(pair)] = value

    def put_k(pair, value):
        gckv_ref[:, column(pair)] = value

    def put_v(pair, value):
        gckv_ref[:, column(pair, width)] = value

    attend_backward(
        lambda pair: cq_ref[:, column(pair)],
        lambda pair: ckv_ref[:, column(pair)],
        lambda pair: ckv_ref[:, column(pair, width)],
        lambda pair: grad_mixed[:, column(pair)],
        ids_e_ref[...] == ids_d_row_ref[...],
        ctotals_ref, put_q, put_k, put_v,
    )
    grad_q = gq_ref[...]
    grad_kv = gckv_ref[...]
    put_shards(cross_ref, 0, mm_tn(after_low, grad_q))
    put_shards(cross_ref, rows, mm_tn(src_ref[...], grad_kv))
    cross_ref[:, 4 * rows : 5 * rows, :] = grad_place_ref[...]
    after_d_grad[...] = grad_res + mm_nt(grad_q, cq_w_ref[...])
    grad_src = mm_nt(grad_kv, ckv_w_ref[...]).astype(BF16).astype(F32)
    grad_res, gain_grad, bias_grad = norm_back(res_e_ref[...], norms_ref[0:1, :], grad_src)
    vectors_ref[0:1, :] = gain_grad
    vectors_ref[1:2, :] = bias_grad
    vectors_ref[6:8, :] = jnp.zeros((2, width), F32)
    wait_enc(0)
    wait_enc(1)
    after_e_grad[...] = feed_back(
        grad_res, after_e_ref[...].astype(BF16), up_e, down_e, hid_e_ref, slope_e_ref,
        *feed_puts(grad_e, 4),
    )
    move_e = [
        pltpu.make_async_copy(grad_e, own_ref, out_sems.at[1]),
        pltpu.make_async_copy(grad_e, other_ref, out_sems.at[1]),
    ]

    @pl.when(phase == 0)
    def _():
        move_e[0].start()
        keep_ref[...] = after_e_grad[...]
        send_ref[...] = after_d_grad[...]

    @pl.when(phase != 0)
    def _():
        move_e[1].start()
        keep_ref[...] = after_d_grad[...]
        send_ref[...] = after_e_grad[...]

    move_d[0].wait()
    move_e[0].wait()


def self_backward(
    keep_ref, recv_ref, x_ref, ids_ref, ids_row_ref, qkv_w_ref, mix_w_ref, gain_ref,
    qkv_ref, mixed_ref, res_ref, totals_ref,
    grad_x_ref, shards_ref, vectors_ref,
    after_grad, grad_qkv,
):
    phase = lax.axis_index("phase")
    count, length = ids_ref.shape[0], ids_ref.shape[1]
    width = x_ref.shape[1]
    for row in range(count):
        rows = slice(row * length, (row + 1) * length)

        @pl.when(phase == row)
        def _():
            after_grad[rows, :] = keep_ref[...]

        @pl.when(phase != row)
        def _():
            after_grad[rows, :] = recv_ref[...]

    grad_res, gain_grad, bias_grad = norm_back(res_ref[...], gain_ref[0:1, :], after_grad[...])
    vectors_ref[0:1, :] = gain_grad
    vectors_ref[1:2, :] = bias_grad
    vectors_ref[2:8, :] = jnp.zeros((6, width), F32)
    grad_x_ref[...] = grad_res
    branch = grad_res.astype(BF16)
    rows_each = width // GROUPS
    put_shards(shards_ref, 3 * rows_each, mm_tn(mixed_ref[...], branch))
    grad_mixed = mm_nt(branch, mix_w_ref[...]).astype(BF16)
    for row in range(count):
        rows = slice(row * length, (row + 1) * length)

        def put(offset):
            def store(pair, value):
                grad_qkv[rows, column(pair, offset)] = value

            return store

        attend_backward(
            lambda pair: qkv_ref[rows, column(pair)],
            lambda pair: qkv_ref[rows, column(pair, width)],
            lambda pair: qkv_ref[rows, column(pair, 2 * width)],
            lambda pair: grad_mixed[rows, column(pair)],
            ids_ref[row] == ids_row_ref[row],
            totals_ref.at[row], put(0), put(width), put(2 * width),
        )
    for part in range(3):
        cols = slice(part * width, (part + 1) * width)
        put_shards(shards_ref, part * rows_each, mm_tn(x_ref[...], grad_qkv[:, cols]))
    grad_x_ref[...] += mm_nt(grad_qkv[...], qkv_w_ref[...])


def token_forward(low_ref, weight_ref, probs_ref, totals_ref):
    logits = mm_nt(weight_ref[...], low_ref[...])
    top = jnp.max(logits, axis=0, keepdims=True)
    weights = jnp.exp(logits - top)
    summed = jnp.sum(weights, axis=0, keepdims=True)
    probs_ref[0] = (weights * (1.0 / summed)).astype(BF16)
    totals_ref[0] = top + jnp.log(summed)


def token_backward(
    scale, probs_ref, share_ref, label_ref, low_ref, weight_ref, grad_low_ref, grad_weight_ref, total
):
    step = pl.program_id(0)
    labels = label_ref[0]
    shape = probs_ref.shape[1:]
    offset = (lax.axis_index("dp") * 2 + lax.axis_index("phase")) * shape[0]
    chosen = lax.broadcasted_iota(jnp.int32, shape, 0) == labels - offset
    grads = probs_ref[0].astype(F32) * share_ref[0] - chosen.astype(F32)
    grads = (grads * jnp.where(labels >= 0, scale, 0.0)).astype(BF16)
    grad_low = mm_tn(grads, weight_ref[...]).astype(BF16)
    cap = grad_low_ref.shape[1]
    for block in range(grad_low_ref.shape[0]):
        grad_low_ref[block] = grad_low[block * cap : (block + 1) * cap]
    part = mm(grads, low_ref[...])

    @pl.when(step == 0)
    def _():
        total[...] = part

    @pl.when(step != 0)
    def _():
        total[...] += part

    @pl.when(step == pl.num_programs(0) - 1)
    def _():
        grad_weight_ref[...] = total[...].T


def place_of(dp):
    return lax.rem(dp, 2), lax.rem(dp // 2, 2), dp // 4


def index_of(x, y, z):
    return (z * 2 + y) * 2 + x


def greet(devices):
    barrier = pltpu.get_barrier_semaphore()
    for dp, phase in devices:
        pl.semaphore_signal(barrier, inc=1, device_id=(dp, phase), device_id_type=MESH)
    return lambda: pl.semaphore_wait(barrier, len(devices))


def remote(src, dst, send, recv, device):
    return pltpu.make_async_remote_copy(
        src_ref=src, dst_ref=dst, send_sem=send, recv_sem=recv, device_id=device, device_id_type=MESH
    )


def gather_blocks(block):
    return lax.all_gather(lax.all_gather(block, "dp"), "phase")


def scatter_blocks(part):
    part = lax.psum_scatter(part.astype(F32), "phase", scatter_dimension=0, tiled=False)
    return lax.psum_scatter(part, "dp", scatter_dimension=0, tiled=False)


def token_shares(totals):
    top = lax.pmax(totals, ("dp", "phase"))
    return jnp.exp(totals - top) / lax.psum(jnp.exp(totals - top), ("dp", "phase"))


def pack_labels(labels, flags, out_ref):
    count, length = labels.shape
    before = lax.broadcasted_iota(jnp.int32, (length, length), 0)
    after = lax.broadcasted_iota(jnp.int32, (length, length), 1)
    upto = jnp.where(before <= after, 1.0, 0.0).astype(BF16)
    rows = jnp.concatenate([flags.astype(F32)] + [jnp.zeros((8 - count, length), F32)], axis=0)
    place = mm(rows.astype(BF16), upto)
    for row in range(count):
        flag = rows[row : row + 1]
        chosen = (before.astype(F32) == place[row : row + 1] - 1.0) & (flag > 0.0)
        label = labels[row : row + 1]
        high = lax.shift_right_logical(label, 8)
        parts = [high.astype(F32), (label - high * 256).astype(F32), flag, jnp.zeros((5, length), F32)]
        found = mm_nt(
            jnp.concatenate(parts, axis=0).astype(BF16), jnp.where(chosen, 1.0, 0.0).astype(BF16)
        )
        packed = jnp.where(found[2:3] > 0.5, found[0:1] * 256.0 + found[1:2], -1.0)
        out_ref[row : row + 1, :] = packed.astype(jnp.int32)


FORWARD = (
    "qkv", "mixed", "res", "after", "res_e", "ckv", "cq", "cmixed", "cres",
    "hid_e", "slope_e", "hid_d", "slope_d", "res_d", "src", "low", "grad_low", "grad_place",
)


def forward_kernel(
    scale, x_ref, segments_ref, delete_ref, place_ref, token_ref, mask_ref,
    qkv_w_ref, mix_w_ref, gain_ref, bias_ref, up_own, down_own,
    cq_w_any, ckv_w_any, co_w_any, cgain_ref, cbias_ref, delete_w_ref, place_w_any,
    rows_ref, cols_ref, labels_small_ref, labels_large_ref, most_ref, norms_ref, up_other, down_other,
    totals_ref, ctotals_ref, grad_delete_ref, *rest,
):
    outs, rest = dict(zip(FORWARD, rest)), rest[len(FORWARD) :]
    held, rest = dict(zip(FORWARD, rest)), rest[len(FORWARD) :]
    up, down, cq_w, ckv_w, co_w, place_w, send_after, own_labels, all_labels, turned, load, store, send, recv = rest
    dp, phase = lax.axis_index("dp"), lax.axis_index("phase")
    x, y, z = place_of(dp)
    chips = [
        (lax.rem(x + a, 2), lax.rem(y + b, 2), lax.rem(z + c, 4))
        for c in range(4) for b in range(2) for a in range(2) if a + b + c
    ]
    core = (dp, 1 - phase)
    met = greet([(index_of(*chip), phase) for chip in chips] + [core])
    copies, stores = [], []

    def remote_to(src, dst, device):
        i = len(copies)
        copy = remote(src, dst, send.at[i], recv.at[i], device)
        copy.start()
        copies.append(copy)
        return copy

    def save(*names):
        for name in names:
            copy = pltpu.make_async_copy(held[name], outs[name], store.at[len(stores)])
            copy.start()
            stores.append(copy)

    loads = [
        pltpu.make_async_copy(src, dst, load.at[i])
        for i, (src, dst) in enumerate((
            (up_own, up.at[phase]), (down_own, down.at[phase]), (ckv_w_any, ckv_w), (cq_w_any, cq_w),
            (co_w_any, co_w), (place_w_any, place_w),
        ))
    ]
    for copy in loads:
        copy.start()
    norms_ref[phase, 0:1, :] = gain_ref[1:2, :]
    norms_ref[phase, 1:2, :] = bias_ref[1:2, :]
    pack_labels(token_ref[...], mask_ref[...], own_labels)
    all_labels[z, y, x] = own_labels[...]
    width = x_ref.shape[1]
    qkv, mixed, res = held["qkv"], held["mixed"], held["res"]
    for part in range(3):
        span = slice(part * width, (part + 1) * width)
        qkv[:, span] = mm(x_ref[...], qkv_w_ref[:, span]).astype(BF16)
    save("qkv")
    met()
    from_norms = remote_to(norms_ref.at[phase], norms_ref.at[phase], core)
    from_up = remote_to(up_own, up.at[phase], core)
    from_down = remote_to(down_own, down.at[phase], core)
    for chip in chips:
        remote_to(own_labels, all_labels.at[z, y, x], (index_of(*chip), phase))
    label_copies = copies[3:]
    is_enc = phase == 0
    segments = segments_ref[...].astype(F32)
    length = segments.shape[2]

    def pick(first, second):
        return jnp.where(is_enc, first, second)

    def own_row(ref):
        value = ref[...].astype(F32)
        return pick(value[0:1], value[1:2])

    ids_e = pick(segments[0, 0:1], segments[1, 0:1])
    ids_d = pick(segments[0, 1:2], segments[1, 1:2])
    own_ids = [pick(segments[r, 0:1], segments[r, 1:2]) for r in range(2)]
    block = jnp.concatenate([ids_d] * 8, axis=0)
    later = pltpu.roll(block, length - 1, 1)
    lane = lax.broadcasted_iota(jnp.int32, (8, length), 1)
    valid = jnp.where((block == later) & (lane < length - 1), 1.0, 0.0)[0:1]
    rows = jnp.concatenate(
        own_ids + [ids_e, ids_d, own_row(delete_ref), own_row(place_ref), valid, own_row(mask_ref)], axis=0
    )
    rows_ref[...] = rows
    turned[...] = jnp.zeros(turned.shape, F32)
    turned[0:8, :] = rows
    cols = turned[...].T
    cols_ref[...] = cols
    for turn in range(2):
        row = 1 - phase if turn == 0 else phase
        span = pl.ds(pl.multiple_of(row * length, length), length)
        allowed = jnp.where(row == 0, cols[:, 0:1], cols[:, 1:2]) == jnp.where(
            row == 0, own_ids[0], own_ids[1]
        )
        attend_forward(
            lambda pair: qkv[span, column(pair)],
            lambda pair: qkv[span, column(pair, width)],
            lambda pair: qkv[span, column(pair, 2 * width)],
            allowed, mixed, totals_ref.at[row], span,
        )
        residual = x_ref[span, :].astype(F32) + mm(mixed[span, :], mix_w_ref[...])
        res[span, :] = residual
        after = norm_forward(residual, gain_ref[0:1, :], bias_ref[0:1, :])
        if turn == 0:
            send_after[...] = after
            from_after = remote_to(send_after, held["after"].at[phase], core)
        else:
            held["after"][phase] = after
    save("mixed", "res")
    from_after.wait_recv()
    save("after")
    from_norms.wait_recv()
    from_up.wait_recv()
    from_down.wait_recv()
    for copy in loads:
        copy.wait()
    for i, (src, dst) in enumerate(((up, up_other), (down, down_other))):
        copy = pltpu.make_async_copy(src.at[1 - phase], dst, store.at[len(stores)])
        copy.start()
        stores.append(copy)
    encoder_rows(
        held["after"].at[0], up.at[0], down.at[0], norms_ref[0, 0:1, :], norms_ref[0, 1:2, :], ckv_w,
        held["hid_e"], held["slope_e"], held["res_e"], held["src"], held["ckv"],
    )
    save("hid_e", "slope_e", "res_e", "src", "ckv")
    middle = cross_rows(
        held["after"].at[1], cols[:, 2:3] == rows[3:4], cq_w, co_w, cgain_ref, cbias_ref,
        held["cq"], held["ckv"], held["cmixed"], held["cres"], ctotals_ref,
    )
    save("cq", "cmixed", "cres")
    decoder_rows(
        scale, middle, up.at[1], down.at[1], norms_ref[1, 0:1, :], norms_ref[1, 1:2, :],
        cols[:, 4:5].astype(jnp.int32), cols[:, 5:6].astype(jnp.int32), cols[:, 6:7], delete_w_ref, place_w,
        held["hid_d"], held["slope_d"], held["res_d"], held["low"], held["grad_low"],
        grad_delete_ref, held["grad_place"],
    )
    save("hid_d", "slope_d", "res_d", "low", "grad_low", "grad_place")
    for copy in label_copies:
        copy.wait_recv()
    small = length // 2
    for at, (p, yy, xx, zz) in enumerate(
        (p, yy, xx, zz) for p in range(2) for yy in range(2) for xx in range(2) for zz in range(4)
    ):
        line = all_labels[zz, yy, xx, p : p + 1, :]
        labels_small_ref[:, at * small : (at + 1) * small] = line[:, :small]
        labels_large_ref[:, at * length : (at + 1) * length] = line
    beyond = jnp.max(all_labels[:, :, :, :, small:].astype(F32).reshape(2 * GROUPS, length - small))
    most_ref[...] = jnp.full(most_ref.shape, beyond, F32)
    for copy in copies:
        copy.wait_send()
    for copy in stores:
        copy.wait()


def token_kernel(
    scale, cap, low_ref, rows_ref, cols_ref, labels_ref, head_any,
    grad_ref, grad_weight_ref,
    weight, weight_t, every, probs, totals, near_in, joined, far_in, shares,
    part, core_in, third_in, second_in, z_in, load, send, recv,
):
    dp, phase = lax.axis_index("dp"), lax.axis_index("phase")
    x, y, z = place_of(dp)
    x_first = phase == 0
    x2, y2 = jnp.where(x_first, 1 - x, x), jnp.where(x_first, y, 1 - y)
    x3, y3 = jnp.where(x_first, x, 1 - x), jnp.where(x_first, 1 - y, y)
    second, third, core = (index_of(x2, y2, z), phase), (index_of(x3, y3, z), phase), (dp, 1 - phase)
    zs = [lax.rem(z + k, 4) for k in (1, 2, 3)]
    along = [(index_of(x, y, k), phase) for k in zs]
    shard, length = weight_t.shape[0], low_ref.shape[0]
    near = [
        (index_of(lax.rem(x + a, 2), lax.rem(y + b, 2), z), lax.rem(phase + c, 2))
        for a in range(2) for b in range(2) for c in range(2) if a + b + c
    ]
    met = greet(near + along)
    offset = pl.multiple_of((dp * 2 + phase) * shard, shard)
    weight_copy = pltpu.make_async_copy(head_any.at[:, pl.ds(offset, shard)], weight, load.at[0])
    weight_copy.start()
    copies = []

    def remote_to(src, dst, device):
        i = len(copies)
        copy = remote(src, dst, send.at[i], recv.at[i], device)
        copy.start()
        copies.append(copy)
        return copy

    def unit(p, yy, xx):
        return (p * 2 + yy) * 2 + xx

    def block(u, zz):
        return pl.ds(pl.multiple_of((u * 4 + zz) * cap, cap), cap)

    before = lax.broadcasted_iota(jnp.int32, (length, length), 0)
    after = lax.broadcasted_iota(jnp.int32, (length, length), 1)
    rows = rows_ref[...]
    place = mm(rows.astype(BF16), jnp.where(before <= after, 1.0, 0.0).astype(BF16))[7:8]
    slot = lax.broadcasted_iota(jnp.int32, (cap, length), 0).astype(F32)
    chosen = jnp.where((slot == place - 1.0) & (rows[7:8] > 0.0), 1.0, 0.0).astype(BF16)
    own = unit(phase, y, x)
    every[block(own, z), :] = mm(chosen, low_ref[...]).astype(BF16)
    def relay(u, zz, device):
        here = every.at[block(u, zz), :]
        return remote_to(here, here, device)

    beside, across = (index_of(x, y, z + 1 - 2 * lax.rem(z, 2)), phase), (index_of(x, y, lax.rem(z + 2, 4)), phase)
    met()
    firsts = [relay(own, z, beside), relay(own, z, across)]
    cross = [relay(own, z, core)]
    seconds = [relay(own, z, second)]
    thirds = [relay(own, z, third)]
    weight_copy.wait()
    weight_t[...] = weight[...].T
    near_z = z + 1 - 2 * lax.rem(z, 2)
    sources = [near_z, lax.rem(z + 2, 4), lax.rem(near_z + 2, 4)]
    order = [z] + sources
    for k in range(3):
        firsts[k].wait_recv()
        if k == 0:
            firsts.append(relay(own, near_z, across))
        seconds.append(relay(own, sources[k], second))
        thirds.append(relay(own, sources[k], third))
        cross.append(relay(own, sources[k], core))
    tall = 256
    chunks = 4 * cap // tall

    def look(u):
        def step(j, _):
            span = pl.ds(pl.multiple_of((u * chunks + j) * tall, tall), tall)
            logits = mm_nt(weight_t[...], every[span, :])
            top = jnp.max(logits, axis=0, keepdims=True)
            weights = jnp.exp(logits - top)
            summed = jnp.sum(weights, axis=0, keepdims=True)
            probs[:, span] = (weights * (1.0 / summed)).astype(BF16)
            totals[:, span] = top + jnp.log(summed)
            return 0

        lax.fori_loop(0, chunks, step, 0)

    def arrived(some):
        for copy in some:
            copy.wait_recv()

    look(own)
    for k in range(4):
        seconds[k].wait_recv()
        thirds.append(relay(unit(phase, y2, x2), order[k], third))
        cross.append(relay(unit(phase, y2, x2), order[k], core))
    arrived(cross[0:4])
    look(unit(1 - phase, y, x))
    look(unit(phase, y2, x2))
    for k in range(4):
        thirds[k].wait_recv()
        cross.append(relay(unit(phase, y3, x3), order[k], core))
    arrived(cross[4:8])
    look(unit(1 - phase, y3, x3))
    for k in range(4):
        thirds[4 + k].wait_recv()
        cross.append(relay(unit(phase, 1 - y, 1 - x), order[k], core))
    look(unit(phase, y3, x3))
    arrived(cross[8:12])
    look(unit(1 - phase, y2, x2))
    look(unit(phase, 1 - y, 1 - x))
    arrived(cross[12:16])
    look(unit(1 - phase, 1 - y, 1 - x))

    def join(parts):
        top = parts[0]
        for piece in parts[1:]:
            top = jnp.maximum(top, piece)
        summed = jnp.exp(parts[0] - top)
        for piece in parts[1:]:
            summed = summed + jnp.exp(piece - top)
        return top + jnp.log(summed)

    near_copies = [remote_to(totals, near_in.at[j], device) for j, device in enumerate(near)]
    arrived(near_copies)
    total = join([totals[...]] + [near_in[j] for j in range(7)])
    joined[...] = total
    far_copies = [remote_to(joined, far_in.at[j], device) for j, device in enumerate(along)]
    arrived(far_copies)
    shares[...] = jnp.exp(totals[...] - join([total] + [far_in[j] for j in range(3)]))

    per = tall // cap

    def learn(u):
        def step(j, _):
            span = pl.ds(pl.multiple_of((u * chunks + j) * tall, tall), tall)
            labels = labels_ref[:, span]
            hit = lax.broadcasted_iota(jnp.int32, (shard, tall), 0) == labels - offset
            grads = probs[:, span].astype(F32) * shares[:, span] - jnp.where(hit, 1.0, 0.0)
            grads = (grads * jnp.where(labels >= 0, scale, 0.0)).astype(BF16)
            probs[:, span] = grads
            back = mm(weight[...], grads).astype(BF16)
            for k in range(per):
                part[u, j * per + k] = back[:, k * cap : (k + 1) * cap]
            return 0

        lax.fori_loop(0, chunks, step, 0)

    def add(u, zz, *others):
        value = part[u, zz].astype(F32)
        for other in others:
            value = value + other.astype(F32)
        part[u, zz] = value.astype(BF16)

    mine = [unit(phase, 1 - y, 1 - x), unit(phase, y3, x3), unit(phase, y2, x2), own]
    theirs = [
        unit(1 - phase, 1 - y, 1 - x), unit(1 - phase, y2, x2), unit(1 - phase, y3, x3), unit(1 - phase, y, x)
    ]
    route = zs + [z]
    core_copies, third_copies = [], []

    def to_third(k):
        core_copies[k].wait_recv()
        for j, zz in enumerate(route):
            add(mine[k], zz, core_in[k, zz])
            third_copies.append(remote_to(part.at[mine[k], zz], third_in.at[k, j], third))

    for k in range(4):
        learn(theirs[k])
        core_copies.append(remote_to(part.at[theirs[k]], core_in.at[k], core))
        learn(mine[k])
        if k < 2:
            to_third(k)
    core_copies[2].wait_recv()
    second_copies = []
    for j, zz in enumerate(route):
        third_copies[j].wait_recv()
        add(mine[2], zz, core_in[2, zz], third_in[0, j])
        second_copies.append(remote_to(part.at[mine[2], zz], second_in.at[j], second))

    slab = min(256, shard)

    def weigh(k):
        value = mm(probs[k * slab : (k + 1) * slab, :], every[...])
        grad_weight_ref[:, k * slab : (k + 1) * slab] = value.T

    slabs = shard // slab
    for k in range((slabs + 1) // 2):
        weigh(k)
    core_copies[3].wait_recv()
    z_copies = []
    for j, zz in enumerate(route):
        third_copies[4 + j].wait_recv()
        second_copies[j].wait_recv()
        add(own, zz, core_in[3, zz], third_in[1, j], second_in[j])
        if j < 3:
            z_copies.append(remote_to(part.at[own, zz], z_in.at[j], along[j]))
    for k in range((slabs + 1) // 2, slabs):
        weigh(k)
    arrived(z_copies)
    back = part[own, z].astype(F32)
    for j in range(3):
        back = back + z_in[j].astype(F32)
    place = mm(jnp.where(after <= before, 1.0, 0.0).astype(BF16), cols_ref[...].astype(BF16))[:, 7:8]
    slot = lax.broadcasted_iota(jnp.int32, (length, cap), 1).astype(F32)
    spread = jnp.where((slot == place - 1.0) & (cols_ref[:, 7:8] > 0.0), 1.0, 0.0).astype(BF16)
    grad_ref[...] = mm_nt(spread, back.astype(BF16))
    for copy in copies:
        copy.wait_send()


def token_chips(number, cap, low, rows, cols, labels, head):
    length, width = low.shape
    shard = head.shape[1] // (2 * GROUPS)
    count = 2 * GROUPS * cap
    scale = float(2 * length * GROUPS) ** (-0.5)
    copies = 64
    return pl.pallas_call(
        partial(token_kernel, scale, cap),
        out_shape=(whole((length, width), F32), whole((width, shard), F32)),
        in_specs=in_vmem(4) + [pl.BlockSpec(memory_space=pl.ANY)],
        out_specs=tuple(in_vmem(2)),
        scratch_shapes=[
            VMEM((width, shard), BF16), VMEM((shard, width), BF16), VMEM((count, width), BF16),
            VMEM((shard, count), BF16), VMEM((1, count), F32), VMEM((7, 1, count), F32), VMEM((1, count), F32),
            VMEM((3, 1, count), F32), VMEM((1, count), F32),
            VMEM((8, 4, width, cap), BF16), VMEM((4, 4, width, cap), BF16), VMEM((2, 4, width, cap), BF16),
            VMEM((4, width, cap), BF16), VMEM((3, width, cap), BF16),
            pltpu.SemaphoreType.DMA((1,)), pltpu.SemaphoreType.DMA((copies + 8,)), pltpu.SemaphoreType.DMA((copies + 8,)),
        ],
        compiler_params=pltpu.CompilerParams(
            collective_id=number, has_side_effects=True, vmem_limit_bytes=60 * 1024 * 1024
        ),
        name="token_head",
    )(low, rows, cols, labels, head)


class Exchange:
    def __init__(self, send, recv):
        self.dp, self.phase = lax.axis_index("dp"), lax.axis_index("phase")
        self.x, self.y, self.z = place_of(self.dp)
        x, y, z = self.x, self.y, self.z
        low, high = lax.rem(z, 2), z // 2
        self.own = {"b": high, "a": low, "y": y, "x": x}
        self.partner = {
            "b": index_of(x, y, (1 - high) * 2 + low), "a": index_of(x, y, high * 2 + 1 - low),
            "y": index_of(x, 1 - y, z), "x": index_of(1 - x, y, z),
        }
        self.send, self.recv, self.used, self.copies = send, recv, 0, []

    def greet(self):
        return greet([(self.partner[step], self.phase) for step in "bayx"] + [(self.dp, 1 - self.phase)])

    def copy(self, src, dst, device):
        copy = remote(src, dst, self.send.at[self.used], self.recv.at[self.used], device)
        self.used += 1
        copy.start()
        self.copies.append(copy)
        return copy

    def to_core(self, src, dst):
        return self.copy(src, dst, (self.dp, 1 - self.phase))

    def to_core_either(self, first, second):
        i = self.used
        self.used += 1
        made = [remote(*pair, self.send.at[i], self.recv.at[i], (self.dp, 1 - self.phase)) for pair in (first, second)]

        @pl.when(self.phase == 0)
        def _():
            made[0].start()

        @pl.when(self.phase != 0)
        def _():
            made[1].start()

        self.copies.append(made[0])
        return made[0]

    def finish(self):
        for copy in self.copies:
            copy.wait_send()


class Batch:
    def __init__(self, shards, ins, put, own=None):
        self.shards, self.ins, self.put, self.own, self.arriving = shards, ins, put, own, []


class Chunk:
    def __init__(self, exchange, batch, start, size, order):
        self.exchange, self.batch, self.order = exchange, batch, order
        self.rows, self.step, self.fixed = pl.ds(start, size), -1, {}

    def at(self, fixed, free):
        free = list(free)
        return tuple(fixed[name] if name in fixed else free.pop(0) for name in "bayx") + (self.rows,)

    def advance(self):
        batch, ex, rows = self.batch, self.exchange, self.rows
        shards = batch.shards
        if self.step < 0 and batch.own is not None:
            for copy in batch.arriving:
                copy.wait_recv()
            batch.arriving = []
            own = batch.own

            def join(i, _):
                at = (i // 8, lax.rem(i // 4, 2), lax.rem(i // 2, 2), lax.rem(i, 2), rows)
                shards[at] = (shards[at].astype(F32) + own[at].astype(F32)).astype(BF16)
                return 0

            lax.fori_loop(0, GROUPS, join, 0)
        elif self.step >= 0:
            self.arriving.wait_recv()
            name = self.order[self.step]
            self.fixed[name] = ex.own[name]
            free = 3 - self.step
            arrived = batch.ins[self.step]
            if free == 0:
                batch.put(rows, shards[self.at(self.fixed, ())].astype(F32) + arrived[rows].astype(F32))
            else:

                def add(i, _):
                    spot = tuple(lax.rem(i // 2 ** (free - 1 - k), 2) for k in range(free))
                    at = self.at(self.fixed, spot)
                    shards[at] = (shards[at].astype(F32) + arrived[spot + (rows,)].astype(F32)).astype(BF16)
                    return 0

                lax.fori_loop(0, 2**free, add, 0)
        self.step += 1
        if self.step < 4:
            name = self.order[self.step]
            free = (slice(None),) * (3 - self.step)
            src = shards.at[self.at({**self.fixed, name: 1 - ex.own[name]}, free)]
            dst = batch.ins[self.step].at[free + (rows,)]
            self.arriving = ex.copy(src, dst, (ex.partner[name], ex.phase))


PARTS = (
    ((0, 48, "yabx"), (48, 32, "xayb"), (80, 48, "axyb"),),
    ((0, 16, "xayb"), (16, 32, "xayb"), (48, 32, "yxab"),),
    ((0, 32, "xyab"), (32, 32, "byxa"), (64, 48, "yxab"), (112, 16, "yxab"),),
    (
        (0, 16, "ayxb"), (16, 16, "yxab"), (32, 16, "xyab"), (48, 16, "xyab"), (64, 16, "yxab"), (80, 16,
        "xyab"), (96, 16, "axby"), (112, 16, "yxab"),
    ),
)
SCHEDULE = (
    (),
    (0, 1, 2),
    (),
    (),
    (),
    (),
    (),
    (),
    (1, 3, 5),
    (4, 0, 2),
    (),
    (1, 3),
    (7, 8, 5),
    (),
    (1,),
    (0,),
    (3,),
    (),
    (6,),
    (),
    (4, 2, 3),
    (5, 9),
    (),
    (8,),
    (10, 6, 2),
    (
        9, 4, 16, 5, 12, 11, 1, 3, 0, 8, 6, 14, 13, 9, 10, 4, 0, 15, 17, 11, 2, 12, 5, 10, 9, 16, 13, 6, 8, 14, 4,
        7, 11, 12, 9, 10, 17, 15, 13, 11, 16, 12, 14, 6, 7, 10, 8, 17, 15, 13, 11, 14, 12, 7, 16, 17, 15, 13, 14,
        16, 7, 17, 15,
    ),
)
CROSS, CROSS_END, ENCODER, SELF, WEIGHTS, TAIL = 0, 5, 6, 11, 21, 25


BACKWARD = (
    "grad_low", "grad_token", "res_d", "cres", "co_w", "cmixed", "cq", "ckv", "grad_place", "after", "src", "cq_w", "ckv_w", "res_e",
    "res", "mix_w", "qkv", "mixed", "x", "qkv_w",
)


def backward_kernel(
    rows_ref, cols_ref, norms_ref, cgain_ref, cbias_ref, ctotals_ref, totals_ref, grad_delete_ref, gain_ref,
    up_own, up_other, down_own, down_other, hid_e_any, slope_e_any, hid_d_any, slope_d_any, *rest,
):
    held_any, rest = dict(zip(BACKWARD, rest)), rest[len(BACKWARD) :]
    grad_x_any, red_ff_ref, red_attention_ref, red_cross_ref, vectors_ref = rest[:5]
    held, rest = dict(zip(BACKWARD, rest[5:])), rest[5 + len(BACKWARD) :]
    (
        up, down, hid, slope, grad_d, grad_e, grad_c, grad_a, core_d, core_e, core_c,
        in0_d, in0_e, in0_c, in0_a, in1_d, in1_e, in1_c, in1_a,
        in2_d, in2_e, in2_c, in2_a, in3_d, in3_e, in3_c, in3_a,
        after_grads, after_in, gq_ref, gckv_ref, grad_qkv, sums, grad_x_ref,
        vec_own, vec_core, vec_sums, vec_in, sems, held_sems, send, recv,
    ) = rest
    phase = lax.axis_index("phase")
    ex = Exchange(send, recv)
    met = ex.greet()

    def moved(name):
        i = BACKWARD.index(name)
        return pltpu.make_async_copy(held_any[name], held[name], held_sems.at[i])

    waited = set()

    def get(name):
        if name not in waited:
            waited.add(name)
            moved(name).wait()
        return held[name]

    length, width = held["grad_low"].shape
    each = width // GROUPS

    def load(own_side, i):
        hidden, slopes = (hid_e_any, slope_e_any) if own_side == 0 else (hid_d_any, slope_d_any)

        @pl.when(phase == own_side)
        def _():
            pltpu.make_async_copy(up_own, up, sems.at[i]).start()
            pltpu.make_async_copy(down_own, down, sems.at[i + 1]).start()

        @pl.when(phase != own_side)
        def _():
            pltpu.make_async_copy(up_other, up, sems.at[i]).start()
            pltpu.make_async_copy(down_other, down, sems.at[i + 1]).start()

        pltpu.make_async_copy(hidden, hid, sems.at[i + 2]).start()
        pltpu.make_async_copy(slopes, slope, sems.at[i + 3]).start()

    def loaded(i):
        for k, (src, dst) in enumerate(
            ((up_own, up), (down_own, down), (hid_e_any, hid), (slope_e_any, slope))
        ):
            pltpu.make_async_copy(src, dst, sems.at[i + k]).wait()

    def puts(ref):
        def put_up(part, value):
            ref[0, :, :, :, :, part * each : (part + 1) * each, :] = value.astype(BF16).reshape(
                2, 2, 2, 2, each, width
            )

        def put_down(part, value):
            ref[1, part // 2, part % 2] = value.astype(BF16).reshape(2, 2, width // 4, width)

        return put_up, put_down

    def put_ff(half):
        def put(rows, value):
            sums[half, rows, :] = value

        return put

    def put_attention(rows, value):
        red_attention_ref[rows, :] = value

    cross_sum = red_cross_ref.at[phase]

    def put_cross_sum(rows, value):
        cross_sum[rows, :] = value

    batch_d = Batch(core_d, (in0_d, in1_d, in2_d, in3_d), put_ff(1), grad_d.at[phase])
    batch_c = Batch(core_c, (in0_c, in1_c, in2_c, in3_c), put_cross_sum, grad_c.at[phase])
    batch_e = Batch(core_e, (in0_e, in1_e, in2_e, in3_e), put_ff(0), grad_e.at[phase])
    batch_a = Batch(grad_a, (in0_a, in1_a, in2_a, in3_a), put_attention)
    chunks = [
        Chunk(ex, batch, *part)
        for batch, parts in zip((batch_d, batch_c, batch_e, batch_a), PARTS) for part in parts
    ]

    def go_on(place):
        for name in SCHEDULE[place]:
            chunks[name].advance()

    def halves_to_core(batch, ref, core_ref, part):
        rows = pl.ds(part * each, each)
        batch.arriving.append(ex.to_core_either(
            (ref.at[1, part // 2, part % 2], core_ref.at[part // 2, part % 2]),
            (ref.at[0, :, :, :, :, rows], core_ref.at[:, :, :, :, rows]),
        ))

    for name in BACKWARD[:4]:
        moved(name).start()
    load(1, 0)
    for name in BACKWARD[4:]:
        moved(name).start()
    grad_out = get("grad_low")[...] + get("grad_token")[...]
    grad_res, gain_grad, bias_grad = norm_back(get("res_d")[...], norms_ref[1, 0:1, :], grad_out)
    vec_own[2:3, :] = gain_grad
    vec_own[3:4, :] = bias_grad
    vec_own[6:8, :] = grad_delete_ref[0:2, :]
    cres = get("cres")[...]
    middle_low = norm_forward(cres, cgain_ref[...], cbias_ref[...]).astype(BF16)
    loaded(0)
    met()
    grad_middle = feed_back(
        grad_res, middle_low, up, down, hid, slope, *puts(grad_d),
        lambda part: halves_to_core(batch_d, grad_d, core_d, part),
    )
    load(0, 4)
    grad_res, gain_grad, bias_grad = norm_back(cres, cgain_ref[...], grad_middle)
    vec_own[4:5, :] = gain_grad
    vec_own[5:6, :] = bias_grad
    branch = grad_res.astype(BF16)

    def put_cross(first, value):
        half_rows = grad_c.shape[5]
        value = value.astype(BF16).reshape(2, 2, 2, 2, each, width)
        for at in range(0, each, 16):
            half, row = divmod(first + at, half_rows)
            grad_c[half, :, :, :, :, row : row + 16, :] = value[:, :, :, :, at : at + 16, :]

    put_cross(3 * each, mm_tn(get("cmixed")[...], branch))
    put_cross(4 * each, get("grad_place")[...])
    grad_mixed = mm_nt(branch, get("co_w")[...]).astype(BF16)
    cq_ref, ckv_ref = get("cq"), get("ckv")

    def put_q(pair, value):
        gq_ref[:, column(pair)] = value

    def put_k(pair, value):
        gckv_ref[:, column(pair)] = value

    def put_v(pair, value):
        gckv_ref[:, column(pair, width)] = value

    go_on(CROSS)

    def between(pair):
        go_on(CROSS + 1 + pair)

    attend_backward(
        lambda pair: cq_ref[:, column(pair)],
        lambda pair: ckv_ref[:, column(pair)],
        lambda pair: ckv_ref[:, column(pair, width)],
        lambda pair: grad_mixed[:, column(pair)],
        cols_ref[:, 2:3] == rows_ref[3:4, :],
        ctotals_ref, put_q, put_k, put_v, between,
    )
    grad_q = gq_ref[...]
    put_cross(0, mm_tn(get("after")[1].astype(BF16), grad_q))
    for part in range(2):
        put_cross((1 + part) * each, mm_tn(get("src")[...], gckv_ref[:, part * width : (part + 1) * width]))
    batch_c.arriving.append(ex.to_core(grad_c.at[1 - phase], core_c))
    after_grads[1] = grad_res + mm_nt(grad_q, get("cq_w")[...])
    go_on(CROSS_END)
    grad_src = mm_nt(gckv_ref[...], get("ckv_w")[...]).astype(BF16).astype(F32)
    grad_res, gain_grad, bias_grad = norm_back(get("res_e")[...], norms_ref[0, 0:1, :], grad_src)
    vec_own[0:1, :] = gain_grad
    vec_own[1:2, :] = bias_grad
    from_v = ex.to_core(vec_own, vec_core)
    loaded(4)

    go_on(ENCODER)

    def between(part):
        halves_to_core(batch_e, grad_e, core_e, part)
        go_on(ENCODER + 1 + part)

    after_grads[0] = feed_back(
        grad_res, get("after")[0].astype(BF16), up, down, hid, slope, *puts(grad_e), between
    )
    from_after = ex.to_core(after_grads.at[1 - phase], after_in)
    res_ref, mix_w_ref, qkv_ref, mixed_ref, x_ref = [get(n) for n in ("res", "mix_w", "qkv", "mixed", "x")]
    first_vectors = []
    for turn in range(2):
        row = phase if turn == 0 else 1 - phase
        rows = pl.ds(pl.multiple_of(row * length, length), length)
        if turn == 0:
            grad_after = after_grads[phase]
        else:
            from_after.wait_recv()
            grad_after = after_in[...]
        grad_res, gain_grad, bias_grad = norm_back(res_ref[rows, :], gain_ref[0:1, :], grad_after)
        first_vectors.append((gain_grad, bias_grad))
        grad_x_ref[rows, :] = grad_res
        branch = grad_res.astype(BF16)
        if turn == 0:
            first_branch, first_rows = branch, rows
        grad_mixed = mm_nt(branch, mix_w_ref[...]).astype(BF16)

        def put(offset):
            def store(pair, value):
                grad_qkv[rows, column(pair, offset)] = value

            return store

        go_on(SELF + 5 * turn)

        def between(pair):
            go_on(SELF + 5 * turn + 1 + pair)

        attend_backward(
            lambda pair: qkv_ref[rows, column(pair)],
            lambda pair: qkv_ref[rows, column(pair, width)],
            lambda pair: qkv_ref[rows, column(pair, 2 * width)],
            lambda pair: grad_mixed[:, column(pair)],
            jnp.where(row == 0, cols_ref[:, 0:1], cols_ref[:, 1:2])
            == jnp.where(row == 0, rows_ref[0:1, :], rows_ref[1:2, :]),
            totals_ref.at[row], put(0), put(width), put(2 * width), between,
        )
    shape = (2, 2, 2, 2, each, width)
    grad_mix = mm_tn(mixed_ref[first_rows, :], first_branch) + mm_tn(mixed_ref[rows, :], branch)
    grad_a[:, :, :, :, 3 * each :, :] = grad_mix.astype(BF16).reshape(shape)
    go_on(WEIGHTS)
    for part in range(3):
        cols = slice(part * width, (part + 1) * width)
        value = mm_tn(x_ref[...], grad_qkv[:, cols])
        grad_a[:, :, :, :, part * each : (part + 1) * each, :] = value.astype(BF16).reshape(shape)
        go_on(WEIGHTS + 1 + part)
    grad_x_ref[...] += mm_nt(grad_qkv[...], get("qkv_w")[...])
    grad_x_copy = pltpu.make_async_copy(grad_x_ref, grad_x_any, held_sems.at[len(BACKWARD)])
    grad_x_copy.start()
    from_v.wait_recv()
    vec_sums[0, 0:8, :] = vec_own[...] + vec_core[...]
    vec_sums[0, 8:9, :] = first_vectors[0][0] + first_vectors[1][0]
    vec_sums[0, 9:10, :] = first_vectors[0][1] + first_vectors[1][1]
    vec_sums[0, 10:16, :] = jnp.zeros((6, width), F32)
    tail = SCHEDULE[TAIL]
    left = [sum(chunks[item].batch is batch for item in tail) for batch in (batch_d, batch_c, batch_e)]
    vector_copies = []

    def vector_step(stage):
        if stage > 0:
            vector_copies[-1].wait_recv()
            vec_sums[stage] = vec_sums[stage - 1] + vec_in[stage - 1]
        if stage < 4:
            step = "xyab"[stage]
            vector_copies.append(ex.copy(vec_sums.at[stage], vec_in.at[stage], (ex.partner[step], phase)))

    vector_step(0)
    after_each = len(tail) // 5
    for at, name in enumerate(tail):
        chunks[name].advance()
        if at % after_each == after_each - 1 and len(vector_copies) < 4:
            vector_step(len(vector_copies))
        for i, batch in enumerate((batch_d, batch_c, batch_e)):
            left[i] -= chunks[name].batch is batch
        if chunks[name].batch is batch_c and left[1] == 0:
            cross_copy = ex.to_core(cross_sum, red_cross_ref.at[phase])
        if chunks[name].batch in (batch_d, batch_e) and left[0] + left[2] == 0:
            ff_copy = ex.to_core(sums.at[1 - phase], red_ff_ref.at[phase])
            red_ff_ref[phase] = sums[phase]
    vector_step(4)
    vectors_ref[...] = vec_sums[4]
    cross_copy.wait_recv()
    ff_copy.wait_recv()
    grad_x_copy.wait()
    ex.finish()


def unpack_kernel(
    ff_any, attention_any, cross_any, vectors_any, own_any, other_any,
    qkv_ref, mix_ref, up_ref, down_any, cq_ref, ckv_ref, co_ref, place_ref,
    gain_ref, bias_ref, cgain_ref, cbias_ref, delete_ref, token_any,
    ff_ref, attention_ref, cross_halves_ref, vectors_ref, halves, sems, token_sems,
):
    phase, dp = lax.axis_index("phase"), lax.axis_index("dp")
    shard, pieces = own_any.shape[1], token_sems.shape[1]
    tall = own_any.shape[0] // pieces
    arrive, leave = [], []
    for i in range(pieces):
        rows = pl.ds(i * tall, tall)
        for side, (src, at) in enumerate(((own_any, phase), (other_any, 1 - phase))):
            arrive.append(pltpu.make_async_copy(src.at[rows], halves.at[side, rows], token_sems.at[side, i]))
            cols = pl.ds(pl.multiple_of(at * shard, shard), shard)
            leave.append(pltpu.make_async_copy(halves.at[side, rows], token_any.at[rows, cols], token_sems.at[side, i]))
    moves = [
        pltpu.make_async_copy(src, dst, sems.at[i])
        for i, (src, dst) in enumerate((
            (vectors_any, vectors_ref), (ff_any, ff_ref), (attention_any, attention_ref), (cross_any, cross_halves_ref),
        ))
    ]
    for move in arrive[:2] + moves + arrive[2:]:
        move.start()
    for i in range(2 * pieces):
        arrive[i].wait()
        leave[i].start()
    for move in moves:
        move.wait()
    down_move = pltpu.make_async_copy(ff_ref.at[1], down_any, sems.at[4])
    down_move.start()
    each = gain_ref.shape[2]
    vectors = vectors_ref[...]
    whole_width = vectors.shape[1]
    vectors = pltpu.roll(vectors, lax.rem(whole_width - dp * each, whole_width), 1)[:, :each]
    gain_ref[0, 0:1, :] = vectors[8:9]
    gain_ref[0, 1:2, :] = jnp.where(phase == 0, vectors[0:1], vectors[2:3])
    bias_ref[0, 0:1, :] = vectors[9:10]
    bias_ref[0, 1:2, :] = jnp.where(phase == 0, vectors[1:2], vectors[3:4])
    cgain_ref[...] = vectors[4:5]
    cbias_ref[...] = vectors[5:6]
    delete_ref[...] = vectors[6:8]
    width = mix_ref.shape[1]
    high = mix_ref.shape[0]
    for block in range(up_ref.shape[1] // width):
        up_ref[:, block * width : (block + 1) * width] = ff_ref[0, block * high : (block + 1) * high, :]
    for block in range(3):
        qkv_ref[:, block * width : (block + 1) * width] = attention_ref[block * high : (block + 1) * high, :]
    mix_ref[...] = attention_ref[3 * high :, :]
    half_rows = cross_halves_ref.shape[1]

    def cross(start):
        half, row = divmod(start, half_rows)
        return cross_halves_ref[half, row : row + 16, :]

    for start in range(0, 5 * high, 16):
        part, inner = start // high, slice(start % high, start % high + 16)
        if part == 0:
            cq_ref[inner, :] = cross(start)
        elif part < 3:
            ckv_ref[inner, (part - 1) * width : part * width] = cross(start)
        elif part == 3:
            co_ref[inner, :] = cross(start)
        else:
            value = cross(start)
            cols = place_ref.shape[1]
            at = start % high
            place_ref[at : at + 16, :] = value[:, :cols]
            place_ref[high + at : high + at + 16, :] = value[:, cols:]
    down_move.wait()
    for move in leave:
        move.wait()


def whole(shape, dtype):
    return jax.ShapeDtypeStruct(shape, dtype)


def in_vmem(count):
    return [pl.BlockSpec(memory_space=VMEM)] * count


def swap(value):
    return lax.ppermute(value, "phase", [(0, 1), (1, 0)])


def unpacked(shards, height, columns):
    groups, rows, width = shards.shape
    blocks = columns // width
    parts = shards.reshape(groups, blocks, rows // blocks, width)
    return parts.transpose(0, 2, 1, 3).reshape(height, columns)


def token_head(cap, block_rows, low, flags, labels_all, flags_all, weight, weight_t, scale):
    length, width = low.shape
    dp = lax.axis_size("dp")
    shard = weight_t.shape[0]

    def choice(flags):
        place = jnp.cumsum(flags, axis=-1) - 1
        places = lax.broadcasted_iota(jnp.int32, flags.shape[:-1] + (cap, flags.shape[-1]), flags.ndim - 1)
        return (places == place[..., None, :]) & (flags[..., None, :] > 0)

    chosen = choice(flags)
    packed = mm(chosen.astype(BF16), low).astype(BF16)
    every = gather_blocks(packed).reshape(2 * dp * cap, width)
    labels = jnp.max(jnp.where(choice(flags_all), labels_all[:, None, :], -1), axis=-1)
    labels = labels.reshape(dp, 2, cap).transpose(1, 0, 2).reshape(2 * dp * cap)
    tall = block_rows
    count = 2 * dp * cap // tall
    probs, totals = pl.pallas_call(
        token_forward,
        grid=(count,),
        out_shape=(whole((count, shard, tall), BF16), whole((count, 1, tall), F32)),
        in_specs=[
            pl.BlockSpec((tall, width), lambda i: (i, 0)),
            pl.BlockSpec((shard, width), lambda i: (0, 0)),
        ],
        out_specs=(
            pl.BlockSpec((1, shard, tall), lambda i: (i, 0, 0)),
            pl.BlockSpec((1, 1, tall), lambda i: (i, 0, 0)),
        ),
        compiler_params=pltpu.CompilerParams(vmem_limit_bytes=48 * 1024 * 1024),
        name="token_forward",
    )(every, weight_t)
    shares = token_shares(totals)
    each = tall // cap
    grad_low, grad_weight = pl.pallas_call(
        partial(token_backward, scale),
        grid=(count,),
        out_shape=(whole((2 * dp, cap, width), BF16), whole((width, shard), F32)),
        in_specs=[
            pl.BlockSpec((1, shard, tall), lambda i: (i, 0, 0)),
            pl.BlockSpec((1, 1, tall), lambda i: (i, 0, 0)),
            pl.BlockSpec((1, 1, tall), lambda i: (i, 0, 0)),
            pl.BlockSpec((tall, width), lambda i: (i, 0)),
            pl.BlockSpec((shard, width), lambda i: (0, 0)),
        ],
        out_specs=(
            pl.BlockSpec((each, cap, width), lambda i: (i, 0, 0)),
            pl.BlockSpec((width, shard), lambda i: (0, 0)),
        ),
        scratch_shapes=[VMEM((shard, width), F32)],
        compiler_params=pltpu.CompilerParams(vmem_limit_bytes=48 * 1024 * 1024),
        name="token_backward",
    )(probs, shares, labels.reshape(count, 1, tall), every, weight_t)
    back = scatter_blocks(grad_low.reshape(2, dp, cap, width))
    return mm_tn(chosen.astype(BF16), back.astype(BF16)), grad_weight


def on_chips(
    inputs, segments, delete_target, place_target, token_target, token_mask,
    attention_in, attention_out, feedforward_in, feedforward_out, norm_gain, norm_bias,
    cross_query, cross_keyvalue, cross_out, cross_gain, cross_bias,
    head_delete, head_place, head_token,
):
    phase, dp_index = lax.axis_index("phase"), lax.axis_index("dp")
    count, length, width = inputs.shape[1:]
    hidden, classes = feedforward_in.shape[2], head_place.shape[1]
    each = width // GROUPS
    scale = float(count * length * GROUPS) ** (-0.5)
    any_space = pl.BlockSpec(memory_space=pl.ANY)
    is_enc = phase == 0
    states = inputs[0].reshape(count * length, width)
    up_own, down_own = feedforward_in[0], feedforward_out[0]
    qkv_w, mix_w = attention_in[0], attention_out[0]
    delete_weight = head_delete.T
    gain_row, bias_row = cross_gain[None, :], cross_bias[None, :]
    shapes = {
        "qkv": ((count * length, 3 * width), BF16), "mixed": ((count * length, width), BF16),
        "res": ((count * length, width), F32), "after": ((2, length, width), F32),
        "res_e": ((length, width), F32), "ckv": ((length, 2 * width), BF16), "cq": ((length, width), BF16),
        "cmixed": ((length, width), BF16), "cres": ((length, width), F32),
        "hid_e": ((length, hidden), BF16), "slope_e": ((length, hidden), BF16),
        "hid_d": ((length, hidden), BF16), "slope_d": ((length, hidden), BF16),
        "res_d": ((length, width), F32), "src": ((length, width), BF16), "low": ((length, width), BF16),
        "grad_low": ((length, width), F32), "grad_place": ((GROUPS, each, 2 * classes), BF16),
        "co_w": ((width, width), BF16), "cq_w": ((width, width), BF16), "ckv_w": ((width, 2 * width), BF16),
        "mix_w": ((width, width), BF16), "qkv_w": ((width, 3 * width), BF16), "x": ((count * length, width), BF16),
        "grad_token": ((length, width), F32),
    }
    outs = pl.pallas_call(
        partial(forward_kernel, scale),
        out_shape=(
            whole((8, length), F32), whole((length, 128), F32),
            whole((1, GROUPS * length), jnp.int32), whole((1, 2 * GROUPS * length), jnp.int32), whole((1, 1), F32),
            whole((2, 2, width), F32), whole((width, hidden), BF16), whole((hidden, width), BF16),
            whole((count, HEADS, length), F32), whole((HEADS, length), F32), whole((8, width), F32),
            *[whole(*shapes[name]) for name in FORWARD],
        ),
        in_specs=in_vmem(10) + [any_space] * 5 + in_vmem(3) + [any_space],
        out_specs=tuple(in_vmem(6) + [any_space] * 2 + in_vmem(3) + [any_space] * len(FORWARD)),
        scratch_shapes=[
            *[VMEM(*shapes[name]) for name in FORWARD],
            VMEM((2, width, hidden), BF16), VMEM((2, hidden, width), BF16),
            VMEM((width, width), BF16), VMEM((width, 2 * width), BF16), VMEM((width, width), BF16),
            VMEM((2 * width, classes), BF16), VMEM((length, width), F32),
            VMEM((2, length), jnp.int32), VMEM((4, 2, 2, 2, length), jnp.int32), VMEM((128, length), F32),
            pltpu.SemaphoreType.DMA((6,)), pltpu.SemaphoreType.DMA((len(FORWARD) + 2,)),
            pltpu.SemaphoreType.DMA((20,)), pltpu.SemaphoreType.DMA((20,)),
        ],
        compiler_params=pltpu.CompilerParams(
            collective_id=1, has_side_effects=True, vmem_limit_bytes=56 * 1024 * 1024
        ),
        name="forward",
    )(
        states, segments, delete_target, place_target, token_target, token_mask,
        qkv_w, mix_w, norm_gain[0], norm_bias[0], up_own, down_own,
        cross_query, cross_keyvalue, cross_out, gain_row, bias_row, delete_weight, head_place,
    )
    rows, cols, labels_small, labels_large, most, norms, up_other, down_other, totals, ctotals, grad_delete = outs[:11]
    saved = dict(zip(FORWARD, outs[11:]))
    grad_token, grad_weight = lax.cond(
        most[0, 0] < 0.0,
        lambda: token_chips(2, length // 2, saved["low"], rows, cols, labels_small, head_token),
        lambda: token_chips(3, length, saved["low"], rows, cols, labels_large, head_token),
    )
    other_weight = swap(grad_weight)
    saved.update(co_w=cross_out, cq_w=cross_query, ckv_w=cross_keyvalue, mix_w=mix_w, qkv_w=qkv_w, x=states, grad_token=grad_token)
    half_rows, ff_half, attention_rows = 5 * each // 2, hidden // GROUPS, 4 * each
    rows_of = (ff_half, ff_half, half_rows, attention_rows)

    def shards(tall, *lead):
        return VMEM(lead + (tall, width), BF16)

    grad_states, red_ff, red_attention, red_cross, vectors = pl.pallas_call(
        backward_kernel,
        out_shape=(
            whole((count * length, width), F32), whole((2, ff_half, width), F32),
            whole((attention_rows, width), F32), whole((2, half_rows, width), F32), whole((16, width), F32),
        ),
        in_specs=in_vmem(9) + [any_space] * (8 + len(BACKWARD)),
        out_specs=tuple([any_space] + in_vmem(4)),
        scratch_shapes=[
            *[VMEM(*shapes[name]) for name in BACKWARD],
            VMEM((width, hidden), BF16), VMEM((hidden, width), BF16),
            VMEM((length, hidden), BF16), VMEM((length, hidden), BF16),
            shards(ff_half, 2, 2, 2, 2, 2), shards(ff_half, 2, 2, 2, 2, 2), shards(half_rows, 2, 2, 2, 2, 2),
            shards(attention_rows, 2, 2, 2, 2),
            shards(ff_half, 2, 2, 2, 2), shards(ff_half, 2, 2, 2, 2), shards(half_rows, 2, 2, 2, 2),
            *[shards(tall, 2, 2, 2) for tall in rows_of],
            *[shards(tall, 2, 2) for tall in rows_of],
            *[shards(tall, 2) for tall in rows_of],
            *[shards(tall) for tall in rows_of],
            VMEM((2, length, width), F32), VMEM((length, width), F32),
            VMEM((length, width), BF16), VMEM((length, 2 * width), BF16), VMEM((count * length, 3 * width), BF16),
            VMEM((2, ff_half, width), F32), VMEM((count * length, width), F32),
            VMEM((8, width), F32), VMEM((8, width), F32),
            VMEM((5, 16, width), F32), VMEM((4, 16, width), F32),
            pltpu.SemaphoreType.DMA((8,)), pltpu.SemaphoreType.DMA((len(BACKWARD) + 1,)),
            pltpu.SemaphoreType.DMA((128,)), pltpu.SemaphoreType.DMA((128,)),
        ],
        compiler_params=pltpu.CompilerParams(
            collective_id=0, has_side_effects=True, vmem_limit_bytes=62 * 1024 * 1024
        ),
        name="backward",
    )(
        rows, cols, norms, gain_row, bias_row, ctotals, totals, grad_delete, norm_gain[0],
        up_own, up_other, down_own, down_other,
        saved["hid_e"], saved["slope_e"], saved["hid_d"], saved["slope_d"],
        *[saved[name] for name in BACKWARD],
    )
    vocabulary = head_token.shape[1]
    g_qkv, g_mix, g_up, g_down, g_cq, g_ckv, g_co, g_place, g_gain, g_bias, g_cgain, g_cbias, g_delete, g_token = (
        pl.pallas_call(
            unpack_kernel,
            out_shape=(
                whole((each, 3 * width), F32), whole((each, width), F32), whole((each, hidden), F32),
                whole((hidden // GROUPS, width), F32), whole((each, width), F32), whole((each, 2 * width), F32),
                whole((each, width), F32), whole((2 * each, classes), F32),
                whole((1, 2, each), F32), whole((1, 2, each), F32), whole((1, each), F32), whole((1, each), F32),
                whole((2, each), F32), whole((width, vocabulary // GROUPS), F32),
            ),
            in_specs=[any_space] * 6,
            out_specs=tuple(in_vmem(3) + [any_space] + in_vmem(9) + [any_space]),
            scratch_shapes=[
                VMEM(red_ff.shape, F32), VMEM(red_attention.shape, F32), VMEM(red_cross.shape, F32),
                VMEM(vectors.shape, F32), VMEM((2,) + grad_weight.shape, F32),
                pltpu.SemaphoreType.DMA((5,)), pltpu.SemaphoreType.DMA((2, 2)),
            ],
            compiler_params=pltpu.CompilerParams(vmem_limit_bytes=60 * 1024 * 1024),
            name="unpack",
        )(red_ff, red_attention, red_cross, vectors, grad_weight, other_weight)
    )
    return (
        grad_states.reshape(1, count, length, width),
        g_qkv[None], g_mix[None], g_up[None], g_down[None], g_gain, g_bias,
        g_cq, g_ckv, g_co, g_cgain[0], g_cbias[0], g_delete.T, g_place, g_token,
    )


def on_any(
    inputs, segments, delete_target, place_target, token_target, token_mask,
    attention_in, attention_out, feedforward_in, feedforward_out, norm_gain, norm_bias,
    cross_query, cross_keyvalue, cross_out, cross_gain, cross_bias,
    head_delete, head_place, head_token,
):
    phase = lax.axis_index("phase")
    dp_index, dp = lax.axis_index("dp"), lax.axis_size("dp")
    count, length, width = inputs.shape[1:]
    assert count == 2
    hidden = feedforward_in.shape[2]
    scale = float(count * length * dp) ** (-0.5)
    any_space = pl.BlockSpec(memory_space=pl.ANY)
    params = pltpu.CompilerParams(vmem_limit_bytes=56 * 1024 * 1024)

    coded = jnp.where(token_mask == 1, token_target, -1)
    labels_all = lax.all_gather(coded, "dp", tiled=True)
    flags_all = (labels_all >= 0).astype(jnp.int32)

    def row_of(value):
        return lax.dynamic_index_in_dim(value, phase, 0, keepdims=False)

    own_norms = jnp.stack([norm_gain[0, 1], norm_bias[0, 1]])
    up_other, down_other = swap(feedforward_in[0]), swap(feedforward_out[0])
    other_norms = swap(own_norms)
    is_enc = phase == 0
    norms = jnp.concatenate(
        [jnp.where(is_enc, own_norms, other_norms), jnp.where(is_enc, other_norms, own_norms)]
    )
    ids = row_of(segments)
    own_ids = lax.dynamic_index_in_dim(segments, phase, 1, keepdims=False)
    states = inputs[0].reshape(count * length, width)

    qkv, mixed, res, totals, keep, send = pl.pallas_call(
        self_forward,
        out_shape=(
            whole((count * length, 3 * width), BF16),
            whole((count * length, width), BF16),
            whole((count * length, width), F32),
            whole((count, HEADS, length), F32),
            whole((length, width), F32),
            whole((length, width), F32),
        ),
        in_specs=in_vmem(7),
        out_specs=tuple(in_vmem(6)),
        compiler_params=params,
        name="self_forward",
    )(states, own_ids[:, :, None], own_ids[:, None, :], attention_in[0], attention_out[0], norm_gain[0], norm_bias[0])
    received = swap(send)

    ids_e, ids_d_row = ids[0][:, None], ids[1][None, :]
    pair_valid = jnp.concatenate([ids[1, :-1] == ids[1, 1:], jnp.zeros((1,), bool)])
    targets = jnp.stack(
        [row_of(delete_target), row_of(place_target), pair_valid.astype(jnp.int32)], axis=1
    )
    delete_weight = head_delete.T
    gain_row, bias_row = cross_gain[None, :], cross_bias[None, :]
    ff_scratch = [
        VMEM((width, hidden), BF16), VMEM((hidden, width), BF16),
        VMEM((width, hidden), BF16), VMEM((hidden, width), BF16),
    ]
    saved_shapes = (
        whole((length, width), F32),
        whole((length, width), F32),
        whole((length, width), F32),
        whole((length, 2 * width), BF16),
        whole((length, width), BF16),
        whole((length, width), BF16),
        whole((length, width), F32),
        whole((HEADS, length), F32),
        whole((length, hidden), BF16), whole((length, hidden), BF16),
        whole((length, hidden), BF16), whole((length, hidden), BF16),
        whole((length, width), F32),
        whole((length, width), BF16),
    )
    classes = head_place.shape[1]
    each = width // GROUPS
    outs = pl.pallas_call(
        partial(rows_forward, scale),
        out_shape=saved_shapes + (
            whole((length, width), BF16),
            whole((length, width), F32),
            whole((8, width), F32),
            whole((GROUPS, each, 2 * classes), BF16),
        ),
        in_specs=in_vmem(5) + [any_space] * 4 + in_vmem(8),
        out_specs=tuple(in_vmem(18)),
        scratch_shapes=ff_scratch + [pltpu.SemaphoreType.DMA((2, 2))],
        compiler_params=params,
        name="rows_forward",
    )(
        keep, received, ids_e, ids_d_row, targets,
        feedforward_in[0], up_other, feedforward_out[0], down_other, norms,
        cross_query, cross_keyvalue, cross_out, gain_row, bias_row, delete_weight, head_place,
    )
    saved = outs[:14]
    low, grad_low, grad_delete, grad_place = outs[14:]

    shard = head_token.shape[1] // (2 * dp)
    weight = lax.dynamic_slice_in_dim(head_token, (dp_index * 2 + phase) * shard, shard, 1)
    weight_t = weight.T
    flags = row_of(token_mask)

    def run_head(cap, block_rows):
        return token_head(cap, block_rows, low, flags, labels_all, flags_all, weight, weight_t, scale)

    small = length // 2
    fits = jnp.max(jnp.sum(flags_all, axis=1)) <= small
    grad_token, grad_weight = lax.cond(
        fits, lambda: run_head(small, 4 * small), lambda: run_head(length, 2 * length)
    )
    other_weight = swap(grad_weight)
    grad_head_token = jnp.concatenate(
        [jnp.where(is_enc, grad_weight, other_weight), jnp.where(is_enc, other_weight, grad_weight)], axis=1
    )

    each = width // GROUPS
    ff_rows = 2 * hidden // GROUPS
    keep, send, ff_own, ff_other, cross_shards, vectors = pl.pallas_call(
        rows_backward,
        out_shape=(
            whole((length, width), F32), whole((length, width), F32),
            whole((GROUPS, ff_rows, width), BF16), whole((GROUPS, ff_rows, width), BF16),
            whole((GROUPS, 5 * each, width), BF16), whole((8, width), F32),
        ),
        in_specs=in_vmem(4) + [any_space] * 4 + in_vmem(6 + 14 + 1),
        out_specs=(in_vmem(2) + [any_space] * 2 + in_vmem(2)),
        scratch_shapes=ff_scratch + [
            VMEM((GROUPS, ff_rows, width), BF16), VMEM((GROUPS, ff_rows, width), BF16),
            VMEM((length, width), F32), VMEM((length, width), F32),
            VMEM((length, width), BF16), VMEM((length, 2 * width), BF16),
            pltpu.SemaphoreType.DMA((2, 2)), pltpu.SemaphoreType.DMA((2,)),
        ],
        compiler_params=params,
        name="rows_backward",
    )(
        grad_low, grad_token, ids_e, ids_d_row,
        feedforward_in[0], up_other, feedforward_out[0], down_other, norms,
        cross_query, cross_keyvalue, cross_out, gain_row, bias_row, *saved, grad_place,
    )
    received = swap(send)
    ff_received = swap(ff_other)
    half_rows = 5 * each // 2
    cross_keep = lax.dynamic_slice_in_dim(cross_shards, phase * half_rows, half_rows, 1)
    cross_received = swap(lax.dynamic_slice_in_dim(cross_shards, (1 - phase) * half_rows, half_rows, 1))
    shared = jnp.concatenate([vectors[4:6], grad_delete[:2]])
    norm_own = jnp.where(is_enc, vectors[0:2], vectors[2:4])
    norm_other = jnp.where(is_enc, vectors[2:4], vectors[0:2])
    vector_received = swap(jnp.concatenate([norm_other, shared]))
    vector_sums = jnp.concatenate([norm_own, shared]) + vector_received

    grad_states, attention_shards, first_vectors = pl.pallas_call(
        self_backward,
        out_shape=(
            whole((count * length, width), F32), whole((GROUPS, 4 * each, width), BF16), whole((8, width), F32),
        ),
        in_specs=in_vmem(12),
        out_specs=tuple(in_vmem(3)),
        scratch_shapes=[VMEM((count * length, width), F32), VMEM((count * length, 3 * width), BF16)],
        compiler_params=params,
        name="self_backward",
    )(
        keep, received, states, own_ids[:, :, None], own_ids[:, None, :], attention_in[0], attention_out[0],
        norm_gain[0], qkv, mixed, res, totals,
    )

    all_vectors = jnp.stack([
        first_vectors[0], vector_sums[0], first_vectors[1], vector_sums[1],
        vector_sums[2], vector_sums[3], vector_sums[4], vector_sums[5],
    ])
    ff_sum = (ff_own.astype(F32) + ff_received.astype(F32)).astype(BF16)
    cross_sum = (cross_keep.astype(F32) + cross_received.astype(F32)).astype(BF16)
    cross_other = swap(cross_sum)
    cross_all = jnp.concatenate(
        [jnp.where(is_enc, cross_sum, cross_other), jnp.where(is_enc, cross_other, cross_sum)], axis=1
    )
    ff_up = hidden // width * each

    def spread(value):
        return lax.psum_scatter(value.astype(F32), "dp", scatter_dimension=0, tiled=True)

    g_qkv = spread(unpacked(attention_shards[:, : 3 * each], width, 3 * width))
    g_mix = spread(unpacked(attention_shards[:, 3 * each :], width, width))
    g_up = spread(unpacked(ff_sum[:, :ff_up], width, hidden))
    g_down = spread(unpacked(ff_sum[:, ff_up:], hidden, width))
    g_cq = spread(unpacked(cross_all[:, :each], width, width))
    g_ckv = spread(unpacked(cross_all[:, each : 3 * each], width, 2 * width))
    g_co = spread(unpacked(cross_all[:, 3 * each : 4 * each], width, width))
    place = cross_all[:, 4 * each :].reshape(GROUPS, each, 2, classes)
    g_place = spread(place.transpose(0, 2, 1, 3).reshape(2 * width, classes))
    vector_out = lax.psum_scatter(all_vectors, "dp", scatter_dimension=1, tiled=True)
    return (
        grad_states.reshape(1, count, length, width),
        g_qkv[None], g_mix[None], g_up[None], g_down[None],
        vector_out[None, 0:2], vector_out[None, 2:4],
        g_cq, g_ckv, g_co, vector_out[4], vector_out[5], vector_out[6:8].T, g_place, grad_head_token,
    )


def on_device(*args):
    chips = lax.axis_size("dp") == GROUPS and args[0].shape[1] == 2
    return on_chips(*args) if chips else on_any(*args)


def solution(mesh):
    layer, row = P("phase", None, None), P("dp", None)
    return jax.shard_map(
        on_device,
        mesh=mesh,
        in_specs=(P("phase", "dp", None, None), P("dp", None, None), row, row, row, row)
        + (layer,) * 6 + (P(),) * 8,
        out_specs=(P("phase", "dp", None, None),) + (P("phase", "dp", None),) * 4
        + (P("phase", None, "dp"),) * 2 + (row,) * 3 + (P("dp"),) * 2 + (row,) * 2 + (P(None, "dp"),),
        check_vma=False,
    )
```

```python
from functools import partial

import jax
import jax.numpy as jnp
from jax import lax
from jax.experimental import pallas as pl
from jax.experimental.pallas import tpu as pltpu
from jax.sharding import PartitionSpec as P

HEADS = 8
HEAD = 64
PAIR = 2 * HEAD
MASKED_SCORE = -1e30
NORM_EPSILON = 1e-05
GROUPS = 16
F32 = jnp.float32
BF16 = jnp.bfloat16
MESH = pl.DeviceIdType.MESH
VMEM = pltpu.VMEM
GELU_C = 0.7978845608028654
GELU_A = 0.044715


def mm(left, right):
    return jnp.dot(left, right, preferred_element_type=F32)


def mm_nt(left, right):
    return lax.dot_general(left, right, (((1,), (1,)), ((), ())), preferred_element_type=F32)


def mm_tn(left, right):
    return lax.dot_general(left, right, (((0,), (0,)), ((), ())), preferred_element_type=F32)


def norm_forward(residual, gain, bias):
    centered = residual - jnp.mean(residual, axis=-1, keepdims=True)
    variance = jnp.mean(centered * centered, axis=-1, keepdims=True)
    return centered * lax.rsqrt(variance + NORM_EPSILON) * gain + bias


def norm_back(residual, gain, grad_out):
    centered = residual - jnp.mean(residual, axis=-1, keepdims=True)
    variance = jnp.mean(centered * centered, axis=-1, keepdims=True)
    scale = lax.rsqrt(variance + NORM_EPSILON)
    unit = centered * scale
    grad_unit = grad_out * gain
    grad_gain = jnp.sum(grad_out * unit, axis=0, keepdims=True)
    grad_bias = jnp.sum(grad_out, axis=0, keepdims=True)
    grad_res = scale * (
        grad_unit
        - jnp.mean(grad_unit, axis=-1, keepdims=True)
        - unit * jnp.mean(grad_unit * unit, axis=-1, keepdims=True)
    )
    return grad_res, grad_gain, grad_bias


def gelu_both(pre):
    square = pre * pre
    bent = jnp.tanh(GELU_C * pre * (1.0 + GELU_A * square))
    half = 0.5 * (1.0 + bent)
    slope = half + (0.5 * GELU_C) * pre * (1.0 - bent * bent) * (1.0 + 3.0 * GELU_A * square)
    return pre * half, slope


def attend_forward(queries, keys, values, allowed, out_ref, totals_ref, rows):
    lane = lax.broadcasted_iota(jnp.int32, (1, PAIR), 1)
    for pair in range(HEADS // 2):
        q, k, v = queries(pair), keys(pair), values(pair)
        mixed = None
        for side in range(2):
            own = (lane < HEAD) if side == 0 else (lane >= HEAD)
            scores = mm_nt(k, jnp.where(own, q * HEAD ** (-0.5), 0))
            scores = jnp.where(allowed, scores, MASKED_SCORE)
            top = jnp.max(scores, axis=0, keepdims=True)
            weights = jnp.exp(scores - top)
            summed = jnp.sum(weights, axis=0, keepdims=True)
            probs = (weights * (1.0 / summed)).astype(BF16)
            totals_ref[2 * pair + side : 2 * pair + side + 1, :] = top + jnp.log(summed)
            part = mm_tn(probs, jnp.where(own, v, 0))
            mixed = part if mixed is None else mixed + part
        out_ref[rows, pair * PAIR : (pair + 1) * PAIR] = mixed.astype(BF16)


def attend_backward(
    queries, keys, values, grads, allowed, totals_ref, put_q, put_k, put_v, between=None
):
    lane = lax.broadcasted_iota(jnp.int32, (1, PAIR), 1)
    for pair in range(HEADS // 2):
        q, k, v, da = queries(pair), keys(pair), values(pair), grads(pair)
        grad_q = grad_k = grad_v = None
        for side in range(2):
            own = (lane < HEAD) if side == 0 else (lane >= HEAD)
            q_own = jnp.where(own, q * HEAD ** (-0.5), 0)
            da_own = jnp.where(own, da, 0)
            scores = jnp.where(allowed, mm_nt(k, q_own), MASKED_SCORE)
            probs = jnp.exp(scores - totals_ref[2 * pair + side : 2 * pair + side + 1, :])
            grad_probs = mm_nt(v, da_own)
            part_v = mm(probs.astype(BF16), da_own)
            shared = jnp.sum(probs * grad_probs, axis=0, keepdims=True)
            grad_scores = (probs * (grad_probs - shared)).astype(BF16)
            part_k = mm(grad_scores, q_own)
            part_q = mm_tn(grad_scores, jnp.where(own, k, 0))
            grad_q = part_q if grad_q is None else grad_q + part_q
            grad_k = part_k if grad_k is None else grad_k + part_k
            grad_v = part_v if grad_v is None else grad_v + part_v
        put_q(pair, (grad_q * HEAD ** (-0.5)).astype(BF16))
        put_k(pair, grad_k.astype(BF16))
        put_v(pair, grad_v.astype(BF16))
        if between is not None:
            between(pair)


def column(pair, offset=0):
    return slice(offset + pair * PAIR, offset + (pair + 1) * PAIR)


def put_shards(ref, first, grad):
    height = grad.shape[0] // GROUPS
    width = ref.shape[2]
    for block in range(grad.shape[1] // width):
        piece = grad[:, block * width : (block + 1) * width].astype(BF16)
        ref[:, first + block * height : first + (block + 1) * height, :] = piece.reshape(
            GROUPS, height, width
        )


def self_forward(
    x_ref, ids_ref, ids_row_ref, qkv_w_ref, mix_w_ref, gain_ref, bias_ref,
    qkv_ref, mixed_ref, res_ref, totals_ref, keep_ref, send_ref,
):
    phase = lax.axis_index("phase")
    count, length = ids_ref.shape[0], ids_ref.shape[1]
    width = x_ref.shape[1]
    for part in range(3):
        cols = slice(part * width, (part + 1) * width)
        qkv_ref[:, cols] = mm(x_ref[...], qkv_w_ref[:, cols]).astype(BF16)
    for row in range(count):
        rows = slice(row * length, (row + 1) * length)
        attend_forward(
            lambda pair: qkv_ref[rows, column(pair)],
            lambda pair: qkv_ref[rows, column(pair, width)],
            lambda pair: qkv_ref[rows, column(pair, 2 * width)],
            ids_ref[row] == ids_row_ref[row],
            mixed_ref, totals_ref.at[row], rows,
        )
    for row in range(count):
        rows = slice(row * length, (row + 1) * length)
        residual = x_ref[rows, :].astype(F32) + mm(mixed_ref[rows, :], mix_w_ref[...])
        res_ref[rows, :] = residual
        after = norm_forward(residual, gain_ref[0:1, :], bias_ref[0:1, :])

        @pl.when(phase == row)
        def _():
            keep_ref[...] = after

        @pl.when(phase != row)
        def _():
            send_ref[...] = after


def load_sided(phase, own_refs, other_refs, enc_refs, dec_refs, sems):
    for i, (own, other, enc, dec) in enumerate(zip(own_refs, other_refs, enc_refs, dec_refs)):
        @pl.when(phase == 0)
        def _():
            pltpu.make_async_copy(own, enc, sems.at[0, i]).start()
            pltpu.make_async_copy(other, dec, sems.at[1, i]).start()

        @pl.when(phase != 0)
        def _():
            pltpu.make_async_copy(other, enc, sems.at[0, i]).start()
            pltpu.make_async_copy(own, dec, sems.at[1, i]).start()

    def wait_enc(i):
        pltpu.make_async_copy(own_refs[i], enc_refs[i], sems.at[0, i]).wait()

    def wait_dec(i):
        pltpu.make_async_copy(own_refs[i], dec_refs[i], sems.at[1, i]).wait()

    return wait_enc, wait_dec


def feed_forward(middle, up_ref, down_ref, hidden_ref, slope_ref):
    width = middle.shape[1]
    low = middle.astype(BF16)
    total = middle
    for part in range(up_ref.shape[1] // width):
        cols = slice(part * width, (part + 1) * width)
        hidden, slope = gelu_both(mm(low, up_ref[:, cols]))
        hidden = hidden.astype(BF16)
        hidden_ref[:, cols] = hidden
        slope_ref[:, cols] = slope.astype(BF16)
        total = total + mm(hidden, down_ref[cols, :])
    return total


def feed_back(grad_res, middle_low, up_ref, down_ref, hidden_ref, slope_ref, put_up, put_down, between=None):
    width = grad_res.shape[1]
    branch = grad_res.astype(BF16)
    total = grad_res
    for part in range(up_ref.shape[1] // width):
        cols = slice(part * width, (part + 1) * width)
        put_down(part, mm_tn(hidden_ref[:, cols], branch))
        grad_hidden = mm_nt(branch, down_ref[cols, :])
        grad_pre = (grad_hidden * slope_ref[:, cols].astype(F32)).astype(BF16)
        put_up(part, mm_tn(middle_low, grad_pre))
        total = total + mm_nt(grad_pre, up_ref[:, cols])
        if between is not None:
            between(part)
    return total


def feed_puts(ref, parts):
    width = ref.shape[2]
    rows = width // GROUPS
    per, tall = GROUPS // parts, parts * rows

    def put_up(part, value):
        put_shards(ref, part * rows, value)

    def put_down(part, value):
        ref[part * per : (part + 1) * per, tall : 2 * tall, :] = value.astype(BF16).reshape(
            per, tall, width
        )

    return put_up, put_down


def class_grads(logits, labels, row_weight, valid):
    lane = lax.broadcasted_iota(jnp.int32, logits.shape, 1)
    logits = jnp.where(lane < valid, logits, -jnp.inf) if valid < logits.shape[1] else logits
    top = jnp.max(logits, axis=-1, keepdims=True)
    weights = jnp.exp(logits - top)
    probs = weights * (1.0 / jnp.sum(weights, axis=-1, keepdims=True))
    return (probs - (lane == labels).astype(F32)) * row_weight


def rows_forward(
    scale, keep_ref, recv_ref, ids_e_ref, ids_d_row_ref, targets_ref,
    up_own, up_other, down_own, down_other, norms_ref,
    cq_w_ref, ckv_w_ref, co_w_ref, cgain_ref, cbias_ref, delete_w_ref, place_w_ref,
    after_e_ref, res_e_ref, after_d_ref, ckv_ref, cq_ref, cmixed_ref, cres_ref, ctotals_ref,
    hid_e_ref, slope_e_ref, hid_d_ref, slope_d_ref, res_d_ref, src_ref,
    low_ref, grad_ref, grad_delete_ref, grad_place_ref,
    up_e, down_e, up_d, down_d, sems,
):
    phase = lax.axis_index("phase")
    width = keep_ref.shape[1]
    wait_enc, wait_dec = load_sided(
        phase, (up_own, down_own), (up_other, down_other), (up_e, down_e), (up_d, down_d), sems
    )

    @pl.when(phase == 0)
    def _():
        after_e_ref[...] = keep_ref[...]
        after_d_ref[...] = recv_ref[...]

    @pl.when(phase != 0)
    def _():
        after_e_ref[...] = recv_ref[...]
        after_d_ref[...] = keep_ref[...]

    wait_enc(0)
    wait_enc(1)
    encoder_rows(
        after_e_ref, up_e, down_e, norms_ref[0:1, :], norms_ref[1:2, :], ckv_w_ref,
        hid_e_ref, slope_e_ref, res_e_ref, src_ref, ckv_ref,
    )
    middle = cross_rows(
        after_d_ref, ids_e_ref[...] == ids_d_row_ref[...], cq_w_ref, co_w_ref, cgain_ref, cbias_ref,
        cq_ref, ckv_ref, cmixed_ref, cres_ref, ctotals_ref,
    )
    wait_dec(0)
    wait_dec(1)
    targets = targets_ref[...]
    decoder_rows(
        scale, middle, up_d, down_d, norms_ref[2:3, :], norms_ref[3:4, :],
        targets[:, 0:1], targets[:, 1:2], targets[:, 2:3], delete_w_ref, place_w_ref,
        hid_d_ref, slope_d_ref, res_d_ref, low_ref, grad_ref, grad_delete_ref, grad_place_ref,
    )


def encoder_rows(
    after_ref, up, down, gain, bias, ckv_w_ref, hid_ref, slope_ref, res_ref, src_ref, ckv_ref
):
    residual = feed_forward(after_ref[...], up, down, hid_ref, slope_ref)
    res_ref[...] = residual
    src = norm_forward(residual, gain, bias).astype(BF16)
    src_ref[...] = src
    width = src.shape[1]
    for part in range(2):
        cols = slice(part * width, (part + 1) * width)
        ckv_ref[:, cols] = mm(src, ckv_w_ref[:, cols]).astype(BF16)


def cross_rows(
    after_ref, allowed, cq_w_ref, co_w_ref, cgain_ref, cbias_ref, cq_ref, ckv_ref, cmixed_ref, cres_ref, ctotals_ref
):
    width = after_ref.shape[1]
    cq_ref[...] = mm(after_ref[...].astype(BF16), cq_w_ref[...]).astype(BF16)
    attend_forward(
        lambda pair: cq_ref[:, column(pair)],
        lambda pair: ckv_ref[:, column(pair)],
        lambda pair: ckv_ref[:, column(pair, width)],
        allowed, cmixed_ref, ctotals_ref, slice(None),
    )
    residual = after_ref[...] + mm(cmixed_ref[...], co_w_ref[...])
    cres_ref[...] = residual
    return norm_forward(residual, cgain_ref[...], cbias_ref[...])


def decoder_rows(
    scale, middle, up, down, gain, bias, delete_label, place_label, pair_valid, delete_w_ref, place_w_ref,
    hid_ref, slope_ref, res_ref, low_ref, grad_ref, grad_delete_ref, grad_place_ref,
):
    residual = feed_forward(middle, up, down, hid_ref, slope_ref)
    res_ref[...] = residual
    low = norm_forward(residual, gain, bias).astype(BF16)
    low_ref[...] = low
    length, width = low.shape
    valid = delete_w_ref.shape[0]
    weight = jnp.concatenate([delete_w_ref[...], jnp.zeros((128 - valid, width), BF16)], axis=0)
    grads = class_grads(mm_nt(low, weight), delete_label, scale, valid).astype(BF16)
    grad_delete_ref[...] = mm_tn(grads, low)[:8]
    grad_low = mm(grads, weight)
    logits = mm(low, place_w_ref[:width, :]) + pltpu.roll(
        mm(low, place_w_ref[width:, :]), length - 1, 0
    )
    weight = pair_valid.astype(F32) * scale
    grads = class_grads(logits, place_label, weight, logits.shape[1])
    later = pltpu.roll(grads, 1, 0).astype(BF16)
    grads = grads.astype(BF16)
    classes = grads.shape[1]
    for top, part in enumerate((grads, later)):
        part = mm_tn(low, part).astype(BF16).reshape(GROUPS // 2, 2, width // GROUPS, classes)
        at = slice(top * GROUPS // 2, (top + 1) * GROUPS // 2)
        for half in range(2):
            grad_place_ref[at, :, half * classes : (half + 1) * classes] = part[:, half]
    grad_low = grad_low + mm_nt(grads, place_w_ref[:width, :]) + mm_nt(later, place_w_ref[width:, :])
    grad_ref[...] = grad_low


def rows_backward(
    grad_low_ref, grad_token_ref, ids_e_ref, ids_d_row_ref,
    up_own, up_other, down_own, down_other, norms_ref,
    cq_w_ref, ckv_w_ref, co_w_ref, cgain_ref, cbias_ref,
    after_e_ref, res_e_ref, after_d_ref, ckv_ref, cq_ref, cmixed_ref, cres_ref, ctotals_ref,
    hid_e_ref, slope_e_ref, hid_d_ref, slope_d_ref, res_d_ref, src_ref, grad_place_ref,
    keep_ref, send_ref, own_ref, other_ref, cross_ref, vectors_ref,
    up_e, down_e, up_d, down_d, grad_e, grad_d, after_e_grad, after_d_grad, gq_ref, gckv_ref, sems, out_sems,
):
    phase = lax.axis_index("phase")
    width = grad_low_ref.shape[1]
    wait_enc, wait_dec = load_sided(
        phase, (up_own, down_own), (up_other, down_other), (up_e, down_e), (up_d, down_d), sems
    )
    grad_out = grad_low_ref[...] + grad_token_ref[...]
    grad_res, gain_grad, bias_grad = norm_back(res_d_ref[...], norms_ref[2:3, :], grad_out)
    vectors_ref[2:3, :] = gain_grad
    vectors_ref[3:4, :] = bias_grad
    cres = cres_ref[...]
    middle_low = norm_forward(cres, cgain_ref[...], cbias_ref[...]).astype(BF16)
    wait_dec(0)
    wait_dec(1)
    grad_middle = feed_back(grad_res, middle_low, up_d, down_d, hid_d_ref, slope_d_ref, *feed_puts(grad_d, 4))
    move_d = [
        pltpu.make_async_copy(grad_d, own_ref, out_sems.at[0]),
        pltpu.make_async_copy(grad_d, other_ref, out_sems.at[0]),
    ]

    @pl.when(phase == 0)
    def _():
        move_d[1].start()

    @pl.when(phase != 0)
    def _():
        move_d[0].start()

    grad_res, gain_grad, bias_grad = norm_back(cres, cgain_ref[...], grad_middle)
    vectors_ref[4:5, :] = gain_grad
    vectors_ref[5:6, :] = bias_grad
    branch = grad_res.astype(BF16)
    after_low = after_d_ref[...].astype(BF16)
    rows = width // GROUPS
    put_shards(cross_ref, 3 * rows, mm_tn(cmixed_ref[...], branch))
    grad_mixed = mm_nt(branch, co_w_ref[...]).astype(BF16)

    def put_q(pair, value):
        gq_ref[:, column(pair)] = value

    def put_k(pair, value):
        gckv_ref[:, column(pair)] = value

    def put_v(pair, value):
        gckv_ref[:, column(pair, width)] = value

    attend_backward(
        lambda pair: cq_ref[:, column(pair)],
        lambda pair: ckv_ref[:, column(pair)],
        lambda pair: ckv_ref[:, column(pair, width)],
        lambda pair: grad_mixed[:, column(pair)],
        ids_e_ref[...] == ids_d_row_ref[...],
        ctotals_ref, put_q, put_k, put_v,
    )
    grad_q = gq_ref[...]
    grad_kv = gckv_ref[...]
    put_shards(cross_ref, 0, mm_tn(after_low, grad_q))
    put_shards(cross_ref, rows, mm_tn(src_ref[...], grad_kv))
    cross_ref[:, 4 * rows : 5 * rows, :] = grad_place_ref[...]
    after_d_grad[...] = grad_res + mm_nt(grad_q, cq_w_ref[...])
    grad_src = mm_nt(grad_kv, ckv_w_ref[...]).astype(BF16).astype(F32)
    grad_res, gain_grad, bias_grad = norm_back(res_e_ref[...], norms_ref[0:1, :], grad_src)
    vectors_ref[0:1, :] = gain_grad
    vectors_ref[1:2, :] = bias_grad
    vectors_ref[6:8, :] = jnp.zeros((2, width), F32)
    wait_enc(0)
    wait_enc(1)
    after_e_grad[...] = feed_back(
        grad_res, after_e_ref[...].astype(BF16), up_e, down_e, hid_e_ref, slope_e_ref,
        *feed_puts(grad_e, 4),
    )
    move_e = [
        pltpu.make_async_copy(grad_e, own_ref, out_sems.at[1]),
        pltpu.make_async_copy(grad_e, other_ref, out_sems.at[1]),
    ]

    @pl.when(phase == 0)
    def _():
        move_e[0].start()
        keep_ref[...] = after_e_grad[...]
        send_ref[...] = after_d_grad[...]

    @pl.when(phase != 0)
    def _():
        move_e[1].start()
        keep_ref[...] = after_d_grad[...]
        send_ref[...] = after_e_grad[...]

    move_d[0].wait()
    move_e[0].wait()


def self_backward(
    keep_ref, recv_ref, x_ref, ids_ref, ids_row_ref, qkv_w_ref, mix_w_ref, gain_ref,
    qkv_ref, mixed_ref, res_ref, totals_ref,
    grad_x_ref, shards_ref, vectors_ref,
    after_grad, grad_qkv,
):
    phase = lax.axis_index("phase")
    count, length = ids_ref.shape[0], ids_ref.shape[1]
    width = x_ref.shape[1]
    for row in range(count):
        rows = slice(row * length, (row + 1) * length)

        @pl.when(phase == row)
        def _():
            after_grad[rows, :] = keep_ref[...]

        @pl.when(phase != row)
        def _():
            after_grad[rows, :] = recv_ref[...]

    grad_res, gain_grad, bias_grad = norm_back(res_ref[...], gain_ref[0:1, :], after_grad[...])
    vectors_ref[0:1, :] = gain_grad
    vectors_ref[1:2, :] = bias_grad
    vectors_ref[2:8, :] = jnp.zeros((6, width), F32)
    grad_x_ref[...] = grad_res
    branch = grad_res.astype(BF16)
    rows_each = width // GROUPS
    put_shards(shards_ref, 3 * rows_each, mm_tn(mixed_ref[...], branch))
    grad_mixed = mm_nt(branch, mix_w_ref[...]).astype(BF16)
    for row in range(count):
        rows = slice(row * length, (row + 1) * length)

        def put(offset):
            def store(pair, value):
                grad_qkv[rows, column(pair, offset)] = value

            return store

        attend_backward(
            lambda pair: qkv_ref[rows, column(pair)],
            lambda pair: qkv_ref[rows, column(pair, width)],
            lambda pair: qkv_ref[rows, column(pair, 2 * width)],
            lambda pair: grad_mixed[rows, column(pair)],
            ids_ref[row] == ids_row_ref[row],
            totals_ref.at[row], put(0), put(width), put(2 * width),
        )
    for part in range(3):
        cols = slice(part * width, (part + 1) * width)
        put_shards(shards_ref, part * rows_each, mm_tn(x_ref[...], grad_qkv[:, cols]))
    grad_x_ref[...] += mm_nt(grad_qkv[...], qkv_w_ref[...])


def token_forward(low_ref, weight_ref, probs_ref, totals_ref):
    logits = mm_nt(weight_ref[...], low_ref[...])
    top = jnp.max(logits, axis=0, keepdims=True)
    weights = jnp.exp(logits - top)
    summed = jnp.sum(weights, axis=0, keepdims=True)
    probs_ref[0] = (weights * (1.0 / summed)).astype(BF16)
    totals_ref[0] = top + jnp.log(summed)


def token_backward(
    scale, probs_ref, share_ref, label_ref, low_ref, weight_ref, grad_low_ref, grad_weight_ref, total
):
    step = pl.program_id(0)
    labels = label_ref[0]
    shape = probs_ref.shape[1:]
    offset = (lax.axis_index("dp") * 2 + lax.axis_index("phase")) * shape[0]
    chosen = lax.broadcasted_iota(jnp.int32, shape, 0) == labels - offset
    grads = probs_ref[0].astype(F32) * share_ref[0] - chosen.astype(F32)
    grads = (grads * jnp.where(labels >= 0, scale, 0.0)).astype(BF16)
    grad_low = mm_tn(grads, weight_ref[...]).astype(BF16)
    cap = grad_low_ref.shape[1]
    for block in range(grad_low_ref.shape[0]):
        grad_low_ref[block] = grad_low[block * cap : (block + 1) * cap]
    part = mm(grads, low_ref[...])

    @pl.when(step == 0)
    def _():
        total[...] = part

    @pl.when(step != 0)
    def _():
        total[...] += part

    @pl.when(step == pl.num_programs(0) - 1)
    def _():
        grad_weight_ref[...] = total[...].T


def place_of(dp):
    return lax.rem(dp, 2), lax.rem(dp // 2, 2), dp // 4


def index_of(x, y, z):
    return (z * 2 + y) * 2 + x


def greet(devices):
    barrier = pltpu.get_barrier_semaphore()
    for dp, phase in devices:
        pl.semaphore_signal(barrier, inc=1, device_id=(dp, phase), device_id_type=MESH)
    return lambda: pl.semaphore_wait(barrier, len(devices))


def remote(src, dst, send, recv, device):
    return pltpu.make_async_remote_copy(
        src_ref=src, dst_ref=dst, send_sem=send, recv_sem=recv, device_id=device, device_id_type=MESH
    )


def gather_blocks(block):
    return lax.all_gather(lax.all_gather(block, "dp"), "phase")


def scatter_blocks(part):
    part = lax.psum_scatter(part.astype(F32), "phase", scatter_dimension=0, tiled=False)
    return lax.psum_scatter(part, "dp", scatter_dimension=0, tiled=False)


def token_shares(totals):
    top = lax.pmax(totals, ("dp", "phase"))
    return jnp.exp(totals - top) / lax.psum(jnp.exp(totals - top), ("dp", "phase"))


def pack_labels(labels, flags, out_ref):
    count, length = labels.shape
    before = lax.broadcasted_iota(jnp.int32, (length, length), 0)
    after = lax.broadcasted_iota(jnp.int32, (length, length), 1)
    upto = jnp.where(before <= after, 1.0, 0.0).astype(BF16)
    rows = jnp.concatenate([flags.astype(F32)] + [jnp.zeros((8 - count, length), F32)], axis=0)
    place = mm(rows.astype(BF16), upto)
    for row in range(count):
        flag = rows[row : row + 1]
        chosen = (before.astype(F32) == place[row : row + 1] - 1.0) & (flag > 0.0)
        label = labels[row : row + 1]
        high = lax.shift_right_logical(label, 8)
        parts = [high.astype(F32), (label - high * 256).astype(F32), flag, jnp.zeros((5, length), F32)]
        found = mm_nt(
            jnp.concatenate(parts, axis=0).astype(BF16), jnp.where(chosen, 1.0, 0.0).astype(BF16)
        )
        packed = jnp.where(found[2:3] > 0.5, found[0:1] * 256.0 + found[1:2], -1.0)
        out_ref[row : row + 1, :] = packed.astype(jnp.int32)


FORWARD = (
    "qkv", "mixed", "res", "after", "res_e", "ckv", "cq", "cmixed", "cres",
    "hid_e", "slope_e", "hid_d", "slope_d", "res_d", "src", "low", "grad_low", "grad_place",
)


def forward_kernel(
    scale, x_ref, segments_ref, delete_ref, place_ref, token_ref, mask_ref,
    qkv_w_ref, mix_w_ref, gain_ref, bias_ref, up_own, down_own,
    cq_w_any, ckv_w_any, co_w_any, cgain_ref, cbias_ref, delete_w_ref, place_w_any,
    rows_ref, cols_ref, labels_small_ref, labels_large_ref, most_ref, norms_ref, up_other, down_other,
    totals_ref, ctotals_ref, grad_delete_ref, *rest,
):
    outs, rest = dict(zip(FORWARD, rest)), rest[len(FORWARD) :]
    held, rest = dict(zip(FORWARD, rest)), rest[len(FORWARD) :]
    up, down, cq_w, ckv_w, co_w, place_w, send_after, own_labels, all_labels, turned, load, store, send, recv = rest
    dp, phase = lax.axis_index("dp"), lax.axis_index("phase")
    x, y, z = place_of(dp)
    chips = [
        (lax.rem(x + a, 2), lax.rem(y + b, 2), lax.rem(z + c, 4))
        for c in range(4) for b in range(2) for a in range(2) if a + b + c
    ]
    core = (dp, 1 - phase)
    met = greet([(index_of(*chip), phase) for chip in chips] + [core])
    copies, stores = [], []

    def remote_to(src, dst, device):
        i = len(copies)
        copy = remote(src, dst, send.at[i], recv.at[i], device)
        copy.start()
        copies.append(copy)
        return copy

    def save(*names):
        for name in names:
            copy = pltpu.make_async_copy(held[name], outs[name], store.at[len(stores)])
            copy.start()
            stores.append(copy)

    loads = [
        pltpu.make_async_copy(src, dst, load.at[i])
        for i, (src, dst) in enumerate((
            (up_own, up.at[phase]), (down_own, down.at[phase]), (ckv_w_any, ckv_w), (cq_w_any, cq_w),
            (co_w_any, co_w), (place_w_any, place_w),
        ))
    ]
    for copy in loads:
        copy.start()
    norms_ref[phase, 0:1, :] = gain_ref[1:2, :]
    norms_ref[phase, 1:2, :] = bias_ref[1:2, :]
    pack_labels(token_ref[...], mask_ref[...], own_labels)
    all_labels[z, y, x] = own_labels[...]
    width = x_ref.shape[1]
    qkv, mixed, res = held["qkv"], held["mixed"], held["res"]
    for part in range(3):
        span = slice(part * width, (part + 1) * width)
        qkv[:, span] = mm(x_ref[...], qkv_w_ref[:, span]).astype(BF16)
    save("qkv")
    met()
    from_norms = remote_to(norms_ref.at[phase], norms_ref.at[phase], core)
    from_up = remote_to(up_own, up.at[phase], core)
    from_down = remote_to(down_own, down.at[phase], core)
    for chip in chips:
        remote_to(own_labels, all_labels.at[z, y, x], (index_of(*chip), phase))
    label_copies = copies[3:]
    is_enc = phase == 0
    segments = segments_ref[...].astype(F32)
    length = segments.shape[2]

    def pick(first, second):
        return jnp.where(is_enc, first, second)

    def own_row(ref):
        value = ref[...].astype(F32)
        return pick(value[0:1], value[1:2])

    ids_e = pick(segments[0, 0:1], segments[1, 0:1])
    ids_d = pick(segments[0, 1:2], segments[1, 1:2])
    own_ids = [pick(segments[r, 0:1], segments[r, 1:2]) for r in range(2)]
    block = jnp.concatenate([ids_d] * 8, axis=0)
    later = pltpu.roll(block, length - 1, 1)
    lane = lax.broadcasted_iota(jnp.int32, (8, length), 1)
    valid = jnp.where((block == later) & (lane < length - 1), 1.0, 0.0)[0:1]
    rows = jnp.concatenate(
        own_ids + [ids_e, ids_d, own_row(delete_ref), own_row(place_ref), valid, own_row(mask_ref)], axis=0
    )
    rows_ref[...] = rows
    turned[...] = jnp.zeros(turned.shape, F32)
    turned[0:8, :] = rows
    cols = turned[...].T
    cols_ref[...] = cols
    for turn in range(2):
        row = 1 - phase if turn == 0 else phase
        span = pl.ds(pl.multiple_of(row * length, length), length)
        allowed = jnp.where(row == 0, cols[:, 0:1], cols[:, 1:2]) == jnp.where(
            row == 0, own_ids[0], own_ids[1]
        )
        attend_forward(
            lambda pair: qkv[span, column(pair)],
            lambda pair: qkv[span, column(pair, width)],
            lambda pair: qkv[span, column(pair, 2 * width)],
            allowed, mixed, totals_ref.at[row], span,
        )
        residual = x_ref[span, :].astype(F32) + mm(mixed[span, :], mix_w_ref[...])
        res[span, :] = residual
        after = norm_forward(residual, gain_ref[0:1, :], bias_ref[0:1, :])
        if turn == 0:
            send_after[...] = after
            from_after = remote_to(send_after, held["after"].at[phase], core)
        else:
            held["after"][phase] = after
    save("mixed", "res")
    from_after.wait_recv()
    save("after")
    from_norms.wait_recv()
    from_up.wait_recv()
    from_down.wait_recv()
    for copy in loads:
        copy.wait()
    for i, (src, dst) in enumerate(((up, up_other), (down, down_other))):
        copy = pltpu.make_async_copy(src.at[1 - phase], dst, store.at[len(stores)])
        copy.start()
        stores.append(copy)
    encoder_rows(
        held["after"].at[0], up.at[0], down.at[0], norms_ref[0, 0:1, :], norms_ref[0, 1:2, :], ckv_w,
        held["hid_e"], held["slope_e"], held["res_e"], held["src"], held["ckv"],
    )
    save("hid_e", "slope_e", "res_e", "src", "ckv")
    middle = cross_rows(
        held["after"].at[1], cols[:, 2:3] == rows[3:4], cq_w, co_w, cgain_ref, cbias_ref,
        held["cq"], held["ckv"], held["cmixed"], held["cres"], ctotals_ref,
    )
    save("cq", "cmixed", "cres")
    decoder_rows(
        scale, middle, up.at[1], down.at[1], norms_ref[1, 0:1, :], norms_ref[1, 1:2, :],
        cols[:, 4:5].astype(jnp.int32), cols[:, 5:6].astype(jnp.int32), cols[:, 6:7], delete_w_ref, place_w,
        held["hid_d"], held["slope_d"], held["res_d"], held["low"], held["grad_low"],
        grad_delete_ref, held["grad_place"],
    )
    save("hid_d", "slope_d", "res_d", "low", "grad_low", "grad_place")
    for copy in label_copies:
        copy.wait_recv()
    small = length // 2
    for at, (p, yy, xx, zz) in enumerate(
        (p, yy, xx, zz) for p in range(2) for yy in range(2) for xx in range(2) for zz in range(4)
    ):
        line = all_labels[zz, yy, xx, p : p + 1, :]
        labels_small_ref[:, at * small : (at + 1) * small] = line[:, :small]
        labels_large_ref[:, at * length : (at + 1) * length] = line
    beyond = jnp.max(all_labels[:, :, :, :, small:].astype(F32).reshape(2 * GROUPS, length - small))
    most_ref[...] = jnp.full(most_ref.shape, beyond, F32)
    for copy in copies:
        copy.wait_send()
    for copy in stores:
        copy.wait()


def token_kernel(
    scale, cap, low_ref, rows_ref, cols_ref, labels_ref, head_any,
    grad_ref, grad_weight_ref,
    weight, weight_t, every, probs, totals, near_in, joined, far_in, shares,
    part, core_in, third_in, second_in, z_in, load, send, recv,
):
    dp, phase = lax.axis_index("dp"), lax.axis_index("phase")
    x, y, z = place_of(dp)
    x_first = phase == 0
    x2, y2 = jnp.where(x_first, 1 - x, x), jnp.where(x_first, y, 1 - y)
    x3, y3 = jnp.where(x_first, x, 1 - x), jnp.where(x_first, 1 - y, y)
    second, third, core = (index_of(x2, y2, z), phase), (index_of(x3, y3, z), phase), (dp, 1 - phase)
    zs = [lax.rem(z + k, 4) for k in (1, 2, 3)]
    along = [(index_of(x, y, k), phase) for k in zs]
    shard, length = weight_t.shape[0], low_ref.shape[0]
    near = [
        (index_of(lax.rem(x + a, 2), lax.rem(y + b, 2), z), lax.rem(phase + c, 2))
        for a in range(2) for b in range(2) for c in range(2) if a + b + c
    ]
    met = greet(near + along)
    offset = pl.multiple_of((dp * 2 + phase) * shard, shard)
    weight_copy = pltpu.make_async_copy(head_any.at[:, pl.ds(offset, shard)], weight, load.at[0])
    weight_copy.start()
    copies = []

    def remote_to(src, dst, device):
        i = len(copies)
        copy = remote(src, dst, send.at[i], recv.at[i], device)
        copy.start()
        copies.append(copy)
        return copy

    def unit(p, yy, xx):
        return (p * 2 + yy) * 2 + xx

    def block(u, zz):
        return pl.ds(pl.multiple_of((u * 4 + zz) * cap, cap), cap)

    before = lax.broadcasted_iota(jnp.int32, (length, length), 0)
    after = lax.broadcasted_iota(jnp.int32, (length, length), 1)
    rows = rows_ref[...]
    place = mm(rows.astype(BF16), jnp.where(before <= after, 1.0, 0.0).astype(BF16))[7:8]
    slot = lax.broadcasted_iota(jnp.int32, (cap, length), 0).astype(F32)
    chosen = jnp.where((slot == place - 1.0) & (rows[7:8] > 0.0), 1.0, 0.0).astype(BF16)
    own = unit(phase, y, x)
    every[block(own, z), :] = mm(chosen, low_ref[...]).astype(BF16)
    def relay(u, zz, device):
        here = every.at[block(u, zz), :]
        return remote_to(here, here, device)

    beside, across = (index_of(x, y, z + 1 - 2 * lax.rem(z, 2)), phase), (index_of(x, y, lax.rem(z + 2, 4)), phase)
    met()
    firsts = [relay(own, z, beside), relay(own, z, across)]
    cross = [relay(own, z, core)]
    seconds = [relay(own, z, second)]
    thirds = [relay(own, z, third)]
    weight_copy.wait()
    weight_t[...] = weight[...].T
    near_z = z + 1 - 2 * lax.rem(z, 2)
    sources = [near_z, lax.rem(z + 2, 4), lax.rem(near_z + 2, 4)]
    order = [z] + sources
    for k in range(3):
        firsts[k].wait_recv()
        if k == 0:
            firsts.append(relay(own, near_z, across))
        seconds.append(relay(own, sources[k], second))
        thirds.append(relay(own, sources[k], third))
        cross.append(relay(own, sources[k], core))
    tall = 256
    chunks = 4 * cap // tall

    def look(u):
        def step(j, _):
            span = pl.ds(pl.multiple_of((u * chunks + j) * tall, tall), tall)
            logits = mm_nt(weight_t[...], every[span, :])
            top = jnp.max(logits, axis=0, keepdims=True)
            weights = jnp.exp(logits - top)
            summed = jnp.sum(weights, axis=0, keepdims=True)
            probs[:, span] = (weights * (1.0 / summed)).astype(BF16)
            totals[:, span] = top + jnp.log(summed)
            return 0

        lax.fori_loop(0, chunks, step, 0)

    def arrived(some):
        for copy in some:
            copy.wait_recv()

    look(own)
    for k in range(4):
        seconds[k].wait_recv()
        thirds.append(relay(unit(phase, y2, x2), order[k], third))
        cross.append(relay(unit(phase, y2, x2), order[k], core))
    arrived(cross[0:4])
    look(unit(1 - phase, y, x))
    look(unit(phase, y2, x2))
    for k in range(4):
        thirds[k].wait_recv()
        cross.append(relay(unit(phase, y3, x3), order[k], core))
    arrived(cross[4:8])
    look(unit(1 - phase, y3, x3))
    for k in range(4):
        thirds[4 + k].wait_recv()
        cross.append(relay(unit(phase, 1 - y, 1 - x), order[k], core))
    look(unit(phase, y3, x3))
    arrived(cross[8:12])
    look(unit(1 - phase, y2, x2))
    look(unit(phase, 1 - y, 1 - x))
    arrived(cross[12:16])
    look(unit(1 - phase, 1 - y, 1 - x))

    def join(parts):
        top = parts[0]
        for piece in parts[1:]:
            top = jnp.maximum(top, piece)
        summed = jnp.exp(parts[0] - top)
        for piece in parts[1:]:
            summed = summed + jnp.exp(piece - top)
        return top + jnp.log(summed)

    near_copies = [remote_to(totals, near_in.at[j], device) for j, device in enumerate(near)]
    arrived(near_copies)
    total = join([totals[...]] + [near_in[j] for j in range(7)])
    joined[...] = total
    far_copies = [remote_to(joined, far_in.at[j], device) for j, device in enumerate(along)]
    arrived(far_copies)
    shares[...] = jnp.exp(totals[...] - join([total] + [far_in[j] for j in range(3)]))

    per = tall // cap

    def learn(u):
        def step(j, _):
            span = pl.ds(pl.multiple_of((u * chunks + j) * tall, tall), tall)
            labels = labels_ref[:, span]
            hit = lax.broadcasted_iota(jnp.int32, (shard, tall), 0) == labels - offset
            grads = probs[:, span].astype(F32) * shares[:, span] - jnp.where(hit, 1.0, 0.0)
            grads = (grads * jnp.where(labels >= 0, scale, 0.0)).astype(BF16)
            probs[:, span] = grads
            back = mm(weight[...], grads).astype(BF16)
            for k in range(per):
                part[u, j * per + k] = back[:, k * cap : (k + 1) * cap]
            return 0

        lax.fori_loop(0, chunks, step, 0)

    def add(u, zz, *others):
        value = part[u, zz].astype(F32)
        for other in others:
            value = value + other.astype(F32)
        part[u, zz] = value.astype(BF16)

    mine = [unit(phase, 1 - y, 1 - x), unit(phase, y3, x3), unit(phase, y2, x2), own]
    theirs = [
        unit(1 - phase, 1 - y, 1 - x), unit(1 - phase, y2, x2), unit(1 - phase, y3, x3), unit(1 - phase, y, x)
    ]
    route = zs + [z]
    core_copies, third_copies = [], []

    def to_third(k):
        core_copies[k].wait_recv()
        for j, zz in enumerate(route):
            add(mine[k], zz, core_in[k, zz])
            third_copies.append(remote_to(part.at[mine[k], zz], third_in.at[k, j], third))

    for k in range(4):
        learn(theirs[k])
        core_copies.append(remote_to(part.at[theirs[k]], core_in.at[k], core))
        learn(mine[k])
        if k < 2:
            to_third(k)
    core_copies[2].wait_recv()
    second_copies = []
    for j, zz in enumerate(route):
        third_copies[j].wait_recv()
        add(mine[2], zz, core_in[2, zz], third_in[0, j])
        second_copies.append(remote_to(part.at[mine[2], zz], second_in.at[j], second))

    slab = min(256, shard)

    def weigh(k):
        value = mm(probs[k * slab : (k + 1) * slab, :], every[...])
        grad_weight_ref[:, k * slab : (k + 1) * slab] = value.T

    slabs = shard // slab
    for k in range((slabs + 1) // 2):
        weigh(k)
    core_copies[3].wait_recv()
    z_copies = []
    for j, zz in enumerate(route):
        third_copies[4 + j].wait_recv()
        second_copies[j].wait_recv()
        add(own, zz, core_in[3, zz], third_in[1, j], second_in[j])
        if j < 3:
            z_copies.append(remote_to(part.at[own, zz], z_in.at[j], along[j]))
    for k in range((slabs + 1) // 2, slabs):
        weigh(k)
    arrived(z_copies)
    back = part[own, z].astype(F32)
    for j in range(3):
        back = back + z_in[j].astype(F32)
    place = mm(jnp.where(after <= before, 1.0, 0.0).astype(BF16), cols_ref[...].astype(BF16))[:, 7:8]
    slot = lax.broadcasted_iota(jnp.int32, (length, cap), 1).astype(F32)
    spread = jnp.where((slot == place - 1.0) & (cols_ref[:, 7:8] > 0.0), 1.0, 0.0).astype(BF16)
    grad_ref[...] = mm_nt(spread, back.astype(BF16))
    for copy in copies:
        copy.wait_send()


def token_chips(number, cap, low, rows, cols, labels, head):
    length, width = low.shape
    shard = head.shape[1] // (2 * GROUPS)
    count = 2 * GROUPS * cap
    scale = float(2 * length * GROUPS) ** (-0.5)
    copies = 64
    return pl.pallas_call(
        partial(token_kernel, scale, cap),
        out_shape=(whole((length, width), F32), whole((width, shard), F32)),
        in_specs=in_vmem(4) + [pl.BlockSpec(memory_space=pl.ANY)],
        out_specs=tuple(in_vmem(2)),
        scratch_shapes=[
            VMEM((width, shard), BF16), VMEM((shard, width), BF16), VMEM((count, width), BF16),
            VMEM((shard, count), BF16), VMEM((1, count), F32), VMEM((7, 1, count), F32), VMEM((1, count), F32),
            VMEM((3, 1, count), F32), VMEM((1, count), F32),
            VMEM((8, 4, width, cap), BF16), VMEM((4, 4, width, cap), BF16), VMEM((2, 4, width, cap), BF16),
            VMEM((4, width, cap), BF16), VMEM((3, width, cap), BF16),
            pltpu.SemaphoreType.DMA((1,)), pltpu.SemaphoreType.DMA((copies + 8,)), pltpu.SemaphoreType.DMA((copies + 8,)),
        ],
        compiler_params=pltpu.CompilerParams(
            collective_id=number, has_side_effects=True, vmem_limit_bytes=60 * 1024 * 1024
        ),
        name="token_head",
    )(low, rows, cols, labels, head)


class Exchange:
    def __init__(self, send, recv):
        self.dp, self.phase = lax.axis_index("dp"), lax.axis_index("phase")
        self.x, self.y, self.z = place_of(self.dp)
        x, y, z = self.x, self.y, self.z
        low, high = lax.rem(z, 2), z // 2
        self.own = {"b": high, "a": low, "y": y, "x": x}
        self.partner = {
            "b": index_of(x, y, (1 - high) * 2 + low), "a": index_of(x, y, high * 2 + 1 - low),
            "y": index_of(x, 1 - y, z), "x": index_of(1 - x, y, z),
        }
        self.send, self.recv, self.used, self.copies = send, recv, 0, []

    def greet(self):
        return greet([(self.partner[step], self.phase) for step in "bayx"] + [(self.dp, 1 - self.phase)])

    def copy(self, src, dst, device):
        copy = remote(src, dst, self.send.at[self.used], self.recv.at[self.used], device)
        self.used += 1
        copy.start()
        self.copies.append(copy)
        return copy

    def to_core(self, src, dst):
        return self.copy(src, dst, (self.dp, 1 - self.phase))

    def to_core_either(self, first, second):
        i = self.used
        self.used += 1
        made = [remote(*pair, self.send.at[i], self.recv.at[i], (self.dp, 1 - self.phase)) for pair in (first, second)]

        @pl.when(self.phase == 0)
        def _():
            made[0].start()

        @pl.when(self.phase != 0)
        def _():
            made[1].start()

        self.copies.append(made[0])
        return made[0]

    def finish(self):
        for copy in self.copies:
            copy.wait_send()


class Batch:
    def __init__(self, shards, ins, put, own=None):
        self.shards, self.ins, self.put, self.own, self.arriving = shards, ins, put, own, []


class Chunk:
    def __init__(self, exchange, batch, start, size, order):
        self.exchange, self.batch, self.order = exchange, batch, order
        self.rows, self.step, self.fixed = pl.ds(start, size), -1, {}

    def at(self, fixed, free):
        free = list(free)
        return tuple(fixed[name] if name in fixed else free.pop(0) for name in "bayx") + (self.rows,)

    def advance(self):
        batch, ex, rows = self.batch, self.exchange, self.rows
        shards = batch.shards
        if self.step < 0 and batch.own is not None:
            for copy in batch.arriving:
                copy.wait_recv()
            batch.arriving = []
            own = batch.own

            def join(i, _):
                at = (i // 8, lax.rem(i // 4, 2), lax.rem(i // 2, 2), lax.rem(i, 2), rows)
                shards[at] = (shards[at].astype(F32) + own[at].astype(F32)).astype(BF16)
                return 0

            lax.fori_loop(0, GROUPS, join, 0)
        elif self.step >= 0:
            self.arriving.wait_recv()
            name = self.order[self.step]
            self.fixed[name] = ex.own[name]
            free = 3 - self.step
            arrived = batch.ins[self.step]
            if free == 0:
                batch.put(rows, shards[self.at(self.fixed, ())].astype(F32) + arrived[rows].astype(F32))
            else:

                def add(i, _):
                    spot = tuple(lax.rem(i // 2 ** (free - 1 - k), 2) for k in range(free))
                    at = self.at(self.fixed, spot)
                    shards[at] = (shards[at].astype(F32) + arrived[spot + (rows,)].astype(F32)).astype(BF16)
                    return 0

                lax.fori_loop(0, 2**free, add, 0)
        self.step += 1
        if self.step < 4:
            name = self.order[self.step]
            free = (slice(None),) * (3 - self.step)
            src = shards.at[self.at({**self.fixed, name: 1 - ex.own[name]}, free)]
            dst = batch.ins[self.step].at[free + (rows,)]
            self.arriving = ex.copy(src, dst, (ex.partner[name], ex.phase))


PARTS = (
    ((0, 48, "yabx"), (48, 32, "xayb"), (80, 48, "axyb"),),
    ((0, 16, "xayb"), (16, 32, "xayb"), (48, 32, "yxab"),),
    ((0, 32, "xyab"), (32, 32, "byxa"), (64, 48, "yxab"), (112, 16, "yxab"),),
    (
        (0, 16, "ayxb"), (16, 16, "yxab"), (32, 16, "xyab"), (48, 16, "xyab"), (64, 16, "yxab"), (80, 16,
        "xyab"), (96, 16, "axby"), (112, 16, "yxab"),
    ),
)
SCHEDULE = (
    (),
    (0, 1, 2),
    (),
    (),
    (),
    (),
    (),
    (),
    (1, 3, 5),
    (4, 0, 2),
    (),
    (1, 3),
    (7, 8, 5),
    (),
    (1,),
    (0,),
    (3,),
    (),
    (6,),
    (),
    (4, 2, 3),
    (5, 9),
    (),
    (8,),
    (10, 6, 2),
    (
        9, 4, 16, 5, 12, 11, 1, 3, 0, 8, 6, 14, 13, 9, 10, 4, 0, 15, 17, 11, 2, 12, 5, 10, 9, 16, 13, 6, 8, 14, 4,
        7, 11, 12, 9, 10, 17, 15, 13, 11, 16, 12, 14, 6, 7, 10, 8, 17, 15, 13, 11, 14, 12, 7, 16, 17, 15, 13, 14,
        16, 7, 17, 15,
    ),
)
CROSS, CROSS_END, ENCODER, SELF, WEIGHTS, TAIL = 0, 5, 6, 11, 21, 25


BACKWARD = (
    "grad_low", "grad_token", "res_d", "cres", "co_w", "cmixed", "cq", "ckv", "grad_place", "after", "src", "cq_w", "ckv_w", "res_e",
    "res", "mix_w", "qkv", "mixed", "x", "qkv_w",
)


def backward_kernel(
    rows_ref, cols_ref, norms_ref, cgain_ref, cbias_ref, ctotals_ref, totals_ref, grad_delete_ref, gain_ref,
    up_own, up_other, down_own, down_other, hid_e_any, slope_e_any, hid_d_any, slope_d_any, *rest,
):
    held_any, rest = dict(zip(BACKWARD, rest)), rest[len(BACKWARD) :]
    grad_x_any, red_ff_ref, red_attention_ref, red_cross_ref, vectors_ref = rest[:5]
    held, rest = dict(zip(BACKWARD, rest[5:])), rest[5 + len(BACKWARD) :]
    (
        up, down, hid, slope, grad_d, grad_e, grad_c, grad_a, core_d, core_e, core_c,
        in0_d, in0_e, in0_c, in0_a, in1_d, in1_e, in1_c, in1_a,
        in2_d, in2_e, in2_c, in2_a, in3_d, in3_e, in3_c, in3_a,
        after_grads, after_in, gq_ref, gckv_ref, grad_qkv, sums, grad_x_ref,
        vec_own, vec_core, vec_sums, vec_in, sems, held_sems, send, recv,
    ) = rest
    phase = lax.axis_index("phase")
    ex = Exchange(send, recv)
    met = ex.greet()

    def moved(name):
        i = BACKWARD.index(name)
        return pltpu.make_async_copy(held_any[name], held[name], held_sems.at[i])

    waited = set()

    def get(name):
        if name not in waited:
            waited.add(name)
            moved(name).wait()
        return held[name]

    length, width = held["grad_low"].shape
    each = width // GROUPS

    def load(own_side, i):
        hidden, slopes = (hid_e_any, slope_e_any) if own_side == 0 else (hid_d_any, slope_d_any)

        @pl.when(phase == own_side)
        def _():
            pltpu.make_async_copy(up_own, up, sems.at[i]).start()
            pltpu.make_async_copy(down_own, down, sems.at[i + 1]).start()

        @pl.when(phase != own_side)
        def _():
            pltpu.make_async_copy(up_other, up, sems.at[i]).start()
            pltpu.make_async_copy(down_other, down, sems.at[i + 1]).start()

        pltpu.make_async_copy(hidden, hid, sems.at[i + 2]).start()
        pltpu.make_async_copy(slopes, slope, sems.at[i + 3]).start()

    def loaded(i):
        for k, (src, dst) in enumerate(
            ((up_own, up), (down_own, down), (hid_e_any, hid), (slope_e_any, slope))
        ):
            pltpu.make_async_copy(src, dst, sems.at[i + k]).wait()

    def puts(ref):
        def put_up(part, value):
            ref[0, :, :, :, :, part * each : (part + 1) * each, :] = value.astype(BF16).reshape(
                2, 2, 2, 2, each, width
            )

        def put_down(part, value):
            ref[1, part // 2, part % 2] = value.astype(BF16).reshape(2, 2, width // 4, width)

        return put_up, put_down

    def put_ff(half):
        def put(rows, value):
            sums[half, rows, :] = value

        return put

    def put_attention(rows, value):
        red_attention_ref[rows, :] = value

    cross_sum = red_cross_ref.at[phase]

    def put_cross_sum(rows, value):
        cross_sum[rows, :] = value

    batch_d = Batch(core_d, (in0_d, in1_d, in2_d, in3_d), put_ff(1), grad_d.at[phase])
    batch_c = Batch(core_c, (in0_c, in1_c, in2_c, in3_c), put_cross_sum, grad_c.at[phase])
    batch_e = Batch(core_e, (in0_e, in1_e, in2_e, in3_e), put_ff(0), grad_e.at[phase])
    batch_a = Batch(grad_a, (in0_a, in1_a, in2_a, in3_a), put_attention)
    chunks = [
        Chunk(ex, batch, *part)
        for batch, parts in zip((batch_d, batch_c, batch_e, batch_a), PARTS) for part in parts
    ]

    def go_on(place):
        for name in SCHEDULE[place]:
            chunks[name].advance()

    def halves_to_core(batch, ref, core_ref, part):
        rows = pl.ds(part * each, each)
        batch.arriving.append(ex.to_core_either(
            (ref.at[1, part // 2, part % 2], core_ref.at[part // 2, part % 2]),
            (ref.at[0, :, :, :, :, rows], core_ref.at[:, :, :, :, rows]),
        ))

    for name in BACKWARD[:4]:
        moved(name).start()
    load(1, 0)
    for name in BACKWARD[4:]:
        moved(name).start()
    grad_out = get("grad_low")[...] + get("grad_token")[...]
    grad_res, gain_grad, bias_grad = norm_back(get("res_d")[...], norms_ref[1, 0:1, :], grad_out)
    vec_own[2:3, :] = gain_grad
    vec_own[3:4, :] = bias_grad
    vec_own[6:8, :] = grad_delete_ref[0:2, :]
    cres = get("cres")[...]
    middle_low = norm_forward(cres, cgain_ref[...], cbias_ref[...]).astype(BF16)
    loaded(0)
    met()
    grad_middle = feed_back(
        grad_res, middle_low, up, down, hid, slope, *puts(grad_d),
        lambda part: halves_to_core(batch_d, grad_d, core_d, part),
    )
    load(0, 4)
    grad_res, gain_grad, bias_grad = norm_back(cres, cgain_ref[...], grad_middle)
    vec_own[4:5, :] = gain_grad
    vec_own[5:6, :] = bias_grad
    branch = grad_res.astype(BF16)

    def put_cross(first, value):
        half_rows = grad_c.shape[5]
        value = value.astype(BF16).reshape(2, 2, 2, 2, each, width)
        for at in range(0, each, 16):
            half, row = divmod(first + at, half_rows)
            grad_c[half, :, :, :, :, row : row + 16, :] = value[:, :, :, :, at : at + 16, :]

    put_cross(3 * each, mm_tn(get("cmixed")[...], branch))
    put_cross(4 * each, get("grad_place")[...])
    grad_mixed = mm_nt(branch, get("co_w")[...]).astype(BF16)
    cq_ref, ckv_ref = get("cq"), get("ckv")

    def put_q(pair, value):
        gq_ref[:, column(pair)] = value

    def put_k(pair, value):
        gckv_ref[:, column(pair)] = value

    def put_v(pair, value):
        gckv_ref[:, column(pair, width)] = value

    go_on(CROSS)

    def between(pair):
        go_on(CROSS + 1 + pair)

    attend_backward(
        lambda pair: cq_ref[:, column(pair)],
        lambda pair: ckv_ref[:, column(pair)],
        lambda pair: ckv_ref[:, column(pair, width)],
        lambda pair: grad_mixed[:, column(pair)],
        cols_ref[:, 2:3] == rows_ref[3:4, :],
        ctotals_ref, put_q, put_k, put_v, between,
    )
    grad_q = gq_ref[...]
    put_cross(0, mm_tn(get("after")[1].astype(BF16), grad_q))
    for part in range(2):
        put_cross((1 + part) * each, mm_tn(get("src")[...], gckv_ref[:, part * width : (part + 1) * width]))
    batch_c.arriving.append(ex.to_core(grad_c.at[1 - phase], core_c))
    after_grads[1] = grad_res + mm_nt(grad_q, get("cq_w")[...])
    go_on(CROSS_END)
    grad_src = mm_nt(gckv_ref[...], get("ckv_w")[...]).astype(BF16).astype(F32)
    grad_res, gain_grad, bias_grad = norm_back(get("res_e")[...], norms_ref[0, 0:1, :], grad_src)
    vec_own[0:1, :] = gain_grad
    vec_own[1:2, :] = bias_grad
    from_v = ex.to_core(vec_own, vec_core)
    loaded(4)

    go_on(ENCODER)

    def between(part):
        halves_to_core(batch_e, grad_e, core_e, part)
        go_on(ENCODER + 1 + part)

    after_grads[0] = feed_back(
        grad_res, get("after")[0].astype(BF16), up, down, hid, slope, *puts(grad_e), between
    )
    from_after = ex.to_core(after_grads.at[1 - phase], after_in)
    res_ref, mix_w_ref, qkv_ref, mixed_ref, x_ref = [get(n) for n in ("res", "mix_w", "qkv", "mixed", "x")]
    first_vectors = []
    for turn in range(2):
        row = phase if turn == 0 else 1 - phase
        rows = pl.ds(pl.multiple_of(row * length, length), length)
        if turn == 0:
            grad_after = after_grads[phase]
        else:
            from_after.wait_recv()
            grad_after = after_in[...]
        grad_res, gain_grad, bias_grad = norm_back(res_ref[rows, :], gain_ref[0:1, :], grad_after)
        first_vectors.append((gain_grad, bias_grad))
        grad_x_ref[rows, :] = grad_res
        branch = grad_res.astype(BF16)
        if turn == 0:
            first_branch, first_rows = branch, rows
        grad_mixed = mm_nt(branch, mix_w_ref[...]).astype(BF16)

        def put(offset):
            def store(pair, value):
                grad_qkv[rows, column(pair, offset)] = value

            return store

        go_on(SELF + 5 * turn)

        def between(pair):
            go_on(SELF + 5 * turn + 1 + pair)

        attend_backward(
            lambda pair: qkv_ref[rows, column(pair)],
            lambda pair: qkv_ref[rows, column(pair, width)],
            lambda pair: qkv_ref[rows, column(pair, 2 * width)],
            lambda pair: grad_mixed[:, column(pair)],
            jnp.where(row == 0, cols_ref[:, 0:1], cols_ref[:, 1:2])
            == jnp.where(row == 0, rows_ref[0:1, :], rows_ref[1:2, :]),
            totals_ref.at[row], put(0), put(width), put(2 * width), between,
        )
    shape = (2, 2, 2, 2, each, width)
    grad_mix = mm_tn(mixed_ref[first_rows, :], first_branch) + mm_tn(mixed_ref[rows, :], branch)
    grad_a[:, :, :, :, 3 * each :, :] = grad_mix.astype(BF16).reshape(shape)
    go_on(WEIGHTS)
    for part in range(3):
        cols = slice(part * width, (part + 1) * width)
        value = mm_tn(x_ref[...], grad_qkv[:, cols])
        grad_a[:, :, :, :, part * each : (part + 1) * each, :] = value.astype(BF16).reshape(shape)
        go_on(WEIGHTS + 1 + part)
    grad_x_ref[...] += mm_nt(grad_qkv[...], get("qkv_w")[...])
    grad_x_copy = pltpu.make_async_copy(grad_x_ref, grad_x_any, held_sems.at[len(BACKWARD)])
    grad_x_copy.start()
    from_v.wait_recv()
    vec_sums[0, 0:8, :] = vec_own[...] + vec_core[...]
    vec_sums[0, 8:9, :] = first_vectors[0][0] + first_vectors[1][0]
    vec_sums[0, 9:10, :] = first_vectors[0][1] + first_vectors[1][1]
    vec_sums[0, 10:16, :] = jnp.zeros((6, width), F32)
    tail = SCHEDULE[TAIL]
    left = [sum(chunks[item].batch is batch for item in tail) for batch in (batch_d, batch_c, batch_e)]
    vector_copies = []

    def vector_step(stage):
        if stage > 0:
            vector_copies[-1].wait_recv()
            vec_sums[stage] = vec_sums[stage - 1] + vec_in[stage - 1]
        if stage < 4:
            step = "xyab"[stage]
            vector_copies.append(ex.copy(vec_sums.at[stage], vec_in.at[stage], (ex.partner[step], phase)))

    vector_step(0)
    after_each = len(tail) // 5
    for at, name in enumerate(tail):
        chunks[name].advance()
        if at % after_each == after_each - 1 and len(vector_copies) < 4:
            vector_step(len(vector_copies))
        for i, batch in enumerate((batch_d, batch_c, batch_e)):
            left[i] -= chunks[name].batch is batch
        if chunks[name].batch is batch_c and left[1] == 0:
            cross_copy = ex.to_core(cross_sum, red_cross_ref.at[phase])
        if chunks[name].batch in (batch_d, batch_e) and left[0] + left[2] == 0:
            ff_copy = ex.to_core(sums.at[1 - phase], red_ff_ref.at[phase])
            red_ff_ref[phase] = sums[phase]
    vector_step(4)
    vectors_ref[...] = vec_sums[4]
    cross_copy.wait_recv()
    ff_copy.wait_recv()
    grad_x_copy.wait()
    ex.finish()


def unpack_kernel(
    ff_any, attention_any, cross_any, vectors_any, own_any, other_any, states_any,
    qkv_ref, mix_ref, up_ref, down_any, cq_ref, ckv_ref, co_ref, place_ref,
    gain_ref, bias_ref, cgain_ref, cbias_ref, delete_ref, token_any, grad_x_any,
    ff_ref, attention_ref, cross_halves_ref, vectors_ref, halves, states, sems, token_sems,
):
    phase, dp = lax.axis_index("phase"), lax.axis_index("dp")
    shard, pieces = own_any.shape[1], token_sems.shape[1]
    tall = own_any.shape[0] // pieces
    arrive, leave = [], []
    for i in range(pieces):
        rows = pl.ds(i * tall, tall)
        for side, (src, at) in enumerate(((own_any, phase), (other_any, 1 - phase))):
            arrive.append(pltpu.make_async_copy(src.at[rows], halves.at[side, rows], token_sems.at[side, i]))
            cols = pl.ds(pl.multiple_of(at * shard, shard), shard)
            leave.append(pltpu.make_async_copy(halves.at[side, rows], token_any.at[rows, cols], token_sems.at[side, i]))
    moves = [
        pltpu.make_async_copy(src, dst, sems.at[i])
        for i, (src, dst) in enumerate((
            (vectors_any, vectors_ref), (ff_any, ff_ref), (attention_any, attention_ref), (cross_any, cross_halves_ref),
        ))
    ]
    states_in = pltpu.make_async_copy(states_any, states, sems.at[5])
    states_out = pltpu.make_async_copy(states, grad_x_any, sems.at[5])
    for move in arrive[:2] + moves + [states_in] + arrive[2:]:
        move.start()
    for i in range(2 * pieces):
        arrive[i].wait()
        leave[i].start()
    states_in.wait()
    states_out.start()
    for move in moves:
        move.wait()
    down_move = pltpu.make_async_copy(ff_ref.at[1], down_any, sems.at[4])
    down_move.start()
    each = gain_ref.shape[2]
    vectors = vectors_ref[...]
    whole_width = vectors.shape[1]
    vectors = pltpu.roll(vectors, lax.rem(whole_width - dp * each, whole_width), 1)[:, :each]
    gain_ref[0, 0:1, :] = vectors[8:9]
    gain_ref[0, 1:2, :] = jnp.where(phase == 0, vectors[0:1], vectors[2:3])
    bias_ref[0, 0:1, :] = vectors[9:10]
    bias_ref[0, 1:2, :] = jnp.where(phase == 0, vectors[1:2], vectors[3:4])
    cgain_ref[...] = vectors[4:5]
    cbias_ref[...] = vectors[5:6]
    delete_ref[...] = vectors[6:8]
    width = mix_ref.shape[1]
    high = mix_ref.shape[0]
    for block in range(up_ref.shape[1] // width):
        up_ref[:, block * width : (block + 1) * width] = ff_ref[0, block * high : (block + 1) * high, :]
    for block in range(3):
        qkv_ref[:, block * width : (block + 1) * width] = attention_ref[block * high : (block + 1) * high, :]
    mix_ref[...] = attention_ref[3 * high :, :]
    half_rows = cross_halves_ref.shape[1]

    def cross(start):
        half, row = divmod(start, half_rows)
        return cross_halves_ref[half, row : row + 16, :]

    for start in range(0, 5 * high, 16):
        part, inner = start // high, slice(start % high, start % high + 16)
        if part == 0:
            cq_ref[inner, :] = cross(start)
        elif part < 3:
            ckv_ref[inner, (part - 1) * width : part * width] = cross(start)
        elif part == 3:
            co_ref[inner, :] = cross(start)
        else:
            value = cross(start)
            cols = place_ref.shape[1]
            at = start % high
            place_ref[at : at + 16, :] = value[:, :cols]
            place_ref[high + at : high + at + 16, :] = value[:, cols:]
    down_move.wait()
    states_out.wait()
    for move in leave:
        move.wait()


def whole(shape, dtype):
    return jax.ShapeDtypeStruct(shape, dtype)


def in_vmem(count):
    return [pl.BlockSpec(memory_space=VMEM)] * count


def swap(value):
    return lax.ppermute(value, "phase", [(0, 1), (1, 0)])


def unpacked(shards, height, columns):
    groups, rows, width = shards.shape
    blocks = columns // width
    parts = shards.reshape(groups, blocks, rows // blocks, width)
    return parts.transpose(0, 2, 1, 3).reshape(height, columns)


def token_head(cap, block_rows, low, flags, labels_all, flags_all, weight, weight_t, scale):
    length, width = low.shape
    dp = lax.axis_size("dp")
    shard = weight_t.shape[0]

    def choice(flags):
        place = jnp.cumsum(flags, axis=-1) - 1
        places = lax.broadcasted_iota(jnp.int32, flags.shape[:-1] + (cap, flags.shape[-1]), flags.ndim - 1)
        return (places == place[..., None, :]) & (flags[..., None, :] > 0)

    chosen = choice(flags)
    packed = mm(chosen.astype(BF16), low).astype(BF16)
    every = gather_blocks(packed).reshape(2 * dp * cap, width)
    labels = jnp.max(jnp.where(choice(flags_all), labels_all[:, None, :], -1), axis=-1)
    labels = labels.reshape(dp, 2, cap).transpose(1, 0, 2).reshape(2 * dp * cap)
    tall = block_rows
    count = 2 * dp * cap // tall
    probs, totals = pl.pallas_call(
        token_forward,
        grid=(count,),
        out_shape=(whole((count, shard, tall), BF16), whole((count, 1, tall), F32)),
        in_specs=[
            pl.BlockSpec((tall, width), lambda i: (i, 0)),
            pl.BlockSpec((shard, width), lambda i: (0, 0)),
        ],
        out_specs=(
            pl.BlockSpec((1, shard, tall), lambda i: (i, 0, 0)),
            pl.BlockSpec((1, 1, tall), lambda i: (i, 0, 0)),
        ),
        compiler_params=pltpu.CompilerParams(vmem_limit_bytes=48 * 1024 * 1024),
        name="token_forward",
    )(every, weight_t)
    shares = token_shares(totals)
    each = tall // cap
    grad_low, grad_weight = pl.pallas_call(
        partial(token_backward, scale),
        grid=(count,),
        out_shape=(whole((2 * dp, cap, width), BF16), whole((width, shard), F32)),
        in_specs=[
            pl.BlockSpec((1, shard, tall), lambda i: (i, 0, 0)),
            pl.BlockSpec((1, 1, tall), lambda i: (i, 0, 0)),
            pl.BlockSpec((1, 1, tall), lambda i: (i, 0, 0)),
            pl.BlockSpec((tall, width), lambda i: (i, 0)),
            pl.BlockSpec((shard, width), lambda i: (0, 0)),
        ],
        out_specs=(
            pl.BlockSpec((each, cap, width), lambda i: (i, 0, 0)),
            pl.BlockSpec((width, shard), lambda i: (0, 0)),
        ),
        scratch_shapes=[VMEM((shard, width), F32)],
        compiler_params=pltpu.CompilerParams(vmem_limit_bytes=48 * 1024 * 1024),
        name="token_backward",
    )(probs, shares, labels.reshape(count, 1, tall), every, weight_t)
    back = scatter_blocks(grad_low.reshape(2, dp, cap, width))
    return mm_tn(chosen.astype(BF16), back.astype(BF16)), grad_weight


def on_chips(
    inputs, segments, delete_target, place_target, token_target, token_mask,
    attention_in, attention_out, feedforward_in, feedforward_out, norm_gain, norm_bias,
    cross_query, cross_keyvalue, cross_out, cross_gain, cross_bias,
    head_delete, head_place, head_token,
):
    phase, dp_index = lax.axis_index("phase"), lax.axis_index("dp")
    count, length, width = inputs.shape[1:]
    hidden, classes = feedforward_in.shape[2], head_place.shape[1]
    each = width // GROUPS
    scale = float(count * length * GROUPS) ** (-0.5)
    any_space = pl.BlockSpec(memory_space=pl.ANY)
    is_enc = phase == 0
    states = inputs[0].reshape(count * length, width)
    up_own, down_own = feedforward_in[0], feedforward_out[0]
    qkv_w, mix_w = attention_in[0], attention_out[0]
    delete_weight = head_delete.T
    gain_row, bias_row = cross_gain[None, :], cross_bias[None, :]
    shapes = {
        "qkv": ((count * length, 3 * width), BF16), "mixed": ((count * length, width), BF16),
        "res": ((count * length, width), F32), "after": ((2, length, width), F32),
        "res_e": ((length, width), F32), "ckv": ((length, 2 * width), BF16), "cq": ((length, width), BF16),
        "cmixed": ((length, width), BF16), "cres": ((length, width), F32),
        "hid_e": ((length, hidden), BF16), "slope_e": ((length, hidden), BF16),
        "hid_d": ((length, hidden), BF16), "slope_d": ((length, hidden), BF16),
        "res_d": ((length, width), F32), "src": ((length, width), BF16), "low": ((length, width), BF16),
        "grad_low": ((length, width), F32), "grad_place": ((GROUPS, each, 2 * classes), BF16),
        "co_w": ((width, width), BF16), "cq_w": ((width, width), BF16), "ckv_w": ((width, 2 * width), BF16),
        "mix_w": ((width, width), BF16), "qkv_w": ((width, 3 * width), BF16), "x": ((count * length, width), BF16),
        "grad_token": ((length, width), F32),
    }
    outs = pl.pallas_call(
        partial(forward_kernel, scale),
        out_shape=(
            whole((8, length), F32), whole((length, 128), F32),
            whole((1, GROUPS * length), jnp.int32), whole((1, 2 * GROUPS * length), jnp.int32), whole((1, 1), F32),
            whole((2, 2, width), F32), whole((width, hidden), BF16), whole((hidden, width), BF16),
            whole((count, HEADS, length), F32), whole((HEADS, length), F32), whole((8, width), F32),
            *[whole(*shapes[name]) for name in FORWARD],
        ),
        in_specs=in_vmem(10) + [any_space] * 5 + in_vmem(3) + [any_space],
        out_specs=tuple(in_vmem(6) + [any_space] * 2 + in_vmem(3) + [any_space] * len(FORWARD)),
        scratch_shapes=[
            *[VMEM(*shapes[name]) for name in FORWARD],
            VMEM((2, width, hidden), BF16), VMEM((2, hidden, width), BF16),
            VMEM((width, width), BF16), VMEM((width, 2 * width), BF16), VMEM((width, width), BF16),
            VMEM((2 * width, classes), BF16), VMEM((length, width), F32),
            VMEM((2, length), jnp.int32), VMEM((4, 2, 2, 2, length), jnp.int32), VMEM((128, length), F32),
            pltpu.SemaphoreType.DMA((6,)), pltpu.SemaphoreType.DMA((len(FORWARD) + 2,)),
            pltpu.SemaphoreType.DMA((20,)), pltpu.SemaphoreType.DMA((20,)),
        ],
        compiler_params=pltpu.CompilerParams(
            collective_id=1, has_side_effects=True, vmem_limit_bytes=56 * 1024 * 1024
        ),
        name="forward",
    )(
        states, segments, delete_target, place_target, token_target, token_mask,
        qkv_w, mix_w, norm_gain[0], norm_bias[0], up_own, down_own,
        cross_query, cross_keyvalue, cross_out, gain_row, bias_row, delete_weight, head_place,
    )
    rows, cols, labels_small, labels_large, most, norms, up_other, down_other, totals, ctotals, grad_delete = outs[:11]
    saved = dict(zip(FORWARD, outs[11:]))
    grad_token, grad_weight = lax.cond(
        most[0, 0] < 0.0,
        lambda: token_chips(2, length // 2, saved["low"], rows, cols, labels_small, head_token),
        lambda: token_chips(3, length, saved["low"], rows, cols, labels_large, head_token),
    )
    other_weight = swap(grad_weight)
    saved.update(co_w=cross_out, cq_w=cross_query, ckv_w=cross_keyvalue, mix_w=mix_w, qkv_w=qkv_w, x=states, grad_token=grad_token)
    half_rows, ff_half, attention_rows = 5 * each // 2, hidden // GROUPS, 4 * each
    rows_of = (ff_half, ff_half, half_rows, attention_rows)

    def shards(tall, *lead):
        return VMEM(lead + (tall, width), BF16)

    grad_states, red_ff, red_attention, red_cross, vectors = pl.pallas_call(
        backward_kernel,
        out_shape=(
            whole((count * length, width), F32), whole((2, ff_half, width), F32),
            whole((attention_rows, width), F32), whole((2, half_rows, width), F32), whole((16, width), F32),
        ),
        in_specs=in_vmem(9) + [any_space] * (8 + len(BACKWARD)),
        out_specs=tuple([any_space] + in_vmem(4)),
        scratch_shapes=[
            *[VMEM(*shapes[name]) for name in BACKWARD],
            VMEM((width, hidden), BF16), VMEM((hidden, width), BF16),
            VMEM((length, hidden), BF16), VMEM((length, hidden), BF16),
            shards(ff_half, 2, 2, 2, 2, 2), shards(ff_half, 2, 2, 2, 2, 2), shards(half_rows, 2, 2, 2, 2, 2),
            shards(attention_rows, 2, 2, 2, 2),
            shards(ff_half, 2, 2, 2, 2), shards(ff_half, 2, 2, 2, 2), shards(half_rows, 2, 2, 2, 2),
            *[shards(tall, 2, 2, 2) for tall in rows_of],
            *[shards(tall, 2, 2) for tall in rows_of],
            *[shards(tall, 2) for tall in rows_of],
            *[shards(tall) for tall in rows_of],
            VMEM((2, length, width), F32), VMEM((length, width), F32),
            VMEM((length, width), BF16), VMEM((length, 2 * width), BF16), VMEM((count * length, 3 * width), BF16),
            VMEM((2, ff_half, width), F32), VMEM((count * length, width), F32),
            VMEM((8, width), F32), VMEM((8, width), F32),
            VMEM((5, 16, width), F32), VMEM((4, 16, width), F32),
            pltpu.SemaphoreType.DMA((8,)), pltpu.SemaphoreType.DMA((len(BACKWARD) + 1,)),
            pltpu.SemaphoreType.DMA((128,)), pltpu.SemaphoreType.DMA((128,)),
        ],
        compiler_params=pltpu.CompilerParams(
            collective_id=0, has_side_effects=True, vmem_limit_bytes=62 * 1024 * 1024
        ),
        name="backward",
    )(
        rows, cols, norms, gain_row, bias_row, ctotals, totals, grad_delete, norm_gain[0],
        up_own, up_other, down_own, down_other,
        saved["hid_e"], saved["slope_e"], saved["hid_d"], saved["slope_d"],
        *[saved[name] for name in BACKWARD],
    )
    vocabulary = head_token.shape[1]
    g_qkv, g_mix, g_up, g_down, g_cq, g_ckv, g_co, g_place, g_gain, g_bias, g_cgain, g_cbias, g_delete, g_token, grad_states = (
        pl.pallas_call(
            unpack_kernel,
            out_shape=(
                whole((each, 3 * width), F32), whole((each, width), F32), whole((each, hidden), F32),
                whole((hidden // GROUPS, width), F32), whole((each, width), F32), whole((each, 2 * width), F32),
                whole((each, width), F32), whole((2 * each, classes), F32),
                whole((1, 2, each), F32), whole((1, 2, each), F32), whole((1, each), F32), whole((1, each), F32),
                whole((2, each), F32), whole((width, vocabulary // GROUPS), F32), whole(grad_states.shape, F32),
            ),
            in_specs=[any_space] * 7,
            out_specs=tuple(in_vmem(3) + [any_space] + in_vmem(9) + [any_space] * 2),
            scratch_shapes=[
                VMEM(red_ff.shape, F32), VMEM(red_attention.shape, F32), VMEM(red_cross.shape, F32),
                VMEM(vectors.shape, F32), VMEM((2,) + grad_weight.shape, F32), VMEM(grad_states.shape, F32),
                pltpu.SemaphoreType.DMA((6,)), pltpu.SemaphoreType.DMA((2, 2)),
            ],
            compiler_params=pltpu.CompilerParams(vmem_limit_bytes=60 * 1024 * 1024),
            name="unpack",
        )(red_ff, red_attention, red_cross, vectors, grad_weight, other_weight, grad_states)
    )
    return (
        grad_states.reshape(1, count, length, width),
        g_qkv[None], g_mix[None], g_up[None], g_down[None], g_gain, g_bias,
        g_cq, g_ckv, g_co, g_cgain[0], g_cbias[0], g_delete.T, g_place, g_token,
    )


def on_any(
    inputs, segments, delete_target, place_target, token_target, token_mask,
    attention_in, attention_out, feedforward_in, feedforward_out, norm_gain, norm_bias,
    cross_query, cross_keyvalue, cross_out, cross_gain, cross_bias,
    head_delete, head_place, head_token,
):
    phase = lax.axis_index("phase")
    dp_index, dp = lax.axis_index("dp"), lax.axis_size("dp")
    count, length, width = inputs.shape[1:]
    assert count == 2
    hidden = feedforward_in.shape[2]
    scale = float(count * length * dp) ** (-0.5)
    any_space = pl.BlockSpec(memory_space=pl.ANY)
    params = pltpu.CompilerParams(vmem_limit_bytes=56 * 1024 * 1024)

    coded = jnp.where(token_mask == 1, token_target, -1)
    labels_all = lax.all_gather(coded, "dp", tiled=True)
    flags_all = (labels_all >= 0).astype(jnp.int32)

    def row_of(value):
        return lax.dynamic_index_in_dim(value, phase, 0, keepdims=False)

    own_norms = jnp.stack([norm_gain[0, 1], norm_bias[0, 1]])
    up_other, down_other = swap(feedforward_in[0]), swap(feedforward_out[0])
    other_norms = swap(own_norms)
    is_enc = phase == 0
    norms = jnp.concatenate(
        [jnp.where(is_enc, own_norms, other_norms), jnp.where(is_enc, other_norms, own_norms)]
    )
    ids = row_of(segments)
    own_ids = lax.dynamic_index_in_dim(segments, phase, 1, keepdims=False)
    states = inputs[0].reshape(count * length, width)

    qkv, mixed, res, totals, keep, send = pl.pallas_call(
        self_forward,
        out_shape=(
            whole((count * length, 3 * width), BF16),
            whole((count * length, width), BF16),
            whole((count * length, width), F32),
            whole((count, HEADS, length), F32),
            whole((length, width), F32),
            whole((length, width), F32),
        ),
        in_specs=in_vmem(7),
        out_specs=tuple(in_vmem(6)),
        compiler_params=params,
        name="self_forward",
    )(states, own_ids[:, :, None], own_ids[:, None, :], attention_in[0], attention_out[0], norm_gain[0], norm_bias[0])
    received = swap(send)

    ids_e, ids_d_row = ids[0][:, None], ids[1][None, :]
    pair_valid = jnp.concatenate([ids[1, :-1] == ids[1, 1:], jnp.zeros((1,), bool)])
    targets = jnp.stack(
        [row_of(delete_target), row_of(place_target), pair_valid.astype(jnp.int32)], axis=1
    )
    delete_weight = head_delete.T
    gain_row, bias_row = cross_gain[None, :], cross_bias[None, :]
    ff_scratch = [
        VMEM((width, hidden), BF16), VMEM((hidden, width), BF16),
        VMEM((width, hidden), BF16), VMEM((hidden, width), BF16),
    ]
    saved_shapes = (
        whole((length, width), F32),
        whole((length, width), F32),
        whole((length, width), F32),
        whole((length, 2 * width), BF16),
        whole((length, width), BF16),
        whole((length, width), BF16),
        whole((length, width), F32),
        whole((HEADS, length), F32),
        whole((length, hidden), BF16), whole((length, hidden), BF16),
        whole((length, hidden), BF16), whole((length, hidden), BF16),
        whole((length, width), F32),
        whole((length, width), BF16),
    )
    classes = head_place.shape[1]
    each = width // GROUPS
    outs = pl.pallas_call(
        partial(rows_forward, scale),
        out_shape=saved_shapes + (
            whole((length, width), BF16),
            whole((length, width), F32),
            whole((8, width), F32),
            whole((GROUPS, each, 2 * classes), BF16),
        ),
        in_specs=in_vmem(5) + [any_space] * 4 + in_vmem(8),
        out_specs=tuple(in_vmem(18)),
        scratch_shapes=ff_scratch + [pltpu.SemaphoreType.DMA((2, 2))],
        compiler_params=params,
        name="rows_forward",
    )(
        keep, received, ids_e, ids_d_row, targets,
        feedforward_in[0], up_other, feedforward_out[0], down_other, norms,
        cross_query, cross_keyvalue, cross_out, gain_row, bias_row, delete_weight, head_place,
    )
    saved = outs[:14]
    low, grad_low, grad_delete, grad_place = outs[14:]

    shard = head_token.shape[1] // (2 * dp)
    weight = lax.dynamic_slice_in_dim(head_token, (dp_index * 2 + phase) * shard, shard, 1)
    weight_t = weight.T
    flags = row_of(token_mask)

    def run_head(cap, block_rows):
        return token_head(cap, block_rows, low, flags, labels_all, flags_all, weight, weight_t, scale)

    small = length // 2
    fits = jnp.max(jnp.sum(flags_all, axis=1)) <= small
    grad_token, grad_weight = lax.cond(
        fits, lambda: run_head(small, 4 * small), lambda: run_head(length, 2 * length)
    )
    other_weight = swap(grad_weight)
    grad_head_token = jnp.concatenate(
        [jnp.where(is_enc, grad_weight, other_weight), jnp.where(is_enc, other_weight, grad_weight)], axis=1
    )

    each = width // GROUPS
    ff_rows = 2 * hidden // GROUPS
    keep, send, ff_own, ff_other, cross_shards, vectors = pl.pallas_call(
        rows_backward,
        out_shape=(
            whole((length, width), F32), whole((length, width), F32),
            whole((GROUPS, ff_rows, width), BF16), whole((GROUPS, ff_rows, width), BF16),
            whole((GROUPS, 5 * each, width), BF16), whole((8, width), F32),
        ),
        in_specs=in_vmem(4) + [any_space] * 4 + in_vmem(6 + 14 + 1),
        out_specs=(in_vmem(2) + [any_space] * 2 + in_vmem(2)),
        scratch_shapes=ff_scratch + [
            VMEM((GROUPS, ff_rows, width), BF16), VMEM((GROUPS, ff_rows, width), BF16),
            VMEM((length, width), F32), VMEM((length, width), F32),
            VMEM((length, width), BF16), VMEM((length, 2 * width), BF16),
            pltpu.SemaphoreType.DMA((2, 2)), pltpu.SemaphoreType.DMA((2,)),
        ],
        compiler_params=params,
        name="rows_backward",
    )(
        grad_low, grad_token, ids_e, ids_d_row,
        feedforward_in[0], up_other, feedforward_out[0], down_other, norms,
        cross_query, cross_keyvalue, cross_out, gain_row, bias_row, *saved, grad_place,
    )
    received = swap(send)
    ff_received = swap(ff_other)
    half_rows = 5 * each // 2
    cross_keep = lax.dynamic_slice_in_dim(cross_shards, phase * half_rows, half_rows, 1)
    cross_received = swap(lax.dynamic_slice_in_dim(cross_shards, (1 - phase) * half_rows, half_rows, 1))
    shared = jnp.concatenate([vectors[4:6], grad_delete[:2]])
    norm_own = jnp.where(is_enc, vectors[0:2], vectors[2:4])
    norm_other = jnp.where(is_enc, vectors[2:4], vectors[0:2])
    vector_received = swap(jnp.concatenate([norm_other, shared]))
    vector_sums = jnp.concatenate([norm_own, shared]) + vector_received

    grad_states, attention_shards, first_vectors = pl.pallas_call(
        self_backward,
        out_shape=(
            whole((count * length, width), F32), whole((GROUPS, 4 * each, width), BF16), whole((8, width), F32),
        ),
        in_specs=in_vmem(12),
        out_specs=tuple(in_vmem(3)),
        scratch_shapes=[VMEM((count * length, width), F32), VMEM((count * length, 3 * width), BF16)],
        compiler_params=params,
        name="self_backward",
    )(
        keep, received, states, own_ids[:, :, None], own_ids[:, None, :], attention_in[0], attention_out[0],
        norm_gain[0], qkv, mixed, res, totals,
    )

    all_vectors = jnp.stack([
        first_vectors[0], vector_sums[0], first_vectors[1], vector_sums[1],
        vector_sums[2], vector_sums[3], vector_sums[4], vector_sums[5],
    ])
    ff_sum = (ff_own.astype(F32) + ff_received.astype(F32)).astype(BF16)
    cross_sum = (cross_keep.astype(F32) + cross_received.astype(F32)).astype(BF16)
    cross_other = swap(cross_sum)
    cross_all = jnp.concatenate(
        [jnp.where(is_enc, cross_sum, cross_other), jnp.where(is_enc, cross_other, cross_sum)], axis=1
    )
    ff_up = hidden // width * each

    def spread(value):
        return lax.psum_scatter(value.astype(F32), "dp", scatter_dimension=0, tiled=True)

    g_qkv = spread(unpacked(attention_shards[:, : 3 * each], width, 3 * width))
    g_mix = spread(unpacked(attention_shards[:, 3 * each :], width, width))
    g_up = spread(unpacked(ff_sum[:, :ff_up], width, hidden))
    g_down = spread(unpacked(ff_sum[:, ff_up:], hidden, width))
    g_cq = spread(unpacked(cross_all[:, :each], width, width))
    g_ckv = spread(unpacked(cross_all[:, each : 3 * each], width, 2 * width))
    g_co = spread(unpacked(cross_all[:, 3 * each : 4 * each], width, width))
    place = cross_all[:, 4 * each :].reshape(GROUPS, each, 2, classes)
    g_place = spread(place.transpose(0, 2, 1, 3).reshape(2 * width, classes))
    vector_out = lax.psum_scatter(all_vectors, "dp", scatter_dimension=1, tiled=True)
    return (
        grad_states.reshape(1, count, length, width),
        g_qkv[None], g_mix[None], g_up[None], g_down[None],
        vector_out[None, 0:2], vector_out[None, 2:4],
        g_cq, g_ckv, g_co, vector_out[4], vector_out[5], vector_out[6:8].T, g_place, grad_head_token,
    )


def on_device(*args):
    chips = lax.axis_size("dp") == GROUPS and args[0].shape[1] == 2
    return on_chips(*args) if chips else on_any(*args)


def solution(mesh):
    layer, row = P("phase", None, None), P("dp", None)
    return jax.shard_map(
        on_device,
        mesh=mesh,
        in_specs=(P("phase", "dp", None, None), P("dp", None, None), row, row, row, row)
        + (layer,) * 6 + (P(),) * 8,
        out_specs=(P("phase", "dp", None, None),) + (P("phase", "dp", None),) * 4
        + (P("phase", None, "dp"),) * 2 + (row,) * 3 + (P("dp"),) * 2 + (row,) * 2 + (P(None, "dp"),),
        check_vma=False,
    )
```
